32 devices in a mesh: dp: 4 (over y, x), fsdp: 8 (over z, core).
Axes of the slice: x: 2, y: 2, z: 4, core: 2. Of those that a mesh axis runs over, the one named last changes fastest.
Arguments:
- images: bfloat16 [64, 2304, 320], P(('dp', 'fsdp')), may hold values from -6 to 6
- cotangent: bfloat16 [64, 2304, 320], P(('dp', 'fsdp')), may hold values from -6 to 6
- kv_sides: int32 [64], P(('dp', 'fsdp')), may hold values from 14 to 24, as said below
- params: float32 [1658880], P(('dp', 'fsdp')), may hold values from -2 to 2
- first_moment: float32 [1658880], P(('dp', 'fsdp')), may hold values from -1 to 1
- second_moment: float32 [1658880], P(('dp', 'fsdp')), may hold values from 0 to 1, as said below
Outputs:
- output: bfloat16 [64, 2304, 320], P(('dp', 'fsdp'))
- grad_images: float32 [64, 2304, 320], P(('dp', 'fsdp'))
- grad_norm: float32 [], replicated
- new_first: float32 [1658880], P(('dp', 'fsdp'))
- new_second: float32 [1658880], P(('dp', 'fsdp'))
- new_params: float32 [1658880], P(('dp', 'fsdp'))
The draws below stay inside these ranges and needn't reach their ends.
Inputs may be any that keep to these rules, and one draw needn't show every extreme that they name: `kv_sides`: each entry is 14, 20 or 24: token grids of 28, 40 or 48 per side at real sizes, the segment-3 grids of 448, 640 or 768 pixel images; some image has 24. `second_moment`: positive.
All inputs are finite; a program needn't handle non-finite values.
Results may differ from the reference program's by a relative error of at most 0.0089.
Values may be sent and summed in bfloat16 or wider, within the bound.
A program may use at most 256 MiB of HBM per device.

```python
import math
import jax
import jax.numpy as jnp
from jax import lax

HEADS = 5
HEAD_DIM = 64
D = 320
FF = 1280
GRID = 48
KV = 24
IMAGES = 64
STEP = 10
PRAW = 1656000
PTOT = 1658880


def draw_kv_sides(key, part):
    key = jax.random.fold_in(key, 11)
    levels = jax.random.randint(key, (IMAGES,), 0, 3)
    chosen = jax.random.randint(jax.random.fold_in(key, 1), (), 0, IMAGES)
    levels = jnp.where(jnp.arange(IMAGES) == chosen, 2, levels)
    sides = jnp.where(levels == 0, KV * 7 // 12, jnp.where(levels == 1, KV * 10 // 12, KV))
    return sides.astype(jnp.int32)


def draw_params(key, part):
    key = jax.random.fold_in(key, 7)
    sections = [(D, 1.0, 0.1), (D, 0.0, 0.1), (D * D, 0.0, 1.0 / math.sqrt(D)), (D, 0.0, 0.1), (4 * D * D, 0.0, 1.0 / math.sqrt(4 * D)), (D, 0.0, 0.1), (D, 1.0, 0.1), (D, 0.0, 0.1), (2 * D * D, 0.0, 1.0 / math.sqrt(D)), (D, 0.0, 0.1), (D * D, 0.0, 3.0 / math.sqrt(D)), (D, 0.0, 0.1), (D, 1.0, 0.1), (D, 0.0, 0.1), (D * FF, 0.0, 1.0 / math.sqrt(D)), (FF, 0.0, 0.1), (9 * FF, 0.0, 1.0 / 3.0), (FF, 0.0, 0.1), (FF * D, 0.0, 1.0 / math.sqrt(FF)), (D, 0.0, 0.1), (PTOT - PRAW, 0.0, 0.02)]
    pieces = []
    for index, section in enumerate(sections):
        count, centre, spread = section
        noise = jax.random.truncated_normal(jax.random.fold_in(key, index), -4.0, 4.0, (count,), jnp.float32)
        pieces.append(centre + spread * noise)
    return jnp.concatenate(pieces).astype(jnp.float32)


def draw_first_moment(key, part):
    key = jax.random.fold_in(key, 21)
    noise = jax.random.truncated_normal(key, -4.0, 4.0, (PTOT,), jnp.float32)
    return 0.111 / math.sqrt(PRAW) * noise


def draw_second_moment(key, part):
    key = jax.random.fold_in(key, 31)
    factor = jnp.exp(jax.random.uniform(key, (PTOT,), jnp.float32, 0.0, math.log(4.0)))
    return 0.001 / PRAW * factor


def steps_of(rng, extent, cuts, least, largest):
    def one(dim, shards_of):
        steps = jax.random.uniform(jax.random.fold_in(jax.random.fold_in(rng, 6), dim), (shards_of,), jnp.float32, least / len(cuts), largest / len(cuts))
        return jnp.repeat(jnp.exp(steps), extent[dim] // shards_of).reshape((-1,) + (1,) * (len(extent) - dim - 1))

    level = one(*cuts[0])
    for cut in cuts[1:]:
        level = level * one(*cut)
    return level


def normal_values(stream_key, dims, width, bound, shards=(), kind=jnp.bfloat16):
    array = jax.random.normal(stream_key, dims, jnp.float32) * width
    if len(shards) > 0:
        array = steps_of(stream_key, dims, shards, -0.22, 0.18) * array
    return jnp.clip(array, min=-bound, max=bound).astype(kind)


def setup_inputs(seed: int = 0) -> dict:
    seeds = jax.random.split(jax.random.key(seed), 7)
    return {
        "images": normal_values(seeds[0], (IMAGES, GRID * GRID, D), 1.0, 6.0, ((0, 32),)),
        "cotangent": normal_values(seeds[1], (IMAGES, GRID * GRID, D), 1.0, 6.0, ((0, 32),)),
        "kv_sides": draw_kv_sides(jax.random.fold_in(seeds[6], 71), 0),
        "params": draw_params(jax.random.fold_in(seeds[6], 71), 0),
        "first_moment": draw_first_moment(jax.random.fold_in(seeds[6], 71), 0),
        "second_moment": draw_second_moment(jax.random.fold_in(seeds[6], 71), 0),
    }


CLIP_NORM = 1.0
BETA_FIRST = 0.9
BETA_SECOND = 0.999
RATE = 0.04
DECAY = 0.05
EPSILON = 1e-08
PRECISE = lax.Precision.HIGHEST

@jax.custom_vjp
def low(v):
    return lax.optimization_barrier(v.astype(jnp.bfloat16)).astype(jnp.float32)

@jax.custom_vjp
def low_back(v):
    return v

def low_keep(v):
    return (low(v), None)

def low_pass(kept, grad):
    return (grad,)

def back_keep(v):
    return (v, None)

def back_low(kept, grad):
    return (low(grad),)
low.defvjp(low_keep, low_pass)
low_back.defvjp(back_keep, back_low)

def layout_shapes(model_width, hidden_width):
    return [(model_width,), (model_width,), (model_width, model_width), (model_width,), (4 * model_width, model_width), (model_width,), (model_width,), (model_width,), (model_width, 2 * model_width), (model_width,), (model_width, model_width), (model_width,), (model_width,), (model_width,), (model_width, hidden_width), (hidden_width,), (9, hidden_width), (hidden_width,), (hidden_width, model_width), (model_width,)]

def unpack_params(flat, model_width, hidden_width):
    pieces = []
    offset = 0
    for shape in layout_shapes(model_width, hidden_width):
        count = math.prod(shape)
        pieces.append(flat[offset:offset + count].reshape(shape))
        offset += count
    return pieces

def layer_norm(values, gain, shift):
    centred = values - lax.optimization_barrier(jnp.mean(values, axis=-1, keepdims=True))
    variance = lax.optimization_barrier(jnp.mean(centred * centred, axis=-1, keepdims=True))
    return centred * lax.rsqrt(variance + 1e-06) * gain + shift

def matmul(left, right):
    return jnp.dot(left, right, precision=PRECISE)

def image_forward(pieces, image, side):
    pre_gain, pre_shift, query_weight, query_bias, reduce_weight, reduce_bias, reduce_gain, reduce_shift, pair_weight, value_bias, output_weight, output_bias, mlp_gain, mlp_shift, expand_weight, expand_bias, spatial_weight, spatial_bias, shrink_weight, shrink_bias = pieces
    model_width = image.shape[1]
    tokens_image = GRID * GRID
    positions = jnp.arange(tokens_image, dtype=jnp.int32)
    row_mask = ((positions // GRID < 2 * side) & (positions % GRID < 2 * side)).astype(jnp.float32)[:, None]
    cells = jnp.arange(KV * KV, dtype=jnp.int32)
    key_mask = (cells // KV < side) & (cells % KV < side)
    inputs = image * row_mask
    pre = low(layer_norm(inputs, pre_gain, pre_shift))
    queries = low(low_back(matmul(pre, query_weight) + query_bias))
    patches = pre.reshape(KV, 2, KV, 2, model_width).transpose(0, 2, 1, 3, 4).reshape(KV * KV, 4 * model_width)
    reduced = low_back(matmul(patches, reduce_weight) + reduce_bias)
    memory = low(layer_norm(reduced, reduce_gain, reduce_shift))
    paired = matmul(memory, pair_weight)
    keys = low(low_back(paired[:, :model_width]))
    values = low(low_back(paired[:, model_width:] + value_bias))
    query_heads = queries.reshape(tokens_image, HEADS, HEAD_DIM)
    key_heads = keys.reshape(KV * KV, HEADS, HEAD_DIM)
    value_heads = values.reshape(KV * KV, HEADS, HEAD_DIM)
    scores = jnp.einsum('shd,khd->hsk', query_heads, key_heads, precision=PRECISE) * HEAD_DIM ** (-0.5)
    scores = low_back(scores)
    scores = jnp.where(key_mask[None, None, :], scores, -1e+30)
    attend = low(jax.nn.softmax(scores, axis=-1))
    mixed = jnp.einsum('hsk,khd->shd', attend, value_heads, precision=PRECISE).reshape(tokens_image, model_width)
    mixed = low(low_back(mixed))
    middle = inputs + low_back(matmul(mixed, output_weight) + output_bias)
    post = low(layer_norm(middle, mlp_gain, mlp_shift))
    expanded = low_back(matmul(post, expand_weight) + expand_bias)
    filled = low(expanded * row_mask)
    hidden_width = filled.shape[1]
    padded = jnp.pad(filled.reshape(GRID, GRID, hidden_width), ((1, 1), (1, 1), (0, 0)))
    conv = jnp.zeros((GRID, GRID, hidden_width), jnp.float32) + spatial_bias
    for index in range(9):
        row_step = index // 3
        col_step = index % 3
        conv = conv + spatial_weight[index] * padded[row_step:row_step + GRID, col_step:col_step + GRID]
    activated = low(jax.nn.gelu(conv.reshape(tokens_image, hidden_width), approximate=True))
    shrunk = low_back(matmul(activated, shrink_weight) + shrink_bias)
    return (middle + shrunk) * row_mask

def reference(images, cotangent, kv_sides, params, first_moment, second_moment):
    model_width = images.shape[2]
    hidden_width = 4 * model_width
    image_values = images.astype(jnp.float32)
    grad_values = cotangent.astype(jnp.float32)

    def forward(flat, inputs):
        pieces = unpack_params(low(flat), model_width, hidden_width)

        def one_image(pair):
            return image_forward(pieces, pair[0], pair[1])
        return lax.map(jax.checkpoint(one_image), (inputs, kv_sides))
    outputs, pullback = jax.vjp(forward, params, image_values)
    grads, grad_images = pullback(grad_values)
    grad_norm = jnp.sqrt(jnp.sum(grads * grads))
    clipped = grads * jnp.minimum(1.0, CLIP_NORM / (grad_norm + 1e-06))
    new_first = BETA_FIRST * first_moment + (1.0 - BETA_FIRST) * clipped
    new_second = BETA_SECOND * second_moment + (1.0 - BETA_SECOND) * clipped * clipped
    first_hat = new_first / (1.0 - BETA_FIRST ** STEP)
    second_hat = new_second / (1.0 - BETA_SECOND ** STEP)
    new_params = params - RATE * (first_hat / (jnp.sqrt(second_hat) + EPSILON) + DECAY * params)
    return (outputs.astype(jnp.bfloat16), grad_images, grad_norm, new_first, new_second, new_params)
```

```python
from functools import partial
import math

import jax
import jax.numpy as jnp
import numpy as np
from jax import lax
from jax.experimental import pallas as pl
from jax.experimental.pallas import tpu as pltpu
from jax.sharding import PartitionSpec as P

HEADS = 5
HEAD_DIM = 64
GRID = 48
KV = 24
STEP = 10

CLIP_NORM = 1.0
BETA_FIRST = 0.9
BETA_SECOND = 0.999
RATE = 0.04
DECAY = 0.05
EPSILON = 1e-08

F32 = jnp.float32
BF = jnp.bfloat16
NN = (((1,), (0,)), ((), ()))
NT = (((1,), (1,)), ((), ()))
TOKENS = GRID * GRID
KEYS = KV * KV
PITCH = GRID + 8
EXT = 16
LOG2E = math.log2(math.e)
QUERY_SCALE = HEAD_DIM**-0.5 * LOG2E
GELU_A = math.sqrt(2.0 / math.pi)
GELU_B = GELU_A * 0.044715
VMEM_BYTES = 63 * 1024 * 1024


def mm(left, right, dims=NN):
    return lax.dot_general(left, right, dims, preferred_element_type=F32)


def patch_order():
    matrix = np.zeros((8 * GRID, 8 * GRID), np.float32)
    for p in range(4):
        for a in range(4):
            for b in range(KV):
                matrix[p * 96 + a * KV + b, (2 * a + p // 2) * GRID + 2 * b + p % 2] = 1.0
    return matrix


def fold_rows(x):
    return jnp.sum(x.reshape(x.shape[0] // 8, 8, x.shape[1]), axis=0)


def norm_columns(x):
    scale = 1.0 / x.shape[0]
    centred = x - jnp.sum(x, axis=0, keepdims=True) * scale
    rstd = lax.rsqrt(jnp.sum(centred * centred, axis=0, keepdims=True) * scale + 1e-06)
    return centred * rstd, rstd


def norm_columns_back(normed, rstd, scaled):
    scale = 1.0 / scaled.shape[0]
    plain = jnp.sum(scaled, axis=0, keepdims=True) * scale
    mixed = jnp.sum(scaled * normed, axis=0, keepdims=True) * scale
    return rstd * (scaled - plain - normed * mixed)


def norm_rows(x):
    centred = x - jnp.mean(x, axis=-1, keepdims=True)
    rstd = lax.rsqrt(jnp.mean(centred * centred, axis=-1, keepdims=True) + 1e-06)
    return centred * rstd, rstd


def norm_rows_back(normed, rstd, scaled):
    plain = jnp.mean(scaled, axis=-1, keepdims=True)
    mixed = jnp.mean(scaled * normed, axis=-1, keepdims=True)
    return rstd * (scaled - plain - normed * mixed)


def first_row(row, rows=EXT):
    index = lax.broadcasted_iota(jnp.int32, (rows, row.shape[-1]), 0)
    return jnp.where(index == 0, row, 0.0)


def three_parts(x):
    high = x.astype(BF).astype(F32)
    middle = (x - high).astype(BF).astype(F32)
    return high, middle, (x - high - middle).astype(BF).astype(F32)


def whole(x):
    zeros = (0,) * len(x.shape)
    return pl.BlockSpec(x.shape, lambda *_: zeros)


def per_image(x, **kwargs):
    zeros = (0,) * (len(x.shape) - 1)
    return pl.BlockSpec((1,) + tuple(x.shape[1:]), lambda i, *_: (i,) + zeros, **kwargs)


def key_columns(ref, side, h_range, ones_from, ones_to, with_mask):
    lane = lax.broadcasted_iota(jnp.int32, (KV, 64), 1)
    cell = lax.broadcasted_iota(jnp.int32, (KV, 64), 0)
    ones = jnp.where((lane >= ones_from) & (lane <= ones_to), 1.0, 0.0)
    for a in range(KV):
        block = ones
        if with_mask:
            bias = jnp.where((cell < side) & (a < side), 0.0, -1e30)
            block = jnp.where(lane == 0, bias, ones)
        block = block.astype(BF)
        for h in h_range:
            ref[h, a * KV : (a + 1) * KV, 64:128] = block


def attention_forward_kernel(
    sides, images, mask, perm, vec, rows, wqt, wr, wk, wvt, wot,
    pre, patches, reduced, memory, mixed, lse, middle, post,
    key_ref, value_ref,
):
    i = pl.program_id(0)
    width = images.shape[1]

    def first_norm(t, _):
        for u in range(3):
            at = pl.ds(pl.multiple_of(t * 384 + u * 128, 128), 128)
            x = images[0, :, at].astype(F32) * mask[0, 0:1, at]
            normed, _unused = norm_columns(x)
            pre[0, 0:width, at] = (normed * vec[0] + vec[1]).astype(BF)
            pre[0, width : width + EXT, at] = first_row(jnp.ones((1, 128), F32)).astype(BF)
        at = pl.ds(pl.multiple_of(t * 384, 128), 384)
        picked = mm(perm[...], pre[0, 0:width, at], NT).astype(BF)
        for p in range(4):
            patches[0, p, pl.ds(pl.multiple_of(t * 96, 32), 96), :] = picked[p * 96 : (p + 1) * 96]
        return 0

    lax.fori_loop(0, TOKENS // 384, first_norm, 0)

    total = rows[0:1, :]
    for p in range(4):
        total = total + mm(patches[0, p], wr[p])
    reduced[0] = total
    normed, _unused = norm_rows(total)
    memory[0, :, 0:width] = (normed * rows[1:2, :] + rows[2:3, :]).astype(BF)
    lane = lax.broadcasted_iota(jnp.int32, (KEYS, 64), 1)
    memory[0, :, width : width + 64] = jnp.where(lane == 0, 1.0, 0.0).astype(BF)
    keys = mm(memory[0, :, 0:width], wk[...]).astype(BF)
    key_columns(key_ref, sides[i], range(HEADS), 1, 0, True)
    values = mm(wvt[...], memory[0], NT).astype(BF)
    ones = first_row(jnp.ones((1, KEYS), F32)).astype(BF)
    for h in range(HEADS):
        at = slice(h * HEAD_DIM, (h + 1) * HEAD_DIM)
        key_ref[h, :, 0:HEAD_DIM] = keys[:, at]
        value_ref[h, 0:HEAD_DIM, :] = values[at]
        value_ref[h, HEAD_DIM : HEAD_DIM + EXT, :] = ones
    mixed[0, width : width + EXT, :] = first_row(jnp.ones((1, TOKENS), F32)).astype(BF)
    queries = (mm(wqt[...], pre[0]) * QUERY_SCALE).astype(BF)
    tail = first_row(jnp.ones((1, TOKENS), F32), 64).astype(BF)
    for h in range(HEADS):
        at = slice(h * HEAD_DIM, (h + 1) * HEAD_DIM)
        scores = mm(key_ref[h], jnp.concatenate([queries[at], tail], axis=0))
        top = jnp.max(scores, axis=0, keepdims=True)
        weights = jnp.exp2(scores - top).astype(BF)
        out = mm(value_ref[h], weights)
        total = out[HEAD_DIM : HEAD_DIM + 1]
        mixed[0, at, :] = (out[0:HEAD_DIM] * (1.0 / total)).astype(BF)
        lse[0, h : h + 1, :] = top + jnp.log2(total)

    def second_norm(t, _):
        at = pl.ds(pl.multiple_of(t * 384, 128), 384)
        branch = mm(wot[...], mixed[0, :, at])
        for u in range(3):
            at = pl.ds(pl.multiple_of(t * 384 + u * 128, 128), 128)
            here = mask[0, 0:1, at]
            x = images[0, :, at].astype(F32) * here + branch[:, u * 128 : (u + 1) * 128]
            middle[0, :, at] = x
            normed, _unused = norm_columns(x)
            post[0, 0:width, at] = ((normed * vec[2] + vec[3]) * here).astype(BF)
            post[0, width : width + EXT, at] = first_row(here).astype(BF)
        return 0

    lax.fori_loop(0, TOKENS // 384, second_norm, 0)


def attention_forward(sides, images, mask, perm, vec, rows, wqt, wr, wk, wvt, wot):
    n, width, tokens = images.shape
    shape = jax.ShapeDtypeStruct
    outs = [
        shape((n, width + EXT, tokens), BF),
        shape((n, 4, KEYS, width), BF),
        shape((n, KEYS, width), F32),
        shape((n, KEYS, width + 64), BF),
        shape((n, width + EXT, tokens), BF),
        shape((n, 8, tokens), F32),
        shape((n, width, tokens), F32),
        shape((n, width + EXT, tokens), BF),
    ]
    weights = (perm, vec, rows, wqt, wr, wk, wvt, wot)
    return pl.pallas_call(
        attention_forward_kernel,
        grid_spec=pltpu.PrefetchScalarGridSpec(
            num_scalar_prefetch=1,
            grid=(n,),
            in_specs=[per_image(images), per_image(mask)] + [whole(x) for x in weights],
            out_specs=[per_image(x) for x in outs],
            scratch_shapes=[
                pltpu.VMEM((HEADS, KEYS, 128), BF),
                pltpu.VMEM((HEADS, HEAD_DIM + EXT, KEYS), BF),
            ],
        ),
        out_shape=outs,
        compiler_params=pltpu.CompilerParams(vmem_limit_bytes=VMEM_BYTES),
        name="attention_forward",
    )(sides, images, mask, *weights)


def feed_forward_kernel(
    post, cot, mask, middle, we, wst, taps, vec,
    output, grad_post, gwe, gwst, gtaps, gbias,
    padded, grad_padded, grad_act, act, grad_exp, post_rows, out_grad, out_grad_rows, total,
):
    i = pl.program_id(0)
    j = pl.program_id(1)
    width, block = wst.shape
    halves = block // 128
    rows = 8
    chunks = GRID // rows
    span = rows * GRID
    cols = 16

    @pl.when((i == 0) & (j == 0))
    def _():
        for ref in (padded, grad_padded, gwe, gwst, gtaps, gbias, post_rows):
            ref[...] = jnp.zeros_like(ref)

    @pl.when(j == 0)
    def _():
        for t in range(TOKENS // 384):
            at = slice(t * 384, (t + 1) * 384)
            grad = cot[0, :, at].astype(F32) * mask[0, 0:1, at]
            gbias[...] += grad[:, 0:128] + grad[:, 128:256] + grad[:, 256:384]
            grad = grad.astype(BF)
            out_grad[:, at] = grad
            out_grad_rows[at, :] = grad.T
            post_rows[at, 0 : width + EXT] = post[0, :, at].T

    def expand(t, _):
        at = pl.ds(pl.multiple_of(t * span, span), span)
        filled = mm(post_rows[at, :], we[...]).astype(BF).astype(F32)
        for h in range(halves):
            for r in range(rows):
                start = pl.multiple_of((t * rows + r + 1) * PITCH + 8, 8)
                padded[h, pl.ds(start, GRID), :] = filled[
                    r * GRID : (r + 1) * GRID, h * 128 : (h + 1) * 128
                ]
        grad_act[at, :] = mm(out_grad_rows[at, :], wst[...])
        return 0

    lax.fori_loop(0, chunks, expand, 0)

    def convolve(t, _):
        for h in range(halves):
            hs = slice(h * 128, (h + 1) * 128)
            w = [jnp.broadcast_to(taps[k : k + 1, hs], (cols, 128)) for k in range(10)]
            sums = jnp.zeros((8, 128), F32)
            for ct in range(GRID // cols):
                open_rows = {}
                for q in range(-1, rows + 1):
                    base = (t * rows + q + 1) * PITCH + 8 + ct * cols
                    x = [padded[h, pl.ds(base + s, cols), :] for s in (-1, 0, 1)]
                    for a in (2, 1, 0):
                        r = q + 1 - a
                        if 0 <= r < rows:
                            part = w[3 * a] * x[0] + w[3 * a + 1] * x[1] + w[3 * a + 2] * x[2]
                            open_rows[r] = part + open_rows.get(r, w[9])
                    r = q - 1
                    if r < 0:
                        continue
                    conv = open_rows.pop(r)
                    square = conv * conv
                    half = 0.5 * jnp.tanh(conv * (GELU_B * square + GELU_A)) + 0.5
                    gelu = conv * half
                    slope = half + gelu * (1.0 - half) * ((6.0 * GELU_B) * square + 2.0 * GELU_A)
                    at = pl.ds(pl.multiple_of((t * rows + r) * GRID + ct * cols, cols), cols)
                    act[at, hs] = gelu.astype(BF)
                    grad = grad_act[at, hs] * slope
                    start = pl.multiple_of((t * rows + r + 1) * PITCH + 8 + ct * cols, 8)
                    grad_padded[h, pl.ds(start, cols), :] = grad
                    sums = sums + grad[0:8] + grad[8:16]
            js = pl.ds(pl.multiple_of(j * block + h * 128, 128), 128)
            gtaps[72:80, js] += sums
        return 0

    lax.fori_loop(0, chunks, convolve, 0)

    def convolve_back(t, _):
        for h in range(halves):
            hs = slice(h * 128, (h + 1) * 128)
            w = [jnp.broadcast_to(taps[k : k + 1, hs], (cols, 128)) for k in range(9)]
            sums = [jnp.zeros((8, 128), F32) for _ in range(9)]
            for ct in range(GRID // cols):
                open_rows = {}
                x = {}
                for q in range(-1, rows + 1):
                    base = (t * rows + q + 1) * PITCH + 8 + ct * cols
                    grads = [grad_padded[h, pl.ds(base + 1 - b, cols), :] for b in range(3)]
                    if q + 1 < rows:
                        start = pl.multiple_of((t * rows + q + 2) * PITCH + 8 + ct * cols, 8)
                        x[q + 1] = padded[h, pl.ds(start, cols), :]
                    for a in range(3):
                        r = q + a - 1
                        if not 0 <= r < rows:
                            continue
                        part = w[3 * a] * grads[0] + w[3 * a + 1] * grads[1] + w[3 * a + 2] * grads[2]
                        open_rows[r] = part + open_rows[r] if r in open_rows else part
                        for b in range(3):
                            product = x[r] * grads[b]
                            sums[3 * a + b] = sums[3 * a + b] + product[0:8] + product[8:16]
                    r = q - 1
                    if r >= 0:
                        at = pl.ds(pl.multiple_of((t * rows + r) * GRID + ct * cols, cols), cols)
                        grad_exp[at, hs] = open_rows.pop(r).astype(BF)
                        x.pop(r)
            js = pl.ds(pl.multiple_of(j * block + h * 128, 128), 128)
            for k in range(9):
                gtaps[8 * k : 8 * k + 8, js] += sums[k]
        return 0

    lax.fori_loop(0, chunks, convolve_back, 0)

    js = pl.ds(pl.multiple_of(j * block, block), block)
    gwst[:, js] += mm(out_grad[...], act[...])
    gwe[:, js] += mm(post[0], grad_exp[...])
    shrunk = mm(wst[...], act[...], NT)
    back = mm(we[0:width, :], grad_exp[...], NT)

    @pl.when(j == 0)
    def _():
        total[...] = shrunk
        grad_post[0] = back

    @pl.when(j != 0)
    def _():
        total[...] += shrunk
        grad_post[0] += back

    @pl.when(j == pl.num_programs(1) - 1)
    def _():
        for t in range(TOKENS // 128):
            at = slice(t * 128, (t + 1) * 128)
            output[0, :, at] = ((middle[0, :, at] + total[:, at] + vec[4]) * mask[0, 0:1, at]).astype(BF)


def feed_forward(post, cot, mask, middle, we, wst, taps, vec, block=256):
    n, width, tokens = cot.shape
    hidden = wst.shape[1]
    shape = jax.ShapeDtypeStruct
    outs = [
        shape((n, width, tokens), BF),
        shape((n, width, tokens), F32),
        shape((width + EXT, hidden), F32),
        shape((width, hidden), F32),
        shape((80, hidden), F32),
        shape((width, 128), F32),
    ]
    one = {"pipeline_mode": pl.Buffered(1)}
    columns = lambda x: pl.BlockSpec((x.shape[0], block), lambda i, j: (0, j))
    return pl.pallas_call(
        feed_forward_kernel,
        grid=(n, hidden // block),
        in_specs=[per_image(post), per_image(cot), per_image(mask), per_image(middle, **one)]
        + [columns(we), columns(wst), columns(taps), whole(vec)],
        out_specs=[per_image(x) for x in outs[:2]] + [whole(x) for x in outs[2:]],
        out_shape=outs,
        scratch_shapes=[
            pltpu.VMEM((block // 128, (GRID + 2) * PITCH + 8, 128), F32),
            pltpu.VMEM((block // 128, (GRID + 2) * PITCH + 8, 128), F32),
            pltpu.VMEM((tokens, block), F32),
            pltpu.VMEM((tokens, block), BF),
            pltpu.VMEM((tokens, block), BF),
            pltpu.VMEM((tokens, width + 64), BF),
            pltpu.VMEM((width, tokens), BF),
            pltpu.VMEM((tokens, width), BF),
            pltpu.VMEM((width, tokens), F32),
        ],
        compiler_params=pltpu.CompilerParams(vmem_limit_bytes=VMEM_BYTES),
        name="feed_forward",
    )(post, cot, mask, middle, we, wst, taps, vec)


def attention_backward_kernel(
    sides, images, cot, mask, pre, patches, reduced, memory, mixed, lse, middle, grad_post,
    perm, vec, rows, wq, wqt, wr, wk, wv, wvt, wo,
    grad_images, gwo, gwq, gpair, gwr, gcols, grows,
    branch, grad_mixed, queries, grad_queries, key_ref, value_ref, keys_t, grad_keys, grad_values, grad_patches,
):
    i = pl.program_id(0)
    width = images.shape[1]

    @pl.when(i == 0)
    def _():
        for ref in (gwo, gwq, gpair, gwr, gcols, grows):
            ref[...] = jnp.zeros_like(ref)

    def mlp_norm_back(t, _):
        gain = shift = jnp.zeros((width, 128), F32)
        for u in range(3):
            at = pl.ds(pl.multiple_of(t * 384 + u * 128, 128), 128)
            here = mask[0, 0:1, at]
            normed, rstd = norm_columns(middle[0, :, at])
            grad = grad_post[0, :, at] * here
            gain = gain + grad * normed
            shift = shift + grad
            grad = cot[0, :, at].astype(F32) * here + norm_columns_back(normed, rstd, grad * vec[2])
            grad_images[0, :, at] = grad
            branch[:, at] = grad.astype(BF)
        gcols[2] += gain
        gcols[3] += shift
        return 0

    lax.fori_loop(0, TOKENS // 384, mlp_norm_back, 0)
    gwo[...] += mm(mixed[0], branch[...], NT)
    grad_mixed[...] = mm(wo[...], branch[...]).astype(BF)
    queries[...] = (mm(wqt[...], pre[0]) * QUERY_SCALE).astype(BF)
    keys = mm(memory[0, :, 0:width], wk[...]).astype(BF)
    keys_t[...] = keys.T
    values = mm(wvt[...], memory[0], NT).astype(BF).T
    key_columns(key_ref, sides[i], range(HEADS), 1, 3, True)
    key_columns(value_ref, sides[i], range(HEADS), 1, 3, False)
    for h in range(HEADS):
        at = slice(h * HEAD_DIM, (h + 1) * HEAD_DIM)
        key_ref[h, :, 0:HEAD_DIM] = keys[:, at]
        value_ref[h, :, 0:HEAD_DIM] = values[:, at]

    span = TOKENS // 2
    index = lax.broadcasted_iota(jnp.int32, (64, span), 0)
    for t in range(TOKENS // span):
        at = slice(t * span, (t + 1) * span)
        for h in range(HEADS):
            hs = slice(h * HEAD_DIM, (h + 1) * HEAD_DIM)
            one, two, three = three_parts(-lse[0, h : h + 1, at])
            tail = jnp.where(index == 2, two, jnp.where(index == 3, three, 0.0))
            tail = jnp.where(index == 0, 1.0, jnp.where(index == 1, one, tail)).astype(BF)
            query = queries[hs, at]
            attend = jnp.exp2(mm(key_ref[h], jnp.concatenate([query, tail], axis=0)))
            low = attend.astype(BF)
            grad = grad_mixed[hs, at]
            inner = grad.astype(F32) * mixed[0, hs, at].astype(F32)
            one, two, three = three_parts(-jnp.sum(inner, axis=0, keepdims=True))
            tail = jnp.where(index == 2, two, jnp.where(index == 3, three, 0.0))
            tail = jnp.where(index == 1, one, tail).astype(BF)
            grad_attend = mm(value_ref[h], jnp.concatenate([grad, tail], axis=0))
            grad_scores = (attend * grad_attend).astype(BF)
            grad_value = mm(grad, low, NT)
            grad_key = mm(query, grad_scores, NT) * (1.0 / LOG2E)
            if t == 0:
                grad_values[hs, :] = grad_value
                grad_keys[hs, :] = grad_key
            else:
                grad_values[hs, :] += grad_value
                grad_keys[hs, :] += grad_key
            grad_queries[hs, at] = (mm(keys_t[hs, :], grad_scores) * HEAD_DIM**-0.5).astype(BF)

    low_keys = grad_keys[...].astype(BF)
    low_values = grad_values[...].astype(BF)
    gpair[0:width, :] += mm(low_keys, memory[0])
    gpair[width : 2 * width, :] += mm(low_values, memory[0])
    grad_memory = mm(low_keys.T, wk[...], NT) + mm(low_values.T, wv[...], NT)
    normed, rstd = norm_rows(reduced[0])
    grows[8:16, :] += fold_rows(grad_memory * normed)
    grows[16:24, :] += fold_rows(grad_memory)
    grad_reduced = norm_rows_back(normed, rstd, grad_memory * rows[1:2, :]).astype(BF)
    grows[0:8, :] += fold_rows(grad_reduced.astype(F32))
    grad_reduced_t = grad_reduced.T
    for p in range(4):
        gwr[p] += mm(grad_reduced_t, patches[0, p])
        grad_patches[p] = mm(grad_reduced, wr[p], NT).astype(BF)
    gwq[...] += mm(pre[0], grad_queries[...], NT)

    def pre_norm_back(t, _):
        at = pl.ds(pl.multiple_of(t * 384, 128), 384)
        grad_pre = mm(wq[...], grad_queries[:, at])
        start = pl.ds(pl.multiple_of(t * 96, 32), 96)
        picked = jnp.concatenate([grad_patches[p, start, :] for p in range(4)], axis=0)
        grad_pre = grad_pre + mm(picked.T, perm[...])
        gain = shift = jnp.zeros((width, 128), F32)
        for u in range(3):
            at = pl.ds(pl.multiple_of(t * 384 + u * 128, 128), 128)
            here = mask[0, 0:1, at]
            normed, rstd = norm_columns(images[0, :, at].astype(F32) * here)
            grad = grad_pre[:, u * 128 : (u + 1) * 128]
            gain = gain + grad * normed
            shift = shift + grad
            back = norm_columns_back(normed, rstd, grad * vec[0])
            grad_images[0, :, at] = (grad_images[0, :, at] + back) * here
        gcols[0] += gain
        gcols[1] += shift
        return 0

    lax.fori_loop(0, TOKENS // 384, pre_norm_back, 0)


def attention_backward(
    sides, images, cot, mask, pre, patches, reduced, memory, mixed, lse, middle, grad_post,
    perm, vec, rows, wq, wqt, wr, wk, wv, wvt, wo,
):
    n, width, tokens = images.shape
    shape = jax.ShapeDtypeStruct
    outs = [
        shape((n, width, tokens), F32),
        shape((width + EXT, width), F32),
        shape((width + EXT, width), F32),
        shape((2 * width, width + 64), F32),
        shape((4, width, width), F32),
        shape((4, width, 128), F32),
        shape((24, width), F32),
    ]
    one = {"pipeline_mode": pl.Buffered(1)}
    inputs = (images, cot, mask, pre, patches, reduced, memory, mixed, lse)
    weights = (perm, vec, rows, wq, wqt, wr, wk, wv, wvt, wo)
    return pl.pallas_call(
        attention_backward_kernel,
        grid_spec=pltpu.PrefetchScalarGridSpec(
            num_scalar_prefetch=1,
            grid=(n,),
            in_specs=[per_image(x) for x in inputs]
            + [per_image(middle, **one), per_image(grad_post, **one)]
            + [whole(x) for x in weights],
            out_specs=[per_image(outs[0], **one)] + [whole(x) for x in outs[1:]],
            scratch_shapes=[
                pltpu.VMEM((width, tokens), BF),
                pltpu.VMEM((width, tokens), BF),
                pltpu.VMEM((width, tokens), BF),
                pltpu.VMEM((width, tokens), BF),
                pltpu.VMEM((HEADS, KEYS, 128), BF),
                pltpu.VMEM((HEADS, KEYS, 128), BF),
                pltpu.VMEM((width, KEYS), BF),
                pltpu.VMEM((width, KEYS), F32),
                pltpu.VMEM((width, KEYS), F32),
                pltpu.VMEM((4, KEYS, width), BF),
            ],
        ),
        out_shape=outs,
        compiler_params=pltpu.CompilerParams(vmem_limit_bytes=VMEM_BYTES),
        name="attention_backward",
    )(sides, *inputs, middle, grad_post, *weights)


def layout_shapes(model_width, hidden_width):
    return [
        (model_width,),
        (model_width,),
        (model_width, model_width),
        (model_width,),
        (4 * model_width, model_width),
        (model_width,),
        (model_width,),
        (model_width,),
        (model_width, 2 * model_width),
        (model_width,),
        (model_width, model_width),
        (model_width,),
        (model_width,),
        (model_width,),
        (model_width, hidden_width),
        (hidden_width,),
        (9, hidden_width),
        (hidden_width,),
        (hidden_width, model_width),
        (model_width,),
    ]


def unpack_params(flat, model_width, hidden_width):
    pieces = []
    offset = 0
    for shape in layout_shapes(model_width, hidden_width):
        count = math.prod(shape)
        pieces.append(flat[offset : offset + count].reshape(shape))
        offset += count
    return pieces


def arrange_weights(flat, width, hidden):
    (
        pre_gain,
        pre_shift,
        query_weight,
        query_bias,
        reduce_weight,
        reduce_bias,
        reduce_gain,
        reduce_shift,
        pair_weight,
        value_bias,
        output_weight,
        output_bias,
        mlp_gain,
        mlp_shift,
        expand_weight,
        expand_bias,
        spatial_weight,
        spatial_bias,
        shrink_weight,
        shrink_bias,
    ) = unpack_params(flat, width, hidden)

    def with_bias(weight, bias, extra):
        return jnp.concatenate([weight.T, bias[:, None], jnp.zeros((width, extra - 1), BF)], axis=1)

    columns = jnp.stack([pre_gain, pre_shift, mlp_gain, mlp_shift, shrink_bias]).astype(F32)
    return dict(
        vec=jnp.broadcast_to(columns[:, :, None], (5, width, 128)),
        rows=jnp.stack([reduce_bias, reduce_gain, reduce_shift]).astype(F32),
        wq=query_weight,
        wqt=with_bias(query_weight, query_bias, EXT),
        wr=reduce_weight.reshape(4, width, width),
        wk=pair_weight[:, :width],
        wv=pair_weight[:, width:],
        wvt=with_bias(pair_weight[:, width:], value_bias, 64),
        wo=output_weight,
        wot=with_bias(output_weight, output_bias, EXT),
        we=jnp.concatenate([expand_weight, expand_bias[None], jnp.zeros((63, hidden), BF)]),
        wst=shrink_weight.T,
        taps=jnp.concatenate([spatial_weight, spatial_bias[None]]).astype(F32),
    )


def device_step(images, cotangent, kv_sides, w):
    positions = jnp.arange(TOKENS, dtype=jnp.int32)
    limit = 2 * kv_sides[:, None]
    mask = ((positions[None] // GRID < limit) & (positions[None] % GRID < limit)).astype(F32)
    mask = jnp.broadcast_to(mask[:, None, :], (mask.shape[0], 8, TOKENS))
    perm = jnp.asarray(patch_order(), BF)
    pre, patches, reduced, memory, mixed, lse, middle, post = attention_forward(
        kv_sides, images, mask, perm, w["vec"], w["rows"], w["wqt"], w["wr"], w["wk"], w["wvt"], w["wot"]
    )
    output, grad_post, gwe, gwst, gtaps, gbias = feed_forward(
        post, cotangent, mask, middle, w["we"], w["wst"], w["taps"], w["vec"]
    )
    grad_images, gwo, gwq, gpair, gwr, gcols, grows = attention_backward(
        kv_sides, images, cotangent, mask, pre, patches, reduced, memory, mixed, lse, middle, grad_post,
        perm, w["vec"], w["rows"], w["wq"], w["wqt"], w["wr"], w["wk"], w["wv"], w["wvt"], w["wo"],
    )
    return output, grad_images, (gwe, gwst, gtaps, gbias, gwo, gwq, gpair, gwr, gcols, grows)


def gradient_pieces(grads, width, hidden):
    gwe, gwst, gtaps, gbias, gwo, gwq, gpair, gwr, gcols, grows = grads
    columns = gcols.sum(axis=2)
    sums = grows.reshape(3, 8, width).sum(axis=1)
    taps = gtaps.reshape(10, 8, hidden).sum(axis=1)
    pair = gpair.T
    return [
        columns[0],
        columns[1],
        gwq[:width],
        gwq[width],
        gwr.transpose(0, 2, 1),
        sums[0],
        sums[1],
        sums[2],
        pair[:width],
        pair[width, width:],
        gwo[:width],
        gwo[width],
        columns[2],
        columns[3],
        gwe[:width],
        gwe[width],
        taps[:9],
        taps[9],
        gwst.T,
        gbias.sum(axis=1),
    ]


def local(images, cotangent, kv_sides, params, first_moment, second_moment):
    width = images.shape[2]
    hidden = 4 * width
    total_entries = params.shape[0] * lax.axis_size("dp") * lax.axis_size("fsdp")
    flat = lax.all_gather(params.astype(BF), ("dp", "fsdp"), axis=0, tiled=True)
    output, grad_images, grads = device_step(
        images.transpose(0, 2, 1), cotangent.transpose(0, 2, 1), kv_sides, arrange_weights(flat, width, hidden)
    )
    flat_grads = jnp.concatenate([piece.reshape(-1) for piece in gradient_pieces(grads, width, hidden)])
    flat_grads = jnp.concatenate([flat_grads, jnp.zeros((total_entries - flat_grads.shape[0],), F32)])
    shard = lax.psum_scatter(flat_grads, ("dp", "fsdp"), scatter_dimension=0, tiled=True)
    grad_norm = jnp.sqrt(lax.psum(jnp.sum(shard * shard), ("dp", "fsdp")))
    clipped = shard * jnp.minimum(1.0, CLIP_NORM / (grad_norm + 1e-06))
    new_first = BETA_FIRST * first_moment + (1.0 - BETA_FIRST) * clipped
    new_second = BETA_SECOND * second_moment + (1.0 - BETA_SECOND) * clipped * clipped
    first_hat = new_first / (1.0 - BETA_FIRST**STEP)
    second_hat = new_second / (1.0 - BETA_SECOND**STEP)
    new_params = params - RATE * (first_hat / (jnp.sqrt(second_hat) + EPSILON) + DECAY * params)
    return (
        output.transpose(0, 2, 1),
        grad_images.transpose(0, 2, 1),
        grad_norm,
        new_first,
        new_second,
        new_params,
    )


def solution(mesh):
    data = P(("dp", "fsdp"), None, None)
    flat = P(("dp", "fsdp"))
    return jax.shard_map(
        local,
        mesh=mesh,
        in_specs=(data, data, flat, flat, flat, flat),
        out_specs=(data, data, P(), flat, flat, flat),
        check_vma=False,
    )
```

```python
from functools import partial
import math

import jax
import jax.numpy as jnp
import numpy as np
from jax import lax
from jax.experimental import pallas as pl
from jax.experimental.pallas import tpu as pltpu
from jax.sharding import PartitionSpec as P

HEADS = 5
HEAD_DIM = 64
GRID = 48
KV = 24
STEP = 10

CLIP_NORM = 1.0
BETA_FIRST = 0.9
BETA_SECOND = 0.999
RATE = 0.04
DECAY = 0.05
EPSILON = 1e-08

F32 = jnp.float32
BF = jnp.bfloat16
NN = (((1,), (0,)), ((), ()))
NT = (((1,), (1,)), ((), ()))
TOKENS = GRID * GRID
KEYS = KV * KV
PITCH = GRID + 8
EXT = 16
LOG2E = math.log2(math.e)
QUERY_SCALE = HEAD_DIM**-0.5 * LOG2E
GELU_A = math.sqrt(2.0 / math.pi)
GELU_B = GELU_A * 0.044715
VMEM_BYTES = 63 * 1024 * 1024


def mm(left, right, dims=NN):
    return lax.dot_general(left, right, dims, preferred_element_type=F32)


def patch_order():
    matrix = np.zeros((8 * GRID, 8 * GRID), np.float32)
    for p in range(4):
        for a in range(4):
            for b in range(KV):
                matrix[p * 96 + a * KV + b, (2 * a + p // 2) * GRID + 2 * b + p % 2] = 1.0
    return matrix


def fold_rows(x):
    return jnp.sum(x.reshape(x.shape[0] // 8, 8, x.shape[1]), axis=0)


def norm_columns(x):
    scale = 1.0 / x.shape[0]
    centred = x - jnp.sum(x, axis=0, keepdims=True) * scale
    rstd = lax.rsqrt(jnp.sum(centred * centred, axis=0, keepdims=True) * scale + 1e-06)
    return centred * rstd, rstd


def norm_columns_back(normed, rstd, scaled):
    scale = 1.0 / scaled.shape[0]
    plain = jnp.sum(scaled, axis=0, keepdims=True) * scale
    mixed = jnp.sum(scaled * normed, axis=0, keepdims=True) * scale
    return rstd * (scaled - plain - normed * mixed)


def norm_rows(x):
    centred = x - jnp.mean(x, axis=-1, keepdims=True)
    rstd = lax.rsqrt(jnp.mean(centred * centred, axis=-1, keepdims=True) + 1e-06)
    return centred * rstd, rstd


def norm_rows_back(normed, rstd, scaled):
    plain = jnp.mean(scaled, axis=-1, keepdims=True)
    mixed = jnp.mean(scaled * normed, axis=-1, keepdims=True)
    return rstd * (scaled - plain - normed * mixed)


def first_row(row, rows=EXT):
    index = lax.broadcasted_iota(jnp.int32, (rows, row.shape[-1]), 0)
    return jnp.where(index == 0, row, 0.0)


def three_parts(x):
    high = x.astype(BF).astype(F32)
    middle = (x - high).astype(BF).astype(F32)
    return high, middle, (x - high - middle).astype(BF).astype(F32)


def whole(x):
    zeros = (0,) * len(x.shape)
    return pl.BlockSpec(x.shape, lambda *_: zeros)


def per_image(x, **kwargs):
    zeros = (0,) * (len(x.shape) - 1)
    return pl.BlockSpec((1,) + tuple(x.shape[1:]), lambda i, *_: (i,) + zeros, **kwargs)


def key_columns(ref, side, h_range, ones_from, ones_to, with_mask):
    lane = lax.broadcasted_iota(jnp.int32, (KV, 64), 1)
    cell = lax.broadcasted_iota(jnp.int32, (KV, 64), 0)
    ones = jnp.where((lane >= ones_from) & (lane <= ones_to), 1.0, 0.0)
    for a in range(KV):
        block = ones
        if with_mask:
            bias = jnp.where((cell < side) & (a < side), 0.0, -1e30)
            block = jnp.where(lane == 0, bias, ones)
        block = block.astype(BF)
        for h in h_range:
            ref[h, a * KV : (a + 1) * KV, 64:128] = block


def attention_forward_kernel(
    sides, images, mask, perm, vec, rows, wqt, wr, wk, wvt, wot,
    pre, patches, reduced, memory, mixed, lse, middle, post,
    key_ref, value_ref,
):
    i = pl.program_id(0)
    width = images.shape[1]

    def first_norm(t, _):
        for u in range(3):
            at = pl.ds(pl.multiple_of(t * 384 + u * 128, 128), 128)
            x = images[0, :, at].astype(F32) * mask[0, 0:1, at]
            normed, _unused = norm_columns(x)
            pre[0, 0:width, at] = (normed * vec[0] + vec[1]).astype(BF)
            pre[0, width : width + EXT, at] = first_row(jnp.ones((1, 128), F32)).astype(BF)
        at = pl.ds(pl.multiple_of(t * 384, 128), 384)
        picked = mm(perm[...], pre[0, 0:width, at], NT).astype(BF)
        for p in range(4):
            patches[0, p, pl.ds(pl.multiple_of(t * 96, 32), 96), :] = picked[p * 96 : (p + 1) * 96]
        return 0

    lax.fori_loop(0, TOKENS // 384, first_norm, 0)

    total = rows[0:1, :]
    for p in range(4):
        total = total + mm(patches[0, p], wr[p])
    reduced[0] = total
    normed, _unused = norm_rows(total)
    memory[0, :, 0:width] = (normed * rows[1:2, :] + rows[2:3, :]).astype(BF)
    lane = lax.broadcasted_iota(jnp.int32, (KEYS, 64), 1)
    memory[0, :, width : width + 64] = jnp.where(lane == 0, 1.0, 0.0).astype(BF)
    keys = mm(memory[0, :, 0:width], wk[...]).astype(BF)
    key_columns(key_ref, sides[i], range(HEADS), 1, 0, True)
    values = mm(wvt[...], memory[0], NT).astype(BF)
    ones = first_row(jnp.ones((1, KEYS), F32)).astype(BF)
    for h in range(HEADS):
        at = slice(h * HEAD_DIM, (h + 1) * HEAD_DIM)
        key_ref[h, :, 0:HEAD_DIM] = keys[:, at]
        value_ref[h, 0:HEAD_DIM, :] = values[at]
        value_ref[h, HEAD_DIM : HEAD_DIM + EXT, :] = ones
    mixed[0, width : width + EXT, :] = first_row(jnp.ones((1, TOKENS), F32)).astype(BF)
    queries = (mm(wqt[...], pre[0]) * QUERY_SCALE).astype(BF)
    tail = first_row(jnp.ones((1, TOKENS), F32), 64).astype(BF)
    for h in range(HEADS):
        at = slice(h * HEAD_DIM, (h + 1) * HEAD_DIM)
        scores = mm(key_ref[h], jnp.concatenate([queries[at], tail], axis=0))
        top = jnp.max(scores, axis=0, keepdims=True)
        weights = jnp.exp2(scores - top).astype(BF)
        out = mm(value_ref[h], weights)
        total = out[HEAD_DIM : HEAD_DIM + 1]
        mixed[0, at, :] = (out[0:HEAD_DIM] * (1.0 / total)).astype(BF)
        lse[0, h : h + 1, :] = top + jnp.log2(total)

    def second_norm(t, _):
        at = pl.ds(pl.multiple_of(t * 384, 128), 384)
        branch = mm(wot[...], mixed[0, :, at])
        for u in range(3):
            at = pl.ds(pl.multiple_of(t * 384 + u * 128, 128), 128)
            here = mask[0, 0:1, at]
            x = images[0, :, at].astype(F32) * here + branch[:, u * 128 : (u + 1) * 128]
            middle[0, :, at] = x
            normed, _unused = norm_columns(x)
            post[0, 0:width, at] = ((normed * vec[2] + vec[3]) * here).astype(BF)
            post[0, width : width + EXT, at] = first_row(here).astype(BF)
        return 0

    lax.fori_loop(0, TOKENS // 384, second_norm, 0)


def attention_forward(sides, images, mask, perm, vec, rows, wqt, wr, wk, wvt, wot):
    n, width, tokens = images.shape
    shape = jax.ShapeDtypeStruct
    outs = [
        shape((n, width + EXT, tokens), BF),
        shape((n, 4, KEYS, width), BF),
        shape((n, KEYS, width), F32),
        shape((n, KEYS, width + 64), BF),
        shape((n, width + EXT, tokens), BF),
        shape((n, 8, tokens), F32),
        shape((n, width, tokens), F32),
        shape((n, width + EXT, tokens), BF),
    ]
    weights = (perm, vec, rows, wqt, wr, wk, wvt, wot)
    return pl.pallas_call(
        attention_forward_kernel,
        grid_spec=pltpu.PrefetchScalarGridSpec(
            num_scalar_prefetch=1,
            grid=(n,),
            in_specs=[per_image(images), per_image(mask)] + [whole(x) for x in weights],
            out_specs=[per_image(x) for x in outs],
            scratch_shapes=[
                pltpu.VMEM((HEADS, KEYS, 128), BF),
                pltpu.VMEM((HEADS, HEAD_DIM + EXT, KEYS), BF),
            ],
        ),
        out_shape=outs,
        compiler_params=pltpu.CompilerParams(vmem_limit_bytes=VMEM_BYTES),
        name="attention_forward",
    )(sides, images, mask, *weights)


def feed_forward_kernel(
    post, cot, mask, middle, we, wst, taps, vec,
    output, grad_post, gwe, gwst, gtaps, gbias,
    padded, grad_padded, grad_act, act, grad_exp, post_rows, out_grad, out_grad_rows, total,
):
    i = pl.program_id(0)
    j = pl.program_id(1)
    width, block = wst.shape
    halves = block // 128
    rows = 8
    chunks = GRID // rows
    span = rows * GRID
    cols = 16

    @pl.when((i == 0) & (j == 0))
    def _():
        for ref in (padded, grad_padded, gwe, gwst, gtaps, gbias, post_rows):
            ref[...] = jnp.zeros_like(ref)

    @pl.when(j == 0)
    def _():
        for t in range(TOKENS // 384):
            at = slice(t * 384, (t + 1) * 384)
            grad = cot[0, :, at].astype(F32) * mask[0, 0:1, at]
            gbias[...] += grad[:, 0:128] + grad[:, 128:256] + grad[:, 256:384]
            grad = grad.astype(BF)
            out_grad[:, at] = grad
            out_grad_rows[at, :] = grad.T
            post_rows[at, 0 : width + EXT] = post[0, :, at].T

    def expand(t, _):
        at = pl.ds(pl.multiple_of(t * span, span), span)
        filled = mm(post_rows[at, :], we[...]).astype(BF).astype(F32)
        for h in range(halves):
            for r in range(rows):
                start = pl.multiple_of((t * rows + r + 1) * PITCH + 8, 8)
                padded[h, pl.ds(start, GRID), :] = filled[
                    r * GRID : (r + 1) * GRID, h * 128 : (h + 1) * 128
                ]
        grad_act[at, :] = mm(out_grad_rows[at, :], wst[...])
        return 0

    lax.fori_loop(0, chunks, expand, 0)

    def convolve(t, _):
        for h in range(halves):
            hs = slice(h * 128, (h + 1) * 128)
            w = [jnp.broadcast_to(taps[k : k + 1, hs], (cols, 128)) for k in range(10)]
            sums = jnp.zeros((8, 128), F32)
            for ct in range(GRID // cols):
                open_rows = {}
                for q in range(-1, rows + 1):
                    base = (t * rows + q + 1) * PITCH + 8 + ct * cols
                    x = [padded[h, pl.ds(base + s, cols), :] for s in (-1, 0, 1)]
                    for a in (2, 1, 0):
                        r = q + 1 - a
                        if 0 <= r < rows:
                            part = w[3 * a] * x[0] + w[3 * a + 1] * x[1] + w[3 * a + 2] * x[2]
                            open_rows[r] = part + open_rows.get(r, w[9])
                    r = q - 1
                    if r < 0:
                        continue
                    conv = open_rows.pop(r)
                    square = conv * conv
                    half = 0.5 * jnp.tanh(conv * (GELU_B * square + GELU_A)) + 0.5
                    gelu = conv * half
                    slope = half + gelu * (1.0 - half) * ((6.0 * GELU_B) * square + 2.0 * GELU_A)
                    at = pl.ds(pl.multiple_of((t * rows + r) * GRID + ct * cols, cols), cols)
                    act[at, hs] = gelu.astype(BF)
                    grad = grad_act[at, hs] * slope
                    start = pl.multiple_of((t * rows + r + 1) * PITCH + 8 + ct * cols, 8)
                    grad_padded[h, pl.ds(start, cols), :] = grad
                    sums = sums + grad[0:8] + grad[8:16]
            js = pl.ds(pl.multiple_of(j * block + h * 128, 128), 128)
            gtaps[72:80, js] += sums
        return 0

    lax.fori_loop(0, chunks, convolve, 0)

    def convolve_back(t, _):
        for h in range(halves):
            hs = slice(h * 128, (h + 1) * 128)
            w = [jnp.broadcast_to(taps[k : k + 1, hs], (cols, 128)) for k in range(9)]
            sums = [jnp.zeros((8, 128), F32) for _ in range(9)]
            for ct in range(GRID // cols):
                open_rows = {}
                x = {}
                for q in range(-1, rows + 1):
                    base = (t * rows + q + 1) * PITCH + 8 + ct * cols
                    grads = [grad_padded[h, pl.ds(base + 1 - b, cols), :] for b in range(3)]
                    if q + 1 < rows:
                        start = pl.multiple_of((t * rows + q + 2) * PITCH + 8 + ct * cols, 8)
                        x[q + 1] = padded[h, pl.ds(start, cols), :]
                    for a in range(3):
                        r = q + a - 1
                        if not 0 <= r < rows:
                            continue
                        part = w[3 * a] * grads[0] + w[3 * a + 1] * grads[1] + w[3 * a + 2] * grads[2]
                        open_rows[r] = part + open_rows[r] if r in open_rows else part
                        for b in range(3):
                            product = x[r] * grads[b]
                            sums[3 * a + b] = sums[3 * a + b] + product[0:8] + product[8:16]
                    r = q - 1
                    if r >= 0:
                        at = pl.ds(pl.multiple_of((t * rows + r) * GRID + ct * cols, cols), cols)
                        grad_exp[at, hs] = open_rows.pop(r).astype(BF)
                        x.pop(r)
            js = pl.ds(pl.multiple_of(j * block + h * 128, 128), 128)
            for k in range(9):
                gtaps[8 * k : 8 * k + 8, js] += sums[k]
        return 0

    lax.fori_loop(0, chunks, convolve_back, 0)

    js = pl.ds(pl.multiple_of(j * block, block), block)
    gwst[:, js] += mm(out_grad[...], act[...])
    gwe[:, js] += mm(post[0], grad_exp[...])
    shrunk = mm(wst[...], act[...], NT)
    back = mm(we[0:width, :], grad_exp[...], NT)

    @pl.when(j == 0)
    def _():
        total[...] = shrunk
        grad_post[0] = back

    @pl.when(j != 0)
    def _():
        total[...] += shrunk
        grad_post[0] += back

    @pl.when(j == pl.num_programs(1) - 1)
    def _():
        for t in range(TOKENS // 128):
            at = slice(t * 128, (t + 1) * 128)
            output[0, :, at] = ((middle[0, :, at] + total[:, at] + vec[4]) * mask[0, 0:1, at]).astype(BF)


def feed_forward(post, cot, mask, middle, we, wst, taps, vec, block=256):
    n, width, tokens = cot.shape
    hidden = wst.shape[1]
    shape = jax.ShapeDtypeStruct
    outs = [
        shape((n, width, tokens), BF),
        shape((n, width, tokens), F32),
        shape((width + EXT, hidden), F32),
        shape((width, hidden), F32),
        shape((80, hidden), F32),
        shape((width, 128), F32),
    ]
    one = {"pipeline_mode": pl.Buffered(1)}
    columns = lambda x: pl.BlockSpec((x.shape[0], block), lambda i, j: (0, j))
    return pl.pallas_call(
        feed_forward_kernel,
        grid=(n, hidden // block),
        in_specs=[per_image(post), per_image(cot), per_image(mask), per_image(middle, **one)]
        + [columns(we), columns(wst), columns(taps), whole(vec)],
        out_specs=[per_image(x) for x in outs[:2]] + [whole(x) for x in outs[2:]],
        out_shape=outs,
        scratch_shapes=[
            pltpu.VMEM((block // 128, (GRID + 2) * PITCH + 8, 128), F32),
            pltpu.VMEM((block // 128, (GRID + 2) * PITCH + 8, 128), F32),
            pltpu.VMEM((tokens, block), F32),
            pltpu.VMEM((tokens, block), BF),
            pltpu.VMEM((tokens, block), BF),
            pltpu.VMEM((tokens, width + 64), BF),
            pltpu.VMEM((width, tokens), BF),
            pltpu.VMEM((tokens, width), BF),
            pltpu.VMEM((width, tokens), F32),
        ],
        compiler_params=pltpu.CompilerParams(vmem_limit_bytes=VMEM_BYTES),
        name="feed_forward",
    )(post, cot, mask, middle, we, wst, taps, vec)


def attention_backward_kernel(
    sides, images, cot, mask, pre, patches, reduced, memory, mixed, lse, middle, grad_post,
    perm, vec, rows, wq, wqt, wr, wk, wv, wvt, wo,
    grad_images, gwo, gwq, gpair, gwr, gcols, grows,
    branch, grad_mixed, queries, grad_queries, key_ref, value_ref, keys_t, grad_keys, grad_values, grad_patches,
):
    i = pl.program_id(0)
    width = images.shape[1]

    @pl.when(i == 0)
    def _():
        for ref in (gwo, gwq, gpair, gwr, gcols, grows):
            ref[...] = jnp.zeros_like(ref)

    def mlp_norm_back(t, _):
        gain = shift = jnp.zeros((width, 128), F32)
        for u in range(3):
            at = pl.ds(pl.multiple_of(t * 384 + u * 128, 128), 128)
            here = mask[0, 0:1, at]
            normed, rstd = norm_columns(middle[0, :, at])
            grad = grad_post[0, :, at] * here
            gain = gain + grad * normed
            shift = shift + grad
            grad = cot[0, :, at].astype(F32) * here + norm_columns_back(normed, rstd, grad * vec[2])
            grad_images[0, :, at] = grad
            branch[:, at] = grad.astype(BF)
        gcols[2] += gain
        gcols[3] += shift
        return 0

    lax.fori_loop(0, TOKENS // 384, mlp_norm_back, 0)
    gwo[...] += mm(mixed[0], branch[...], NT)
    grad_mixed[...] = mm(wo[...], branch[...]).astype(BF)
    queries[...] = (mm(wqt[...], pre[0]) * QUERY_SCALE).astype(BF)
    keys = mm(memory[0, :, 0:width], wk[...]).astype(BF)
    keys_t[...] = keys.T
    values = mm(wvt[...], memory[0], NT).astype(BF).T
    key_columns(key_ref, sides[i], range(HEADS), 1, 3, True)
    key_columns(value_ref, sides[i], range(HEADS), 1, 3, False)
    for h in range(HEADS):
        at = slice(h * HEAD_DIM, (h + 1) * HEAD_DIM)
        key_ref[h, :, 0:HEAD_DIM] = keys[:, at]
        value_ref[h, :, 0:HEAD_DIM] = values[:, at]

    span = TOKENS // 2
    index = lax.broadcasted_iota(jnp.int32, (64, span), 0)
    for t in range(TOKENS // span):
        at = slice(t * span, (t + 1) * span)
        for h in range(HEADS):
            hs = slice(h * HEAD_DIM, (h + 1) * HEAD_DIM)
            one, two, three = three_parts(-lse[0, h : h + 1, at])
            tail = jnp.where(index == 2, two, jnp.where(index == 3, three, 0.0))
            tail = jnp.where(index == 0, 1.0, jnp.where(index == 1, one, tail)).astype(BF)
            query = queries[hs, at]
            attend = jnp.exp2(mm(key_ref[h], jnp.concatenate([query, tail], axis=0)))
            low = attend.astype(BF)
            grad = grad_mixed[hs, at]
            inner = grad.astype(F32) * mixed[0, hs, at].astype(F32)
            one, two, three = three_parts(-jnp.sum(inner, axis=0, keepdims=True))
            tail = jnp.where(index == 2, two, jnp.where(index == 3, three, 0.0))
            tail = jnp.where(index == 1, one, tail).astype(BF)
            grad_attend = mm(value_ref[h], jnp.concatenate([grad, tail], axis=0))
            grad_scores = (attend * grad_attend).astype(BF)
            grad_value = mm(grad, low, NT)
            grad_key = mm(query, grad_scores, NT) * (1.0 / LOG2E)
            if t == 0:
                grad_values[hs, :] = grad_value
                grad_keys[hs, :] = grad_key
            else:
                grad_values[hs, :] += grad_value
                grad_keys[hs, :] += grad_key
            grad_queries[hs, at] = (mm(keys_t[hs, :], grad_scores) * HEAD_DIM**-0.5).astype(BF)

    low_keys = grad_keys[...].astype(BF)
    low_values = grad_values[...].astype(BF)
    gpair[0:width, :] += mm(low_keys, memory[0])
    gpair[width : 2 * width, :] += mm(low_values, memory[0])
    grad_memory = mm(low_keys.T, wk[...], NT) + mm(low_values.T, wv[...], NT)
    normed, rstd = norm_rows(reduced[0])
    grows[8:16, :] += fold_rows(grad_memory * normed)
    grows[16:24, :] += fold_rows(grad_memory)
    grad_reduced = norm_rows_back(normed, rstd, grad_memory * rows[1:2, :]).astype(BF)
    grows[0:8, :] += fold_rows(grad_reduced.astype(F32))
    grad_reduced_t = grad_reduced.T
    for p in range(4):
        gwr[p] += mm(grad_reduced_t, patches[0, p])
        grad_patches[p] = mm(grad_reduced, wr[p], NT).astype(BF)
    gwq[...] += mm(pre[0], grad_queries[...], NT)

    def pre_norm_back(t, _):
        at = pl.ds(pl.multiple_of(t * 384, 128), 384)
        grad_pre = mm(wq[...], grad_queries[:, at])
        start = pl.ds(pl.multiple_of(t * 96, 32), 96)
        picked = jnp.concatenate([grad_patches[p, start, :] for p in range(4)], axis=0)
        grad_pre = grad_pre + mm(picked.T, perm[...])
        gain = shift = jnp.zeros((width, 128), F32)
        for u in range(3):
            at = pl.ds(pl.multiple_of(t * 384 + u * 128, 128), 128)
            here = mask[0, 0:1, at]
            normed, rstd = norm_columns(images[0, :, at].astype(F32) * here)
            grad = grad_pre[:, u * 128 : (u + 1) * 128]
            gain = gain + grad * normed
            shift = shift + grad
            back = norm_columns_back(normed, rstd, grad * vec[0])
            grad_images[0, :, at] = (grad_images[0, :, at] + back) * here
        gcols[0] += gain
        gcols[1] += shift
        return 0

    lax.fori_loop(0, TOKENS // 384, pre_norm_back, 0)


def attention_backward(
    sides, images, cot, mask, pre, patches, reduced, memory, mixed, lse, middle, grad_post,
    perm, vec, rows, wq, wqt, wr, wk, wv, wvt, wo,
):
    n, width, tokens = images.shape
    shape = jax.ShapeDtypeStruct
    outs = [
        shape((n, width, tokens), F32),
        shape((width + EXT, width), F32),
        shape((width + EXT, width), F32),
        shape((2 * width, width + 64), F32),
        shape((4, width, width), F32),
        shape((4, width, 128), F32),
        shape((24, width), F32),
    ]
    one = {"pipeline_mode": pl.Buffered(1)}
    inputs = (images, cot, mask, pre, patches, reduced, memory, mixed, lse)
    weights = (perm, vec, rows, wq, wqt, wr, wk, wv, wvt, wo)
    return pl.pallas_call(
        attention_backward_kernel,
        grid_spec=pltpu.PrefetchScalarGridSpec(
            num_scalar_prefetch=1,
            grid=(n,),
            in_specs=[per_image(x) for x in inputs]
            + [per_image(middle, **one), per_image(grad_post, **one)]
            + [whole(x) for x in weights],
            out_specs=[per_image(outs[0], **one)] + [whole(x) for x in outs[1:]],
            scratch_shapes=[
                pltpu.VMEM((width, tokens), BF),
                pltpu.VMEM((width, tokens), BF),
                pltpu.VMEM((width, tokens), BF),
                pltpu.VMEM((width, tokens), BF),
                pltpu.VMEM((HEADS, KEYS, 128), BF),
                pltpu.VMEM((HEADS, KEYS, 128), BF),
                pltpu.VMEM((width, KEYS), BF),
                pltpu.VMEM((width, KEYS), F32),
                pltpu.VMEM((width, KEYS), F32),
                pltpu.VMEM((4, KEYS, width), BF),
            ],
        ),
        out_shape=outs,
        compiler_params=pltpu.CompilerParams(vmem_limit_bytes=VMEM_BYTES),
        name="attention_backward",
    )(sides, *inputs, middle, grad_post, *weights)

MESH = pl.DeviceIdType.MESH


class Place:
    def __init__(self):
        self.dp = lax.axis_index("dp")
        fsdp = lax.axis_index("fsdp")
        self.y, self.x = self.dp // 2, self.dp % 2
        self.z, self.core = fsdp // 2, fsdp % 2
        self.beside_x = (self.dp + 1 - 2 * self.x, fsdp)
        self.beside_y = (self.dp + 2 - 4 * self.y, fsdp)
        self.beside_core = (self.dp, fsdp + 1 - 2 * self.core)

    def up(self, k):
        return (self.z + k) % 4

    def along_z(self, k):
        return (self.dp, self.up(k) * 2 + self.core)

    def partners(self):
        return [self.beside_core, self.beside_x, self.beside_y] + [self.along_z(k) for k in (1, 2, 3)]

    def greet(self):
        barrier = pltpu.get_barrier_semaphore()
        partners = self.partners()
        for device in partners:
            pl.semaphore_signal(barrier, inc=1, device_id=device, device_id_type=MESH)
        pl.semaphore_wait(barrier, len(partners))


class Sender:
    def __init__(self, send, recv):
        self.send, self.recv, self.started = send, recv, []

    def __call__(self, source, target, device):
        k = len(self.started)
        copy = pltpu.make_async_remote_copy(
            src_ref=source,
            dst_ref=target,
            send_sem=self.send.at[k],
            recv_sem=self.recv.at[k],
            device_id=device,
            device_id_type=MESH,
        )
        copy.start()
        self.started.append(copy)
        return copy

    def finish(self):
        for copy in self.started:
            copy.wait_send()


def gather_kernel(own, out, own_sem, send_sem, recv_sem):
    me = Place()
    half = own.shape[0] // 2
    first, second = pl.ds(0, half), pl.ds(half, half)
    send = Sender(send_sem, recv_sem)
    copy = pltpu.make_async_copy(own, out.at[me.core, me.dp, me.z], own_sem)
    copy.start()
    me.greet()
    slot = out.at[me.core, me.dp, me.z]
    z_copies = [send(own, slot, me.along_z(k)) for k in (1, 2, 3)]
    x_copies = [send(own, slot, me.beside_x)]
    y_copies = [send(own, slot, me.beside_y)]
    core_copies = [send(own, slot, me.beside_core)]
    half_copies = []

    def forward(k):
        z = (me.z + 4 - k) % 4
        x_copies[k].wait_recv()
        dp = me.beside_x[0]
        slot = out.at[me.core, dp, z]
        half_copies.append(send(slot.at[first], slot.at[first], me.beside_y))
        core_copies.append(send(slot, slot, me.beside_core))
        y_copies[k].wait_recv()
        dp = me.beside_y[0]
        slot = out.at[me.core, dp, z]
        half_copies.append(send(slot.at[second], slot.at[second], me.beside_x))
        core_copies.append(send(slot, slot, me.beside_core))

    forward(0)
    for k in (1, 2, 3):
        z_copies[k - 1].wait_recv()
        slot = out.at[me.core, me.dp, (me.z + 4 - k) % 4]
        x_copies.append(send(slot, slot, me.beside_x))
        y_copies.append(send(slot, slot, me.beside_y))
        core_copies.append(send(slot, slot, me.beside_core))
        forward(k)
    for k in range(4):
        half_copies[2 * k].wait_recv()
        half_copies[2 * k + 1].wait_recv()
        slot = out.at[me.core, 3 - me.dp, (me.z + 4 - k) % 4]
        core_copies.append(send(slot, slot, me.beside_core))
    for copied in core_copies:
        copied.wait_recv()
    copy.wait()
    send.finish()


def gather_slots(own):
    count = 35
    return pl.pallas_call(
        gather_kernel,
        out_shape=jax.ShapeDtypeStruct((2, 4, 4) + own.shape, own.dtype),
        in_specs=[pl.BlockSpec(memory_space=pltpu.VMEM)],
        out_specs=pl.BlockSpec(memory_space=pltpu.VMEM),
        scratch_shapes=[
            pltpu.SemaphoreType.DMA(()),
            pltpu.SemaphoreType.DMA((count,)),
            pltpu.SemaphoreType.DMA((count,)),
        ],
        compiler_params=pltpu.CompilerParams(
            collective_id=0, has_side_effects=True, vmem_limit_bytes=VMEM_BYTES
        ),
        name="gather_weights",
    )(own)


def reduce_kernel(grads, shard, squares, core_in, y_in, x_in, x_last, y_last, z_in, small, send_sem, recv_sem):
    me = Place()
    rows = grads.shape[3]
    half = rows // 2
    first, second = pl.ds(0, half), pl.ds(half, half)
    send = Sender(send_sem, recv_sem)
    other_x, other_y = 1 - me.x, 1 - me.y
    me.greet()
    order = [2 * other_y + other_x, 2 * other_y + me.x, 2 * me.y + other_x, me.dp]
    core_copies = [send(grads.at[1 - me.core, dp], core_in.at[dp], me.beside_core) for dp in order]

    def add(dp):
        for z in range(4):
            core_in[dp, z] = (core_in[dp, z].astype(F32) + grads[me.core, dp, z].astype(F32)).astype(BF)

    core_copies[0].wait_recv()
    add(order[0])
    y_copies = [send(core_in.at[order[0], :, first], y_in.at[0], me.beside_y)]
    x_copies = [send(core_in.at[order[0], :, second], x_in.at[0], me.beside_x)]
    core_copies[1].wait_recv()
    add(order[1])
    y_copies.append(send(core_in.at[order[1], :, first], y_in.at[1], me.beside_y))
    core_copies[2].wait_recv()
    add(order[2])
    x_copies.append(send(core_in.at[order[2], :, second], x_in.at[1], me.beside_x))
    core_copies[3].wait_recv()
    add(order[3])
    y_copies[0].wait_recv()
    x_copies[0].wait_recv()
    last = []
    for k in (0, 1, 2, 3):
        z = (me.z + k) % 4
        y_in[0, z] = (y_in[0, z].astype(F32) + core_in[order[2], z, first].astype(F32)).astype(BF)
        last.append(send(y_in.at[0, z], x_last.at[z], me.beside_x))
        x_in[0, z] = (x_in[0, z].astype(F32) + core_in[order[1], z, second].astype(F32)).astype(BF)
        last.append(send(x_in.at[0, z], y_last.at[z], me.beside_y))
    y_copies[1].wait_recv()
    x_copies[1].wait_recv()
    z_copies = []
    for k in (1, 2, 3, 0):
        z = (me.z + k) % 4
        last[2 * k].wait_recv()
        last[2 * k + 1].wait_recv()
        low = y_in[1, z].astype(F32) + core_in[me.dp, z, first].astype(F32) + x_last[z].astype(F32)
        high = x_in[1, z].astype(F32) + core_in[me.dp, z, second].astype(F32) + y_last[z].astype(F32)
        if k == 0:
            shard[first, :] = low
            shard[second, :] = high
        else:
            z_in[k - 1, first] = low.astype(BF)
            z_in[k - 1, second] = high.astype(BF)
            z_copies.append(send(z_in.at[k - 1], z_in.at[k + 2], me.along_z(k)))
    for k in (0, 1, 2):
        z_copies[k].wait_recv()
        shard[...] += z_in[k + 3].astype(F32)
    total = shard[0:8, :] * shard[0:8, :]
    for k in range(1, rows // 8):
        part = shard[8 * k : 8 * k + 8, :]
        total = total + part * part
    small[0] = total
    for k, device in enumerate((me.beside_core, me.beside_x, me.beside_y)):
        copied = send(small.at[k], small.at[4 + k], device)
        copied.wait_recv()
        small[k + 1] = small[k] + small[4 + k]
    copies = [send(small.at[3], small.at[8 + me.z], me.along_z(k)) for k in (1, 2, 3)]
    small[8 + me.z] = small[3]
    for copied in copies:
        copied.wait_recv()
    squares[...] = ((small[8] + small[9]) + small[10]) + small[11]
    send.finish()


def reduce_slots(grads):
    rows = grads.shape[3]
    half = rows // 2
    count = 4 + 4 + 8 + 3 + 6
    return pl.pallas_call(
        reduce_kernel,
        out_shape=[jax.ShapeDtypeStruct((rows, 128), F32), jax.ShapeDtypeStruct((8, 128), F32)],
        in_specs=[pl.BlockSpec(memory_space=pltpu.VMEM)],
        out_specs=[pl.BlockSpec(memory_space=pltpu.VMEM)] * 2,
        scratch_shapes=[
            pltpu.VMEM((4, 4, rows, 128), BF),
            pltpu.VMEM((2, 4, half, 128), BF),
            pltpu.VMEM((2, 4, half, 128), BF),
            pltpu.VMEM((4, half, 128), BF),
            pltpu.VMEM((4, half, 128), BF),
            pltpu.VMEM((6, rows, 128), BF),
            pltpu.VMEM((12, 8, 128), F32),
            pltpu.SemaphoreType.DMA((count,)),
            pltpu.SemaphoreType.DMA((count,)),
        ],
        compiler_params=pltpu.CompilerParams(
            collective_id=1, has_side_effects=True, vmem_limit_bytes=VMEM_BYTES
        ),
        name="reduce_gradients",
    )(grads)


def layout_shapes(model_width, hidden_width):
    return [
        ("pre_gain", (model_width,)),
        ("pre_shift", (model_width,)),
        ("query_weight", (model_width, model_width)),
        ("query_bias", (model_width,)),
        ("reduce_weight", (4 * model_width, model_width)),
        ("reduce_bias", (model_width,)),
        ("reduce_gain", (model_width,)),
        ("reduce_shift", (model_width,)),
        ("pair_weight", (model_width, 2 * model_width)),
        ("value_bias", (model_width,)),
        ("output_weight", (model_width, model_width)),
        ("output_bias", (model_width,)),
        ("mlp_gain", (model_width,)),
        ("mlp_shift", (model_width,)),
        ("expand_weight", (model_width, hidden_width)),
        ("expand_bias", (hidden_width,)),
        ("spatial_weight", (9, hidden_width)),
        ("spatial_bias", (hidden_width,)),
        ("shrink_weight", (hidden_width, model_width)),
        ("shrink_bias", (model_width,)),
    ]


def row_bases(width, hidden):
    bases = {}
    row = 0
    for name, shape in layout_shapes(width, hidden):
        bases[name] = row
        row += math.prod(shape) // width
    return bases, row


SPAN = 96


def unpack_kernel(
    order, slot_rows, bases,
    slots, vec, rows, wq, wqt, wr, wk, wv, wvt, wo, wot, we, wst, taps,
    flat, wide,
):
    width = wq.shape[0]
    hidden = wst.shape[1]
    for slot, place in enumerate(order):
        flat[pl.ds(slot * slot_rows, slots.shape[1]), :] = slots[place].astype(F32)
    low = lax.broadcasted_iota(jnp.int32, (SPAN, 128), 1) < 64

    def regroup(t, _):
        part = [flat[pl.ds(t * (5 * SPAN) + k, SPAN, stride=5), :] for k in range(5)]
        turned = [pltpu.roll(part[k], 64, 1) for k in (2, 3, 4)]
        even = pl.ds(t * (2 * SPAN), SPAN, stride=2)
        odd = pl.ds(t * (2 * SPAN) + 1, SPAN, stride=2)
        for k in range(3):
            wide[k, even, :] = part[k]
        wide[0, odd, :] = jnp.where(low, turned[0], turned[1])
        wide[1, odd, :] = jnp.where(low, turned[1], turned[2])
        wide[2, odd, :] = turned[2]
        return 0

    lax.fori_loop(0, wide.shape[1] // (2 * SPAN), regroup, 0)

    def take(base, count, stride=1):
        at = pl.ds(base, count, stride=stride) if stride > 1 else pl.ds(base, count)
        return jnp.concatenate([wide[0, at, :], wide[1, at, :], wide[2, at, :][:, 0 : width - 256]], axis=1)

    def take_hidden(base, count):
        return jnp.concatenate([take(base + q, count, hidden // width) for q in range(hidden // width)], axis=1)

    def bordered(weight, bias, extra):
        index = lax.broadcasted_iota(jnp.int32, (extra, weight.shape[1]), 0)
        return jnp.concatenate([weight, jnp.where(index == 0, bias, 0.0)], axis=0)

    names = ("pre_gain", "pre_shift", "mlp_gain", "mlp_shift", "shrink_bias")
    for k, name in enumerate(names):
        vec[k] = jnp.broadcast_to(take(bases[name], 1), (128, width)).T
    for k, name in enumerate(("reduce_bias", "reduce_gain", "reduce_shift")):
        rows[k : k + 1, :] = take(bases[name], 1)
    query = take(bases["query_weight"], width)
    wq[...] = query.astype(BF)
    wqt[...] = bordered(query, take(bases["query_bias"], 1), EXT).T.astype(BF)
    for p in range(4):
        wr[p] = take(bases["reduce_weight"] + p * width, width).astype(BF)
    wk[...] = take(bases["pair_weight"], width, 2).astype(BF)
    value = take(bases["pair_weight"] + 1, width, 2)
    wv[...] = value.astype(BF)
    wvt[...] = bordered(value, take(bases["value_bias"], 1), 64).T.astype(BF)
    out = take(bases["output_weight"], width)
    wo[...] = out.astype(BF)
    wot[...] = bordered(out, take(bases["output_bias"], 1), EXT).T.astype(BF)
    we[0:width, :] = take_hidden(bases["expand_weight"], width).astype(BF)
    we[width : width + 64, :] = first_row(take_hidden(bases["expand_bias"], 1), 64).astype(BF)
    taps[0:9, :] = take_hidden(bases["spatial_weight"], 9)
    taps[9:10, :] = take_hidden(bases["spatial_bias"], 1)
    for k in range(hidden // 128):
        wst[:, 128 * k : 128 * k + 128] = take(bases["shrink_weight"] + 128 * k, 128).T.astype(BF)


def wide_rows(count):
    return -(-count // (2 * SPAN)) * 2 * SPAN


def unpack_weights(slots, order, slot_rows, width):
    hidden = 4 * width
    bases, count = row_bases(width, hidden)
    shape = jax.ShapeDtypeStruct
    outs = dict(
        vec=shape((5, width, 128), F32),
        rows=shape((3, width), F32),
        wq=shape((width, width), BF),
        wqt=shape((width, width + EXT), BF),
        wr=shape((4, width, width), BF),
        wk=shape((width, width), BF),
        wv=shape((width, width), BF),
        wvt=shape((width, width + 64), BF),
        wo=shape((width, width), BF),
        wot=shape((width, width + EXT), BF),
        we=shape((width + 64, hidden), BF),
        wst=shape((width, hidden), BF),
        taps=shape((10, hidden), F32),
    )
    flat_rows = max(len(order) * slot_rows, wide_rows(count) * width // 128) + slots.shape[1]
    values = pl.pallas_call(
        partial(unpack_kernel, order, slot_rows, bases),
        out_shape=list(outs.values()),
        in_specs=[pl.BlockSpec(memory_space=pltpu.VMEM)],
        out_specs=[pl.BlockSpec(memory_space=pltpu.VMEM)] * len(outs),
        scratch_shapes=[pltpu.VMEM((flat_rows, 128), F32), pltpu.VMEM((3, wide_rows(count), 128), F32)],
        compiler_params=pltpu.CompilerParams(vmem_limit_bytes=VMEM_BYTES),
        name="unpack_weights",
    )(slots)
    return dict(zip(outs, values, strict=True))


def pack_kernel(
    order, slot_rows, bases,
    gwe, gwst, gtaps, gbias, gwo, gwq, gpair, gwr, gcols, grows, slots,
    flat, wide,
):
    width = gwst.shape[0]
    hidden = gwst.shape[1]
    used = bases["shrink_bias"] + 1
    for k in range(3):
        wide[k, pl.ds(used, wide.shape[1] - used), :] = jnp.zeros((wide.shape[1] - used, 128), F32)
    done = wide.shape[1] * width // 128
    flat[done:, :] = jnp.zeros((flat.shape[0] - done, 128), F32)

    def put(base, value, stride=1):
        count = value.shape[0]
        at = pl.ds(base, count, stride=stride) if stride > 1 else pl.ds(base, count)
        wide[0, at, :] = value[:, 0:128]
        wide[1, at, :] = value[:, 128:256]
        wide[2, at, 0 : width - 256] = value[:, 256:width]

    for k, name in enumerate(("pre_gain", "pre_shift", "mlp_gain", "mlp_shift")):
        put(bases[name], jnp.sum(gcols[k].T, axis=0, keepdims=True))
    put(bases["shrink_bias"], jnp.sum(gbias[...].T, axis=0, keepdims=True))
    for k, name in enumerate(("reduce_bias", "reduce_gain", "reduce_shift")):
        put(bases[name], jnp.sum(grows[8 * k : 8 * k + 8, :], axis=0, keepdims=True))
    put(bases["query_weight"], gwq[0 : width + 1, :])
    for p in range(4):
        put(bases["reduce_weight"] + p * width, gwr[p].T)
    put(bases["pair_weight"], gpair[0:width, :].T[0:width], 2)
    value = gpair[width : 2 * width, :].T
    put(bases["pair_weight"] + 1, value[0:width], 2)
    put(bases["value_bias"], value[width : width + 1])
    put(bases["output_weight"], gwo[0 : width + 1, :])
    sums = jnp.concatenate(
        [jnp.sum(gtaps[8 * k : 8 * k + 8, :], axis=0, keepdims=True) for k in range(10)], axis=0
    )
    for q in range(hidden // width):
        put(bases["expand_weight"] + q, gwe[0 : width + 1, q * width : (q + 1) * width], hidden // width)
        put(bases["spatial_weight"] + q, sums[:, q * width : (q + 1) * width], hidden // width)
    for k in range(hidden // 128):
        put(bases["shrink_weight"] + 128 * k, gwst[:, 128 * k : 128 * k + 128].T)
    low = lax.broadcasted_iota(jnp.int32, (SPAN, 128), 1) < 64

    def regroup(t, _):
        even = pl.ds(t * (2 * SPAN), SPAN, stride=2)
        odd = pl.ds(t * (2 * SPAN) + 1, SPAN, stride=2)
        turned = [pltpu.roll(wide[k, odd, :], 64, 1) for k in range(3)]
        part = [
            wide[0, even, :],
            wide[1, even, :],
            jnp.where(low, wide[2, even, :], turned[0]),
            jnp.where(low, turned[0], turned[1]),
            jnp.where(low, turned[1], turned[2]),
        ]
        for k in range(5):
            flat[pl.ds(t * (5 * SPAN) + k, SPAN, stride=5), :] = part[k]
        return 0

    lax.fori_loop(0, wide.shape[1] // (2 * SPAN), regroup, 0)
    inside = lax.broadcasted_iota(jnp.int32, slots.shape[1:], 0) < slot_rows
    for slot, place in enumerate(order):
        slots[place] = jnp.where(inside, flat[pl.ds(slot * slot_rows, slots.shape[1]), :], 0.0).astype(BF)


def pack_gradients(grads, order, slot_rows, padded_rows, width):
    bases, count = row_bases(width, 4 * width)
    flat_rows = max(len(order) * slot_rows, wide_rows(count) * width // 128) + padded_rows
    return pl.pallas_call(
        partial(pack_kernel, order, slot_rows, bases),
        out_shape=jax.ShapeDtypeStruct((len(order), padded_rows, 128), BF),
        in_specs=[pl.BlockSpec(memory_space=pltpu.VMEM)] * len(grads),
        out_specs=pl.BlockSpec(memory_space=pltpu.VMEM),
        scratch_shapes=[pltpu.VMEM((flat_rows, 128), F32), pltpu.VMEM((3, wide_rows(count), 128), F32)],
        compiler_params=pltpu.CompilerParams(vmem_limit_bytes=VMEM_BYTES),
        name="pack_gradients",
    )(*grads)


def device_step(images, cotangent, kv_sides, w):
    positions = jnp.arange(TOKENS, dtype=jnp.int32)
    limit = 2 * kv_sides[:, None]
    mask = ((positions[None] // GRID < limit) & (positions[None] % GRID < limit)).astype(F32)
    mask = jnp.broadcast_to(mask[:, None, :], (mask.shape[0], 8, TOKENS))
    perm = jnp.asarray(patch_order(), BF)
    pre, patches, reduced, memory, mixed, lse, middle, post = attention_forward(
        kv_sides, images, mask, perm, w["vec"], w["rows"], w["wqt"], w["wr"], w["wk"], w["wvt"], w["wot"]
    )
    output, grad_post, gwe, gwst, gtaps, gbias = feed_forward(
        post, cotangent, mask, middle, w["we"], w["wst"], w["taps"], w["vec"]
    )
    grad_images, gwo, gwq, gpair, gwr, gcols, grows = attention_backward(
        kv_sides, images, cotangent, mask, pre, patches, reduced, memory, mixed, lse, middle, grad_post,
        perm, w["vec"], w["rows"], w["wq"], w["wqt"], w["wr"], w["wk"], w["wv"], w["wvt"], w["wo"],
    )
    return output, grad_images, (gwe, gwst, gtaps, gbias, gwo, gwq, gpair, gwr, gcols, grows)


def step(on_grid, images, cotangent, kv_sides, params, first_moment, second_moment):
    width = images.shape[2]
    axes = ("dp", "fsdp")
    outer, inner = lax.axis_size("dp"), lax.axis_size("fsdp")
    slot_rows = params.shape[0] // 128
    padded_rows = -(-slot_rows // 32) * 32
    own = jnp.pad(params.reshape(slot_rows, 128).astype(BF), ((0, padded_rows - slot_rows), (0, 0)))
    if on_grid:
        order = [(s % 2) * 16 + s // 8 * 4 + s % 8 // 2 for s in range(32)]
        slots = gather_slots(own).reshape(32, padded_rows, 128)
    else:
        order = list(range(outer * inner))
        slots = lax.all_gather(own, axes)
    weights = unpack_weights(slots, order, slot_rows, width)
    output, grad_images, grads = device_step(
        images.transpose(0, 2, 1), cotangent.transpose(0, 2, 1), kv_sides, weights
    )
    slots = pack_gradients(grads, order, slot_rows, padded_rows, width)
    if on_grid:
        shard, squares = reduce_slots(slots.reshape(2, 4, 4, padded_rows, 128))
        squares = jnp.sum(squares)
    else:
        shard = lax.psum_scatter(slots.astype(F32), axes)
        squares = lax.psum(jnp.sum(shard * shard), axes)
    shard = shard[:slot_rows].reshape(-1)
    grad_norm = jnp.sqrt(squares)
    clipped = shard * jnp.minimum(1.0, CLIP_NORM / (grad_norm + 1e-06))
    new_first = BETA_FIRST * first_moment + (1.0 - BETA_FIRST) * clipped
    new_second = BETA_SECOND * second_moment + (1.0 - BETA_SECOND) * clipped * clipped
    first_hat = new_first / (1.0 - BETA_FIRST**STEP)
    second_hat = new_second / (1.0 - BETA_SECOND**STEP)
    new_params = params - RATE * (first_hat / (jnp.sqrt(second_hat) + EPSILON) + DECAY * params)
    return (
        output.transpose(0, 2, 1),
        grad_images.transpose(0, 2, 1),
        grad_norm,
        new_first,
        new_second,
        new_params,
    )


def solution(mesh):
    data = P(("dp", "fsdp"), None, None)
    flat = P(("dp", "fsdp"))
    on_grid = dict(mesh.shape) == {"dp": 4, "fsdp": 8}
    return jax.shard_map(
        partial(step, on_grid),
        mesh=mesh,
        in_specs=(data, data, flat, flat, flat, flat),
        out_specs=(data, data, P(), flat, flat, flat),
        check_vma=False,
    )
```

```python
from functools import partial
import math

import jax
import jax.numpy as jnp
import numpy as np
from jax import lax
from jax.experimental import pallas as pl
from jax.experimental.pallas import tpu as pltpu
from jax.sharding import PartitionSpec as P

HEADS = 5
HEAD_DIM = 64
GRID = 48
KV = 24
STEP = 10

CLIP_NORM = 1.0
BETA_FIRST = 0.9
BETA_SECOND = 0.999
RATE = 0.04
DECAY = 0.05
EPSILON = 1e-08

F32 = jnp.float32
BF = jnp.bfloat16
NN = (((1,), (0,)), ((), ()))
NT = (((1,), (1,)), ((), ()))
TOKENS = GRID * GRID
KEYS = KV * KV
PITCH = GRID + 8
EXT = 16
LOG2E = math.log2(math.e)
QUERY_SCALE = HEAD_DIM**-0.5 * LOG2E
GELU_A = math.sqrt(2.0 / math.pi)
GELU_B = GELU_A * 0.044715
VMEM_BYTES = 63 * 1024 * 1024


def mm(left, right, dims=NN):
    return lax.dot_general(left, right, dims, preferred_element_type=F32)


def patch_order():
    matrix = np.zeros((8 * GRID, 8 * GRID), np.float32)
    for p in range(4):
        for a in range(4):
            for b in range(KV):
                matrix[p * 96 + a * KV + b, (2 * a + p // 2) * GRID + 2 * b + p % 2] = 1.0
    return matrix


def fold_rows(x):
    return jnp.sum(x.reshape(x.shape[0] // 8, 8, x.shape[1]), axis=0)


def norm_columns(x):
    scale = 1.0 / x.shape[0]
    centred = x - jnp.sum(x, axis=0, keepdims=True) * scale
    rstd = lax.rsqrt(jnp.sum(centred * centred, axis=0, keepdims=True) * scale + 1e-06)
    return centred * rstd, rstd


def norm_columns_back(normed, rstd, scaled):
    scale = 1.0 / scaled.shape[0]
    plain = jnp.sum(scaled, axis=0, keepdims=True) * scale
    mixed = jnp.sum(scaled * normed, axis=0, keepdims=True) * scale
    return rstd * (scaled - plain - normed * mixed)


def norm_rows(x):
    centred = x - jnp.mean(x, axis=-1, keepdims=True)
    rstd = lax.rsqrt(jnp.mean(centred * centred, axis=-1, keepdims=True) + 1e-06)
    return centred * rstd, rstd


def norm_rows_back(normed, rstd, scaled):
    plain = jnp.mean(scaled, axis=-1, keepdims=True)
    mixed = jnp.mean(scaled * normed, axis=-1, keepdims=True)
    return rstd * (scaled - plain - normed * mixed)


def first_row(row, rows=EXT):
    index = lax.broadcasted_iota(jnp.int32, (rows, row.shape[-1]), 0)
    return jnp.where(index == 0, row, 0.0)


def three_parts(x):
    high = x.astype(BF).astype(F32)
    middle = (x - high).astype(BF).astype(F32)
    return high, middle, (x - high - middle).astype(BF).astype(F32)


def whole(x):
    zeros = (0,) * len(x.shape)
    return pl.BlockSpec(x.shape, lambda *_: zeros)


def per_image(x, **kwargs):
    zeros = (0,) * (len(x.shape) - 1)
    return pl.BlockSpec((1,) + tuple(x.shape[1:]), lambda i, *_: (i,) + zeros, **kwargs)


def key_columns(ref, side, h_range, ones_from, ones_to, with_mask):
    lane = lax.broadcasted_iota(jnp.int32, (KV, 64), 1)
    cell = lax.broadcasted_iota(jnp.int32, (KV, 64), 0)
    ones = jnp.where((lane >= ones_from) & (lane <= ones_to), 1.0, 0.0)
    for a in range(KV):
        block = ones
        if with_mask:
            bias = jnp.where((cell < side) & (a < side), 0.0, -1e30)
            block = jnp.where(lane == 0, bias, ones)
        block = block.astype(BF)
        for h in h_range:
            ref[h, a * KV : (a + 1) * KV, 64:128] = block


def attention_forward_kernel(
    sides, images, mask, perm, vec, rows, wqt, wr, wk, wvt, wot,
    pre, patches, reduced, memory, mixed, lse, middle, post,
    key_ref, value_ref,
):
    i = pl.program_id(0)
    width = images.shape[1]

    def first_norm(t, _):
        for u in range(3):
            at = pl.ds(pl.multiple_of(t * 384 + u * 128, 128), 128)
            x = images[0, :, at].astype(F32) * mask[0, 0:1, at]
            normed, _unused = norm_columns(x)
            pre[0, 0:width, at] = (normed * vec[0] + vec[1]).astype(BF)
            pre[0, width : width + EXT, at] = first_row(jnp.ones((1, 128), F32)).astype(BF)
        at = pl.ds(pl.multiple_of(t * 384, 128), 384)
        picked = mm(perm[...], pre[0, 0:width, at], NT).astype(BF)
        for p in range(4):
            patches[0, p, pl.ds(pl.multiple_of(t * 96, 32), 96), :] = picked[p * 96 : (p + 1) * 96]
        return 0

    lax.fori_loop(0, TOKENS // 384, first_norm, 0)

    total = rows[0:1, :]
    for p in range(4):
        total = total + mm(patches[0, p], wr[p])
    reduced[0] = total
    normed, _unused = norm_rows(total)
    memory[0, :, 0:width] = (normed * rows[1:2, :] + rows[2:3, :]).astype(BF)
    lane = lax.broadcasted_iota(jnp.int32, (KEYS, 64), 1)
    memory[0, :, width : width + 64] = jnp.where(lane == 0, 1.0, 0.0).astype(BF)
    keys = mm(memory[0, :, 0:width], wk[...]).astype(BF)
    key_columns(key_ref, sides[i], range(HEADS), 1, 0, True)
    values = mm(wvt[...], memory[0], NT).astype(BF)
    ones = first_row(jnp.ones((1, KEYS), F32)).astype(BF)
    for h in range(HEADS):
        at = slice(h * HEAD_DIM, (h + 1) * HEAD_DIM)
        key_ref[h, :, 0:HEAD_DIM] = keys[:, at]
        value_ref[h, 0:HEAD_DIM, :] = values[at]
        value_ref[h, HEAD_DIM : HEAD_DIM + EXT, :] = ones
    mixed[0, width : width + EXT, :] = first_row(jnp.ones((1, TOKENS), F32)).astype(BF)
    queries = (mm(wqt[...], pre[0]) * QUERY_SCALE).astype(BF)
    tail = first_row(jnp.ones((1, TOKENS), F32), 64).astype(BF)
    for h in range(HEADS):
        at = slice(h * HEAD_DIM, (h + 1) * HEAD_DIM)
        scores = mm(key_ref[h], jnp.concatenate([queries[at], tail], axis=0))
        top = jnp.max(scores, axis=0, keepdims=True)
        weights = jnp.exp2(scores - top).astype(BF)
        out = mm(value_ref[h], weights)
        total = out[HEAD_DIM : HEAD_DIM + 1]
        mixed[0, at, :] = (out[0:HEAD_DIM] * (1.0 / total)).astype(BF)
        lse[0, h : h + 1, :] = top + jnp.log2(total)

    def second_norm(t, _):
        at = pl.ds(pl.multiple_of(t * 384, 128), 384)
        branch = mm(wot[...], mixed[0, :, at])
        for u in range(3):
            at = pl.ds(pl.multiple_of(t * 384 + u * 128, 128), 128)
            here = mask[0, 0:1, at]
            x = images[0, :, at].astype(F32) * here + branch[:, u * 128 : (u + 1) * 128]
            middle[0, :, at] = x
            normed, _unused = norm_columns(x)
            post[0, 0:width, at] = ((normed * vec[2] + vec[3]) * here).astype(BF)
            post[0, width : width + EXT, at] = first_row(here).astype(BF)
        return 0

    lax.fori_loop(0, TOKENS // 384, second_norm, 0)


def attention_forward(sides, images, mask, perm, vec, rows, wqt, wr, wk, wvt, wot):
    n, width, tokens = images.shape
    shape = jax.ShapeDtypeStruct
    outs = [
        shape((n, width + EXT, tokens), BF),
        shape((n, 4, KEYS, width), BF),
        shape((n, KEYS, width), F32),
        shape((n, KEYS, width + 64), BF),
        shape((n, width + EXT, tokens), BF),
        shape((n, 8, tokens), F32),
        shape((n, width, tokens), F32),
        shape((n, width + EXT, tokens), BF),
    ]
    weights = (perm, vec, rows, wqt, wr, wk, wvt, wot)
    return pl.pallas_call(
        attention_forward_kernel,
        grid_spec=pltpu.PrefetchScalarGridSpec(
            num_scalar_prefetch=1,
            grid=(n,),
            in_specs=[per_image(images), per_image(mask)] + [whole(x) for x in weights],
            out_specs=[per_image(x) for x in outs],
            scratch_shapes=[
                pltpu.VMEM((HEADS, KEYS, 128), BF),
                pltpu.VMEM((HEADS, HEAD_DIM + EXT, KEYS), BF),
            ],
        ),
        out_shape=outs,
        compiler_params=pltpu.CompilerParams(vmem_limit_bytes=VMEM_BYTES),
        name="attention_forward",
    )(sides, images, mask, *weights)


def feed_forward_kernel(
    post_next, cot_next, mask_next, we_next, wst_next, taps,
    post, cot, mask, middle, we, wst, vec,
    output, grad_post, gwe, gwst, gtaps, gbias,
    padded_0, padded_1, grad_padded, grad_act, act_0, act_1, grad_exp_0, grad_exp_1,
    post_rows, out_grad_rows, out_grad, total,
):
    s = pl.program_id(0)
    last = pl.num_programs(0) - 1
    width, block = wst.shape
    blocks = gwst.shape[1] // block
    halves = block // 128
    rows = 16
    chunks = GRID // rows
    span = rows * GRID
    js = pl.ds(pl.multiple_of(lax.rem(s, blocks) * block, block), block)
    js_done = pl.ds(pl.multiple_of(lax.rem(jnp.maximum(s - 1, 0), blocks) * block, block), block)

    def tokens(t):
        return pl.ds(pl.multiple_of(t * span, span), span)

    def expand(t, padded, we, wst):
        at = tokens(t)
        filled = mm(post_rows[at, :], we[...]).astype(BF).astype(F32)
        for h in range(halves):
            for r in range(rows):
                start = pl.multiple_of((t * rows + r + 1) * PITCH + 8, 8)
                padded[h, pl.ds(start, GRID), :] = filled[r * GRID : (r + 1) * GRID, h * 128 : (h + 1) * 128]
        grad_act[at, :] = mm(out_grad_rows[at, :], wst[...]).astype(BF)

    def finish(t, act, grad_exp):
        at = tokens(t)
        total[:, at] += mm(wst[...], act[at, :], NT)
        grad_post[0, :, at] += mm(we[0:width, :], grad_exp[at, :], NT)
        gwst[:, js_done] += mm(out_grad[:, at], act[at, :])
        gwe[:, js_done] += mm(post[0, :, at], grad_exp[at, :])

    def convolve(t, padded, act):
        for h in range(halves):
            hs = slice(h * 128, (h + 1) * 128)
            w = [jnp.broadcast_to(taps[k : k + 1, hs], (GRID, 128)).astype(BF) for k in range(10)]
            sums = jnp.zeros((8, 128), F32)
            open_rows = {}
            for q in range(-1, rows + 1):
                base = (t * rows + q + 1) * PITCH + 8
                x = [padded[h, pl.ds(base + d, GRID), :].astype(BF) for d in (-1, 0, 1)]
                for a in (2, 1, 0):
                    r = q + 1 - a
                    if 0 <= r < rows:
                        part = w[3 * a] * x[0] + w[3 * a + 1] * x[1] + w[3 * a + 2] * x[2]
                        open_rows[r] = part + open_rows.get(r, w[9])
                r = q - 1
                if r < 0:
                    continue
                at = pl.ds(pl.multiple_of((t * rows + r) * GRID, GRID), GRID)
                gelu, slope = gelu_pair(open_rows.pop(r))
                act[at, hs] = gelu
                grad = (grad_act[at, hs] * slope).astype(F32)
                start = pl.multiple_of((t * rows + r + 1) * PITCH + 8, 8)
                grad_padded[h, pl.ds(start, GRID), :] = grad
                sums = sums + fold_rows(grad)
            cols = pl.ds(pl.multiple_of(lax.rem(s, blocks) * block + h * 128, 128), 128)
            gtaps[72:80, cols] += sums

    def convolve_back(t, padded, grad_exp):
        for h in range(halves):
            hs = slice(h * 128, (h + 1) * 128)
            w = [jnp.broadcast_to(taps[k : k + 1, hs], (GRID, 128)).astype(BF) for k in range(9)]
            sums = [jnp.zeros((8, 128), F32) for _ in range(9)]
            waiting = {}
            open_rows = {}
            x = {}
            for q in range(-1, rows + 1):
                base = (t * rows + q + 1) * PITCH + 8
                grads = [grad_padded[h, pl.ds(base + 1 - b, GRID), :].astype(BF) for b in range(3)]
                if q + 1 < rows:
                    start = pl.multiple_of((t * rows + q + 2) * PITCH + 8, 8)
                    x[q + 1] = padded[h, pl.ds(start, GRID), :].astype(BF)
                for a in range(3):
                    r = q + a - 1
                    if not 0 <= r < rows:
                        continue
                    part = w[3 * a] * grads[0] + w[3 * a + 1] * grads[1] + w[3 * a + 2] * grads[2]
                    open_rows[r] = part + open_rows[r] if r in open_rows else part
                    for b in range(3):
                        k = 3 * a + b
                        product = x[r] * grads[b]
                        product = product[0:16] + product[16:32] + product[32:48]
                        if k in waiting:
                            product = (product + waiting.pop(k)).astype(F32)
                            sums[k] = sums[k] + product[0:8] + product[8:16]
                        else:
                            waiting[k] = product
                r = q - 1
                if r >= 0:
                    at = pl.ds(pl.multiple_of((t * rows + r) * GRID, GRID), GRID)
                    grad_exp[at, hs] = open_rows.pop(r)
                    x.pop(r)
            cols = pl.ds(pl.multiple_of(lax.rem(s, blocks) * block + h * 128, 128), 128)
            for k in range(9):
                gtaps[8 * k : 8 * k + 8, cols] += sums[k]

    @pl.when(s == 0)
    def _():
        for ref in (padded_0, padded_1, grad_padded, act_1, grad_exp_1, out_grad, gwe, gwst, gtaps, gbias, post_rows):
            ref[...] = jnp.zeros_like(ref)

    @pl.when((s == 0) | ((lax.rem(s + 1, blocks) == 0) & (s + 1 < last)))
    def _():
        for t in range(TOKENS // 384):
            at = slice(t * 384, (t + 1) * 384)
            grad = cot_next[0, :, at].astype(F32) * mask_next[0, 0:1, at]
            gbias[...] += grad[:, 0:128] + grad[:, 128:256] + grad[:, 256:384]
            out_grad_rows[at, :] = grad.astype(BF).T
            post_rows[at, 0 : width + EXT] = post_next[0, :, at].T

    @pl.when(lax.rem(s, blocks) == min(1, blocks - 1))
    def _():
        for t in range(TOKENS // 384):
            at = slice(t * 384, (t + 1) * 384)
            out_grad[:, at] = (cot[0, :, at].astype(F32) * mask[0, 0:1, at]).astype(BF)

    @pl.when((s == 0) | (lax.rem(s, blocks) == min(1, blocks - 1)))
    def _():
        total[...] = jnp.zeros_like(total)
        grad_post[...] = jnp.zeros_like(grad_post)

    @pl.when(s == 0)
    def _():
        def first(t, _):
            expand(t, padded_0, we, wst)
            return 0

        lax.fori_loop(0, chunks, first, 0)

    def work(padded, padded_next, act, act_done, grad_exp, grad_exp_done):
        def forward(t, _):
            finish(t, act_done, grad_exp_done)
            convolve(t, padded, act)
            return 0

        def backward(t, _):
            expand(t, padded_next, we_next, wst_next)
            convolve_back(t, padded, grad_exp)
            return 0

        lax.fori_loop(0, chunks, forward, 0)
        lax.fori_loop(0, chunks, backward, 0)

    @pl.when((s < last) & (lax.rem(s, 2) == 0))
    def _():
        work(padded_0, padded_1, act_0, act_1, grad_exp_0, grad_exp_1)

    @pl.when((s < last) & (lax.rem(s, 2) == 1))
    def _():
        work(padded_1, padded_0, act_1, act_0, grad_exp_1, grad_exp_0)

    @pl.when(s == last)
    def _():
        def rest(t, _):
            @pl.when(lax.rem(s, 2) == 0)
            def _():
                finish(t, act_1, grad_exp_1)

            @pl.when(lax.rem(s, 2) == 1)
            def _():
                finish(t, act_0, grad_exp_0)

            return 0

        lax.fori_loop(0, chunks, rest, 0)

    @pl.when((s > 0) & (lax.rem(s, blocks) == 0))
    def _():
        for t in range(TOKENS // 128):
            at = slice(t * 128, (t + 1) * 128)
            output[0, :, at] = ((middle[0, :, at] + total[:, at] + vec[4]) * mask[0, 0:1, at]).astype(BF)


def gelu_pair(x):
    kind = x.dtype.type
    square = x * x
    half = kind(0.5) * jnp.tanh(x * (kind(GELU_B) * square + kind(GELU_A))) + kind(0.5)
    gelu = x * half
    return gelu, half + gelu * (kind(1.0) - half) * (kind(6.0 * GELU_B) * square + kind(2.0 * GELU_A))


def feed_forward(post, cot, mask, middle, we, wst, taps, vec, block=256):
    n, width, tokens = cot.shape
    hidden = wst.shape[1]
    blocks = hidden // block
    count = n * blocks
    shape = jax.ShapeDtypeStruct
    outs = [
        shape((n, width, tokens), BF),
        shape((n, width, tokens), F32),
        shape((width + EXT, hidden), F32),
        shape((width, hidden), F32),
        shape((80, hidden), F32),
        shape((width, 128), F32),
    ]

    def ahead(s):
        return jnp.minimum(s + 1, count - 1)

    def behind(s):
        return jnp.maximum(s - 1, 0)

    def image(x, step):
        zeros = (0,) * (len(x.shape) - 1)
        return pl.BlockSpec((1,) + tuple(x.shape[1:]), lambda s: (step(s) // blocks,) + zeros)

    def columns(x, step):
        return pl.BlockSpec((x.shape[0], block), lambda s: (0, lax.rem(step(s), blocks)))

    return pl.pallas_call(
        feed_forward_kernel,
        grid=(count + 1,),
        in_specs=[image(x, ahead) for x in (post, cot, mask)]
        + [columns(we, ahead), columns(wst, ahead), columns(taps, lambda s: jnp.minimum(s, count - 1))]
        + [image(x, behind) for x in (post, cot, mask, middle)]
        + [columns(we, behind), columns(wst, behind), whole(vec)],
        out_specs=[image(x, behind) for x in outs[:2]] + [whole(x) for x in outs[2:]],
        out_shape=outs,
        scratch_shapes=[pltpu.VMEM((block // 128, (GRID + 2) * PITCH + 8, 128), F32)] * 3
        + [pltpu.VMEM((tokens, block), BF)] * 5
        + [
            pltpu.VMEM((tokens, width + 64), BF),
            pltpu.VMEM((tokens, width), BF),
            pltpu.VMEM((width, tokens), BF),
            pltpu.VMEM((width, tokens), F32),
        ],
        compiler_params=pltpu.CompilerParams(vmem_limit_bytes=VMEM_BYTES),
        name="feed_forward",
    )(post, cot, mask, we, wst, taps, post, cot, mask, middle, we, wst, vec)


def attention_backward_kernel(
    sides, images, cot, mask, pre, patches, reduced, memory, mixed, lse, middle, grad_post,
    perm, vec, rows, wq, wqt, wr, wk, wv, wvt, wo,
    grad_images, gwo, gwq, gpair, gwr, gcols, grows,
    branch, grad_mixed, queries, grad_queries, key_ref, value_ref, keys_t, grad_keys, grad_values, grad_patches,
):
    i = pl.program_id(0)
    width = images.shape[1]

    @pl.when(i == 0)
    def _():
        for ref in (gwo, gwq, gpair, gwr, gcols, grows):
            ref[...] = jnp.zeros_like(ref)

    def mlp_norm_back(t, _):
        gain = shift = jnp.zeros((width, 128), F32)
        for u in range(3):
            at = pl.ds(pl.multiple_of(t * 384 + u * 128, 128), 128)
            here = mask[0, 0:1, at]
            normed, rstd = norm_columns(middle[0, :, at])
            grad = grad_post[0, :, at] * here
            gain = gain + grad * normed
            shift = shift + grad
            grad = cot[0, :, at].astype(F32) * here + norm_columns_back(normed, rstd, grad * vec[2])
            grad_images[0, :, at] = grad
            branch[:, at] = grad.astype(BF)
        gcols[2] += gain
        gcols[3] += shift
        return 0

    lax.fori_loop(0, TOKENS // 384, mlp_norm_back, 0)
    gwo[...] += mm(mixed[0], branch[...], NT)
    grad_mixed[...] = mm(wo[...], branch[...]).astype(BF)
    queries[...] = (mm(wqt[...], pre[0]) * QUERY_SCALE).astype(BF)
    keys = mm(memory[0, :, 0:width], wk[...]).astype(BF)
    keys_t[...] = keys.T
    values = mm(wvt[...], memory[0], NT).astype(BF).T
    key_columns(key_ref, sides[i], range(HEADS), 1, 3, True)
    key_columns(value_ref, sides[i], range(HEADS), 1, 3, False)
    for h in range(HEADS):
        at = slice(h * HEAD_DIM, (h + 1) * HEAD_DIM)
        key_ref[h, :, 0:HEAD_DIM] = keys[:, at]
        value_ref[h, :, 0:HEAD_DIM] = values[:, at]

    span = TOKENS // 2
    index = lax.broadcasted_iota(jnp.int32, (64, span), 0)
    for t in range(TOKENS // span):
        at = slice(t * span, (t + 1) * span)
        for h in range(HEADS):
            hs = slice(h * HEAD_DIM, (h + 1) * HEAD_DIM)
            one, two, three = three_parts(-lse[0, h : h + 1, at])
            tail = jnp.where(index == 2, two, jnp.where(index == 3, three, 0.0))
            tail = jnp.where(index == 0, 1.0, jnp.where(index == 1, one, tail)).astype(BF)
            query = queries[hs, at]
            attend = jnp.exp2(mm(key_ref[h], jnp.concatenate([query, tail], axis=0)))
            low = attend.astype(BF)
            grad = grad_mixed[hs, at]
            inner = grad.astype(F32) * mixed[0, hs, at].astype(F32)
            one, two, three = three_parts(-jnp.sum(inner, axis=0, keepdims=True))
            tail = jnp.where(index == 2, two, jnp.where(index == 3, three, 0.0))
            tail = jnp.where(index == 1, one, tail).astype(BF)
            grad_attend = mm(value_ref[h], jnp.concatenate([grad, tail], axis=0))
            grad_scores = (attend * grad_attend).astype(BF)
            grad_value = mm(grad, low, NT)
            grad_key = mm(query, grad_scores, NT) * (1.0 / LOG2E)
            if t == 0:
                grad_values[hs, :] = grad_value
                grad_keys[hs, :] = grad_key
            else:
                grad_values[hs, :] += grad_value
                grad_keys[hs, :] += grad_key
            grad_queries[hs, at] = (mm(keys_t[hs, :], grad_scores) * HEAD_DIM**-0.5).astype(BF)

    low_keys = grad_keys[...].astype(BF)
    low_values = grad_values[...].astype(BF)
    gpair[0:width, :] += mm(low_keys, memory[0])
    gpair[width : 2 * width, :] += mm(low_values, memory[0])
    grad_memory = mm(low_keys.T, wk[...], NT) + mm(low_values.T, wv[...], NT)
    normed, rstd = norm_rows(reduced[0])
    grows[8:16, :] += fold_rows(grad_memory * normed)
    grows[16:24, :] += fold_rows(grad_memory)
    grad_reduced = norm_rows_back(normed, rstd, grad_memory * rows[1:2, :]).astype(BF)
    grows[0:8, :] += fold_rows(grad_reduced.astype(F32))
    grad_reduced_t = grad_reduced.T
    for p in range(4):
        gwr[p] += mm(grad_reduced_t, patches[0, p])
        grad_patches[p] = mm(grad_reduced, wr[p], NT).astype(BF)
    gwq[...] += mm(pre[0], grad_queries[...], NT)

    def pre_norm_back(t, _):
        at = pl.ds(pl.multiple_of(t * 384, 128), 384)
        grad_pre = mm(wq[...], grad_queries[:, at])
        start = pl.ds(pl.multiple_of(t * 96, 32), 96)
        picked = jnp.concatenate([grad_patches[p, start, :] for p in range(4)], axis=0)
        grad_pre = grad_pre + mm(picked.T, perm[...])
        gain = shift = jnp.zeros((width, 128), F32)
        for u in range(3):
            at = pl.ds(pl.multiple_of(t * 384 + u * 128, 128), 128)
            here = mask[0, 0:1, at]
            normed, rstd = norm_columns(images[0, :, at].astype(F32) * here)
            grad = grad_pre[:, u * 128 : (u + 1) * 128]
            gain = gain + grad * normed
            shift = shift + grad
            back = norm_columns_back(normed, rstd, grad * vec[0])
            grad_images[0, :, at] = (grad_images[0, :, at] + back) * here
        gcols[0] += gain
        gcols[1] += shift
        return 0

    lax.fori_loop(0, TOKENS // 384, pre_norm_back, 0)


def attention_backward(
    sides, images, cot, mask, pre, patches, reduced, memory, mixed, lse, middle, grad_post,
    perm, vec, rows, wq, wqt, wr, wk, wv, wvt, wo,
):
    n, width, tokens = images.shape
    shape = jax.ShapeDtypeStruct
    outs = [
        shape((n, width, tokens), F32),
        shape((width + EXT, width), F32),
        shape((width + EXT, width), F32),
        shape((2 * width, width + 64), F32),
        shape((4, width, width), F32),
        shape((4, width, 128), F32),
        shape((24, width), F32),
    ]
    one = {"pipeline_mode": pl.Buffered(1)}
    inputs = (images, cot, mask, pre, patches, reduced, memory, mixed, lse)
    weights = (perm, vec, rows, wq, wqt, wr, wk, wv, wvt, wo)
    return pl.pallas_call(
        attention_backward_kernel,
        grid_spec=pltpu.PrefetchScalarGridSpec(
            num_scalar_prefetch=1,
            grid=(n,),
            in_specs=[per_image(x) for x in inputs]
            + [per_image(middle, **one), per_image(grad_post, **one)]
            + [whole(x) for x in weights],
            out_specs=[per_image(outs[0], **one)] + [whole(x) for x in outs[1:]],
            scratch_shapes=[
                pltpu.VMEM((width, tokens), BF),
                pltpu.VMEM((width, tokens), BF),
                pltpu.VMEM((width, tokens), BF),
                pltpu.VMEM((width, tokens), BF),
                pltpu.VMEM((HEADS, KEYS, 128), BF),
                pltpu.VMEM((HEADS, KEYS, 128), BF),
                pltpu.VMEM((width, KEYS), BF),
                pltpu.VMEM((width, KEYS), F32),
                pltpu.VMEM((width, KEYS), F32),
                pltpu.VMEM((4, KEYS, width), BF),
            ],
        ),
        out_shape=outs,
        compiler_params=pltpu.CompilerParams(vmem_limit_bytes=VMEM_BYTES),
        name="attention_backward",
    )(sides, *inputs, middle, grad_post, *weights)

MESH = pl.DeviceIdType.MESH


class Place:
    def __init__(self):
        self.dp = lax.axis_index("dp")
        fsdp = lax.axis_index("fsdp")
        self.y, self.x = self.dp // 2, self.dp % 2
        self.z, self.core = fsdp // 2, fsdp % 2
        self.beside_x = (self.dp + 1 - 2 * self.x, fsdp)
        self.beside_y = (self.dp + 2 - 4 * self.y, fsdp)
        self.beside_core = (self.dp, fsdp + 1 - 2 * self.core)

    def up(self, k):
        return (self.z + k) % 4

    def along_z(self, k):
        return (self.dp, self.up(k) * 2 + self.core)

    def partners(self):
        return [self.beside_core, self.beside_x, self.beside_y] + [self.along_z(k) for k in (1, 2, 3)]

    def greet(self):
        barrier = pltpu.get_barrier_semaphore()
        partners = self.partners()
        for device in partners:
            pl.semaphore_signal(barrier, inc=1, device_id=device, device_id_type=MESH)
        pl.semaphore_wait(barrier, len(partners))


class Sender:
    def __init__(self, send, recv):
        self.send, self.recv, self.started = send, recv, []

    def __call__(self, source, target, device):
        k = len(self.started)
        copy = pltpu.make_async_remote_copy(
            src_ref=source,
            dst_ref=target,
            send_sem=self.send.at[k],
            recv_sem=self.recv.at[k],
            device_id=device,
            device_id_type=MESH,
        )
        copy.start()
        self.started.append(copy)
        return copy

    def finish(self):
        for copy in self.started:
            copy.wait_send()


def gather_kernel(own, out, own_sem, send_sem, recv_sem):
    me = Place()
    half = own.shape[0] // 2
    first, second = pl.ds(0, half), pl.ds(half, half)
    send = Sender(send_sem, recv_sem)
    copy = pltpu.make_async_copy(own, out.at[me.core, me.dp, me.z], own_sem)
    copy.start()
    me.greet()
    slot = out.at[me.core, me.dp, me.z]
    z_copies = [send(own, slot, me.along_z(k)) for k in (1, 2, 3)]
    x_copies = [send(own, slot, me.beside_x)]
    y_copies = [send(own, slot, me.beside_y)]
    core_copies = [send(own, slot, me.beside_core)]
    half_copies = []

    def forward(k):
        z = (me.z + 4 - k) % 4
        x_copies[k].wait_recv()
        dp = me.beside_x[0]
        slot = out.at[me.core, dp, z]
        half_copies.append(send(slot.at[first], slot.at[first], me.beside_y))
        core_copies.append(send(slot, slot, me.beside_core))
        y_copies[k].wait_recv()
        dp = me.beside_y[0]
        slot = out.at[me.core, dp, z]
        half_copies.append(send(slot.at[second], slot.at[second], me.beside_x))
        core_copies.append(send(slot, slot, me.beside_core))

    forward(0)
    for k in (1, 2, 3):
        z_copies[k - 1].wait_recv()
        slot = out.at[me.core, me.dp, (me.z + 4 - k) % 4]
        x_copies.append(send(slot, slot, me.beside_x))
        y_copies.append(send(slot, slot, me.beside_y))
        core_copies.append(send(slot, slot, me.beside_core))
        forward(k)
    for k in range(4):
        half_copies[2 * k].wait_recv()
        half_copies[2 * k + 1].wait_recv()
        slot = out.at[me.core, 3 - me.dp, (me.z + 4 - k) % 4]
        core_copies.append(send(slot, slot, me.beside_core))
    for copied in core_copies:
        copied.wait_recv()
    copy.wait()
    send.finish()


def gather_slots(own):
    count = 35
    return pl.pallas_call(
        gather_kernel,
        out_shape=jax.ShapeDtypeStruct((2, 4, 4) + own.shape, own.dtype),
        in_specs=[pl.BlockSpec(memory_space=pltpu.VMEM)],
        out_specs=pl.BlockSpec(memory_space=pltpu.VMEM),
        scratch_shapes=[
            pltpu.SemaphoreType.DMA(()),
            pltpu.SemaphoreType.DMA((count,)),
            pltpu.SemaphoreType.DMA((count,)),
        ],
        compiler_params=pltpu.CompilerParams(
            collective_id=0, has_side_effects=True, vmem_limit_bytes=VMEM_BYTES
        ),
        name="gather_weights",
    )(own)


def reduce_kernel(grads, shard, squares, core_in, y_in, x_in, x_last, y_last, z_in, small, send_sem, recv_sem):
    me = Place()
    rows = grads.shape[3]
    half = rows // 2
    first, second = pl.ds(0, half), pl.ds(half, half)
    send = Sender(send_sem, recv_sem)
    other_x, other_y = 1 - me.x, 1 - me.y
    me.greet()
    order = [2 * other_y + other_x, 2 * other_y + me.x, 2 * me.y + other_x, me.dp]
    core_copies = [send(grads.at[1 - me.core, dp], core_in.at[dp], me.beside_core) for dp in order]

    def add(dp):
        for z in range(4):
            core_in[dp, z] = (core_in[dp, z].astype(F32) + grads[me.core, dp, z].astype(F32)).astype(BF)

    core_copies[0].wait_recv()
    add(order[0])
    y_copies = [send(core_in.at[order[0], :, first], y_in.at[0], me.beside_y)]
    x_copies = [send(core_in.at[order[0], :, second], x_in.at[0], me.beside_x)]
    core_copies[1].wait_recv()
    add(order[1])
    y_copies.append(send(core_in.at[order[1], :, first], y_in.at[1], me.beside_y))
    core_copies[2].wait_recv()
    add(order[2])
    x_copies.append(send(core_in.at[order[2], :, second], x_in.at[1], me.beside_x))
    core_copies[3].wait_recv()
    add(order[3])
    y_copies[0].wait_recv()
    x_copies[0].wait_recv()
    last = []
    for k in (0, 1, 2, 3):
        z = (me.z + k) % 4
        y_in[0, z] = (y_in[0, z].astype(F32) + core_in[order[2], z, first].astype(F32)).astype(BF)
        last.append(send(y_in.at[0, z], x_last.at[z], me.beside_x))
        x_in[0, z] = (x_in[0, z].astype(F32) + core_in[order[1], z, second].astype(F32)).astype(BF)
        last.append(send(x_in.at[0, z], y_last.at[z], me.beside_y))
    y_copies[1].wait_recv()
    x_copies[1].wait_recv()
    z_copies = []
    for k in (1, 2, 3, 0):
        z = (me.z + k) % 4
        last[2 * k].wait_recv()
        last[2 * k + 1].wait_recv()
        low = y_in[1, z].astype(F32) + core_in[me.dp, z, first].astype(F32) + x_last[z].astype(F32)
        high = x_in[1, z].astype(F32) + core_in[me.dp, z, second].astype(F32) + y_last[z].astype(F32)
        if k == 0:
            shard[first, :] = low
            shard[second, :] = high
        else:
            z_in[k - 1, first] = low.astype(BF)
            z_in[k - 1, second] = high.astype(BF)
            z_copies.append(send(z_in.at[k - 1], z_in.at[k + 2], me.along_z(k)))
    for k in (0, 1, 2):
        z_copies[k].wait_recv()
        shard[...] += z_in[k + 3].astype(F32)
    total = shard[0:8, :] * shard[0:8, :]
    for k in range(1, rows // 8):
        part = shard[8 * k : 8 * k + 8, :]
        total = total + part * part
    small[0] = total
    for k, device in enumerate((me.beside_core, me.beside_x, me.beside_y)):
        copied = send(small.at[k], small.at[4 + k], device)
        copied.wait_recv()
        small[k + 1] = small[k] + small[4 + k]
    copies = [send(small.at[3], small.at[8 + me.z], me.along_z(k)) for k in (1, 2, 3)]
    small[8 + me.z] = small[3]
    for copied in copies:
        copied.wait_recv()
    squares[...] = ((small[8] + small[9]) + small[10]) + small[11]
    send.finish()


def reduce_slots(grads):
    rows = grads.shape[3]
    half = rows // 2
    count = 4 + 4 + 8 + 3 + 6
    return pl.pallas_call(
        reduce_kernel,
        out_shape=[jax.ShapeDtypeStruct((rows, 128), F32), jax.ShapeDtypeStruct((8, 128), F32)],
        in_specs=[pl.BlockSpec(memory_space=pltpu.VMEM)],
        out_specs=[pl.BlockSpec(memory_space=pltpu.VMEM)] * 2,
        scratch_shapes=[
            pltpu.VMEM((4, 4, rows, 128), BF),
            pltpu.VMEM((2, 4, half, 128), BF),
            pltpu.VMEM((2, 4, half, 128), BF),
            pltpu.VMEM((4, half, 128), BF),
            pltpu.VMEM((4, half, 128), BF),
            pltpu.VMEM((6, rows, 128), BF),
            pltpu.VMEM((12, 8, 128), F32),
            pltpu.SemaphoreType.DMA((count,)),
            pltpu.SemaphoreType.DMA((count,)),
        ],
        compiler_params=pltpu.CompilerParams(
            collective_id=1, has_side_effects=True, vmem_limit_bytes=VMEM_BYTES
        ),
        name="reduce_gradients",
    )(grads)


def layout_shapes(model_width, hidden_width):
    return [
        ("pre_gain", (model_width,)),
        ("pre_shift", (model_width,)),
        ("query_weight", (model_width, model_width)),
        ("query_bias", (model_width,)),
        ("reduce_weight", (4 * model_width, model_width)),
        ("reduce_bias", (model_width,)),
        ("reduce_gain", (model_width,)),
        ("reduce_shift", (model_width,)),
        ("pair_weight", (model_width, 2 * model_width)),
        ("value_bias", (model_width,)),
        ("output_weight", (model_width, model_width)),
        ("output_bias", (model_width,)),
        ("mlp_gain", (model_width,)),
        ("mlp_shift", (model_width,)),
        ("expand_weight", (model_width, hidden_width)),
        ("expand_bias", (hidden_width,)),
        ("spatial_weight", (9, hidden_width)),
        ("spatial_bias", (hidden_width,)),
        ("shrink_weight", (hidden_width, model_width)),
        ("shrink_bias", (model_width,)),
    ]


def row_bases(width, hidden):
    bases = {}
    row = 0
    for name, shape in layout_shapes(width, hidden):
        bases[name] = row
        row += math.prod(shape) // width
    return bases, row


SPAN = 96


def unpack_kernel(
    order, slot_rows, bases,
    slots, vec, rows, wq, wqt, wr, wk, wv, wvt, wo, wot, we, wst, taps,
    flat, wide,
):
    width = wq.shape[0]
    hidden = wst.shape[1]
    for slot, place in enumerate(order):
        flat[pl.ds(slot * slot_rows, slots.shape[1]), :] = slots[place].astype(F32)
    low = lax.broadcasted_iota(jnp.int32, (SPAN, 128), 1) < 64

    def regroup(t, _):
        part = [flat[pl.ds(t * (5 * SPAN) + k, SPAN, stride=5), :] for k in range(5)]
        turned = [pltpu.roll(part[k], 64, 1) for k in (2, 3, 4)]
        even = pl.ds(t * (2 * SPAN), SPAN, stride=2)
        odd = pl.ds(t * (2 * SPAN) + 1, SPAN, stride=2)
        for k in range(3):
            wide[k, even, :] = part[k]
        wide[0, odd, :] = jnp.where(low, turned[0], turned[1])
        wide[1, odd, :] = jnp.where(low, turned[1], turned[2])
        wide[2, odd, :] = turned[2]
        return 0

    lax.fori_loop(0, wide.shape[1] // (2 * SPAN), regroup, 0)

    def take(base, count, stride=1):
        at = pl.ds(base, count, stride=stride) if stride > 1 else pl.ds(base, count)
        return jnp.concatenate([wide[0, at, :], wide[1, at, :], wide[2, at, :][:, 0 : width - 256]], axis=1)

    def take_hidden(base, count):
        return jnp.concatenate([take(base + q, count, hidden // width) for q in range(hidden // width)], axis=1)

    def bordered(weight, bias, extra):
        index = lax.broadcasted_iota(jnp.int32, (extra, weight.shape[1]), 0)
        return jnp.concatenate([weight, jnp.where(index == 0, bias, 0.0)], axis=0)

    names = ("pre_gain", "pre_shift", "mlp_gain", "mlp_shift", "shrink_bias")
    for k, name in enumerate(names):
        vec[k] = jnp.broadcast_to(take(bases[name], 1), (128, width)).T
    for k, name in enumerate(("reduce_bias", "reduce_gain", "reduce_shift")):
        rows[k : k + 1, :] = take(bases[name], 1)
    query = take(bases["query_weight"], width)
    wq[...] = query.astype(BF)
    wqt[...] = bordered(query, take(bases["query_bias"], 1), EXT).T.astype(BF)
    for p in range(4):
        wr[p] = take(bases["reduce_weight"] + p * width, width).astype(BF)
    wk[...] = take(bases["pair_weight"], width, 2).astype(BF)
    value = take(bases["pair_weight"] + 1, width, 2)
    wv[...] = value.astype(BF)
    wvt[...] = bordered(value, take(bases["value_bias"], 1), 64).T.astype(BF)
    out = take(bases["output_weight"], width)
    wo[...] = out.astype(BF)
    wot[...] = bordered(out, take(bases["output_bias"], 1), EXT).T.astype(BF)
    we[0:width, :] = take_hidden(bases["expand_weight"], width).astype(BF)
    we[width : width + 64, :] = first_row(take_hidden(bases["expand_bias"], 1), 64).astype(BF)
    taps[0:9, :] = take_hidden(bases["spatial_weight"], 9)
    taps[9:10, :] = take_hidden(bases["spatial_bias"], 1)
    for k in range(hidden // 128):
        wst[:, 128 * k : 128 * k + 128] = take(bases["shrink_weight"] + 128 * k, 128).T.astype(BF)


def wide_rows(count):
    return -(-count // (2 * SPAN)) * 2 * SPAN


def unpack_weights(slots, order, slot_rows, width):
    hidden = 4 * width
    bases, count = row_bases(width, hidden)
    shape = jax.ShapeDtypeStruct
    outs = dict(
        vec=shape((5, width, 128), F32),
        rows=shape((3, width), F32),
        wq=shape((width, width), BF),
        wqt=shape((width, width + EXT), BF),
        wr=shape((4, width, width), BF),
        wk=shape((width, width), BF),
        wv=shape((width, width), BF),
        wvt=shape((width, width + 64), BF),
        wo=shape((width, width), BF),
        wot=shape((width, width + EXT), BF),
        we=shape((width + 64, hidden), BF),
        wst=shape((width, hidden), BF),
        taps=shape((10, hidden), F32),
    )
    flat_rows = max(len(order) * slot_rows, wide_rows(count) * width // 128) + slots.shape[1]
    values = pl.pallas_call(
        partial(unpack_kernel, order, slot_rows, bases),
        out_shape=list(outs.values()),
        in_specs=[pl.BlockSpec(memory_space=pltpu.VMEM)],
        out_specs=[pl.BlockSpec(memory_space=pltpu.VMEM)] * len(outs),
        scratch_shapes=[pltpu.VMEM((flat_rows, 128), F32), pltpu.VMEM((3, wide_rows(count), 128), F32)],
        compiler_params=pltpu.CompilerParams(vmem_limit_bytes=VMEM_BYTES),
        name="unpack_weights",
    )(slots)
    return dict(zip(outs, values, strict=True))


def pack_kernel(
    order, slot_rows, bases,
    gwe, gwst, gtaps, gbias, gwo, gwq, gpair, gwr, gcols, grows, slots,
    flat, wide,
):
    width = gwst.shape[0]
    hidden = gwst.shape[1]
    used = bases["shrink_bias"] + 1
    for k in range(3):
        wide[k, pl.ds(used, wide.shape[1] - used), :] = jnp.zeros((wide.shape[1] - used, 128), F32)
    done = wide.shape[1] * width // 128
    flat[done:, :] = jnp.zeros((flat.shape[0] - done, 128), F32)

    def put(base, value, stride=1):
        count = value.shape[0]
        at = pl.ds(base, count, stride=stride) if stride > 1 else pl.ds(base, count)
        wide[0, at, :] = value[:, 0:128]
        wide[1, at, :] = value[:, 128:256]
        wide[2, at, 0 : width - 256] = value[:, 256:width]

    for k, name in enumerate(("pre_gain", "pre_shift", "mlp_gain", "mlp_shift")):
        put(bases[name], jnp.sum(gcols[k].T, axis=0, keepdims=True))
    put(bases["shrink_bias"], jnp.sum(gbias[...].T, axis=0, keepdims=True))
    for k, name in enumerate(("reduce_bias", "reduce_gain", "reduce_shift")):
        put(bases[name], jnp.sum(grows[8 * k : 8 * k + 8, :], axis=0, keepdims=True))
    put(bases["query_weight"], gwq[0 : width + 1, :])
    for p in range(4):
        put(bases["reduce_weight"] + p * width, gwr[p].T)
    put(bases["pair_weight"], gpair[0:width, :].T[0:width], 2)
    value = gpair[width : 2 * width, :].T
    put(bases["pair_weight"] + 1, value[0:width], 2)
    put(bases["value_bias"], value[width : width + 1])
    put(bases["output_weight"], gwo[0 : width + 1, :])
    sums = jnp.concatenate(
        [jnp.sum(gtaps[8 * k : 8 * k + 8, :], axis=0, keepdims=True) for k in range(10)], axis=0
    )
    for q in range(hidden // width):
        put(bases["expand_weight"] + q, gwe[0 : width + 1, q * width : (q + 1) * width], hidden // width)
        put(bases["spatial_weight"] + q, sums[:, q * width : (q + 1) * width], hidden // width)
    for k in range(hidden // 128):
        put(bases["shrink_weight"] + 128 * k, gwst[:, 128 * k : 128 * k + 128].T)
    low = lax.broadcasted_iota(jnp.int32, (SPAN, 128), 1) < 64

    def regroup(t, _):
        even = pl.ds(t * (2 * SPAN), SPAN, stride=2)
        odd = pl.ds(t * (2 * SPAN) + 1, SPAN, stride=2)
        turned = [pltpu.roll(wide[k, odd, :], 64, 1) for k in range(3)]
        part = [
            wide[0, even, :],
            wide[1, even, :],
            jnp.where(low, wide[2, even, :], turned[0]),
            jnp.where(low, turned[0], turned[1]),
            jnp.where(low, turned[1], turned[2]),
        ]
        for k in range(5):
            flat[pl.ds(t * (5 * SPAN) + k, SPAN, stride=5), :] = part[k]
        return 0

    lax.fori_loop(0, wide.shape[1] // (2 * SPAN), regroup, 0)
    inside = lax.broadcasted_iota(jnp.int32, slots.shape[1:], 0) < slot_rows
    for slot, place in enumerate(order):
        slots[place] = jnp.where(inside, flat[pl.ds(slot * slot_rows, slots.shape[1]), :], 0.0).astype(BF)


def pack_gradients(grads, order, slot_rows, padded_rows, width):
    bases, count = row_bases(width, 4 * width)
    flat_rows = max(len(order) * slot_rows, wide_rows(count) * width // 128) + padded_rows
    return pl.pallas_call(
        partial(pack_kernel, order, slot_rows, bases),
        out_shape=jax.ShapeDtypeStruct((len(order), padded_rows, 128), BF),
        in_specs=[pl.BlockSpec(memory_space=pltpu.VMEM)] * len(grads),
        out_specs=pl.BlockSpec(memory_space=pltpu.VMEM),
        scratch_shapes=[pltpu.VMEM((flat_rows, 128), F32), pltpu.VMEM((3, wide_rows(count), 128), F32)],
        compiler_params=pltpu.CompilerParams(vmem_limit_bytes=VMEM_BYTES),
        name="pack_gradients",
    )(*grads)


def device_step(images, cotangent, kv_sides, w):
    positions = jnp.arange(TOKENS, dtype=jnp.int32)
    limit = 2 * kv_sides[:, None]
    mask = ((positions[None] // GRID < limit) & (positions[None] % GRID < limit)).astype(F32)
    mask = jnp.broadcast_to(mask[:, None, :], (mask.shape[0], 8, TOKENS))
    perm = jnp.asarray(patch_order(), BF)
    pre, patches, reduced, memory, mixed, lse, middle, post = attention_forward(
        kv_sides, images, mask, perm, w["vec"], w["rows"], w["wqt"], w["wr"], w["wk"], w["wvt"], w["wot"]
    )
    output, grad_post, gwe, gwst, gtaps, gbias = feed_forward(
        post, cotangent, mask, middle, w["we"], w["wst"], w["taps"], w["vec"]
    )
    grad_images, gwo, gwq, gpair, gwr, gcols, grows = attention_backward(
        kv_sides, images, cotangent, mask, pre, patches, reduced, memory, mixed, lse, middle, grad_post,
        perm, w["vec"], w["rows"], w["wq"], w["wqt"], w["wr"], w["wk"], w["wv"], w["wvt"], w["wo"],
    )
    return output, grad_images, (gwe, gwst, gtaps, gbias, gwo, gwq, gpair, gwr, gcols, grows)


def step(on_grid, images, cotangent, kv_sides, params, first_moment, second_moment):
    width = images.shape[2]
    axes = ("dp", "fsdp")
    outer, inner = lax.axis_size("dp"), lax.axis_size("fsdp")
    slot_rows = params.shape[0] // 128
    padded_rows = -(-slot_rows // 32) * 32
    own = jnp.pad(params.reshape(slot_rows, 128).astype(BF), ((0, padded_rows - slot_rows), (0, 0)))
    if on_grid:
        order = [(s % 2) * 16 + s // 8 * 4 + s % 8 // 2 for s in range(32)]
        slots = gather_slots(own).reshape(32, padded_rows, 128)
    else:
        order = list(range(outer * inner))
        slots = lax.all_gather(own, axes)
    weights = unpack_weights(slots, order, slot_rows, width)
    output, grad_images, grads = device_step(
        images.transpose(0, 2, 1), cotangent.transpose(0, 2, 1), kv_sides, weights
    )
    slots = pack_gradients(grads, order, slot_rows, padded_rows, width)
    if on_grid:
        shard, squares = reduce_slots(slots.reshape(2, 4, 4, padded_rows, 128))
        squares = jnp.sum(squares)
    else:
        shard = lax.psum_scatter(slots.astype(F32), axes)
        squares = lax.psum(jnp.sum(shard * shard), axes)
    shard = shard[:slot_rows].reshape(-1)
    grad_norm = jnp.sqrt(squares)
    clipped = shard * jnp.minimum(1.0, CLIP_NORM / (grad_norm + 1e-06))
    new_first = BETA_FIRST * first_moment + (1.0 - BETA_FIRST) * clipped
    new_second = BETA_SECOND * second_moment + (1.0 - BETA_SECOND) * clipped * clipped
    first_hat = new_first / (1.0 - BETA_FIRST**STEP)
    second_hat = new_second / (1.0 - BETA_SECOND**STEP)
    new_params = params - RATE * (first_hat / (jnp.sqrt(second_hat) + EPSILON) + DECAY * params)
    return (
        output.transpose(0, 2, 1),
        grad_images.transpose(0, 2, 1),
        grad_norm,
        new_first,
        new_second,
        new_params,
    )


def solution(mesh):
    data = P(("dp", "fsdp"), None, None)
    flat = P(("dp", "fsdp"))
    on_grid = dict(mesh.shape) == {"dp": 4, "fsdp": 8}
    return jax.shard_map(
        partial(step, on_grid),
        mesh=mesh,
        in_specs=(data, data, flat, flat, flat, flat),
        out_specs=(data, data, P(), flat, flat, flat),
        check_vma=False,
    )
```

```python
from functools import partial
import math

import jax
import jax.numpy as jnp
import numpy as np
from jax import lax
from jax.experimental import pallas as pl
from jax.experimental.pallas import tpu as pltpu
from jax.sharding import PartitionSpec as P

HEADS = 5
HEAD_DIM = 64
GRID = 48
KV = 24
STEP = 10

CLIP_NORM = 1.0
BETA_FIRST = 0.9
BETA_SECOND = 0.999
RATE = 0.04
DECAY = 0.05
EPSILON = 1e-08

F32 = jnp.float32
BF = jnp.bfloat16
NN = (((1,), (0,)), ((), ()))
NT = (((1,), (1,)), ((), ()))
TOKENS = GRID * GRID
KEYS = KV * KV
PITCH = GRID + 8
EXT = 16
LOG2E = math.log2(math.e)
QUERY_SCALE = HEAD_DIM**-0.5 * LOG2E
GELU_A = math.sqrt(2.0 / math.pi)
GELU_B = GELU_A * 0.044715
VMEM_BYTES = 63 * 1024 * 1024


def mm(left, right, dims=NN):
    return lax.dot_general(left, right, dims, preferred_element_type=F32)


def patch_order():
    matrix = np.zeros((8 * GRID, 8 * GRID), np.float32)
    for p in range(4):
        for a in range(4):
            for b in range(KV):
                matrix[p * 96 + a * KV + b, (2 * a + p // 2) * GRID + 2 * b + p % 2] = 1.0
    return matrix


def fold_rows(x):
    return jnp.sum(x.reshape(x.shape[0] // 8, 8, x.shape[1]), axis=0)


def norm_columns(x):
    scale = 1.0 / x.shape[0]
    centred = x - jnp.sum(x, axis=0, keepdims=True) * scale
    rstd = lax.rsqrt(jnp.sum(centred * centred, axis=0, keepdims=True) * scale + 1e-06)
    return centred * rstd, rstd


def norm_columns_back(normed, rstd, scaled):
    scale = 1.0 / scaled.shape[0]
    plain = jnp.sum(scaled, axis=0, keepdims=True) * scale
    mixed = jnp.sum(scaled * normed, axis=0, keepdims=True) * scale
    return rstd * (scaled - plain - normed * mixed)


def norm_rows(x):
    centred = x - jnp.mean(x, axis=-1, keepdims=True)
    rstd = lax.rsqrt(jnp.mean(centred * centred, axis=-1, keepdims=True) + 1e-06)
    return centred * rstd, rstd


def norm_rows_back(normed, rstd, scaled):
    plain = jnp.mean(scaled, axis=-1, keepdims=True)
    mixed = jnp.mean(scaled * normed, axis=-1, keepdims=True)
    return rstd * (scaled - plain - normed * mixed)


def first_row(row, rows=EXT):
    index = lax.broadcasted_iota(jnp.int32, (rows, row.shape[-1]), 0)
    return jnp.where(index == 0, row, 0.0)


def three_parts(x):
    high = x.astype(BF).astype(F32)
    middle = (x - high).astype(BF).astype(F32)
    return high, middle, (x - high - middle).astype(BF).astype(F32)


def whole(x):
    zeros = (0,) * len(x.shape)
    return pl.BlockSpec(x.shape, lambda *_: zeros)


def per_image(x, **kwargs):
    zeros = (0,) * (len(x.shape) - 1)
    return pl.BlockSpec((1,) + tuple(x.shape[1:]), lambda i, *_: (i,) + zeros, **kwargs)


def key_columns(ref, side, h_range, ones_from, ones_to, with_mask):
    lane = lax.broadcasted_iota(jnp.int32, (KV, 64), 1)
    cell = lax.broadcasted_iota(jnp.int32, (KV, 64), 0)
    ones = jnp.where((lane >= ones_from) & (lane <= ones_to), 1.0, 0.0)
    for a in range(KV):
        block = ones
        if with_mask:
            bias = jnp.where((cell < side) & (a < side), 0.0, -1e30)
            block = jnp.where(lane == 0, bias, ones)
        block = block.astype(BF)
        for h in h_range:
            ref[h, a * KV : (a + 1) * KV, 64:128] = block


def attention_forward_kernel(
    sides, images, mask, perm, vec, rows, wqt, wr, wk, wvt, wot,
    pre, patches, reduced, memory, mixed, lse, middle, post,
    key_ref, value_ref,
):
    i = pl.program_id(0)
    width = images.shape[1]

    def first_norm(t, _):
        for u in range(3):
            at = pl.ds(pl.multiple_of(t * 384 + u * 128, 128), 128)
            x = images[0, :, at].astype(F32) * mask[0, 0:1, at]
            normed, _unused = norm_columns(x)
            pre[0, 0:width, at] = (normed * vec[0] + vec[1]).astype(BF)
            pre[0, width : width + EXT, at] = first_row(jnp.ones((1, 128), F32)).astype(BF)
        at = pl.ds(pl.multiple_of(t * 384, 128), 384)
        picked = mm(perm[...], pre[0, 0:width, at], NT).astype(BF)
        for p in range(4):
            patches[0, p, pl.ds(pl.multiple_of(t * 96, 32), 96), :] = picked[p * 96 : (p + 1) * 96]
        return 0

    lax.fori_loop(0, TOKENS // 384, first_norm, 0)

    total = rows[0:1, :]
    for p in range(4):
        total = total + mm(patches[0, p], wr[p])
    reduced[0] = total
    normed, _unused = norm_rows(total)
    memory[0, :, 0:width] = (normed * rows[1:2, :] + rows[2:3, :]).astype(BF)
    lane = lax.broadcasted_iota(jnp.int32, (KEYS, 64), 1)
    memory[0, :, width : width + 64] = jnp.where(lane == 0, 1.0, 0.0).astype(BF)
    keys = mm(memory[0, :, 0:width], wk[...]).astype(BF)
    key_columns(key_ref, sides[i], range(HEADS), 1, 0, True)
    values = mm(wvt[...], memory[0], NT).astype(BF)
    ones = first_row(jnp.ones((1, KEYS), F32)).astype(BF)
    for h in range(HEADS):
        at = slice(h * HEAD_DIM, (h + 1) * HEAD_DIM)
        key_ref[h, :, 0:HEAD_DIM] = keys[:, at]
        value_ref[h, 0:HEAD_DIM, :] = values[at]
        value_ref[h, HEAD_DIM : HEAD_DIM + EXT, :] = ones
    mixed[0, width : width + EXT, :] = first_row(jnp.ones((1, TOKENS), F32)).astype(BF)
    queries = (mm(wqt[...], pre[0]) * QUERY_SCALE).astype(BF)
    tail = first_row(jnp.ones((1, TOKENS), F32), 64).astype(BF)
    for h in range(HEADS):
        at = slice(h * HEAD_DIM, (h + 1) * HEAD_DIM)
        scores = mm(key_ref[h], jnp.concatenate([queries[at], tail], axis=0))
        top = jnp.max(scores, axis=0, keepdims=True)
        weights = jnp.exp2(scores - top).astype(BF)
        out = mm(value_ref[h], weights)
        total = out[HEAD_DIM : HEAD_DIM + 1]
        mixed[0, at, :] = (out[0:HEAD_DIM] * (1.0 / total)).astype(BF)
        lse[0, h : h + 1, :] = top + jnp.log2(total)

    def second_norm(t, _):
        at = pl.ds(pl.multiple_of(t * 384, 128), 384)
        branch = mm(wot[...], mixed[0, :, at])
        for u in range(3):
            at = pl.ds(pl.multiple_of(t * 384 + u * 128, 128), 128)
            here = mask[0, 0:1, at]
            x = images[0, :, at].astype(F32) * here + branch[:, u * 128 : (u + 1) * 128]
            middle[0, :, at] = x
            normed, _unused = norm_columns(x)
            post[0, 0:width, at] = ((normed * vec[2] + vec[3]) * here).astype(BF)
            post[0, width : width + EXT, at] = first_row(here).astype(BF)
        return 0

    lax.fori_loop(0, TOKENS // 384, second_norm, 0)


def attention_forward(sides, images, mask, perm, vec, rows, wqt, wr, wk, wvt, wot):
    n, width, tokens = images.shape
    shape = jax.ShapeDtypeStruct
    outs = [
        shape((n, width + EXT, tokens), BF),
        shape((n, 4, KEYS, width), BF),
        shape((n, KEYS, width), F32),
        shape((n, KEYS, width + 64), BF),
        shape((n, width + EXT, tokens), BF),
        shape((n, 8, tokens), F32),
        shape((n, width, tokens), F32),
        shape((n, width + EXT, tokens), BF),
    ]
    weights = (perm, vec, rows, wqt, wr, wk, wvt, wot)
    return pl.pallas_call(
        attention_forward_kernel,
        grid_spec=pltpu.PrefetchScalarGridSpec(
            num_scalar_prefetch=1,
            grid=(n,),
            in_specs=[per_image(images), per_image(mask)] + [whole(x) for x in weights],
            out_specs=[per_image(x) for x in outs],
            scratch_shapes=[
                pltpu.VMEM((HEADS, KEYS, 128), BF),
                pltpu.VMEM((HEADS, HEAD_DIM + EXT, KEYS), BF),
            ],
        ),
        out_shape=outs,
        compiler_params=pltpu.CompilerParams(vmem_limit_bytes=VMEM_BYTES),
        name="attention_forward",
    )(sides, images, mask, *weights)


def feed_forward_kernel(
    post_next, cot_next, mask_next, we_next, wst_next, taps,
    post, cot, mask, middle, we, wst, vec,
    output, grad_post, gwe, gwst, gtaps, gbias,
    padded_0, padded_1, grad_padded, grad_act, act_0, act_1, grad_exp_0, grad_exp_1,
    post_rows, out_grad_rows, out_grad, total,
):
    s = pl.program_id(0)
    last = pl.num_programs(0) - 1
    width, block = wst.shape
    blocks = gwst.shape[1] // block
    halves = block // 128
    rows = 16
    chunks = GRID // rows
    span = rows * GRID
    js = pl.ds(pl.multiple_of(lax.rem(s, blocks) * block, block), block)
    js_done = pl.ds(pl.multiple_of(lax.rem(jnp.maximum(s - 1, 0), blocks) * block, block), block)

    def tokens(t):
        return pl.ds(pl.multiple_of(t * span, span), span)

    def expand(t, padded, we, wst):
        at = tokens(t)
        filled = mm(post_rows[at, :], we[...]).astype(BF).astype(F32)
        for h in range(halves):
            for r in range(rows):
                start = pl.multiple_of((t * rows + r + 1) * PITCH + 8, 8)
                padded[h, pl.ds(start, GRID), :] = filled[r * GRID : (r + 1) * GRID, h * 128 : (h + 1) * 128]
        grad_act[at, :] = mm(out_grad_rows[at, :], wst[...]).astype(BF)

    def finish(t, act, grad_exp):
        at = tokens(t)
        total[:, at] += mm(wst[...], act[at, :], NT)
        grad_post[0, :, at] += mm(we[0:width, :], grad_exp[at, :], NT)
        gwst[:, js_done] += mm(out_grad[:, at], act[at, :])
        gwe[:, js_done] += mm(post[0, :, at], grad_exp[at, :])

    def convolve(t, padded, act):
        for h in range(halves):
            hs = slice(h * 128, (h + 1) * 128)
            w = [jnp.broadcast_to(taps[k : k + 1, hs], (GRID, 128)).astype(BF) for k in range(10)]
            sums = jnp.zeros((8, 128), F32)
            open_rows = {}
            for q in range(-1, rows + 1):
                base = (t * rows + q + 1) * PITCH + 8
                x = [padded[h, pl.ds(base + d, GRID), :].astype(BF) for d in (-1, 0, 1)]
                for a in (2, 1, 0):
                    r = q + 1 - a
                    if 0 <= r < rows:
                        part = w[3 * a] * x[0] + w[3 * a + 1] * x[1] + w[3 * a + 2] * x[2]
                        open_rows[r] = part + open_rows.get(r, w[9])
                r = q - 1
                if r < 0:
                    continue
                at = pl.ds(pl.multiple_of((t * rows + r) * GRID, GRID), GRID)
                gelu, slope = gelu_pair(open_rows.pop(r))
                act[at, hs] = gelu
                grad = (grad_act[at, hs] * slope).astype(F32)
                start = pl.multiple_of((t * rows + r + 1) * PITCH + 8, 8)
                grad_padded[h, pl.ds(start, GRID), :] = grad
                sums = sums + fold_rows(grad)
            cols = pl.ds(pl.multiple_of(lax.rem(s, blocks) * block + h * 128, 128), 128)
            gtaps[72:80, cols] += sums

    def convolve_back(t, padded, grad_exp):
        for h in range(halves):
            hs = slice(h * 128, (h + 1) * 128)
            w = [jnp.broadcast_to(taps[k : k + 1, hs], (GRID, 128)).astype(BF) for k in range(9)]
            sums = [jnp.zeros((8, 128), F32) for _ in range(9)]
            waiting = {}
            open_rows = {}
            x = {}
            for q in range(-1, rows + 1):
                base = (t * rows + q + 1) * PITCH + 8
                grads = [grad_padded[h, pl.ds(base + 1 - b, GRID), :].astype(BF) for b in range(3)]
                if q + 1 < rows:
                    start = pl.multiple_of((t * rows + q + 2) * PITCH + 8, 8)
                    x[q + 1] = padded[h, pl.ds(start, GRID), :].astype(BF)
                for a in range(3):
                    r = q + a - 1
                    if not 0 <= r < rows:
                        continue
                    part = w[3 * a] * grads[0] + w[3 * a + 1] * grads[1] + w[3 * a + 2] * grads[2]
                    open_rows[r] = part + open_rows[r] if r in open_rows else part
                    for b in range(3):
                        k = 3 * a + b
                        product = x[r] * grads[b]
                        product = product[0:16] + product[16:32] + product[32:48]
                        if k in waiting:
                            product = (product + waiting.pop(k)).astype(F32)
                            sums[k] = sums[k] + product[0:8] + product[8:16]
                        else:
                            waiting[k] = product
                r = q - 1
                if r >= 0:
                    at = pl.ds(pl.multiple_of((t * rows + r) * GRID, GRID), GRID)
                    grad_exp[at, hs] = open_rows.pop(r)
                    x.pop(r)
            cols = pl.ds(pl.multiple_of(lax.rem(s, blocks) * block + h * 128, 128), 128)
            for k in range(9):
                gtaps[8 * k : 8 * k + 8, cols] += sums[k]

    @pl.when(s == 0)
    def _():
        for ref in (padded_0, padded_1, grad_padded, act_1, grad_exp_1, out_grad, gwe, gwst, gtaps, gbias, post_rows):
            ref[...] = jnp.zeros_like(ref)

    @pl.when((s == 0) | ((lax.rem(s + 1, blocks) == 0) & (s + 1 < last)))
    def _():
        for t in range(TOKENS // 384):
            at = slice(t * 384, (t + 1) * 384)
            grad = cot_next[0, :, at].astype(F32) * mask_next[0, 0:1, at]
            gbias[...] += grad[:, 0:128] + grad[:, 128:256] + grad[:, 256:384]
            out_grad_rows[at, :] = grad.astype(BF).T
            post_rows[at, 0 : width + EXT] = post_next[0, :, at].T

    @pl.when(lax.rem(s, blocks) == min(1, blocks - 1))
    def _():
        for t in range(TOKENS // 384):
            at = slice(t * 384, (t + 1) * 384)
            out_grad[:, at] = (cot[0, :, at].astype(F32) * mask[0, 0:1, at]).astype(BF)

    @pl.when((s == 0) | (lax.rem(s, blocks) == min(1, blocks - 1)))
    def _():
        total[...] = jnp.zeros_like(total)
        grad_post[...] = jnp.zeros_like(grad_post)

    @pl.when(s == 0)
    def _():
        def first(t, _):
            expand(t, padded_0, we, wst)
            return 0

        lax.fori_loop(0, chunks, first, 0)

    def work(padded, padded_next, act, act_done, grad_exp, grad_exp_done):
        def forward(t, _):
            finish(t, act_done, grad_exp_done)
            convolve(t, padded, act)
            return 0

        def backward(t, _):
            expand(t, padded_next, we_next, wst_next)
            convolve_back(t, padded, grad_exp)
            return 0

        lax.fori_loop(0, chunks, forward, 0)
        lax.fori_loop(0, chunks, backward, 0)

    @pl.when((s < last) & (lax.rem(s, 2) == 0))
    def _():
        work(padded_0, padded_1, act_0, act_1, grad_exp_0, grad_exp_1)

    @pl.when((s < last) & (lax.rem(s, 2) == 1))
    def _():
        work(padded_1, padded_0, act_1, act_0, grad_exp_1, grad_exp_0)

    @pl.when(s == last)
    def _():
        def rest(t, _):
            @pl.when(lax.rem(s, 2) == 0)
            def _():
                finish(t, act_1, grad_exp_1)

            @pl.when(lax.rem(s, 2) == 1)
            def _():
                finish(t, act_0, grad_exp_0)

            return 0

        lax.fori_loop(0, chunks, rest, 0)

    @pl.when((s > 0) & (lax.rem(s, blocks) == 0))
    def _():
        for t in range(TOKENS // 128):
            at = slice(t * 128, (t + 1) * 128)
            output[0, :, at] = ((middle[0, :, at] + total[:, at] + vec[4]) * mask[0, 0:1, at]).astype(BF)


def gelu_pair(x):
    kind = x.dtype.type
    square = x * x
    half = kind(0.5) * jnp.tanh(x * (kind(GELU_B) * square + kind(GELU_A))) + kind(0.5)
    gelu = x * half
    return gelu, half + gelu * (kind(1.0) - half) * (kind(6.0 * GELU_B) * square + kind(2.0 * GELU_A))


def feed_forward(post, cot, mask, middle, we, wst, taps, vec, block=256):
    n, width, tokens = cot.shape
    hidden = wst.shape[1]
    blocks = hidden // block
    count = n * blocks
    shape = jax.ShapeDtypeStruct
    outs = [
        shape((n, width, tokens), BF),
        shape((n, width, tokens), F32),
        shape((width + EXT, hidden), F32),
        shape((width, hidden), F32),
        shape((80, hidden), F32),
        shape((width, 128), F32),
    ]

    def ahead(s):
        return jnp.minimum(s + 1, count - 1)

    def behind(s):
        return jnp.maximum(s - 1, 0)

    def image(x, step):
        zeros = (0,) * (len(x.shape) - 1)
        return pl.BlockSpec((1,) + tuple(x.shape[1:]), lambda s: (step(s) // blocks,) + zeros)

    def columns(x, step):
        return pl.BlockSpec((x.shape[0], block), lambda s: (0, lax.rem(step(s), blocks)))

    return pl.pallas_call(
        feed_forward_kernel,
        grid=(count + 1,),
        in_specs=[image(x, ahead) for x in (post, cot, mask)]
        + [columns(we, ahead), columns(wst, ahead), columns(taps, lambda s: jnp.minimum(s, count - 1))]
        + [image(x, behind) for x in (post, cot, mask, middle)]
        + [columns(we, behind), columns(wst, behind), whole(vec)],
        out_specs=[image(x, behind) for x in outs[:2]] + [whole(x) for x in outs[2:]],
        out_shape=outs,
        scratch_shapes=[pltpu.VMEM((block // 128, (GRID + 2) * PITCH + 8, 128), F32)] * 3
        + [pltpu.VMEM((tokens, block), BF)] * 5
        + [
            pltpu.VMEM((tokens, width + 64), BF),
            pltpu.VMEM((tokens, width), BF),
            pltpu.VMEM((width, tokens), BF),
            pltpu.VMEM((width, tokens), F32),
        ],
        compiler_params=pltpu.CompilerParams(vmem_limit_bytes=VMEM_BYTES),
        name="feed_forward",
    )(post, cot, mask, we, wst, taps, post, cot, mask, middle, we, wst, vec)


def attention_backward_kernel(
    sides, images, cot, mask, pre, patches, reduced, memory, mixed, lse, middle, grad_post,
    perm, vec, rows, wq, wqt, wr, wk, wv, wvt, wo,
    grad_images, gwo, gwq, gpair, gwr, gcols, grows,
    branch, grad_mixed, queries, grad_queries, key_ref, value_ref, keys_t, grad_keys, grad_values, grad_patches,
):
    i = pl.program_id(0)
    width = images.shape[1]

    @pl.when(i == 0)
    def _():
        for ref in (gwo, gwq, gpair, gwr, gcols, grows):
            ref[...] = jnp.zeros_like(ref)

    def mlp_norm_back(t, _):
        gain = shift = jnp.zeros((width, 128), F32)
        for u in range(3):
            at = pl.ds(pl.multiple_of(t * 384 + u * 128, 128), 128)
            here = mask[0, 0:1, at]
            normed, rstd = norm_columns(middle[0, :, at])
            grad = grad_post[0, :, at] * here
            gain = gain + grad * normed
            shift = shift + grad
            grad = cot[0, :, at].astype(F32) * here + norm_columns_back(normed, rstd, grad * vec[2])
            grad_images[0, :, at] = grad
            branch[:, at] = grad.astype(BF)
        gcols[2] += gain
        gcols[3] += shift
        return 0

    lax.fori_loop(0, TOKENS // 384, mlp_norm_back, 0)
    gwo[...] += mm(mixed[0], branch[...], NT)
    grad_mixed[...] = mm(wo[...], branch[...]).astype(BF)
    queries[...] = (mm(wqt[...], pre[0]) * QUERY_SCALE).astype(BF)
    keys = mm(memory[0, :, 0:width], wk[...]).astype(BF)
    keys_t[...] = keys.T
    values = mm(wvt[...], memory[0], NT).astype(BF).T
    key_columns(key_ref, sides[i], range(HEADS), 1, 3, True)
    key_columns(value_ref, sides[i], range(HEADS), 1, 3, False)
    for h in range(HEADS):
        at = slice(h * HEAD_DIM, (h + 1) * HEAD_DIM)
        key_ref[h, :, 0:HEAD_DIM] = keys[:, at]
        value_ref[h, :, 0:HEAD_DIM] = values[:, at]

    span = TOKENS // 2
    index = lax.broadcasted_iota(jnp.int32, (64, span), 0)
    for t in range(TOKENS // span):
        at = slice(t * span, (t + 1) * span)
        for h in range(HEADS):
            hs = slice(h * HEAD_DIM, (h + 1) * HEAD_DIM)
            one, two, three = three_parts(-lse[0, h : h + 1, at])
            tail = jnp.where(index == 2, two, jnp.where(index == 3, three, 0.0))
            tail = jnp.where(index == 0, 1.0, jnp.where(index == 1, one, tail)).astype(BF)
            query = queries[hs, at]
            attend = jnp.exp2(mm(key_ref[h], jnp.concatenate([query, tail], axis=0)))
            low = attend.astype(BF)
            grad = grad_mixed[hs, at]
            inner = grad.astype(F32) * mixed[0, hs, at].astype(F32)
            one, two, three = three_parts(-jnp.sum(inner, axis=0, keepdims=True))
            tail = jnp.where(index == 2, two, jnp.where(index == 3, three, 0.0))
            tail = jnp.where(index == 1, one, tail).astype(BF)
            grad_attend = mm(value_ref[h], jnp.concatenate([grad, tail], axis=0))
            grad_scores = (attend * grad_attend).astype(BF)
            grad_value = mm(grad, low, NT)
            grad_key = mm(query, grad_scores, NT) * (1.0 / LOG2E)
            if t == 0:
                grad_values[hs, :] = grad_value
                grad_keys[hs, :] = grad_key
            else:
                grad_values[hs, :] += grad_value
                grad_keys[hs, :] += grad_key
            grad_queries[hs, at] = (mm(keys_t[hs, :], grad_scores) * HEAD_DIM**-0.5).astype(BF)

    low_keys = grad_keys[...].astype(BF)
    low_values = grad_values[...].astype(BF)
    gpair[0:width, :] += mm(low_keys, memory[0])
    gpair[width : 2 * width, :] += mm(low_values, memory[0])
    grad_memory = mm(low_keys.T, wk[...], NT) + mm(low_values.T, wv[...], NT)
    normed, rstd = norm_rows(reduced[0])
    grows[8:16, :] += fold_rows(grad_memory * normed)
    grows[16:24, :] += fold_rows(grad_memory)
    grad_reduced = norm_rows_back(normed, rstd, grad_memory * rows[1:2, :]).astype(BF)
    grows[0:8, :] += fold_rows(grad_reduced.astype(F32))
    grad_reduced_t = grad_reduced.T
    for p in range(4):
        gwr[p] += mm(grad_reduced_t, patches[0, p])
        grad_patches[p] = mm(grad_reduced, wr[p], NT).astype(BF)
    gwq[...] += mm(pre[0], grad_queries[...], NT)

    def pre_norm_back(t, _):
        at = pl.ds(pl.multiple_of(t * 384, 128), 384)
        grad_pre = mm(wq[...], grad_queries[:, at])
        start = pl.ds(pl.multiple_of(t * 96, 32), 96)
        picked = jnp.concatenate([grad_patches[p, start, :] for p in range(4)], axis=0)
        grad_pre = grad_pre + mm(picked.T, perm[...])
        gain = shift = jnp.zeros((width, 128), F32)
        for u in range(3):
            at = pl.ds(pl.multiple_of(t * 384 + u * 128, 128), 128)
            here = mask[0, 0:1, at]
            normed, rstd = norm_columns(images[0, :, at].astype(F32) * here)
            grad = grad_pre[:, u * 128 : (u + 1) * 128]
            gain = gain + grad * normed
            shift = shift + grad
            back = norm_columns_back(normed, rstd, grad * vec[0])
            grad_images[0, :, at] = (grad_images[0, :, at] + back) * here
        gcols[0] += gain
        gcols[1] += shift
        return 0

    lax.fori_loop(0, TOKENS // 384, pre_norm_back, 0)


def attention_backward(
    sides, images, cot, mask, pre, patches, reduced, memory, mixed, lse, middle, grad_post,
    perm, vec, rows, wq, wqt, wr, wk, wv, wvt, wo,
):
    n, width, tokens = images.shape
    shape = jax.ShapeDtypeStruct
    outs = [
        shape((n, width, tokens), F32),
        shape((width + EXT, width), F32),
        shape((width + EXT, width), F32),
        shape((2 * width, width + 64), F32),
        shape((4, width, width), F32),
        shape((4, width, 128), F32),
        shape((24, width), F32),
    ]
    one = {"pipeline_mode": pl.Buffered(1)}
    inputs = (images, cot, mask, pre, patches, reduced, memory, mixed, lse)
    weights = (perm, vec, rows, wq, wqt, wr, wk, wv, wvt, wo)
    return pl.pallas_call(
        attention_backward_kernel,
        grid_spec=pltpu.PrefetchScalarGridSpec(
            num_scalar_prefetch=1,
            grid=(n,),
            in_specs=[per_image(x) for x in inputs]
            + [per_image(middle, **one), per_image(grad_post, **one)]
            + [whole(x) for x in weights],
            out_specs=[per_image(outs[0], **one)] + [whole(x) for x in outs[1:]],
            scratch_shapes=[
                pltpu.VMEM((width, tokens), BF),
                pltpu.VMEM((width, tokens), BF),
                pltpu.VMEM((width, tokens), BF),
                pltpu.VMEM((width, tokens), BF),
                pltpu.VMEM((HEADS, KEYS, 128), BF),
                pltpu.VMEM((HEADS, KEYS, 128), BF),
                pltpu.VMEM((width, KEYS), BF),
                pltpu.VMEM((width, KEYS), F32),
                pltpu.VMEM((width, KEYS), F32),
                pltpu.VMEM((4, KEYS, width), BF),
            ],
        ),
        out_shape=outs,
        compiler_params=pltpu.CompilerParams(vmem_limit_bytes=VMEM_BYTES),
        name="attention_backward",
    )(sides, *inputs, middle, grad_post, *weights)

MESH = pl.DeviceIdType.MESH


class Place:
    def __init__(self):
        self.dp = lax.axis_index("dp")
        self.fsdp = lax.axis_index("fsdp")
        self.y, self.x = self.dp // 2, self.dp % 2
        self.z, self.core = self.fsdp // 2, self.fsdp % 2
        self.other_core = 1 - self.core
        self.beside_x = (self.dp + 1 - 2 * self.x, self.fsdp)
        self.beside_y = (self.dp + 2 - 4 * self.y, self.fsdp)
        self.across = (3 - self.dp, self.fsdp)
        self.beside_core = (self.dp, self.fsdp + 1 - 2 * self.core)
        self.others = (self.z + 1 - 2 * (self.z % 2), 2 - self.z // 2, 3 * (1 - self.z // 2))

    def at_z(self, z):
        return (self.dp, z * 2 + self.core)

    def along_z(self, k):
        return self.at_z((self.z + k) % 4)

    def greet(self, partners):
        barrier = pltpu.get_barrier_semaphore()
        for device in partners:
            pl.semaphore_signal(barrier, inc=1, device_id=device, device_id_type=MESH)
        pl.semaphore_wait(barrier, len(partners))


class Sender:
    def __init__(self, send, recv):
        self.send, self.recv, self.started = send, recv, []

    def __call__(self, source, target, device, recv=None):
        k = len(self.started)
        copy = pltpu.make_async_remote_copy(
            src_ref=source,
            dst_ref=target,
            send_sem=self.send.at[k],
            recv_sem=self.recv.at[k] if recv is None else recv,
            device_id=device,
            device_id_type=MESH,
        )
        copy.start()
        self.started.append(copy)
        return copy

    def finish(self):
        for copy in self.started:
            copy.wait_send()


def gather_kernel(slot_rows, bases, own, *refs):
    outs, (slots, wide, line, own_sem, send_sem, recv_sem, z_sem) = refs[:13], refs[13:]
    me = Place()
    half = own.shape[0] // 2
    first, second = pl.ds(0, half), pl.ds(half, half)
    send = Sender(send_sem, recv_sem)
    copy = pltpu.make_async_copy(own, slots.at[me.core, me.dp, me.z], own_sem)
    copy.start()
    me.greet([me.beside_core, me.beside_x, me.beside_y] + [me.at_z(z) for z in me.others])
    own_slot = slots.at[me.core, me.dp, me.z]

    def send_z(j):
        return send(own, own_slot, me.at_z(me.others[j]), z_sem.at[me.z])

    send_z(0)
    x_copies = [send(own, own_slot, me.beside_x)]
    y_copies = [send(own, own_slot, me.beside_y)]
    core_copies = [(send(own, own_slot, me.beside_core), me.dp, me.z)]
    send_z(1)
    half_copies = []
    order = (me.z,) + me.others

    def open_slot(core, dp, z):
        spread_slot(slots[core, dp, z], (dp * 8 + z * 2 + core), slot_rows, line, wide)

    def forward(k):
        z = order[k]
        x_copies[k].wait_recv()
        slot = slots.at[me.core, me.beside_x[0], z]
        half_copies.append(send(slot.at[first], slot.at[first], me.beside_y))
        core_copies.append((send(slot, slot, me.beside_core), me.beside_x[0], z))
        y_copies[k].wait_recv()
        slot = slots.at[me.core, me.beside_y[0], z]
        half_copies.append(send(slot.at[second], slot.at[second], me.beside_x))
        core_copies.append((send(slot, slot, me.beside_core), me.beside_y[0], z))
        open_slot(me.core, me.beside_x[0], z)
        open_slot(me.core, me.beside_y[0], z)

    copy.wait()
    open_slot(me.core, me.dp, me.z)
    forward(0)
    for k in (1, 2, 3):
        z = order[k]
        slot = slots.at[me.core, me.dp, z]
        pltpu.make_async_remote_copy(
            src_ref=own,
            dst_ref=slot,
            send_sem=send_sem.at[0],
            recv_sem=z_sem.at[z],
            device_id=me.at_z(z),
            device_id_type=MESH,
        ).wait_recv()
        x_copies.append(send(slot, slot, me.beside_x))
        y_copies.append(send(slot, slot, me.beside_y))
        core_copies.append((send(slot, slot, me.beside_core), me.dp, z))
        if k == 1:
            send_z(2)
        open_slot(me.core, me.dp, z)
        forward(k)
    for k in range(4):
        half_copies[2 * k].wait_recv()
        half_copies[2 * k + 1].wait_recv()
        slot = slots.at[me.core, me.across[0], order[k]]
        core_copies.append((send(slot, slot, me.beside_core), me.across[0], order[k]))
        open_slot(me.core, me.across[0], order[k])
    for copied, dp, z in core_copies:
        copied.wait_recv()
        open_slot(me.other_core, dp, z)
    send.finish()
    write_weights(bases, wide, *outs)


def gather_weights(own, slot_rows, width):
    bases, count = row_bases(width, 4 * width)
    outs = weight_shapes(width)
    copies = 35
    values = pl.pallas_call(
        partial(gather_kernel, slot_rows, bases),
        out_shape=list(outs.values()),
        in_specs=[pl.BlockSpec(memory_space=pltpu.VMEM)],
        out_specs=[pl.BlockSpec(memory_space=pltpu.VMEM)] * len(outs),
        scratch_shapes=[
            pltpu.VMEM((2, 4, 4) + own.shape, BF),
            pltpu.VMEM((3, -(-32 * slot_rows * 128 // width // 8) * 8 + 8, 128), F32),
            pltpu.VMEM(own.shape, F32),
            pltpu.SemaphoreType.DMA(()),
            pltpu.SemaphoreType.DMA((copies,)),
            pltpu.SemaphoreType.DMA((copies,)),
            pltpu.SemaphoreType.DMA((4,)),
        ],
        compiler_params=pltpu.CompilerParams(
            collective_id=0, has_side_effects=True, vmem_limit_bytes=VMEM_BYTES
        ),
        name="gather_weights",
    )(own)
    return dict(zip(outs, values, strict=True))


def reduce_kernel(
    grads, shard, squares,
    core_in, y_in, x_in, x_last, y_last, z_in, small, send_sem, recv_sem,
):
    me = Place()
    rows = grads.shape[3]
    half = rows // 2
    first, second = pl.ds(0, half), pl.ds(half, half)
    send = Sender(send_sem, recv_sem)
    peers = [(me.dp, (me.z + k) % 4 * 2 + core) for k in range(4) for core in (me.core, me.other_core)][1:]
    planes = [me.beside_x, me.beside_y, me.across]
    me.greet(peers + planes)
    units = [(me.z + k) % 4 for k in (2, 1, 3, 0)]
    core_copies = [send(grads.at[me.other_core, z], core_in.at[z], me.beside_core) for z in units]
    y_copies, x_copies, last = [], [], []
    other_x, other_y = 1 - me.x, 1 - me.y

    def cores(k):
        z = units[k]
        core_copies[k].wait_recv()
        for dp in range(4):
            core_in[z, dp] = (core_in[z, dp].astype(F32) + grads[me.core, z, dp].astype(F32)).astype(BF)
        y_copies.append(
            [send(core_in.at[z, 2 * other_y + x, first], y_in.at[z, x], me.beside_y) for x in range(2)]
        )
        x_copies.append(
            [send(core_in.at[z, 2 * y + other_x, second], x_in.at[z, y], me.beside_x) for y in range(2)]
        )

    def plane(k):
        z = units[k]
        for copied in y_copies[k]:
            copied.wait_recv()
        y_in[z, other_x] = (
            y_in[z, other_x].astype(F32) + core_in[z, 2 * me.y + other_x, first].astype(F32)
        ).astype(BF)
        to_x = send(y_in.at[z, other_x], x_last.at[z], me.beside_x)
        for copied in x_copies[k]:
            copied.wait_recv()
        x_in[z, other_y] = (
            x_in[z, other_y].astype(F32) + core_in[z, 2 * other_y + me.x, second].astype(F32)
        ).astype(BF)
        last.append((to_x, send(x_in.at[z, other_y], y_last.at[z], me.beside_y)))

    z_copies = []

    def column(k):
        z = units[k]
        for copied in last[k]:
            copied.wait_recv()
        low = y_in[z, me.x].astype(F32) + core_in[z, me.dp, first].astype(F32) + x_last[z].astype(F32)
        high = x_in[z, me.y].astype(F32) + core_in[z, me.dp, second].astype(F32) + y_last[z].astype(F32)
        if k == 3:
            shard[first, :] = low
            shard[second, :] = high
        else:
            z_in[k, first] = low.astype(BF)
            z_in[k, second] = high.astype(BF)
            z_copies.append(send(z_in.at[k], z_in.at[k + 3], me.at_z(z)))

    cores(0)
    cores(1)
    plane(0)
    cores(2)
    plane(1)
    column(0)
    cores(3)
    plane(2)
    column(1)
    plane(3)
    column(2)
    column(3)
    for k in (0, 1, 2):
        z_copies[k].wait_recv()
        shard[...] += z_in[k + 3].astype(F32)
    total = shard[0:8, :] * shard[0:8, :]
    for k in range(1, rows // 8):
        part = shard[8 * k : 8 * k + 8, :]
        total = total + part * part
    small[0] = total
    small[2 + me.fsdp] = total
    copies = [send(small.at[0], small.at[2 + me.fsdp], device) for device in peers]
    for copied in copies:
        copied.wait_recv()
    total = small[2]
    for k in range(1, 8):
        total = total + small[2 + k]
    small[1] = total
    small[10 + me.dp] = total
    copies = [send(small.at[1], small.at[10 + me.dp], device) for device in planes]
    for copied in copies:
        copied.wait_recv()
    squares[...] = ((small[10] + small[11]) + small[12]) + small[13]
    send.finish()


def reduce_slots(grads):
    rows = grads.shape[3]
    half = rows // 2
    count = 4 + 16 + 8 + 3 + 7 + 3
    return pl.pallas_call(
        reduce_kernel,
        out_shape=[jax.ShapeDtypeStruct((rows, 128), F32), jax.ShapeDtypeStruct((8, 128), F32)],
        in_specs=[pl.BlockSpec(memory_space=pltpu.VMEM)],
        out_specs=[pl.BlockSpec(memory_space=pltpu.VMEM)] * 2,
        scratch_shapes=[
            pltpu.VMEM((4, 4, rows, 128), BF),
            pltpu.VMEM((4, 2, half, 128), BF),
            pltpu.VMEM((4, 2, half, 128), BF),
            pltpu.VMEM((4, half, 128), BF),
            pltpu.VMEM((4, half, 128), BF),
            pltpu.VMEM((6, rows, 128), BF),
            pltpu.VMEM((14, 8, 128), F32),
            pltpu.SemaphoreType.DMA((count,)),
            pltpu.SemaphoreType.DMA((count,)),
        ],
        compiler_params=pltpu.CompilerParams(
            collective_id=1, has_side_effects=True, vmem_limit_bytes=VMEM_BYTES
        ),
        name="reduce_gradients",
    )(grads)


def layout_shapes(model_width, hidden_width):
    return [
        ("pre_gain", (model_width,)),
        ("pre_shift", (model_width,)),
        ("query_weight", (model_width, model_width)),
        ("query_bias", (model_width,)),
        ("reduce_weight", (4 * model_width, model_width)),
        ("reduce_bias", (model_width,)),
        ("reduce_gain", (model_width,)),
        ("reduce_shift", (model_width,)),
        ("pair_weight", (model_width, 2 * model_width)),
        ("value_bias", (model_width,)),
        ("output_weight", (model_width, model_width)),
        ("output_bias", (model_width,)),
        ("mlp_gain", (model_width,)),
        ("mlp_shift", (model_width,)),
        ("expand_weight", (model_width, hidden_width)),
        ("expand_bias", (hidden_width,)),
        ("spatial_weight", (9, hidden_width)),
        ("spatial_bias", (hidden_width,)),
        ("shrink_weight", (hidden_width, model_width)),
        ("shrink_bias", (model_width,)),
    ]


def row_bases(width, hidden):
    bases = {}
    row = 0
    for name, shape in layout_shapes(width, hidden):
        bases[name] = row
        row += math.prod(shape) // width
    return bases, row


SPAN = 96


def regroup_lines(read, write, low):
    part = [read(k) for k in range(5)]
    turned = [pltpu.roll(part[k], 64, 1) for k in (2, 3, 4)]
    for k in range(3):
        write(0, k, part[k])
    write(1, 0, jnp.where(low, turned[0], turned[1]))
    write(1, 1, jnp.where(low, turned[1], turned[2]))
    write(1, 2, turned[2])


def spread_slot(values, slot, slot_rows, line, wide):
    pairs = slot_rows // 5
    line[...] = values.astype(F32)

    def part(start, count):
        low = lax.broadcasted_iota(jnp.int32, (count, 128), 1) < 64

        def write(parity, k, value):
            wide[k, pl.ds(slot * (2 * pairs) + 2 * start + parity, count, stride=2), :] = value

        regroup_lines(lambda k: line[pl.ds(5 * start + k, count, stride=5), :], write, low)

    part(0, pairs // 8 * 8)
    if pairs % 8:
        part(pairs // 8 * 8, pairs % 8)


def unpack_kernel(order, slot_rows, bases, slots, *refs):
    outs, (flat, wide) = refs[:13], refs[13:]
    for slot, place in enumerate(order):
        flat[pl.ds(slot * slot_rows, slots.shape[1]), :] = slots[place].astype(F32)
    low = lax.broadcasted_iota(jnp.int32, (SPAN, 128), 1) < 64

    def regroup(t, _):
        def write(parity, k, value):
            wide[k, pl.ds(t * (2 * SPAN) + parity, SPAN, stride=2), :] = value

        regroup_lines(lambda k: flat[pl.ds(t * (5 * SPAN) + k, SPAN, stride=5), :], write, low)
        return 0

    lax.fori_loop(0, wide.shape[1] // (2 * SPAN), regroup, 0)
    write_weights(bases, wide, *outs)


def write_weights(bases, wide, vec, rows, wq, wqt, wr, wk, wv, wvt, wo, wot, we, wst, taps):
    width = wq.shape[0]
    hidden = wst.shape[1]

    def take(base, count, stride=1):
        at = pl.ds(base, count, stride=stride) if stride > 1 else pl.ds(base, count)
        return jnp.concatenate([wide[0, at, :], wide[1, at, :], wide[2, at, :][:, 0 : width - 256]], axis=1)

    def take_hidden(base, count):
        return jnp.concatenate([take(base + q, count, hidden // width) for q in range(hidden // width)], axis=1)

    def bordered(weight, bias, extra):
        index = lax.broadcasted_iota(jnp.int32, (extra, weight.shape[1]), 0)
        return jnp.concatenate([weight, jnp.where(index == 0, bias, 0.0)], axis=0)

    names = ("pre_gain", "pre_shift", "mlp_gain", "mlp_shift", "shrink_bias")
    for k, name in enumerate(names):
        vec[k] = jnp.broadcast_to(take(bases[name], 1), (128, width)).T
    for k, name in enumerate(("reduce_bias", "reduce_gain", "reduce_shift")):
        rows[k : k + 1, :] = take(bases[name], 1)
    query = take(bases["query_weight"], width)
    wq[...] = query.astype(BF)
    wqt[...] = bordered(query, take(bases["query_bias"], 1), EXT).T.astype(BF)
    for p in range(4):
        wr[p] = take(bases["reduce_weight"] + p * width, width).astype(BF)
    wk[...] = take(bases["pair_weight"], width, 2).astype(BF)
    value = take(bases["pair_weight"] + 1, width, 2)
    wv[...] = value.astype(BF)
    wvt[...] = bordered(value, take(bases["value_bias"], 1), 64).T.astype(BF)
    out = take(bases["output_weight"], width)
    wo[...] = out.astype(BF)
    wot[...] = bordered(out, take(bases["output_bias"], 1), EXT).T.astype(BF)
    we[0:width, :] = take_hidden(bases["expand_weight"], width).astype(BF)
    we[width : width + 64, :] = first_row(take_hidden(bases["expand_bias"], 1), 64).astype(BF)
    taps[0:9, :] = take_hidden(bases["spatial_weight"], 9)
    taps[9:10, :] = take_hidden(bases["spatial_bias"], 1)
    for k in range(hidden // 128):
        wst[:, 128 * k : 128 * k + 128] = take(bases["shrink_weight"] + 128 * k, 128).T.astype(BF)


def wide_rows(count):
    return -(-count // (2 * SPAN)) * 2 * SPAN


def weight_shapes(width):
    hidden = 4 * width
    shape = jax.ShapeDtypeStruct
    return dict(
        vec=shape((5, width, 128), F32),
        rows=shape((3, width), F32),
        wq=shape((width, width), BF),
        wqt=shape((width, width + EXT), BF),
        wr=shape((4, width, width), BF),
        wk=shape((width, width), BF),
        wv=shape((width, width), BF),
        wvt=shape((width, width + 64), BF),
        wo=shape((width, width), BF),
        wot=shape((width, width + EXT), BF),
        we=shape((width + 64, hidden), BF),
        wst=shape((width, hidden), BF),
        taps=shape((10, hidden), F32),
    )


def unpack_weights(slots, order, slot_rows, width):
    bases, count = row_bases(width, 4 * width)
    outs = weight_shapes(width)
    flat_rows = max(len(order) * slot_rows, wide_rows(count) * width // 128) + slots.shape[1]
    values = pl.pallas_call(
        partial(unpack_kernel, order, slot_rows, bases),
        out_shape=list(outs.values()),
        in_specs=[pl.BlockSpec(memory_space=pltpu.VMEM)],
        out_specs=[pl.BlockSpec(memory_space=pltpu.VMEM)] * len(outs),
        scratch_shapes=[pltpu.VMEM((flat_rows, 128), F32), pltpu.VMEM((3, wide_rows(count), 128), F32)],
        compiler_params=pltpu.CompilerParams(vmem_limit_bytes=VMEM_BYTES),
        name="unpack_weights",
    )(slots)
    return dict(zip(outs, values, strict=True))


def pack_kernel(
    order, slot_rows, bases,
    gwe, gwst, gtaps, gbias, gwo, gwq, gpair, gwr, gcols, grows, slots,
    flat, wide,
):
    width = gwst.shape[0]
    hidden = gwst.shape[1]
    used = bases["shrink_bias"] + 1
    for k in range(3):
        wide[k, pl.ds(used, wide.shape[1] - used), :] = jnp.zeros((wide.shape[1] - used, 128), F32)
    done = wide.shape[1] * width // 128
    flat[done:, :] = jnp.zeros((flat.shape[0] - done, 128), F32)

    def put(base, value, stride=1):
        count = value.shape[0]
        at = pl.ds(base, count, stride=stride) if stride > 1 else pl.ds(base, count)
        wide[0, at, :] = value[:, 0:128]
        wide[1, at, :] = value[:, 128:256]
        wide[2, at, 0 : width - 256] = value[:, 256:width]

    for k, name in enumerate(("pre_gain", "pre_shift", "mlp_gain", "mlp_shift")):
        put(bases[name], jnp.sum(gcols[k].T, axis=0, keepdims=True))
    put(bases["shrink_bias"], jnp.sum(gbias[...].T, axis=0, keepdims=True))
    for k, name in enumerate(("reduce_bias", "reduce_gain", "reduce_shift")):
        put(bases[name], jnp.sum(grows[8 * k : 8 * k + 8, :], axis=0, keepdims=True))
    put(bases["query_weight"], gwq[0 : width + 1, :])
    for p in range(4):
        put(bases["reduce_weight"] + p * width, gwr[p].T)
    put(bases["pair_weight"], gpair[0:width, :].T[0:width], 2)
    value = gpair[width : 2 * width, :].T
    put(bases["pair_weight"] + 1, value[0:width], 2)
    put(bases["value_bias"], value[width : width + 1])
    put(bases["output_weight"], gwo[0 : width + 1, :])
    sums = jnp.concatenate(
        [jnp.sum(gtaps[8 * k : 8 * k + 8, :], axis=0, keepdims=True) for k in range(10)], axis=0
    )
    for q in range(hidden // width):
        put(bases["expand_weight"] + q, gwe[0 : width + 1, q * width : (q + 1) * width], hidden // width)
        put(bases["spatial_weight"] + q, sums[:, q * width : (q + 1) * width], hidden // width)
    for k in range(hidden // 128):
        put(bases["shrink_weight"] + 128 * k, gwst[:, 128 * k : 128 * k + 128].T)
    low = lax.broadcasted_iota(jnp.int32, (SPAN, 128), 1) < 64

    def regroup(t, _):
        even = pl.ds(t * (2 * SPAN), SPAN, stride=2)
        odd = pl.ds(t * (2 * SPAN) + 1, SPAN, stride=2)
        turned = [pltpu.roll(wide[k, odd, :], 64, 1) for k in range(3)]
        part = [
            wide[0, even, :],
            wide[1, even, :],
            jnp.where(low, wide[2, even, :], turned[0]),
            jnp.where(low, turned[0], turned[1]),
            jnp.where(low, turned[1], turned[2]),
        ]
        for k in range(5):
            flat[pl.ds(t * (5 * SPAN) + k, SPAN, stride=5), :] = part[k]
        return 0

    lax.fori_loop(0, wide.shape[1] // (2 * SPAN), regroup, 0)
    inside = lax.broadcasted_iota(jnp.int32, slots.shape[1:], 0) < slot_rows
    for slot, place in enumerate(order):
        slots[place] = jnp.where(inside, flat[pl.ds(slot * slot_rows, slots.shape[1]), :], 0.0).astype(BF)


def pack_gradients(grads, order, slot_rows, padded_rows, width):
    bases, count = row_bases(width, 4 * width)
    flat_rows = max(len(order) * slot_rows, wide_rows(count) * width // 128) + padded_rows
    return pl.pallas_call(
        partial(pack_kernel, order, slot_rows, bases),
        out_shape=jax.ShapeDtypeStruct((len(order), padded_rows, 128), BF),
        in_specs=[pl.BlockSpec(memory_space=pltpu.VMEM)] * len(grads),
        out_specs=pl.BlockSpec(memory_space=pltpu.VMEM),
        scratch_shapes=[pltpu.VMEM((flat_rows, 128), F32), pltpu.VMEM((3, wide_rows(count), 128), F32)],
        compiler_params=pltpu.CompilerParams(vmem_limit_bytes=VMEM_BYTES),
        name="pack_gradients",
    )(*grads)


def device_step(images, cotangent, kv_sides, w):
    positions = jnp.arange(TOKENS, dtype=jnp.int32)
    limit = 2 * kv_sides[:, None]
    mask = ((positions[None] // GRID < limit) & (positions[None] % GRID < limit)).astype(F32)
    mask = jnp.broadcast_to(mask[:, None, :], (mask.shape[0], 8, TOKENS))
    perm = jnp.asarray(patch_order(), BF)
    pre, patches, reduced, memory, mixed, lse, middle, post = attention_forward(
        kv_sides, images, mask, perm, w["vec"], w["rows"], w["wqt"], w["wr"], w["wk"], w["wvt"], w["wot"]
    )
    output, grad_post, gwe, gwst, gtaps, gbias = feed_forward(
        post, cotangent, mask, middle, w["we"], w["wst"], w["taps"], w["vec"]
    )
    grad_images, gwo, gwq, gpair, gwr, gcols, grows = attention_backward(
        kv_sides, images, cotangent, mask, pre, patches, reduced, memory, mixed, lse, middle, grad_post,
        perm, w["vec"], w["rows"], w["wq"], w["wqt"], w["wr"], w["wk"], w["wv"], w["wvt"], w["wo"],
    )
    return output, grad_images, (gwe, gwst, gtaps, gbias, gwo, gwq, gpair, gwr, gcols, grows)


def step(on_grid, images, cotangent, kv_sides, params, first_moment, second_moment):
    width = images.shape[2]
    axes = ("dp", "fsdp")
    outer, inner = lax.axis_size("dp"), lax.axis_size("fsdp")
    slot_rows = params.shape[0] // 128
    padded_rows = -(-slot_rows // 32) * 32
    own = jnp.pad(params.reshape(slot_rows, 128).astype(BF), ((0, padded_rows - slot_rows), (0, 0)))
    order = list(range(outer * inner))
    if on_grid:
        weights = gather_weights(own, slot_rows, width)
    else:
        weights = unpack_weights(lax.all_gather(own, axes), order, slot_rows, width)
    output, grad_images, grads = device_step(
        images.transpose(0, 2, 1), cotangent.transpose(0, 2, 1), kv_sides, weights
    )
    if on_grid:
        order = [s % 2 * 16 + s % 8 // 2 * 4 + s // 8 for s in range(32)]
    slots = pack_gradients(grads, order, slot_rows, padded_rows, width)
    if on_grid:
        shard, squares = reduce_slots(slots.reshape(2, 4, 4, padded_rows, 128))
        squares = jnp.sum(squares)
    else:
        shard = lax.psum_scatter(slots.astype(F32), axes)
        squares = lax.psum(jnp.sum(shard * shard), axes)
    shard = shard[:slot_rows].reshape(-1)
    grad_norm = jnp.sqrt(squares)
    clipped = shard * jnp.minimum(1.0, CLIP_NORM / (grad_norm + 1e-06))
    new_first = BETA_FIRST * first_moment + (1.0 - BETA_FIRST) * clipped
    new_second = BETA_SECOND * second_moment + (1.0 - BETA_SECOND) * clipped * clipped
    first_hat = new_first / (1.0 - BETA_FIRST**STEP)
    second_hat = new_second / (1.0 - BETA_SECOND**STEP)
    new_params = params - RATE * (first_hat / (jnp.sqrt(second_hat) + EPSILON) + DECAY * params)
    return (
        output.transpose(0, 2, 1),
        grad_images.transpose(0, 2, 1),
        grad_norm,
        new_first,
        new_second,
        new_params,
    )


def solution(mesh):
    data = P(("dp", "fsdp"), None, None)
    flat = P(("dp", "fsdp"))
    on_grid = dict(mesh.shape) == {"dp": 4, "fsdp": 8}
    return jax.shard_map(
        partial(step, on_grid),
        mesh=mesh,
        in_specs=(data, data, flat, flat, flat, flat),
        out_specs=(data, data, P(), flat, flat, flat),
        check_vma=False,
    )
```

```python
from functools import partial
import math

import jax
import jax.numpy as jnp
import numpy as np
from jax import lax
from jax.experimental import pallas as pl
from jax.experimental.pallas import tpu as pltpu
from jax.sharding import PartitionSpec as P

HEADS = 5
HEAD_DIM = 64
GRID = 48
KV = 24
STEP = 10

CLIP_NORM = 1.0
BETA_FIRST = 0.9
BETA_SECOND = 0.999
RATE = 0.04
DECAY = 0.05
EPSILON = 1e-08

F32 = jnp.float32
BF = jnp.bfloat16
NN = (((1,), (0,)), ((), ()))
NT = (((1,), (1,)), ((), ()))
TOKENS = GRID * GRID
KEYS = KV * KV
PITCH = GRID + 8
EXT = 16
DEPTH = 512
LOG2E = math.log2(math.e)
QUERY_SCALE = HEAD_DIM**-0.5 * LOG2E
GELU_A = math.sqrt(2.0 / math.pi)
GELU_B = GELU_A * 0.044715
VMEM_BYTES = 63 * 1024 * 1024


def mm(left, right, dims=NN):
    return lax.dot_general(left, right, dims, preferred_element_type=F32)


def patch_order():
    matrix = np.zeros((8 * GRID, 8 * GRID), np.float32)
    for p in range(4):
        for a in range(4):
            for b in range(KV):
                matrix[p * 96 + a * KV + b, (2 * a + p // 2) * GRID + 2 * b + p % 2] = 1.0
    return matrix


def fold_rows(x):
    return jnp.sum(x.reshape(x.shape[0] // 8, 8, x.shape[1]), axis=0)


def norm_columns(x):
    scale = 1.0 / x.shape[0]
    centred = x - jnp.sum(x, axis=0, keepdims=True) * scale
    rstd = lax.rsqrt(jnp.sum(centred * centred, axis=0, keepdims=True) * scale + 1e-06)
    return centred * rstd, rstd


def norm_columns_back(normed, rstd, scaled):
    scale = 1.0 / scaled.shape[0]
    plain = jnp.sum(scaled, axis=0, keepdims=True) * scale
    mixed = jnp.sum(scaled * normed, axis=0, keepdims=True) * scale
    return rstd * (scaled - plain - normed * mixed)


def norm_rows(x):
    centred = x - jnp.mean(x, axis=-1, keepdims=True)
    rstd = lax.rsqrt(jnp.mean(centred * centred, axis=-1, keepdims=True) + 1e-06)
    return centred * rstd, rstd


def norm_rows_back(normed, rstd, scaled):
    plain = jnp.mean(scaled, axis=-1, keepdims=True)
    mixed = jnp.mean(scaled * normed, axis=-1, keepdims=True)
    return rstd * (scaled - plain - normed * mixed)


def first_row(row, rows=EXT):
    index = lax.broadcasted_iota(jnp.int32, (rows, row.shape[-1]), 0)
    return jnp.where(index == 0, row, 0.0)


def three_parts(x):
    high = x.astype(BF).astype(F32)
    middle = (x - high).astype(BF).astype(F32)
    return high, middle, (x - high - middle).astype(BF).astype(F32)


def whole(x):
    zeros = (0,) * len(x.shape)
    return pl.BlockSpec(x.shape, lambda *_: zeros)


def per_image(x, **kwargs):
    zeros = (0,) * (len(x.shape) - 1)
    return pl.BlockSpec((1,) + tuple(x.shape[1:]), lambda i, *_: (i,) + zeros, **kwargs)


def key_columns(ref, side, h_range, ones_from, ones_to, with_mask):
    lane = lax.broadcasted_iota(jnp.int32, (KV, 64), 1)
    cell = lax.broadcasted_iota(jnp.int32, (KV, 64), 0)
    ones = jnp.where((lane >= ones_from) & (lane <= ones_to), 1.0, 0.0)
    for a in range(KV):
        block = ones
        if with_mask:
            bias = jnp.where((cell < side) & (a < side), 0.0, -1e30)
            block = jnp.where(lane == 0, bias, ones)
        block = block.astype(BF)
        for h in h_range:
            ref[h, a * KV : (a + 1) * KV, 64:128] = block


def attention_forward_kernel(
    sides, images, mask, perm, vec, rows, wqt, wr, wk, wvt, wot,
    pre, patches, reduced, memory, mixed, lse, middle, post,
    key_ref, value_ref,
):
    i = pl.program_id(0)
    width = images.shape[1]

    def first_norm(t, _):
        for u in range(3):
            at = pl.ds(pl.multiple_of(t * 384 + u * 128, 128), 128)
            x = images[0, :, at].astype(F32) * mask[0, 0:1, at]
            normed, _unused = norm_columns(x)
            pre[0, 0:width, at] = (normed * vec[0] + vec[1]).astype(BF)
            pre[0, width : width + EXT, at] = first_row(jnp.ones((1, 128), F32)).astype(BF)
        at = pl.ds(pl.multiple_of(t * 384, 128), 384)
        picked = mm(perm[...], pre[0, 0:width, at], NT).astype(BF)
        for p in range(4):
            patches[0, p, pl.ds(pl.multiple_of(t * 96, 32), 96), :] = picked[p * 96 : (p + 1) * 96]
        return 0

    lax.fori_loop(0, TOKENS // 384, first_norm, 0)

    total = rows[0:1, :]
    for p in range(4):
        total = total + mm(patches[0, p], wr[p])
    reduced[0] = total
    normed, _unused = norm_rows(total)
    memory[0, :, 0:width] = (normed * rows[1:2, :] + rows[2:3, :]).astype(BF)
    lane = lax.broadcasted_iota(jnp.int32, (KEYS, 64), 1)
    memory[0, :, width : width + 64] = jnp.where(lane == 0, 1.0, 0.0).astype(BF)
    keys = mm(memory[0, :, 0:width], wk[...]).astype(BF)
    key_columns(key_ref, sides[i], range(HEADS), 1, 0, True)
    values = mm(wvt[...], memory[0], NT).astype(BF)
    ones = first_row(jnp.ones((1, KEYS), F32)).astype(BF)
    for h in range(HEADS):
        at = slice(h * HEAD_DIM, (h + 1) * HEAD_DIM)
        key_ref[h, :, 0:HEAD_DIM] = keys[:, at]
        value_ref[h, 0:HEAD_DIM, :] = values[at]
        value_ref[h, HEAD_DIM : HEAD_DIM + EXT, :] = ones
    mixed[0, width : width + EXT, :] = first_row(jnp.ones((1, TOKENS), F32)).astype(BF)
    queries = (mm(wqt[...], pre[0]) * QUERY_SCALE).astype(BF)
    tail = first_row(jnp.ones((1, TOKENS), F32), 64).astype(BF)
    for h in range(HEADS):
        at = slice(h * HEAD_DIM, (h + 1) * HEAD_DIM)
        scores = mm(key_ref[h], jnp.concatenate([queries[at], tail], axis=0))
        top = jnp.max(scores, axis=0, keepdims=True)
        weights = jnp.exp2(scores - top).astype(BF)
        out = mm(value_ref[h], weights)
        total = out[HEAD_DIM : HEAD_DIM + 1]
        mixed[0, at, :] = (out[0:HEAD_DIM] * (1.0 / total)).astype(BF)
        lse[0, h : h + 1, :] = top + jnp.log2(total)

    def second_norm(t, _):
        at = pl.ds(pl.multiple_of(t * 384, 128), 384)
        branch = mm(wot[...], mixed[0, :, at])
        for u in range(3):
            at = pl.ds(pl.multiple_of(t * 384 + u * 128, 128), 128)
            here = mask[0, 0:1, at]
            x = images[0, :, at].astype(F32) * here + branch[:, u * 128 : (u + 1) * 128]
            middle[0, :, at] = x
            normed, _unused = norm_columns(x)
            post[0, 0:width, at] = ((normed * vec[2] + vec[3]) * here).astype(BF)
            post[0, width : width + EXT, at] = first_row(here).astype(BF)
        return 0

    lax.fori_loop(0, TOKENS // 384, second_norm, 0)


def attention_forward(sides, images, mask, perm, vec, rows, wqt, wr, wk, wvt, wot):
    n, width, tokens = images.shape
    shape = jax.ShapeDtypeStruct
    outs = [
        shape((n, width + EXT, tokens), BF),
        shape((n, 4, KEYS, width), BF),
        shape((n, KEYS, width), F32),
        shape((n, KEYS, width + 64), BF),
        shape((n, width + EXT, tokens), BF),
        shape((n, 8, tokens), F32),
        shape((n, width, tokens), F32),
        shape((n, width + EXT, tokens), BF),
    ]
    weights = (perm, vec, rows, wqt, wr, wk, wvt, wot)
    return pl.pallas_call(
        attention_forward_kernel,
        grid_spec=pltpu.PrefetchScalarGridSpec(
            num_scalar_prefetch=1,
            grid=(n,),
            in_specs=[per_image(images), per_image(mask)] + [whole(x) for x in weights],
            out_specs=[per_image(x) for x in outs],
            scratch_shapes=[
                pltpu.VMEM((HEADS, KEYS, 128), BF),
                pltpu.VMEM((HEADS, HEAD_DIM + EXT, KEYS), BF),
            ],
        ),
        out_shape=outs,
        compiler_params=pltpu.CompilerParams(vmem_limit_bytes=VMEM_BYTES),
        name="attention_forward",
    )(sides, images, mask, *weights)


def feed_forward_kernel(
    post_next, cot_next, mask_next, we_next, wst_next, taps,
    post, cot, mask, middle, we, wst, vec,
    output, grad_post, gwe, gwst, gtaps, gbias,
    padded_0, padded_1, grad_padded, grad_act, act_0, act_1, grad_exp_0, grad_exp_1,
    post_rows, out_grad_rows, out_grad, total,
):
    s = pl.program_id(0)
    last = pl.num_programs(0) - 1
    width, block = cot.shape[1], wst.shape[1]
    blocks = gwst.shape[1] // block
    halves = block // 128
    rows = 16
    chunks = GRID // rows
    span = rows * GRID
    js = pl.ds(pl.multiple_of(lax.rem(s, blocks) * block, block), block)
    js_done = pl.ds(pl.multiple_of(lax.rem(jnp.maximum(s - 1, 0), blocks) * block, block), block)

    def tokens(t):
        return pl.ds(pl.multiple_of(t * span, span), span)

    def expand(t, padded, we, wst):
        at = tokens(t)
        filled = mm(post_rows[at, :], we[...])
        for h in range(halves):
            for r in range(rows):
                start = pl.multiple_of((t * rows + r + 1) * PITCH + 8, 8)
                padded[h, pl.ds(start, GRID), :] = filled[r * GRID : (r + 1) * GRID, h * 128 : (h + 1) * 128]
        grad_act[at, :] = mm(out_grad_rows[at, :], wst[...])

    def finish(t, act, grad_exp):
        at = tokens(t)
        total[:, at] += mm(wst[0:width, :], act[at, :], NT)
        grad_post[0, :, at] += mm(we[0:width, :], grad_exp[at, :], NT)
        gwst[:, js_done] += mm(out_grad[:, at], act[at, :])
        gwe[:, js_done] += mm(post[0, :, at], grad_exp[at, :])

    def convolve(t, padded, act):
        for h in range(halves):
            hs = slice(h * 128, (h + 1) * 128)
            w = [jnp.broadcast_to(taps[k : k + 1, hs], (GRID, 128)).astype(BF) for k in range(10)]
            sums = jnp.zeros((8, 128), F32)
            open_rows = {}
            for q in range(-1, rows + 1):
                base = (t * rows + q + 1) * PITCH + 8
                x = [padded[h, pl.ds(base + d, GRID), :].astype(BF) for d in (-1, 0, 1)]
                for a in (2, 1, 0):
                    r = q + 1 - a
                    if 0 <= r < rows:
                        part = w[3 * a] * x[0] + w[3 * a + 1] * x[1] + w[3 * a + 2] * x[2]
                        open_rows[r] = part + open_rows.get(r, w[9])
                r = q - 1
                if r < 0:
                    continue
                at = pl.ds(pl.multiple_of((t * rows + r) * GRID, GRID), GRID)
                gelu, slope = gelu_pair(open_rows.pop(r))
                act[at, hs] = gelu
                grad = (grad_act[at, hs].astype(BF) * slope).astype(F32)
                start = pl.multiple_of((t * rows + r + 1) * PITCH + 8, 8)
                grad_padded[h, pl.ds(start, GRID), :] = grad
                sums = sums + fold_rows(grad)
            cols = pl.ds(pl.multiple_of(lax.rem(s, blocks) * block + h * 128, 128), 128)
            gtaps[72:80, cols] += sums

    def convolve_back(t, padded, grad_exp):
        for h in range(halves):
            hs = slice(h * 128, (h + 1) * 128)
            w = [jnp.broadcast_to(taps[k : k + 1, hs], (GRID, 128)).astype(BF) for k in range(9)]
            sums = [jnp.zeros((8, 128), F32) for _ in range(9)]
            waiting = {}
            open_rows = {}
            x = {}
            for q in range(-1, rows + 1):
                base = (t * rows + q + 1) * PITCH + 8
                grads = [grad_padded[h, pl.ds(base + 1 - b, GRID), :].astype(BF) for b in range(3)]
                if q + 1 < rows:
                    start = pl.multiple_of((t * rows + q + 2) * PITCH + 8, 8)
                    x[q + 1] = padded[h, pl.ds(start, GRID), :].astype(BF)
                for a in range(3):
                    r = q + a - 1
                    if not 0 <= r < rows:
                        continue
                    part = w[3 * a] * grads[0] + w[3 * a + 1] * grads[1] + w[3 * a + 2] * grads[2]
                    open_rows[r] = part + open_rows[r] if r in open_rows else part
                    for b in range(3):
                        k = 3 * a + b
                        product = x[r] * grads[b]
                        product = product[0:16] + product[16:32] + product[32:48]
                        if k in waiting:
                            product = (product + waiting.pop(k)).astype(F32)
                            sums[k] = sums[k] + product[0:8] + product[8:16]
                        else:
                            waiting[k] = product
                r = q - 1
                if r >= 0:
                    at = pl.ds(pl.multiple_of((t * rows + r) * GRID, GRID), GRID)
                    grad_exp[at, hs] = open_rows.pop(r)
                    x.pop(r)
            cols = pl.ds(pl.multiple_of(lax.rem(s, blocks) * block + h * 128, 128), 128)
            for k in range(9):
                gtaps[8 * k : 8 * k + 8, cols] += sums[k]

    @pl.when(s == 0)
    def _():
        for ref in (padded_0, padded_1, grad_padded, act_1, grad_exp_1, out_grad, gwe, gwst, gtaps, gbias, post_rows, out_grad_rows):
            ref[...] = jnp.zeros_like(ref)

    @pl.when((s == 0) | ((lax.rem(s + 1, blocks) == 0) & (s + 1 < last)))
    def _():
        for t in range(TOKENS // 384):
            at = slice(t * 384, (t + 1) * 384)
            grad = cot_next[0, :, at].astype(F32) * mask_next[0, 0:1, at]
            gbias[...] += grad[:, 0:128] + grad[:, 128:256] + grad[:, 256:384]
            out_grad_rows[at, 0:width] = grad.astype(BF).T
            post_rows[at, 0 : width + EXT] = post_next[0, :, at].T

    @pl.when(lax.rem(s, blocks) == min(1, blocks - 1))
    def _():
        for t in range(TOKENS // 384):
            at = slice(t * 384, (t + 1) * 384)
            out_grad[:, at] = (cot[0, :, at].astype(F32) * mask[0, 0:1, at]).astype(BF)

    @pl.when((s == 0) | (lax.rem(s, blocks) == min(1, blocks - 1)))
    def _():
        total[...] = jnp.zeros_like(total)
        grad_post[...] = jnp.zeros_like(grad_post)

    @pl.when(s == 0)
    def _():
        def first(t, _):
            expand(t, padded_0, we, wst)
            return 0

        lax.fori_loop(0, chunks, first, 0)

    def work(padded, padded_next, act, act_done, grad_exp, grad_exp_done):
        def forward(t, _):
            finish(t, act_done, grad_exp_done)
            convolve(t, padded, act)
            return 0

        def backward(t, _):
            expand(t, padded_next, we_next, wst_next)
            convolve_back(t, padded, grad_exp)
            return 0

        lax.fori_loop(0, chunks, forward, 0)
        lax.fori_loop(0, chunks, backward, 0)

    @pl.when((s < last) & (lax.rem(s, 2) == 0))
    def _():
        work(padded_0, padded_1, act_0, act_1, grad_exp_0, grad_exp_1)

    @pl.when((s < last) & (lax.rem(s, 2) == 1))
    def _():
        work(padded_1, padded_0, act_1, act_0, grad_exp_1, grad_exp_0)

    @pl.when(s == last)
    def _():
        def rest(t, _):
            @pl.when(lax.rem(s, 2) == 0)
            def _():
                finish(t, act_1, grad_exp_1)

            @pl.when(lax.rem(s, 2) == 1)
            def _():
                finish(t, act_0, grad_exp_0)

            return 0

        lax.fori_loop(0, chunks, rest, 0)

    @pl.when((s > 0) & (lax.rem(s, blocks) == 0))
    def _():
        for t in range(TOKENS // 128):
            at = slice(t * 128, (t + 1) * 128)
            output[0, :, at] = ((middle[0, :, at] + total[:, at] + vec[4]) * mask[0, 0:1, at]).astype(BF)


def gelu_pair(x):
    kind = x.dtype.type
    square = x * x
    half = kind(0.5) * jnp.tanh(x * (kind(GELU_B) * square + kind(GELU_A))) + kind(0.5)
    gelu = x * half
    return gelu, half + gelu * (kind(1.0) - half) * (kind(6.0 * GELU_B) * square + kind(2.0 * GELU_A))


def feed_forward(post, cot, mask, middle, we, wst, taps, vec, block=256):
    n, width, tokens = cot.shape
    hidden = wst.shape[1]
    blocks = hidden // block
    count = n * blocks
    shape = jax.ShapeDtypeStruct
    outs = [
        shape((n, width, tokens), BF),
        shape((n, width, tokens), F32),
        shape((width + EXT, hidden), F32),
        shape((width, hidden), F32),
        shape((80, hidden), F32),
        shape((width, 128), F32),
    ]

    def ahead(s):
        return jnp.minimum(s + 1, count - 1)

    def behind(s):
        return jnp.maximum(s - 1, 0)

    def image(x, step):
        zeros = (0,) * (len(x.shape) - 1)
        return pl.BlockSpec((1,) + tuple(x.shape[1:]), lambda s: (step(s) // blocks,) + zeros)

    def columns(x, step):
        return pl.BlockSpec((x.shape[0], block), lambda s: (0, lax.rem(step(s), blocks)))

    return pl.pallas_call(
        feed_forward_kernel,
        grid=(count + 1,),
        in_specs=[image(x, ahead) for x in (post, cot, mask)]
        + [columns(we, ahead), columns(wst, ahead), columns(taps, lambda s: jnp.minimum(s, count - 1))]
        + [image(x, behind) for x in (post, cot, mask, middle)]
        + [columns(we, behind), columns(wst, behind), whole(vec)],
        out_specs=[image(x, behind) for x in outs[:2]] + [whole(x) for x in outs[2:]],
        out_shape=outs,
        scratch_shapes=[pltpu.VMEM((block // 128, (GRID + 2) * PITCH + 8, 128), F32)] * 3
        + [pltpu.VMEM((tokens, block), F32)]
        + [pltpu.VMEM((tokens, block), BF)] * 4
        + [
            pltpu.VMEM((tokens, DEPTH), BF),
            pltpu.VMEM((tokens, DEPTH), BF),
            pltpu.VMEM((width, tokens), BF),
            pltpu.VMEM((width, tokens), F32),
        ],
        compiler_params=pltpu.CompilerParams(vmem_limit_bytes=VMEM_BYTES),
        name="feed_forward",
    )(post, cot, mask, we, wst, taps, post, cot, mask, middle, we, wst, vec)


def attention_backward_kernel(
    sides, images, cot, mask, pre, patches, reduced, memory, mixed, lse, middle, grad_post,
    perm, vec, rows, wq, wqt, wr, wk, wv, wvt, wo,
    grad_images, gwo, gwq, gpair, gwr, gcols, grows,
    branch, grad_mixed, queries, grad_queries, key_ref, value_ref, keys_t, grad_keys, grad_values, grad_patches,
):
    i = pl.program_id(0)
    width = images.shape[1]

    @pl.when(i == 0)
    def _():
        for ref in (gwo, gwq, gpair, gwr, gcols, grows):
            ref[...] = jnp.zeros_like(ref)

    def mlp_norm_back(t, _):
        gain = shift = jnp.zeros((width, 128), F32)
        for u in range(3):
            at = pl.ds(pl.multiple_of(t * 384 + u * 128, 128), 128)
            here = mask[0, 0:1, at]
            normed, rstd = norm_columns(middle[0, :, at])
            grad = grad_post[0, :, at] * here
            gain = gain + grad * normed
            shift = shift + grad
            grad = cot[0, :, at].astype(F32) * here + norm_columns_back(normed, rstd, grad * vec[2])
            grad_images[0, :, at] = grad
            branch[:, at] = grad.astype(BF)
        gcols[2] += gain
        gcols[3] += shift
        return 0

    lax.fori_loop(0, TOKENS // 384, mlp_norm_back, 0)
    gwo[...] += mm(mixed[0], branch[...], NT)
    grad_mixed[...] = mm(wo[...], branch[...]).astype(BF)
    queries[...] = (mm(wqt[...], pre[0]) * QUERY_SCALE).astype(BF)
    keys = mm(memory[0, :, 0:width], wk[...]).astype(BF)
    keys_t[...] = keys.T
    values = mm(wvt[...], memory[0], NT).astype(BF).T
    key_columns(key_ref, sides[i], range(HEADS), 1, 3, True)
    key_columns(value_ref, sides[i], range(HEADS), 1, 3, False)
    for h in range(HEADS):
        at = slice(h * HEAD_DIM, (h + 1) * HEAD_DIM)
        key_ref[h, :, 0:HEAD_DIM] = keys[:, at]
        value_ref[h, :, 0:HEAD_DIM] = values[:, at]

    span = TOKENS // 2
    index = lax.broadcasted_iota(jnp.int32, (64, span), 0)
    for t in range(TOKENS // span):
        at = slice(t * span, (t + 1) * span)
        for h in range(HEADS):
            hs = slice(h * HEAD_DIM, (h + 1) * HEAD_DIM)
            one, two, three = three_parts(-lse[0, h : h + 1, at])
            tail = jnp.where(index == 2, two, jnp.where(index == 3, three, 0.0))
            tail = jnp.where(index == 0, 1.0, jnp.where(index == 1, one, tail)).astype(BF)
            query = queries[hs, at]
            attend = jnp.exp2(mm(key_ref[h], jnp.concatenate([query, tail], axis=0)))
            low = attend.astype(BF)
            grad = grad_mixed[hs, at]
            inner = grad.astype(F32) * mixed[0, hs, at].astype(F32)
            one, two, three = three_parts(-jnp.sum(inner, axis=0, keepdims=True))
            tail = jnp.where(index == 2, two, jnp.where(index == 3, three, 0.0))
            tail = jnp.where(index == 1, one, tail).astype(BF)
            grad_attend = mm(value_ref[h], jnp.concatenate([grad, tail], axis=0))
            grad_scores = (attend * grad_attend).astype(BF)
            grad_value = mm(grad, low, NT)
            grad_key = mm(query, grad_scores, NT) * (1.0 / LOG2E)
            if t == 0:
                grad_values[hs, :] = grad_value
                grad_keys[hs, :] = grad_key
            else:
                grad_values[hs, :] += grad_value
                grad_keys[hs, :] += grad_key
            grad_queries[hs, at] = (mm(keys_t[hs, :], grad_scores) * HEAD_DIM**-0.5).astype(BF)

    low_keys = grad_keys[...].astype(BF)
    low_values = grad_values[...].astype(BF)
    gpair[0:width, :] += mm(low_keys, memory[0])
    gpair[width : 2 * width, :] += mm(low_values, memory[0])
    grad_memory = mm(low_keys.T, wk[...], NT) + mm(low_values.T, wv[...], NT)
    normed, rstd = norm_rows(reduced[0])
    grows[8:16, :] += fold_rows(grad_memory * normed)
    grows[16:24, :] += fold_rows(grad_memory)
    grad_reduced = norm_rows_back(normed, rstd, grad_memory * rows[1:2, :]).astype(BF)
    grows[0:8, :] += fold_rows(grad_reduced.astype(F32))
    grad_reduced_t = grad_reduced.T
    for p in range(4):
        gwr[p] += mm(grad_reduced_t, patches[0, p])
        grad_patches[p] = mm(grad_reduced, wr[p], NT).astype(BF)
    gwq[...] += mm(pre[0], grad_queries[...], NT)

    def pre_norm_back(t, _):
        at = pl.ds(pl.multiple_of(t * 384, 128), 384)
        grad_pre = mm(wq[...], grad_queries[:, at])
        start = pl.ds(pl.multiple_of(t * 96, 32), 96)
        picked = jnp.concatenate([grad_patches[p, start, :] for p in range(4)], axis=0)
        grad_pre = grad_pre + mm(picked.T, perm[...])
        gain = shift = jnp.zeros((width, 128), F32)
        for u in range(3):
            at = pl.ds(pl.multiple_of(t * 384 + u * 128, 128), 128)
            here = mask[0, 0:1, at]
            normed, rstd = norm_columns(images[0, :, at].astype(F32) * here)
            grad = grad_pre[:, u * 128 : (u + 1) * 128]
            gain = gain + grad * normed
            shift = shift + grad
            back = norm_columns_back(normed, rstd, grad * vec[0])
            grad_images[0, :, at] = (grad_images[0, :, at] + back) * here
        gcols[0] += gain
        gcols[1] += shift
        return 0

    lax.fori_loop(0, TOKENS // 384, pre_norm_back, 0)


def attention_backward(
    sides, images, cot, mask, pre, patches, reduced, memory, mixed, lse, middle, grad_post,
    perm, vec, rows, wq, wqt, wr, wk, wv, wvt, wo,
):
    n, width, tokens = images.shape
    shape = jax.ShapeDtypeStruct
    outs = [
        shape((n, width, tokens), F32),
        shape((width + EXT, width), F32),
        shape((width + EXT, width), F32),
        shape((2 * width, width + 64), F32),
        shape((4, width, width), F32),
        shape((4, width, 128), F32),
        shape((24, width), F32),
    ]
    one = {"pipeline_mode": pl.Buffered(1)}
    inputs = (images, cot, mask, pre, patches, reduced, memory, mixed, lse)
    weights = (perm, vec, rows, wq, wqt, wr, wk, wv, wvt, wo)
    return pl.pallas_call(
        attention_backward_kernel,
        grid_spec=pltpu.PrefetchScalarGridSpec(
            num_scalar_prefetch=1,
            grid=(n,),
            in_specs=[per_image(x) for x in inputs]
            + [per_image(middle, **one), per_image(grad_post, **one)]
            + [whole(x) for x in weights],
            out_specs=[per_image(outs[0], **one)] + [whole(x) for x in outs[1:]],
            scratch_shapes=[
                pltpu.VMEM((width, tokens), BF),
                pltpu.VMEM((width, tokens), BF),
                pltpu.VMEM((width, tokens), BF),
                pltpu.VMEM((width, tokens), BF),
                pltpu.VMEM((HEADS, KEYS, 128), BF),
                pltpu.VMEM((HEADS, KEYS, 128), BF),
                pltpu.VMEM((width, KEYS), BF),
                pltpu.VMEM((width, KEYS), F32),
                pltpu.VMEM((width, KEYS), F32),
                pltpu.VMEM((4, KEYS, width), BF),
            ],
        ),
        out_shape=outs,
        compiler_params=pltpu.CompilerParams(vmem_limit_bytes=VMEM_BYTES),
        name="attention_backward",
    )(sides, *inputs, middle, grad_post, *weights)

MESH = pl.DeviceIdType.MESH


class Place:
    def __init__(self):
        self.dp = lax.axis_index("dp")
        self.fsdp = lax.axis_index("fsdp")
        self.y, self.x = self.dp // 2, self.dp % 2
        self.z, self.core = self.fsdp // 2, self.fsdp % 2
        self.other_core = 1 - self.core
        self.beside_x = (self.dp + 1 - 2 * self.x, self.fsdp)
        self.beside_y = (self.dp + 2 - 4 * self.y, self.fsdp)
        self.across = (3 - self.dp, self.fsdp)
        self.beside_core = (self.dp, self.fsdp + 1 - 2 * self.core)
        self.others = (self.z + 1 - 2 * (self.z % 2), 2 - self.z // 2, 3 * (1 - self.z // 2))

    def at_z(self, z):
        return (self.dp, z * 2 + self.core)

    def along_z(self, k):
        return self.at_z((self.z + k) % 4)

    def call(self, partners):
        barrier = pltpu.get_barrier_semaphore()
        for device in partners:
            pl.semaphore_signal(barrier, inc=1, device_id=device, device_id_type=MESH)

    def answer(self, count):
        pl.semaphore_wait(pltpu.get_barrier_semaphore(), count)


class Sender:
    def __init__(self, send, recv):
        self.send, self.recv, self.started = send, recv, []

    def __call__(self, source, target, device, recv=None):
        k = len(self.started)
        copy = pltpu.make_async_remote_copy(
            src_ref=source,
            dst_ref=target,
            send_sem=self.send.at[k],
            recv_sem=self.recv.at[k] if recv is None else recv,
            device_id=device,
            device_id_type=MESH,
        )
        copy.start()
        self.started.append(copy)
        return copy

    def finish(self):
        for copy in self.started:
            copy.wait_send()


def gather_kernel(slot_rows, bases, own, *refs):
    outs, (slots, wide, line, own_sem, send_sem, recv_sem, z_sem) = refs[:13], refs[13:]
    me = Place()
    half = own.shape[0] // 2
    first, second = pl.ds(0, half), pl.ds(half, half)
    send = Sender(send_sem, recv_sem)
    copy = pltpu.make_async_copy(own, slots.at[me.core, me.dp, me.z], own_sem)
    copy.start()
    me.call([me.beside_core, me.beside_x, me.beside_y] + [me.at_z(z) for z in me.others])
    me.answer(6)
    own_slot = slots.at[me.core, me.dp, me.z]

    def send_z(j):
        return send(own, own_slot, me.at_z(me.others[j]), z_sem.at[me.z])

    send_z(0)
    x_copies = [send(own, own_slot, me.beside_x)]
    y_copies = [send(own, own_slot, me.beside_y)]
    core_copies = [(send(own, own_slot, me.beside_core), me.dp, me.z)]
    send_z(1)
    half_copies = []
    order = (me.z,) + me.others

    def open_slot(core, dp, z):
        spread_slot(slots[core, dp, z], (dp * 8 + z * 2 + core), slot_rows, line, wide)

    def forward(k):
        z = order[k]
        x_copies[k].wait_recv()
        slot = slots.at[me.core, me.beside_x[0], z]
        half_copies.append(send(slot.at[first], slot.at[first], me.beside_y))
        core_copies.append((send(slot, slot, me.beside_core), me.beside_x[0], z))
        y_copies[k].wait_recv()
        slot = slots.at[me.core, me.beside_y[0], z]
        half_copies.append(send(slot.at[second], slot.at[second], me.beside_x))
        core_copies.append((send(slot, slot, me.beside_core), me.beside_y[0], z))
        open_slot(me.core, me.beside_x[0], z)
        open_slot(me.core, me.beside_y[0], z)

    copy.wait()
    open_slot(me.core, me.dp, me.z)
    forward(0)
    for k in (1, 2, 3):
        z = order[k]
        slot = slots.at[me.core, me.dp, z]
        pltpu.make_async_remote_copy(
            src_ref=own,
            dst_ref=slot,
            send_sem=send_sem.at[0],
            recv_sem=z_sem.at[z],
            device_id=me.at_z(z),
            device_id_type=MESH,
        ).wait_recv()
        x_copies.append(send(slot, slot, me.beside_x))
        y_copies.append(send(slot, slot, me.beside_y))
        core_copies.append((send(slot, slot, me.beside_core), me.dp, z))
        if k == 1:
            send_z(2)
        open_slot(me.core, me.dp, z)
        forward(k)
    for k in range(4):
        half_copies[2 * k].wait_recv()
        half_copies[2 * k + 1].wait_recv()
        slot = slots.at[me.core, me.across[0], order[k]]
        core_copies.append((send(slot, slot, me.beside_core), me.across[0], order[k]))
        open_slot(me.core, me.across[0], order[k])
    for copied, dp, z in core_copies:
        copied.wait_recv()
        open_slot(me.other_core, dp, z)
    send.finish()
    write_weights(bases, wide, *outs)


def gather_weights(own, slot_rows, width):
    bases, count = row_bases(width, 4 * width)
    outs = weight_shapes(width)
    copies = 35
    values = pl.pallas_call(
        partial(gather_kernel, slot_rows, bases),
        out_shape=list(outs.values()),
        in_specs=[pl.BlockSpec(memory_space=pltpu.VMEM)],
        out_specs=[pl.BlockSpec(memory_space=pltpu.VMEM)] * len(outs),
        scratch_shapes=[
            pltpu.VMEM((2, 4, 4) + own.shape, BF),
            pltpu.VMEM((3, -(-32 * slot_rows * 128 // width // 8) * 8 + 8, 128), F32),
            pltpu.VMEM(own.shape, F32),
            pltpu.SemaphoreType.DMA(()),
            pltpu.SemaphoreType.DMA((copies,)),
            pltpu.SemaphoreType.DMA((copies,)),
            pltpu.SemaphoreType.DMA((4,)),
        ],
        compiler_params=pltpu.CompilerParams(
            collective_id=0, has_side_effects=True, vmem_limit_bytes=VMEM_BYTES
        ),
        name="gather_weights",
    )(own)
    return dict(zip(outs, values, strict=True))


def reduce_kernel(slot_rows, bases, *refs):
    grads, (shard, squares) = refs[:10], refs[10:12]
    wide, line, own, core_out, core_in, y_in, x_in, x_last, y_last, z_in, small, send_sem, recv_sem = refs[12:]
    me = Place()
    rows = shard.shape[0]
    half = rows // 2
    first, second = pl.ds(0, half), pl.ds(half, half)
    send = Sender(send_sem, recv_sem)
    peers = [(me.dp, (me.z + k) % 4 * 2 + core) for k in range(4) for core in (me.core, me.other_core)][1:]
    planes = [me.beside_x, me.beside_y, me.across]
    me.call(peers + planes)
    collect_gradients(bases, wide, *grads)
    line[...] = jnp.zeros_like(line)
    me.answer(len(peers + planes))
    units = [(me.z + k) % 4 for k in (2, 1, 3, 0)]
    core_copies, y_copies, x_copies, last = [], [], [], []
    other_x, other_y = 1 - me.x, 1 - me.y

    def give(k):
        z = units[k]
        for dp in range(4):
            join_slot(wide, dp * 8 + z * 2 + me.other_core, slot_rows, line)
            core_out[z, dp] = line[...].astype(BF)
        core_copies.append(send(core_out.at[z], core_in.at[z], me.beside_core))
        for dp in range(4):
            join_slot(wide, dp * 8 + z * 2 + me.core, slot_rows, line)
            own[z, dp] = line[...]

    def cores(k):
        z = units[k]
        core_copies[k].wait_recv()
        for dp in range(4):
            core_in[z, dp] = (core_in[z, dp].astype(F32) + own[z, dp]).astype(BF)
        y_copies.append(
            [send(core_in.at[z, 2 * other_y + x, first], y_in.at[z, x], me.beside_y) for x in range(2)]
        )
        x_copies.append(
            [send(core_in.at[z, 2 * y + other_x, second], x_in.at[z, y], me.beside_x) for y in range(2)]
        )

    def plane(k):
        z = units[k]
        for copied in y_copies[k]:
            copied.wait_recv()
        y_in[z, other_x] = (
            y_in[z, other_x].astype(F32) + core_in[z, 2 * me.y + other_x, first].astype(F32)
        ).astype(BF)
        to_x = send(y_in.at[z, other_x], x_last.at[z], me.beside_x)
        for copied in x_copies[k]:
            copied.wait_recv()
        x_in[z, other_y] = (
            x_in[z, other_y].astype(F32) + core_in[z, 2 * other_y + me.x, second].astype(F32)
        ).astype(BF)
        last.append((to_x, send(x_in.at[z, other_y], y_last.at[z], me.beside_y)))

    z_copies = []

    def column(k):
        z = units[k]
        for copied in last[k]:
            copied.wait_recv()
        low = y_in[z, me.x].astype(F32) + core_in[z, me.dp, first].astype(F32) + x_last[z].astype(F32)
        high = x_in[z, me.y].astype(F32) + core_in[z, me.dp, second].astype(F32) + y_last[z].astype(F32)
        if k == 3:
            shard[first, :] = low
            shard[second, :] = high
        else:
            z_in[k, first] = low.astype(BF)
            z_in[k, second] = high.astype(BF)
            z_copies.append(send(z_in.at[k], z_in.at[k + 3], me.at_z(z)))

    give(0)
    give(1)
    cores(0)
    give(2)
    cores(1)
    plane(0)
    give(3)
    cores(2)
    plane(1)
    column(0)
    cores(3)
    plane(2)
    column(1)
    plane(3)
    column(2)
    column(3)
    for k in (0, 1, 2):
        z_copies[k].wait_recv()
        shard[...] += z_in[k + 3].astype(F32)
    total = shard[0:8, :] * shard[0:8, :]
    for k in range(1, rows // 8):
        part = shard[8 * k : 8 * k + 8, :]
        total = total + part * part
    small[0] = total
    small[2 + me.fsdp] = total
    copies = [send(small.at[0], small.at[2 + me.fsdp], device) for device in peers]
    for copied in copies:
        copied.wait_recv()
    total = small[2]
    for k in range(1, 8):
        total = total + small[2 + k]
    small[1] = total
    small[10 + me.dp] = total
    copies = [send(small.at[1], small.at[10 + me.dp], device) for device in planes]
    for copied in copies:
        copied.wait_recv()
    squares[...] = ((small[10] + small[11]) + small[12]) + small[13]
    send.finish()


def reduce_gradients(grads, slot_rows, rows, width):
    bases, _ = row_bases(width, 4 * width)
    half = rows // 2
    count = 4 + 16 + 8 + 3 + 7 + 3
    return pl.pallas_call(
        partial(reduce_kernel, slot_rows, bases),
        out_shape=[jax.ShapeDtypeStruct((rows, 128), F32), jax.ShapeDtypeStruct((8, 128), F32)],
        in_specs=[pl.BlockSpec(memory_space=pltpu.VMEM)] * len(grads),
        out_specs=[pl.BlockSpec(memory_space=pltpu.VMEM)] * 2,
        scratch_shapes=[
            pltpu.VMEM((3, -(-32 * slot_rows * 128 // width // 8) * 8 + 8, 128), F32),
            pltpu.VMEM((rows, 128), F32),
            pltpu.VMEM((4, 4, rows, 128), F32),
            pltpu.VMEM((4, 4, rows, 128), BF),
            pltpu.VMEM((4, 4, rows, 128), BF),
            pltpu.VMEM((4, 2, half, 128), BF),
            pltpu.VMEM((4, 2, half, 128), BF),
            pltpu.VMEM((4, half, 128), BF),
            pltpu.VMEM((4, half, 128), BF),
            pltpu.VMEM((6, rows, 128), BF),
            pltpu.VMEM((14, 8, 128), F32),
            pltpu.SemaphoreType.DMA((count,)),
            pltpu.SemaphoreType.DMA((count,)),
        ],
        compiler_params=pltpu.CompilerParams(
            collective_id=1, has_side_effects=True, vmem_limit_bytes=VMEM_BYTES
        ),
        name="reduce_gradients",
    )(*grads)


def layout_shapes(model_width, hidden_width):
    return [
        ("pre_gain", (model_width,)),
        ("pre_shift", (model_width,)),
        ("query_weight", (model_width, model_width)),
        ("query_bias", (model_width,)),
        ("reduce_weight", (4 * model_width, model_width)),
        ("reduce_bias", (model_width,)),
        ("reduce_gain", (model_width,)),
        ("reduce_shift", (model_width,)),
        ("pair_weight", (model_width, 2 * model_width)),
        ("value_bias", (model_width,)),
        ("output_weight", (model_width, model_width)),
        ("output_bias", (model_width,)),
        ("mlp_gain", (model_width,)),
        ("mlp_shift", (model_width,)),
        ("expand_weight", (model_width, hidden_width)),
        ("expand_bias", (hidden_width,)),
        ("spatial_weight", (9, hidden_width)),
        ("spatial_bias", (hidden_width,)),
        ("shrink_weight", (hidden_width, model_width)),
        ("shrink_bias", (model_width,)),
    ]


def row_bases(width, hidden):
    bases = {}
    row = 0
    for name, shape in layout_shapes(width, hidden):
        bases[name] = row
        row += math.prod(shape) // width
    return bases, row


SPAN = 96


def regroup_lines(read, write, low):
    part = [read(k) for k in range(5)]
    turned = [pltpu.roll(part[k], 64, 1) for k in (2, 3, 4)]
    for k in range(3):
        write(0, k, part[k])
    write(1, 0, jnp.where(low, turned[0], turned[1]))
    write(1, 1, jnp.where(low, turned[1], turned[2]))
    write(1, 2, turned[2])


def spread_slot(values, slot, slot_rows, line, wide):
    pairs = slot_rows // 5
    line[...] = values.astype(F32)

    def part(start, count):
        low = lax.broadcasted_iota(jnp.int32, (count, 128), 1) < 64

        def write(parity, k, value):
            wide[k, pl.ds(slot * (2 * pairs) + 2 * start + parity, count, stride=2), :] = value

        regroup_lines(lambda k: line[pl.ds(5 * start + k, count, stride=5), :], write, low)

    part(0, pairs // 8 * 8)
    if pairs % 8:
        part(pairs // 8 * 8, pairs % 8)


def unpack_kernel(order, slot_rows, bases, slots, *refs):
    outs, (flat, wide) = refs[:13], refs[13:]
    for slot, place in enumerate(order):
        flat[pl.ds(slot * slot_rows, slots.shape[1]), :] = slots[place].astype(F32)
    low = lax.broadcasted_iota(jnp.int32, (SPAN, 128), 1) < 64

    def regroup(t, _):
        def write(parity, k, value):
            wide[k, pl.ds(t * (2 * SPAN) + parity, SPAN, stride=2), :] = value

        regroup_lines(lambda k: flat[pl.ds(t * (5 * SPAN) + k, SPAN, stride=5), :], write, low)
        return 0

    lax.fori_loop(0, wide.shape[1] // (2 * SPAN), regroup, 0)
    write_weights(bases, wide, *outs)


def write_weights(bases, wide, vec, rows, wq, wqt, wr, wk, wv, wvt, wo, wot, we, wst, taps):
    width = wq.shape[0]
    hidden = wst.shape[1]

    def take(base, count, stride=1):
        at = pl.ds(base, count, stride=stride) if stride > 1 else pl.ds(base, count)
        return jnp.concatenate([wide[0, at, :], wide[1, at, :], wide[2, at, :][:, 0 : width - 256]], axis=1)

    def take_hidden(base, count):
        return jnp.concatenate([take(base + q, count, hidden // width) for q in range(hidden // width)], axis=1)

    def bordered(weight, bias, extra):
        index = lax.broadcasted_iota(jnp.int32, (extra, weight.shape[1]), 0)
        return jnp.concatenate([weight, jnp.where(index == 0, bias, 0.0)], axis=0)

    names = ("pre_gain", "pre_shift", "mlp_gain", "mlp_shift", "shrink_bias")
    for k, name in enumerate(names):
        vec[k] = jnp.broadcast_to(take(bases[name], 1), (128, width)).T
    for k, name in enumerate(("reduce_bias", "reduce_gain", "reduce_shift")):
        rows[k : k + 1, :] = take(bases[name], 1)
    query = take(bases["query_weight"], width)
    wq[...] = query.astype(BF)
    wqt[...] = bordered(query, take(bases["query_bias"], 1), EXT).T.astype(BF)
    for p in range(4):
        wr[p] = take(bases["reduce_weight"] + p * width, width).astype(BF)
    wk[...] = take(bases["pair_weight"], width, 2).astype(BF)
    value = take(bases["pair_weight"] + 1, width, 2)
    wv[...] = value.astype(BF)
    wvt[...] = bordered(value, take(bases["value_bias"], 1), 64).T.astype(BF)
    out = take(bases["output_weight"], width)
    wo[...] = out.astype(BF)
    wot[...] = bordered(out, take(bases["output_bias"], 1), EXT).T.astype(BF)
    we[0:width, :] = take_hidden(bases["expand_weight"], width).astype(BF)
    we[width:DEPTH, :] = first_row(take_hidden(bases["expand_bias"], 1), DEPTH - width).astype(BF)
    taps[0:9, :] = take_hidden(bases["spatial_weight"], 9)
    taps[9:10, :] = take_hidden(bases["spatial_bias"], 1)
    wst[width:DEPTH, :] = jnp.zeros((DEPTH - width, hidden), BF)
    for k in range(hidden // 128):
        wst[0:width, 128 * k : 128 * k + 128] = take(bases["shrink_weight"] + 128 * k, 128).T.astype(BF)


def wide_rows(count):
    return -(-count // (2 * SPAN)) * 2 * SPAN


def weight_shapes(width):
    hidden = 4 * width
    shape = jax.ShapeDtypeStruct
    return dict(
        vec=shape((5, width, 128), F32),
        rows=shape((3, width), F32),
        wq=shape((width, width), BF),
        wqt=shape((width, width + EXT), BF),
        wr=shape((4, width, width), BF),
        wk=shape((width, width), BF),
        wv=shape((width, width), BF),
        wvt=shape((width, width + 64), BF),
        wo=shape((width, width), BF),
        wot=shape((width, width + EXT), BF),
        we=shape((DEPTH, hidden), BF),
        wst=shape((DEPTH, hidden), BF),
        taps=shape((10, hidden), F32),
    )


def unpack_weights(slots, order, slot_rows, width):
    bases, count = row_bases(width, 4 * width)
    outs = weight_shapes(width)
    flat_rows = max(len(order) * slot_rows, wide_rows(count) * width // 128) + slots.shape[1]
    values = pl.pallas_call(
        partial(unpack_kernel, order, slot_rows, bases),
        out_shape=list(outs.values()),
        in_specs=[pl.BlockSpec(memory_space=pltpu.VMEM)],
        out_specs=[pl.BlockSpec(memory_space=pltpu.VMEM)] * len(outs),
        scratch_shapes=[pltpu.VMEM((flat_rows, 128), F32), pltpu.VMEM((3, wide_rows(count), 128), F32)],
        compiler_params=pltpu.CompilerParams(vmem_limit_bytes=VMEM_BYTES),
        name="unpack_weights",
    )(slots)
    return dict(zip(outs, values, strict=True))


def collect_gradients(bases, wide, gwe, gwst, gtaps, gbias, gwo, gwq, gpair, gwr, gcols, grows):
    width = gwst.shape[0]
    hidden = gwst.shape[1]
    used = bases["shrink_bias"] + 1
    for k in range(3):
        wide[k, pl.ds(used, wide.shape[1] - used), :] = jnp.zeros((wide.shape[1] - used, 128), F32)

    def put(base, value, stride=1):
        count = value.shape[0]
        at = pl.ds(base, count, stride=stride) if stride > 1 else pl.ds(base, count)
        wide[0, at, :] = value[:, 0:128]
        wide[1, at, :] = value[:, 128:256]
        wide[2, at, 0 : width - 256] = value[:, 256:width]

    for k, name in enumerate(("pre_gain", "pre_shift", "mlp_gain", "mlp_shift")):
        put(bases[name], jnp.sum(gcols[k].T, axis=0, keepdims=True))
    put(bases["shrink_bias"], jnp.sum(gbias[...].T, axis=0, keepdims=True))
    for k, name in enumerate(("reduce_bias", "reduce_gain", "reduce_shift")):
        put(bases[name], jnp.sum(grows[8 * k : 8 * k + 8, :], axis=0, keepdims=True))
    put(bases["query_weight"], gwq[0 : width + 1, :])
    for p in range(4):
        put(bases["reduce_weight"] + p * width, gwr[p].T)
    put(bases["pair_weight"], gpair[0:width, :].T[0:width], 2)
    value = gpair[width : 2 * width, :].T
    put(bases["pair_weight"] + 1, value[0:width], 2)
    put(bases["value_bias"], value[width : width + 1])
    put(bases["output_weight"], gwo[0 : width + 1, :])
    sums = jnp.concatenate(
        [jnp.sum(gtaps[8 * k : 8 * k + 8, :], axis=0, keepdims=True) for k in range(10)], axis=0
    )
    for q in range(hidden // width):
        put(bases["expand_weight"] + q, gwe[0 : width + 1, q * width : (q + 1) * width], hidden // width)
        put(bases["spatial_weight"] + q, sums[:, q * width : (q + 1) * width], hidden // width)
    for k in range(hidden // 128):
        put(bases["shrink_weight"] + 128 * k, gwst[:, 128 * k : 128 * k + 128].T)

def join_lines(read, write, low):
    turned = [pltpu.roll(read(1, k), 64, 1) for k in range(3)]
    write(0, read(0, 0))
    write(1, read(0, 1))
    write(2, jnp.where(low, read(0, 2), turned[0]))
    write(3, jnp.where(low, turned[0], turned[1]))
    write(4, jnp.where(low, turned[1], turned[2]))


def join_slot(wide, slot, slot_rows, line):
    pairs = slot_rows // 5

    def part(start, count):
        low = lax.broadcasted_iota(jnp.int32, (count, 128), 1) < 64

        def read(parity, k):
            return wide[k, pl.ds(slot * (2 * pairs) + 2 * start + parity, count, stride=2), :]

        def write(k, value):
            line[pl.ds(5 * start + k, count, stride=5), :] = value

        join_lines(read, write, low)

    part(0, pairs // 8 * 8)
    if pairs % 8:
        part(pairs // 8 * 8, pairs % 8)


def pack_kernel(order, slot_rows, bases, *refs):
    grads, (slots, flat, wide) = refs[:10], refs[10:]
    collect_gradients(bases, wide, *grads)
    done = wide.shape[1] * 5 // 2
    flat[done:, :] = jnp.zeros((flat.shape[0] - done, 128), F32)
    low = lax.broadcasted_iota(jnp.int32, (SPAN, 128), 1) < 64

    def regroup(t, _):
        def read(parity, k):
            return wide[k, pl.ds(t * (2 * SPAN) + parity, SPAN, stride=2), :]

        def write(k, value):
            flat[pl.ds(t * (5 * SPAN) + k, SPAN, stride=5), :] = value

        join_lines(read, write, low)
        return 0

    lax.fori_loop(0, wide.shape[1] // (2 * SPAN), regroup, 0)
    inside = lax.broadcasted_iota(jnp.int32, slots.shape[1:], 0) < slot_rows
    for slot, place in enumerate(order):
        slots[place] = jnp.where(inside, flat[pl.ds(slot * slot_rows, slots.shape[1]), :], 0.0).astype(BF)


def pack_gradients(grads, order, slot_rows, padded_rows, width):
    bases, count = row_bases(width, 4 * width)
    flat_rows = max(len(order) * slot_rows, wide_rows(count) * width // 128) + padded_rows
    return pl.pallas_call(
        partial(pack_kernel, order, slot_rows, bases),
        out_shape=jax.ShapeDtypeStruct((len(order), padded_rows, 128), BF),
        in_specs=[pl.BlockSpec(memory_space=pltpu.VMEM)] * len(grads),
        out_specs=pl.BlockSpec(memory_space=pltpu.VMEM),
        scratch_shapes=[pltpu.VMEM((flat_rows, 128), F32), pltpu.VMEM((3, wide_rows(count), 128), F32)],
        compiler_params=pltpu.CompilerParams(vmem_limit_bytes=VMEM_BYTES),
        name="pack_gradients",
    )(*grads)


def device_step(images, cotangent, kv_sides, w):
    positions = jnp.arange(TOKENS, dtype=jnp.int32)
    limit = 2 * kv_sides[:, None]
    mask = ((positions[None] // GRID < limit) & (positions[None] % GRID < limit)).astype(F32)
    mask = jnp.broadcast_to(mask[:, None, :], (mask.shape[0], 8, TOKENS))
    perm = jnp.asarray(patch_order(), BF)
    pre, patches, reduced, memory, mixed, lse, middle, post = attention_forward(
        kv_sides, images, mask, perm, w["vec"], w["rows"], w["wqt"], w["wr"], w["wk"], w["wvt"], w["wot"]
    )
    output, grad_post, gwe, gwst, gtaps, gbias = feed_forward(
        post, cotangent, mask, middle, w["we"], w["wst"], w["taps"], w["vec"]
    )
    grad_images, gwo, gwq, gpair, gwr, gcols, grows = attention_backward(
        kv_sides, images, cotangent, mask, pre, patches, reduced, memory, mixed, lse, middle, grad_post,
        perm, w["vec"], w["rows"], w["wq"], w["wqt"], w["wr"], w["wk"], w["wv"], w["wvt"], w["wo"],
    )
    return output, grad_images, (gwe, gwst, gtaps, gbias, gwo, gwq, gpair, gwr, gcols, grows)


def step(on_grid, images, cotangent, kv_sides, params, first_moment, second_moment):
    width = images.shape[2]
    axes = ("dp", "fsdp")
    outer, inner = lax.axis_size("dp"), lax.axis_size("fsdp")
    slot_rows = params.shape[0] // 128
    padded_rows = -(-slot_rows // 32) * 32
    own = jnp.pad(params.reshape(slot_rows, 128).astype(BF), ((0, padded_rows - slot_rows), (0, 0)))
    order = list(range(outer * inner))
    if on_grid:
        weights = gather_weights(own, slot_rows, width)
    else:
        weights = unpack_weights(lax.all_gather(own, axes), order, slot_rows, width)
    output, grad_images, grads = device_step(
        images.transpose(0, 2, 1), cotangent.transpose(0, 2, 1), kv_sides, weights
    )
    if on_grid:
        shard, squares = reduce_gradients(grads, slot_rows, padded_rows, width)
        squares = jnp.sum(squares)
    else:
        slots = pack_gradients(grads, order, slot_rows, padded_rows, width)
        shard = lax.psum_scatter(slots.astype(F32), axes)
        squares = lax.psum(jnp.sum(shard * shard), axes)
    shard = shard[:slot_rows].reshape(-1)
    grad_norm = jnp.sqrt(squares)
    clipped = shard * jnp.minimum(1.0, CLIP_NORM / (grad_norm + 1e-06))
    new_first = BETA_FIRST * first_moment + (1.0 - BETA_FIRST) * clipped
    new_second = BETA_SECOND * second_moment + (1.0 - BETA_SECOND) * clipped * clipped
    first_hat = new_first / (1.0 - BETA_FIRST**STEP)
    second_hat = new_second / (1.0 - BETA_SECOND**STEP)
    new_params = params - RATE * (first_hat / (jnp.sqrt(second_hat) + EPSILON) + DECAY * params)
    return (
        output.transpose(0, 2, 1),
        grad_images.transpose(0, 2, 1),
        grad_norm,
        new_first,
        new_second,
        new_params,
    )


def solution(mesh):
    data = P(("dp", "fsdp"), None, None)
    flat = P(("dp", "fsdp"))
    on_grid = dict(mesh.shape) == {"dp": 4, "fsdp": 8}
    return jax.shard_map(
        partial(step, on_grid),
        mesh=mesh,
        in_specs=(data, data, flat, flat, flat, flat),
        out_specs=(data, data, P(), flat, flat, flat),
        check_vma=False,
    )
```

```python
from functools import partial
import math

import jax
import jax.numpy as jnp
import numpy as np
from jax import lax
from jax.experimental import pallas as pl
from jax.experimental.pallas import tpu as pltpu
from jax.sharding import PartitionSpec as P

HEADS = 5
HEAD_DIM = 64
GRID = 48
KV = 24
STEP = 10

CLIP_NORM = 1.0
BETA_FIRST = 0.9
BETA_SECOND = 0.999
RATE = 0.04
DECAY = 0.05
EPSILON = 1e-08

F32 = jnp.float32
BF = jnp.bfloat16
NN = (((1,), (0,)), ((), ()))
NT = (((1,), (1,)), ((), ()))
TOKENS = GRID * GRID
KEYS = KV * KV
PITCH = GRID + 8
EXT = 16
DEPTH = 512
LOG2E = math.log2(math.e)
QUERY_SCALE = HEAD_DIM**-0.5 * LOG2E
GELU_A = math.sqrt(2.0 / math.pi)
GELU_B = GELU_A * 0.044715
VMEM_BYTES = 63 * 1024 * 1024


def mm(left, right, dims=NN):
    return lax.dot_general(left, right, dims, preferred_element_type=F32)


def patch_order():
    matrix = np.zeros((8 * GRID, 8 * GRID), np.float32)
    for p in range(4):
        for a in range(4):
            for b in range(KV):
                matrix[p * 96 + a * KV + b, (2 * a + p // 2) * GRID + 2 * b + p % 2] = 1.0
    return matrix


def fold_rows(x):
    return jnp.sum(x.reshape(x.shape[0] // 8, 8, x.shape[1]), axis=0)


def norm_columns(x):
    scale = 1.0 / x.shape[0]
    centred = x - jnp.sum(x, axis=0, keepdims=True) * scale
    rstd = lax.rsqrt(jnp.sum(centred * centred, axis=0, keepdims=True) * scale + 1e-06)
    return centred * rstd, rstd


def norm_columns_back(normed, rstd, scaled):
    scale = 1.0 / scaled.shape[0]
    plain = jnp.sum(scaled, axis=0, keepdims=True) * scale
    mixed = jnp.sum(scaled * normed, axis=0, keepdims=True) * scale
    return rstd * (scaled - plain - normed * mixed)


def norm_rows(x):
    centred = x - jnp.mean(x, axis=-1, keepdims=True)
    rstd = lax.rsqrt(jnp.mean(centred * centred, axis=-1, keepdims=True) + 1e-06)
    return centred * rstd, rstd


def norm_rows_back(normed, rstd, scaled):
    plain = jnp.mean(scaled, axis=-1, keepdims=True)
    mixed = jnp.mean(scaled * normed, axis=-1, keepdims=True)
    return rstd * (scaled - plain - normed * mixed)


def first_row(row, rows=EXT):
    index = lax.broadcasted_iota(jnp.int32, (rows, row.shape[-1]), 0)
    return jnp.where(index == 0, row, 0.0)


def three_parts(x):
    high = x.astype(BF).astype(F32)
    middle = (x - high).astype(BF).astype(F32)
    return high, middle, (x - high - middle).astype(BF).astype(F32)


def whole(x):
    zeros = (0,) * len(x.shape)
    return pl.BlockSpec(x.shape, lambda *_: zeros)


def per_image(x, **kwargs):
    zeros = (0,) * (len(x.shape) - 1)
    return pl.BlockSpec((1,) + tuple(x.shape[1:]), lambda i, *_: (i,) + zeros, **kwargs)


def key_columns(ref, side, h_range, ones_from, ones_to, with_mask):
    lane = lax.broadcasted_iota(jnp.int32, (KV, 64), 1)
    cell = lax.broadcasted_iota(jnp.int32, (KV, 64), 0)
    ones = jnp.where((lane >= ones_from) & (lane <= ones_to), 1.0, 0.0)
    for a in range(KV):
        block = ones
        if with_mask:
            bias = jnp.where((cell < side) & (a < side), 0.0, -1e30)
            block = jnp.where(lane == 0, bias, ones)
        block = block.astype(BF)
        for h in h_range:
            ref[h, a * KV : (a + 1) * KV, 64:128] = block


def attention_forward_kernel(
    sides, images, mask, perm, vec, rows, wqt, wr, wk, wvt, wot,
    pre, patches, reduced, memory, mixed, lse, middle, post,
    key_ref, value_ref,
):
    i = pl.program_id(0)
    width = images.shape[1]

    def first_norm(t, _):
        for u in range(3):
            at = pl.ds(pl.multiple_of(t * 384 + u * 128, 128), 128)
            x = images[0, :, at].astype(F32) * mask[0, 0:1, at]
            normed, _unused = norm_columns(x)
            pre[0, 0:width, at] = (normed * vec[0] + vec[1]).astype(BF)
            pre[0, width : width + EXT, at] = first_row(jnp.ones((1, 128), F32)).astype(BF)
        return 0

    lax.fori_loop(0, TOKENS // 384, first_norm, 0)
    for t in range(TOKENS // 384):
        picked = mm(perm[...], pre[0, 0:width, t * 384 : (t + 1) * 384], NT).astype(BF)
        for p in range(4):
            patches[0, p, t * 96 : (t + 1) * 96, :] = picked[p * 96 : (p + 1) * 96]

    total = rows[0:1, :]
    for p in range(4):
        total = total + mm(patches[0, p], wr[p])
    reduced[0] = total
    normed, _unused = norm_rows(total)
    memory[0, :, 0:width] = (normed * rows[1:2, :] + rows[2:3, :]).astype(BF)
    lane = lax.broadcasted_iota(jnp.int32, (KEYS, 64), 1)
    memory[0, :, width : width + 64] = jnp.where(lane == 0, 1.0, 0.0).astype(BF)
    keys = mm(memory[0, :, 0:width], wk[...]).astype(BF)
    key_columns(key_ref, sides[i], range(HEADS), 1, 0, True)
    values = mm(wvt[...], memory[0], NT).astype(BF)
    ones = first_row(jnp.ones((1, KEYS), F32)).astype(BF)
    for h in range(HEADS):
        at = slice(h * HEAD_DIM, (h + 1) * HEAD_DIM)
        key_ref[h, :, 0:HEAD_DIM] = keys[:, at]
        value_ref[h, 0:HEAD_DIM, :] = values[at]
        value_ref[h, HEAD_DIM : HEAD_DIM + EXT, :] = ones
    mixed[0, width : width + EXT, :] = first_row(jnp.ones((1, TOKENS), F32)).astype(BF)
    queries = (mm(wqt[...], pre[0]) * QUERY_SCALE).astype(BF)
    tail = first_row(jnp.ones((1, TOKENS), F32), 64).astype(BF)
    for h in range(HEADS):
        at = slice(h * HEAD_DIM, (h + 1) * HEAD_DIM)
        scores = mm(key_ref[h], jnp.concatenate([queries[at], tail], axis=0))
        top = jnp.max(scores, axis=0, keepdims=True)
        weights = jnp.exp2(scores - top).astype(BF)
        out = mm(value_ref[h], weights)
        total = out[HEAD_DIM : HEAD_DIM + 1]
        mixed[0, at, :] = (out[0:HEAD_DIM] * (1.0 / total)).astype(BF)
        lse[0, h : h + 1, :] = top + jnp.log2(total)

    middle[0] = mm(wot[...], mixed[0])

    def second_norm(t, _):
        for u in range(3):
            at = pl.ds(pl.multiple_of(t * 384 + u * 128, 128), 128)
            here = mask[0, 0:1, at]
            x = images[0, :, at].astype(F32) * here + middle[0, :, at]
            middle[0, :, at] = x
            normed, _unused = norm_columns(x)
            post[0, 0:width, at] = ((normed * vec[2] + vec[3]) * here).astype(BF)
            post[0, width : width + EXT, at] = first_row(here).astype(BF)
        return 0

    lax.fori_loop(0, TOKENS // 384, second_norm, 0)


def attention_forward(sides, images, mask, perm, vec, rows, wqt, wr, wk, wvt, wot):
    n, width, tokens = images.shape
    shape = jax.ShapeDtypeStruct
    outs = [
        shape((n, width + EXT, tokens), BF),
        shape((n, 4, KEYS, width), BF),
        shape((n, KEYS, width), F32),
        shape((n, KEYS, width + 64), BF),
        shape((n, width + EXT, tokens), BF),
        shape((n, 8, tokens), F32),
        shape((n, width, tokens), F32),
        shape((n, width + EXT, tokens), BF),
    ]
    weights = (perm, vec, rows, wqt, wr, wk, wvt, wot)
    return pl.pallas_call(
        attention_forward_kernel,
        grid_spec=pltpu.PrefetchScalarGridSpec(
            num_scalar_prefetch=1,
            grid=(n,),
            in_specs=[per_image(images), per_image(mask)] + [whole(x) for x in weights],
            out_specs=[per_image(x) for x in outs],
            scratch_shapes=[
                pltpu.VMEM((HEADS, KEYS, 128), BF),
                pltpu.VMEM((HEADS, HEAD_DIM + EXT, KEYS), BF),
            ],
        ),
        out_shape=outs,
        compiler_params=pltpu.CompilerParams(vmem_limit_bytes=VMEM_BYTES),
        name="attention_forward",
    )(sides, images, mask, *weights)


def feed_forward_kernel(
    post_next, cot_next, mask_next, we_next, wst_next, taps,
    post, cot, mask, middle, we, wst, vec,
    output, grad_post, gwe, gwst, gtaps, gbias,
    padded_0, padded_1, grad_padded, grad_act, act_0, act_1, grad_exp_0, grad_exp_1,
    post_rows, out_grad_rows, out_grad, total,
):
    s = pl.program_id(0)
    last = pl.num_programs(0) - 1
    width, block = cot.shape[1], wst.shape[1]
    blocks = gwst.shape[1] // block
    halves = block // 128
    rows = 16
    chunks = GRID // rows
    span = rows * GRID
    js = pl.ds(pl.multiple_of(lax.rem(s, blocks) * block, block), block)
    js_done = pl.ds(pl.multiple_of(lax.rem(jnp.maximum(s - 1, 0), blocks) * block, block), block)

    def tokens(t):
        return pl.ds(pl.multiple_of(t * span, span), span)

    def expand(t, padded, we, wst):
        at = tokens(t)
        filled = mm(post_rows[at, :], we[...])
        for h in range(halves):
            for r in range(rows):
                start = pl.multiple_of((t * rows + r + 1) * PITCH + 8, 8)
                padded[h, pl.ds(start, GRID), :] = filled[r * GRID : (r + 1) * GRID, h * 128 : (h + 1) * 128]
        grad_act[at, :] = mm(out_grad_rows[at, :], wst[...])

    def finish(t, act, grad_exp):
        at = tokens(t)
        total[:, at] += mm(wst[0:width, :], act[at, :], NT)
        grad_post[0, :, at] += mm(we[0:width, :], grad_exp[at, :], NT)
        gwst[:, js_done] += mm(out_grad[:, at], act[at, :])
        gwe[:, js_done] += mm(post[0, :, at], grad_exp[at, :])

    def convolve(t, padded, act):
        for h in range(halves):
            hs = slice(h * 128, (h + 1) * 128)
            w = [jnp.broadcast_to(0.5 * taps[k : k + 1, hs], (GRID, 128)).astype(BF) for k in range(10)]
            sums = jnp.zeros((8, 128), F32)
            open_rows = {}
            for q in range(-1, rows + 1):
                base = (t * rows + q + 1) * PITCH + 8
                x = [padded[h, pl.ds(base + d, GRID), :].astype(BF) for d in (-1, 0, 1)]
                for a in (2, 1, 0):
                    r = q + 1 - a
                    if 0 <= r < rows:
                        part = w[3 * a] * x[0] + w[3 * a + 1] * x[1] + w[3 * a + 2] * x[2]
                        open_rows[r] = part + open_rows.get(r, w[9])
                r = q - 1
                if r < 0:
                    continue
                at = pl.ds(pl.multiple_of((t * rows + r) * GRID, GRID), GRID)
                gelu, slope = gelu_pair(open_rows.pop(r))
                act[at, hs] = gelu
                grad = (grad_act[at, hs].astype(BF) * slope).astype(F32)
                start = pl.multiple_of((t * rows + r + 1) * PITCH + 8, 8)
                grad_padded[h, pl.ds(start, GRID), :] = grad
                sums = sums + fold_rows(grad)
            cols = pl.ds(pl.multiple_of(lax.rem(s, blocks) * block + h * 128, 128), 128)
            gtaps[72:80, cols] += sums

    def convolve_back(t, padded, grad_exp):
        for h in range(halves):
            hs = slice(h * 128, (h + 1) * 128)
            w = [jnp.broadcast_to(taps[k : k + 1, hs], (GRID, 128)).astype(BF) for k in range(9)]
            sums = [jnp.zeros((8, 128), F32) for _ in range(9)]
            waiting = {}
            open_rows = {}
            x = {}
            for q in range(-1, rows + 1):
                base = (t * rows + q + 1) * PITCH + 8
                grads = [grad_padded[h, pl.ds(base + 1 - b, GRID), :].astype(BF) for b in range(3)]
                if q + 1 < rows:
                    start = pl.multiple_of((t * rows + q + 2) * PITCH + 8, 8)
                    x[q + 1] = padded[h, pl.ds(start, GRID), :].astype(BF)
                for a in range(3):
                    r = q + a - 1
                    if not 0 <= r < rows:
                        continue
                    part = w[3 * a] * grads[0] + w[3 * a + 1] * grads[1] + w[3 * a + 2] * grads[2]
                    open_rows[r] = part + open_rows[r] if r in open_rows else part
                    for b in range(3):
                        k = 3 * a + b
                        product = x[r] * grads[b]
                        product = product[0:16] + product[16:32] + product[32:48]
                        waiting[k] = waiting[k] + product if k in waiting else product
                        if r % 4 == 3:
                            product = waiting.pop(k).astype(F32)
                            sums[k] = sums[k] + product[0:8] + product[8:16]
                r = q - 1
                if r >= 0:
                    at = pl.ds(pl.multiple_of((t * rows + r) * GRID, GRID), GRID)
                    grad_exp[at, hs] = open_rows.pop(r)
                    x.pop(r)
            cols = pl.ds(pl.multiple_of(lax.rem(s, blocks) * block + h * 128, 128), 128)
            for k in range(9):
                gtaps[8 * k : 8 * k + 8, cols] += sums[k]

    @pl.when(s == 0)
    def _():
        for ref in (act_1, grad_exp_1, out_grad, gwe, gwst, gtaps, gbias):
            ref[...] = jnp.zeros_like(ref)
        for ref in (post_rows, out_grad_rows):
            ref[:, 256:DEPTH] = jnp.zeros((TOKENS, DEPTH - 256), BF)
        for ref in (padded_0, padded_1, grad_padded):
            for h in range(halves):
                ref[h, 0 : PITCH + 8, :] = jnp.zeros((PITCH + 8, 128), F32)
                ref[h, (GRID + 1) * PITCH :, :] = jnp.zeros((PITCH + 8, 128), F32)
                for r in range(1, GRID):
                    ref[h, (r + 1) * PITCH : (r + 1) * PITCH + 8, :] = jnp.zeros((8, 128), F32)

    @pl.when((s == 0) | ((lax.rem(s + 1, blocks) == 0) & (s + 1 < last)))
    def _():
        for t in range(TOKENS // 384):
            at = slice(t * 384, (t + 1) * 384)
            grad = cot_next[0, :, at].astype(F32) * mask_next[0, 0:1, at]
            gbias[...] += grad[:, 0:128] + grad[:, 128:256] + grad[:, 256:384]
            out_grad_rows[at, 0:width] = (0.5 * grad).astype(BF).T
            post_rows[at, 0 : width + EXT] = post_next[0, :, at].T

    @pl.when(lax.rem(s, blocks) == min(1, blocks - 1))
    def _():
        for t in range(TOKENS // 384):
            at = slice(t * 384, (t + 1) * 384)
            out_grad[:, at] = (cot[0, :, at].astype(F32) * mask[0, 0:1, at]).astype(BF)

    @pl.when((s == 0) | (lax.rem(s, blocks) == min(1, blocks - 1)))
    def _():
        total[...] = jnp.zeros_like(total)
        grad_post[...] = jnp.zeros_like(grad_post)

    @pl.when(s == 0)
    def _():
        def first(t, _):
            expand(t, padded_0, we, wst)
            return 0

        lax.fori_loop(0, chunks, first, 0)

    def work(padded, padded_next, act, act_done, grad_exp, grad_exp_done):
        def forward(t, _):
            finish(t, act_done, grad_exp_done)
            convolve(t, padded, act)
            return 0

        def backward(t, _):
            expand(t, padded_next, we_next, wst_next)
            convolve_back(t, padded, grad_exp)
            return 0

        lax.fori_loop(0, chunks, forward, 0)
        lax.fori_loop(0, chunks, backward, 0)

    @pl.when((s < last) & (lax.rem(s, 2) == 0))
    def _():
        work(padded_0, padded_1, act_0, act_1, grad_exp_0, grad_exp_1)

    @pl.when((s < last) & (lax.rem(s, 2) == 1))
    def _():
        work(padded_1, padded_0, act_1, act_0, grad_exp_1, grad_exp_0)

    @pl.when(s == last)
    def _():
        def rest(t, _):
            @pl.when(lax.rem(s, 2) == 0)
            def _():
                finish(t, act_1, grad_exp_1)

            @pl.when(lax.rem(s, 2) == 1)
            def _():
                finish(t, act_0, grad_exp_0)

            return 0

        lax.fori_loop(0, chunks, rest, 0)

    @pl.when((s > 0) & (lax.rem(s, blocks) == 0))
    def _():
        for t in range(TOKENS // 128):
            at = slice(t * 128, (t + 1) * 128)
            output[0, :, at] = ((middle[0, :, at] + total[:, at] + vec[4]) * mask[0, 0:1, at]).astype(BF)


def gelu_pair(half):
    kind = half.dtype.type
    square = half * half
    upper = jnp.tanh(half * (kind(8.0 * GELU_B) * square + kind(2.0 * GELU_A))) + kind(1.0)
    gelu = half * upper
    return gelu, upper + gelu * (kind(2.0) - upper) * (kind(24.0 * GELU_B) * square + kind(2.0 * GELU_A))


def feed_forward(post, cot, mask, middle, we, wst, taps, vec, block=256):
    n, width, tokens = cot.shape
    hidden = wst.shape[1]
    blocks = hidden // block
    count = n * blocks
    shape = jax.ShapeDtypeStruct
    outs = [
        shape((n, width, tokens), BF),
        shape((n, width, tokens), F32),
        shape((width + EXT, hidden), F32),
        shape((width, hidden), F32),
        shape((80, hidden), F32),
        shape((width, 128), F32),
    ]

    def ahead(s):
        return jnp.minimum(s + 1, count - 1)

    def behind(s):
        return jnp.maximum(s - 1, 0)

    def image(x, step):
        zeros = (0,) * (len(x.shape) - 1)
        return pl.BlockSpec((1,) + tuple(x.shape[1:]), lambda s: (step(s) // blocks,) + zeros)

    def columns(x, step):
        return pl.BlockSpec((x.shape[0], block), lambda s: (0, lax.rem(step(s), blocks)))

    return pl.pallas_call(
        feed_forward_kernel,
        grid=(count + 1,),
        in_specs=[image(x, ahead) for x in (post, cot, mask)]
        + [columns(we, ahead), columns(wst, ahead), columns(taps, lambda s: jnp.minimum(s, count - 1))]
        + [image(x, behind) for x in (post, cot, mask, middle)]
        + [columns(we, behind), columns(wst, behind), whole(vec)],
        out_specs=[image(x, behind) for x in outs[:2]] + [whole(x) for x in outs[2:]],
        out_shape=outs,
        scratch_shapes=[pltpu.VMEM((block // 128, (GRID + 2) * PITCH + 8, 128), F32)] * 3
        + [pltpu.VMEM((tokens, block), F32)]
        + [pltpu.VMEM((tokens, block), BF)] * 4
        + [
            pltpu.VMEM((tokens, DEPTH), BF),
            pltpu.VMEM((tokens, DEPTH), BF),
            pltpu.VMEM((width, tokens), BF),
            pltpu.VMEM((width, tokens), F32),
        ],
        compiler_params=pltpu.CompilerParams(vmem_limit_bytes=VMEM_BYTES),
        name="feed_forward",
    )(post, cot, mask, we, wst, taps, post, cot, mask, middle, we, wst, vec)


def attention_backward_kernel(
    sides, images, cot, mask, pre, patches, reduced, memory, mixed, lse, middle, grad_post,
    perm, vec, rows, wq, wqt, wr, wk, wv, wvt, wo,
    grad_images, gwo, gwq, gpair, gwr, gcols, grows,
    branch, grad_mixed, queries, grad_queries, key_ref, value_ref, keys_t, grad_keys, grad_values, grad_patches,
):
    i = pl.program_id(0)
    width = images.shape[1]

    @pl.when(i == 0)
    def _():
        for ref in (gwo, gwq, gpair, gwr, gcols, grows):
            ref[...] = jnp.zeros_like(ref)

    def mlp_norm_back(t, _):
        gain = shift = jnp.zeros((width, 128), F32)
        for u in range(3):
            at = pl.ds(pl.multiple_of(t * 384 + u * 128, 128), 128)
            here = mask[0, 0:1, at]
            normed, rstd = norm_columns(middle[0, :, at])
            grad = grad_post[0, :, at] * here
            gain = gain + grad * normed
            shift = shift + grad
            grad = cot[0, :, at].astype(F32) * here + norm_columns_back(normed, rstd, grad * vec[2])
            grad_images[0, :, at] = grad
            branch[:, at] = grad.astype(BF)
        gcols[2] += gain
        gcols[3] += shift
        return 0

    lax.fori_loop(0, TOKENS // 384, mlp_norm_back, 0)
    gwo[...] += mm(mixed[0], branch[...], NT)
    grad_mixed[...] = mm(wo[...], branch[...]).astype(BF)
    queries[...] = (mm(wqt[...], pre[0]) * QUERY_SCALE).astype(BF)
    keys = mm(memory[0, :, 0:width], wk[...]).astype(BF)
    keys_t[...] = keys.T
    values = mm(wvt[...], memory[0], NT).astype(BF).T
    key_columns(key_ref, sides[i], range(HEADS), 1, 3, True)
    key_columns(value_ref, sides[i], range(HEADS), 1, 3, False)
    for h in range(HEADS):
        at = slice(h * HEAD_DIM, (h + 1) * HEAD_DIM)
        key_ref[h, :, 0:HEAD_DIM] = keys[:, at]
        value_ref[h, :, 0:HEAD_DIM] = values[:, at]

    span = TOKENS // 3
    index = lax.broadcasted_iota(jnp.int32, (64, span), 0)
    grad_values[...] = jnp.zeros_like(grad_values)
    grad_keys[...] = jnp.zeros_like(grad_keys)

    def part(t, _):
        at = pl.ds(pl.multiple_of(t * span, 128), span)
        for h in range(HEADS):
            hs = slice(h * HEAD_DIM, (h + 1) * HEAD_DIM)
            one, two, three = three_parts(-lse[0, h : h + 1, at])
            tail = jnp.where(index == 2, two, jnp.where(index == 3, three, 0.0))
            tail = jnp.where(index == 0, 1.0, jnp.where(index == 1, one, tail)).astype(BF)
            query = queries[hs, at]
            attend = jnp.exp2(mm(key_ref[h], jnp.concatenate([query, tail], axis=0)))
            low = attend.astype(BF)
            grad = grad_mixed[hs, at]
            inner = grad.astype(F32) * mixed[0, hs, at].astype(F32)
            one, two, three = three_parts(-jnp.sum(inner, axis=0, keepdims=True))
            tail = jnp.where(index == 2, two, jnp.where(index == 3, three, 0.0))
            tail = jnp.where(index == 1, one, tail).astype(BF)
            grad_attend = mm(value_ref[h], jnp.concatenate([grad, tail], axis=0))
            grad_scores = (attend * grad_attend).astype(BF)
            grad_values[hs, :] += mm(grad, low, NT)
            grad_keys[hs, :] += mm(query, grad_scores, NT) * (1.0 / LOG2E)
            grad_queries[hs, at] = (mm(keys_t[hs, :], grad_scores) * HEAD_DIM**-0.5).astype(BF)
        return 0

    lax.fori_loop(0, TOKENS // span, part, 0)

    low_keys = grad_keys[...].astype(BF)
    low_values = grad_values[...].astype(BF)
    gpair[0:width, :] += mm(low_keys, memory[0])
    gpair[width : 2 * width, :] += mm(low_values, memory[0])
    grad_memory = mm(low_keys.T, wk[...], NT) + mm(low_values.T, wv[...], NT)
    normed, rstd = norm_rows(reduced[0])
    grows[8:16, :] += fold_rows(grad_memory * normed)
    grows[16:24, :] += fold_rows(grad_memory)
    grad_reduced = norm_rows_back(normed, rstd, grad_memory * rows[1:2, :]).astype(BF)
    grows[0:8, :] += fold_rows(grad_reduced.astype(F32))
    grad_reduced_t = grad_reduced.T
    for p in range(4):
        gwr[p] += mm(grad_reduced_t, patches[0, p])
        grad_patches[p] = mm(grad_reduced, wr[p], NT).astype(BF)
    gwq[...] += mm(pre[0], grad_queries[...], NT)

    def pre_norm_back(t, _):
        at = pl.ds(pl.multiple_of(t * 384, 128), 384)
        grad_pre = mm(wq[...], grad_queries[:, at])
        start = pl.ds(pl.multiple_of(t * 96, 32), 96)
        picked = jnp.concatenate([grad_patches[p, start, :] for p in range(4)], axis=0)
        grad_pre = grad_pre + mm(picked.T, perm[...])
        gain = shift = jnp.zeros((width, 128), F32)
        for u in range(3):
            at = pl.ds(pl.multiple_of(t * 384 + u * 128, 128), 128)
            here = mask[0, 0:1, at]
            normed, rstd = norm_columns(images[0, :, at].astype(F32) * here)
            grad = grad_pre[:, u * 128 : (u + 1) * 128]
            gain = gain + grad * normed
            shift = shift + grad
            back = norm_columns_back(normed, rstd, grad * vec[0])
            grad_images[0, :, at] = (grad_images[0, :, at] + back) * here
        gcols[0] += gain
        gcols[1] += shift
        return 0

    lax.fori_loop(0, TOKENS // 384, pre_norm_back, 0)


def attention_backward(
    sides, images, cot, mask, pre, patches, reduced, memory, mixed, lse, middle, grad_post,
    perm, vec, rows, wq, wqt, wr, wk, wv, wvt, wo,
):
    n, width, tokens = images.shape
    shape = jax.ShapeDtypeStruct
    outs = [
        shape((n, width, tokens), F32),
        shape((width + EXT, width), F32),
        shape((width + EXT, width), F32),
        shape((2 * width, width + 64), F32),
        shape((4, width, width), F32),
        shape((4, width, 128), F32),
        shape((24, width), F32),
    ]
    one = {"pipeline_mode": pl.Buffered(1)}
    inputs = (images, cot, mask, pre, patches, reduced, memory, mixed, lse)
    weights = (perm, vec, rows, wq, wqt, wr, wk, wv, wvt, wo)
    return pl.pallas_call(
        attention_backward_kernel,
        grid_spec=pltpu.PrefetchScalarGridSpec(
            num_scalar_prefetch=1,
            grid=(n,),
            in_specs=[per_image(x) for x in inputs]
            + [per_image(middle, **one), per_image(grad_post, **one)]
            + [whole(x) for x in weights],
            out_specs=[per_image(outs[0], **one)] + [whole(x) for x in outs[1:]],
            scratch_shapes=[
                pltpu.VMEM((width, tokens), BF),
                pltpu.VMEM((width, tokens), BF),
                pltpu.VMEM((width, tokens), BF),
                pltpu.VMEM((width, tokens), BF),
                pltpu.VMEM((HEADS, KEYS, 128), BF),
                pltpu.VMEM((HEADS, KEYS, 128), BF),
                pltpu.VMEM((width, KEYS), BF),
                pltpu.VMEM((width, KEYS), F32),
                pltpu.VMEM((width, KEYS), F32),
                pltpu.VMEM((4, KEYS, width), BF),
            ],
        ),
        out_shape=outs,
        compiler_params=pltpu.CompilerParams(vmem_limit_bytes=VMEM_BYTES),
        name="attention_backward",
    )(sides, *inputs, middle, grad_post, *weights)

MESH = pl.DeviceIdType.MESH


class Place:
    def __init__(self):
        self.dp = lax.axis_index("dp")
        self.fsdp = lax.axis_index("fsdp")
        self.y, self.x = self.dp // 2, self.dp % 2
        self.z, self.core = self.fsdp // 2, self.fsdp % 2
        self.other_core = 1 - self.core
        self.beside_x = (self.dp + 1 - 2 * self.x, self.fsdp)
        self.beside_y = (self.dp + 2 - 4 * self.y, self.fsdp)
        self.across = (3 - self.dp, self.fsdp)
        self.beside_core = (self.dp, self.fsdp + 1 - 2 * self.core)
        self.others = (self.z + 1 - 2 * (self.z % 2), 2 - self.z // 2, 3 * (1 - self.z // 2))

    def at_z(self, z):
        return (self.dp, z * 2 + self.core)

    def along_z(self, k):
        return self.at_z((self.z + k) % 4)

    def call(self, partners):
        barrier = pltpu.get_barrier_semaphore()
        for device in partners:
            pl.semaphore_signal(barrier, inc=1, device_id=device, device_id_type=MESH)

    def answer(self, count):
        pl.semaphore_wait(pltpu.get_barrier_semaphore(), count)


class Sender:
    def __init__(self, send, recv):
        self.send, self.recv, self.started = send, recv, []

    def __call__(self, source, target, device, recv=None):
        k = len(self.started)
        copy = pltpu.make_async_remote_copy(
            src_ref=source,
            dst_ref=target,
            send_sem=self.send.at[k],
            recv_sem=self.recv.at[k] if recv is None else recv,
            device_id=device,
            device_id_type=MESH,
        )
        copy.start()
        self.started.append(copy)
        return copy

    def finish(self):
        for copy in self.started:
            copy.wait_send()


def gather_kernel(slot_rows, bases, own, *refs):
    outs, (slots, wide, line, own_sem, send_sem, recv_sem, z_sem) = refs[:13], refs[13:]
    me = Place()
    half = own.shape[0] // 2
    first, second = pl.ds(0, half), pl.ds(half, half)
    send = Sender(send_sem, recv_sem)
    copy = pltpu.make_async_copy(own, slots.at[me.core, me.dp, me.z], own_sem)
    copy.start()
    me.call([me.beside_core, me.beside_x, me.beside_y] + [me.at_z(z) for z in me.others])
    me.answer(6)
    own_slot = slots.at[me.core, me.dp, me.z]

    def send_z(j):
        return send(own, own_slot, me.at_z(me.others[j]), z_sem.at[me.z])

    send_z(0)
    x_copies = [send(own, own_slot, me.beside_x)]
    y_copies = [send(own, own_slot, me.beside_y)]
    core_copies = [(send(own, own_slot, me.beside_core), me.dp, me.z)]
    send_z(1)
    half_copies = []
    order = (me.z,) + me.others

    def open_slot(core, dp, z):
        spread_slot(slots[core, dp, z], (dp * 8 + z * 2 + core), slot_rows, line, wide)

    def forward(k):
        z = order[k]
        x_copies[k].wait_recv()
        slot = slots.at[me.core, me.beside_x[0], z]
        half_copies.append(send(slot.at[first], slot.at[first], me.beside_y))
        core_copies.append((send(slot, slot, me.beside_core), me.beside_x[0], z))
        y_copies[k].wait_recv()
        slot = slots.at[me.core, me.beside_y[0], z]
        half_copies.append(send(slot.at[second], slot.at[second], me.beside_x))
        core_copies.append((send(slot, slot, me.beside_core), me.beside_y[0], z))
        open_slot(me.core, me.beside_x[0], z)
        open_slot(me.core, me.beside_y[0], z)

    copy.wait()
    open_slot(me.core, me.dp, me.z)
    forward(0)
    for k in (1, 2, 3):
        z = order[k]
        slot = slots.at[me.core, me.dp, z]
        pltpu.make_async_remote_copy(
            src_ref=own,
            dst_ref=slot,
            send_sem=send_sem.at[0],
            recv_sem=z_sem.at[z],
            device_id=me.at_z(z),
            device_id_type=MESH,
        ).wait_recv()
        x_copies.append(send(slot, slot, me.beside_x))
        y_copies.append(send(slot, slot, me.beside_y))
        core_copies.append((send(slot, slot, me.beside_core), me.dp, z))
        if k == 1:
            send_z(2)
        open_slot(me.core, me.dp, z)
        forward(k)
    for k in range(4):
        half_copies[2 * k].wait_recv()
        half_copies[2 * k + 1].wait_recv()
        slot = slots.at[me.core, me.across[0], order[k]]
        core_copies.append((send(slot, slot, me.beside_core), me.across[0], order[k]))
        open_slot(me.core, me.across[0], order[k])
    for copied, dp, z in core_copies:
        copied.wait_recv()
        open_slot(me.other_core, dp, z)
    send.finish()
    write_weights(bases, wide, *outs)


def gather_weights(own, slot_rows, width):
    bases, count = row_bases(width, 4 * width)
    outs = weight_shapes(width)
    copies = 35
    values = pl.pallas_call(
        partial(gather_kernel, slot_rows, bases),
        out_shape=list(outs.values()),
        in_specs=[pl.BlockSpec(memory_space=pltpu.VMEM)],
        out_specs=[pl.BlockSpec(memory_space=pltpu.VMEM)] * len(outs),
        scratch_shapes=[
            pltpu.VMEM((2, 4, 4) + own.shape, BF),
            pltpu.VMEM((3, -(-32 * slot_rows * 128 // width // 8) * 8 + 8, 128), F32),
            pltpu.VMEM(own.shape, F32),
            pltpu.SemaphoreType.DMA(()),
            pltpu.SemaphoreType.DMA((copies,)),
            pltpu.SemaphoreType.DMA((copies,)),
            pltpu.SemaphoreType.DMA((4,)),
        ],
        compiler_params=pltpu.CompilerParams(
            collective_id=0, has_side_effects=True, vmem_limit_bytes=VMEM_BYTES
        ),
        name="gather_weights",
    )(own)
    return dict(zip(outs, values, strict=True))


def reduce_kernel(slot_rows, bases, *refs):
    grads, (shard, squares) = refs[:10], refs[10:12]
    wide, line, own, core_out, core_in, y_in, x_in, x_last, y_last, z_in, small, send_sem, recv_sem = refs[12:]
    me = Place()
    rows = shard.shape[0]
    half = rows // 2
    first, second = pl.ds(0, half), pl.ds(half, half)
    send = Sender(send_sem, recv_sem)
    peers = [(me.dp, (me.z + k) % 4 * 2 + core) for k in range(4) for core in (me.core, me.other_core)][1:]
    planes = [me.beside_x, me.beside_y, me.across]
    me.call(peers + planes)
    collect_gradients(bases, wide, *grads)
    line[...] = jnp.zeros_like(line)
    me.answer(len(peers + planes))
    units = [(me.z + k) % 4 for k in (2, 1, 3, 0)]
    core_copies, y_copies, x_copies, last = [], [], [], []
    other_x, other_y = 1 - me.x, 1 - me.y

    def give(k):
        z = units[k]
        for dp in range(4):
            join_slot(wide, dp * 8 + z * 2 + me.other_core, slot_rows, line)
            core_out[z, dp] = line[...].astype(BF)
        core_copies.append(send(core_out.at[z], core_in.at[z], me.beside_core))
        for dp in range(4):
            join_slot(wide, dp * 8 + z * 2 + me.core, slot_rows, line)
            own[z, dp] = line[...]

    def cores(k):
        z = units[k]
        core_copies[k].wait_recv()
        for dp in range(4):
            core_in[z, dp] = (core_in[z, dp].astype(F32) + own[z, dp]).astype(BF)
        y_copies.append(
            [send(core_in.at[z, 2 * other_y + x, first], y_in.at[z, x], me.beside_y) for x in range(2)]
        )
        x_copies.append(
            [send(core_in.at[z, 2 * y + other_x, second], x_in.at[z, y], me.beside_x) for y in range(2)]
        )

    def plane(k):
        z = units[k]
        for copied in y_copies[k]:
            copied.wait_recv()
        y_in[z, other_x] = (
            y_in[z, other_x].astype(F32) + core_in[z, 2 * me.y + other_x, first].astype(F32)
        ).astype(BF)
        to_x = send(y_in.at[z, other_x], x_last.at[z], me.beside_x)
        for copied in x_copies[k]:
            copied.wait_recv()
        x_in[z, other_y] = (
            x_in[z, other_y].astype(F32) + core_in[z, 2 * other_y + me.x, second].astype(F32)
        ).astype(BF)
        last.append((to_x, send(x_in.at[z, other_y], y_last.at[z], me.beside_y)))

    z_copies = []

    def column(k):
        z = units[k]
        for copied in last[k]:
            copied.wait_recv()
        low = y_in[z, me.x].astype(F32) + core_in[z, me.dp, first].astype(F32) + x_last[z].astype(F32)
        high = x_in[z, me.y].astype(F32) + core_in[z, me.dp, second].astype(F32) + y_last[z].astype(F32)
        if k == 3:
            shard[first, :] = low
            shard[second, :] = high
        else:
            z_in[k, first] = low.astype(BF)
            z_in[k, second] = high.astype(BF)
            z_copies.append(send(z_in.at[k], z_in.at[k + 3], me.at_z(z)))

    give(0)
    give(1)
    cores(0)
    give(2)
    cores(1)
    plane(0)
    give(3)
    cores(2)
    plane(1)
    column(0)
    cores(3)
    plane(2)
    column(1)
    plane(3)
    column(2)
    column(3)
    for k in (0, 1, 2):
        z_copies[k].wait_recv()
        shard[...] += z_in[k + 3].astype(F32)
    total = shard[0:8, :] * shard[0:8, :]
    for k in range(1, rows // 8):
        part = shard[8 * k : 8 * k + 8, :]
        total = total + part * part
    small[0] = total
    small[2 + me.fsdp] = total
    copies = [send(small.at[0], small.at[2 + me.fsdp], device) for device in peers]
    for copied in copies:
        copied.wait_recv()
    total = small[2]
    for k in range(1, 8):
        total = total + small[2 + k]
    small[1] = total
    small[10 + me.dp] = total
    copies = [send(small.at[1], small.at[10 + me.dp], device) for device in planes]
    for copied in copies:
        copied.wait_recv()
    squares[...] = ((small[10] + small[11]) + small[12]) + small[13]
    send.finish()


def reduce_gradients(grads, slot_rows, rows, width):
    bases, _ = row_bases(width, 4 * width)
    half = rows // 2
    count = 4 + 16 + 8 + 3 + 7 + 3
    return pl.pallas_call(
        partial(reduce_kernel, slot_rows, bases),
        out_shape=[jax.ShapeDtypeStruct((rows, 128), F32), jax.ShapeDtypeStruct((8, 128), F32)],
        in_specs=[pl.BlockSpec(memory_space=pltpu.VMEM)] * len(grads),
        out_specs=[pl.BlockSpec(memory_space=pltpu.VMEM)] * 2,
        scratch_shapes=[
            pltpu.VMEM((3, -(-32 * slot_rows * 128 // width // 8) * 8 + 8, 128), F32),
            pltpu.VMEM((rows, 128), F32),
            pltpu.VMEM((4, 4, rows, 128), F32),
            pltpu.VMEM((4, 4, rows, 128), BF),
            pltpu.VMEM((4, 4, rows, 128), BF),
            pltpu.VMEM((4, 2, half, 128), BF),
            pltpu.VMEM((4, 2, half, 128), BF),
            pltpu.VMEM((4, half, 128), BF),
            pltpu.VMEM((4, half, 128), BF),
            pltpu.VMEM((6, rows, 128), BF),
            pltpu.VMEM((14, 8, 128), F32),
            pltpu.SemaphoreType.DMA((count,)),
            pltpu.SemaphoreType.DMA((count,)),
        ],
        compiler_params=pltpu.CompilerParams(
            collective_id=1, has_side_effects=True, vmem_limit_bytes=VMEM_BYTES
        ),
        name="reduce_gradients",
    )(*grads)


def layout_shapes(model_width, hidden_width):
    return [
        ("pre_gain", (model_width,)),
        ("pre_shift", (model_width,)),
        ("query_weight", (model_width, model_width)),
        ("query_bias", (model_width,)),
        ("reduce_weight", (4 * model_width, model_width)),
        ("reduce_bias", (model_width,)),
        ("reduce_gain", (model_width,)),
        ("reduce_shift", (model_width,)),
        ("pair_weight", (model_width, 2 * model_width)),
        ("value_bias", (model_width,)),
        ("output_weight", (model_width, model_width)),
        ("output_bias", (model_width,)),
        ("mlp_gain", (model_width,)),
        ("mlp_shift", (model_width,)),
        ("expand_weight", (model_width, hidden_width)),
        ("expand_bias", (hidden_width,)),
        ("spatial_weight", (9, hidden_width)),
        ("spatial_bias", (hidden_width,)),
        ("shrink_weight", (hidden_width, model_width)),
        ("shrink_bias", (model_width,)),
    ]


def row_bases(width, hidden):
    bases = {}
    row = 0
    for name, shape in layout_shapes(width, hidden):
        bases[name] = row
        row += math.prod(shape) // width
    return bases, row


SPAN = 96


def regroup_lines(read, write, low):
    part = [read(k) for k in range(5)]
    turned = [pltpu.roll(part[k], 64, 1) for k in (2, 3, 4)]
    for k in range(3):
        write(0, k, part[k])
    write(1, 0, jnp.where(low, turned[0], turned[1]))
    write(1, 1, jnp.where(low, turned[1], turned[2]))
    write(1, 2, turned[2])


def spread_slot(values, slot, slot_rows, line, wide):
    pairs = slot_rows // 5
    line[...] = values.astype(F32)

    def part(start, count):
        low = lax.broadcasted_iota(jnp.int32, (count, 128), 1) < 64

        def write(parity, k, value):
            wide[k, pl.ds(slot * (2 * pairs) + 2 * start + parity, count, stride=2), :] = value

        regroup_lines(lambda k: line[pl.ds(5 * start + k, count, stride=5), :], write, low)

    part(0, pairs // 8 * 8)
    if pairs % 8:
        part(pairs // 8 * 8, pairs % 8)


def unpack_kernel(order, slot_rows, bases, slots, *refs):
    outs, (flat, wide) = refs[:13], refs[13:]
    for slot, place in enumerate(order):
        flat[pl.ds(slot * slot_rows, slots.shape[1]), :] = slots[place].astype(F32)
    low = lax.broadcasted_iota(jnp.int32, (SPAN, 128), 1) < 64

    def regroup(t, _):
        def write(parity, k, value):
            wide[k, pl.ds(t * (2 * SPAN) + parity, SPAN, stride=2), :] = value

        regroup_lines(lambda k: flat[pl.ds(t * (5 * SPAN) + k, SPAN, stride=5), :], write, low)
        return 0

    lax.fori_loop(0, wide.shape[1] // (2 * SPAN), regroup, 0)
    write_weights(bases, wide, *outs)


def write_weights(bases, wide, vec, rows, wq, wqt, wr, wk, wv, wvt, wo, wot, we, wst, taps):
    width = wq.shape[0]
    hidden = wst.shape[1]

    def take(base, count, stride=1):
        at = pl.ds(base, count, stride=stride) if stride > 1 else pl.ds(base, count)
        return jnp.concatenate([wide[0, at, :], wide[1, at, :], wide[2, at, :][:, 0 : width - 256]], axis=1)

    def take_hidden(base, count):
        return jnp.concatenate([take(base + q, count, hidden // width) for q in range(hidden // width)], axis=1)

    def bordered(weight, bias, extra):
        index = lax.broadcasted_iota(jnp.int32, (extra, weight.shape[1]), 0)
        return jnp.concatenate([weight, jnp.where(index == 0, bias, 0.0)], axis=0)

    names = ("pre_gain", "pre_shift", "mlp_gain", "mlp_shift", "shrink_bias")
    for k, name in enumerate(names):
        vec[k] = jnp.broadcast_to(take(bases[name], 1), (128, width)).T
    for k, name in enumerate(("reduce_bias", "reduce_gain", "reduce_shift")):
        rows[k : k + 1, :] = take(bases[name], 1)
    query = take(bases["query_weight"], width)
    wq[...] = query.astype(BF)
    wqt[...] = bordered(query, take(bases["query_bias"], 1), EXT).T.astype(BF)
    for p in range(4):
        wr[p] = take(bases["reduce_weight"] + p * width, width).astype(BF)
    wk[...] = take(bases["pair_weight"], width, 2).astype(BF)
    value = take(bases["pair_weight"] + 1, width, 2)
    wv[...] = value.astype(BF)
    wvt[...] = bordered(value, take(bases["value_bias"], 1), 64).T.astype(BF)
    out = take(bases["output_weight"], width)
    wo[...] = out.astype(BF)
    wot[...] = bordered(out, take(bases["output_bias"], 1), EXT).T.astype(BF)
    we[0:width, :] = take_hidden(bases["expand_weight"], width).astype(BF)
    we[width:DEPTH, :] = first_row(take_hidden(bases["expand_bias"], 1), DEPTH - width).astype(BF)
    taps[0:9, :] = take_hidden(bases["spatial_weight"], 9)
    taps[9:10, :] = take_hidden(bases["spatial_bias"], 1)
    wst[width:DEPTH, :] = jnp.zeros((DEPTH - width, hidden), BF)
    for k in range(hidden // 128):
        wst[0:width, 128 * k : 128 * k + 128] = take(bases["shrink_weight"] + 128 * k, 128).T.astype(BF)


def wide_rows(count):
    return -(-count // (2 * SPAN)) * 2 * SPAN


def weight_shapes(width):
    hidden = 4 * width
    shape = jax.ShapeDtypeStruct
    return dict(
        vec=shape((5, width, 128), F32),
        rows=shape((3, width), F32),
        wq=shape((width, width), BF),
        wqt=shape((width, width + EXT), BF),
        wr=shape((4, width, width), BF),
        wk=shape((width, width), BF),
        wv=shape((width, width), BF),
        wvt=shape((width, width + 64), BF),
        wo=shape((width, width), BF),
        wot=shape((width, width + EXT), BF),
        we=shape((DEPTH, hidden), BF),
        wst=shape((DEPTH, hidden), BF),
        taps=shape((10, hidden), F32),
    )


def unpack_weights(slots, order, slot_rows, width):
    bases, count = row_bases(width, 4 * width)
    outs = weight_shapes(width)
    flat_rows = max(len(order) * slot_rows, wide_rows(count) * width // 128) + slots.shape[1]
    values = pl.pallas_call(
        partial(unpack_kernel, order, slot_rows, bases),
        out_shape=list(outs.values()),
        in_specs=[pl.BlockSpec(memory_space=pltpu.VMEM)],
        out_specs=[pl.BlockSpec(memory_space=pltpu.VMEM)] * len(outs),
        scratch_shapes=[pltpu.VMEM((flat_rows, 128), F32), pltpu.VMEM((3, wide_rows(count), 128), F32)],
        compiler_params=pltpu.CompilerParams(vmem_limit_bytes=VMEM_BYTES),
        name="unpack_weights",
    )(slots)
    return dict(zip(outs, values, strict=True))


def collect_gradients(bases, wide, gwe, gwst, gtaps, gbias, gwo, gwq, gpair, gwr, gcols, grows):
    width = gwst.shape[0]
    hidden = gwst.shape[1]
    used = bases["shrink_bias"] + 1
    for k in range(3):
        wide[k, pl.ds(used, wide.shape[1] - used), :] = jnp.zeros((wide.shape[1] - used, 128), F32)

    def put(base, value, stride=1):
        count = value.shape[0]
        at = pl.ds(base, count, stride=stride) if stride > 1 else pl.ds(base, count)
        wide[0, at, :] = value[:, 0:128]
        wide[1, at, :] = value[:, 128:256]
        wide[2, at, 0 : width - 256] = value[:, 256:width]

    for k, name in enumerate(("pre_gain", "pre_shift", "mlp_gain", "mlp_shift")):
        put(bases[name], jnp.sum(gcols[k].T, axis=0, keepdims=True))
    put(bases["shrink_bias"], jnp.sum(gbias[...].T, axis=0, keepdims=True))
    for k, name in enumerate(("reduce_bias", "reduce_gain", "reduce_shift")):
        put(bases[name], jnp.sum(grows[8 * k : 8 * k + 8, :], axis=0, keepdims=True))
    put(bases["query_weight"], gwq[0 : width + 1, :])
    for p in range(4):
        put(bases["reduce_weight"] + p * width, gwr[p].T)
    put(bases["pair_weight"], gpair[0:width, :].T[0:width], 2)
    value = gpair[width : 2 * width, :].T
    put(bases["pair_weight"] + 1, value[0:width], 2)
    put(bases["value_bias"], value[width : width + 1])
    put(bases["output_weight"], gwo[0 : width + 1, :])
    sums = jnp.concatenate(
        [jnp.sum(gtaps[8 * k : 8 * k + 8, :], axis=0, keepdims=True) for k in range(10)], axis=0
    )
    for q in range(hidden // width):
        put(bases["expand_weight"] + q, gwe[0 : width + 1, q * width : (q + 1) * width], hidden // width)
        put(bases["spatial_weight"] + q, sums[:, q * width : (q + 1) * width], hidden // width)
    for k in range(hidden // 128):
        put(bases["shrink_weight"] + 128 * k, gwst[:, 128 * k : 128 * k + 128].T)

def join_lines(read, write, low):
    turned = [pltpu.roll(read(1, k), 64, 1) for k in range(3)]
    write(0, read(0, 0))
    write(1, read(0, 1))
    write(2, jnp.where(low, read(0, 2), turned[0]))
    write(3, jnp.where(low, turned[0], turned[1]))
    write(4, jnp.where(low, turned[1], turned[2]))


def join_slot(wide, slot, slot_rows, line):
    pairs = slot_rows // 5

    def part(start, count):
        low = lax.broadcasted_iota(jnp.int32, (count, 128), 1) < 64

        def read(parity, k):
            return wide[k, pl.ds(slot * (2 * pairs) + 2 * start + parity, count, stride=2), :]

        def write(k, value):
            line[pl.ds(5 * start + k, count, stride=5), :] = value

        join_lines(read, write, low)

    part(0, pairs // 8 * 8)
    if pairs % 8:
        part(pairs // 8 * 8, pairs % 8)


def pack_kernel(order, slot_rows, bases, *refs):
    grads, (slots, flat, wide) = refs[:10], refs[10:]
    collect_gradients(bases, wide, *grads)
    done = wide.shape[1] * 5 // 2
    flat[done:, :] = jnp.zeros((flat.shape[0] - done, 128), F32)
    low = lax.broadcasted_iota(jnp.int32, (SPAN, 128), 1) < 64

    def regroup(t, _):
        def read(parity, k):
            return wide[k, pl.ds(t * (2 * SPAN) + parity, SPAN, stride=2), :]

        def write(k, value):
            flat[pl.ds(t * (5 * SPAN) + k, SPAN, stride=5), :] = value

        join_lines(read, write, low)
        return 0

    lax.fori_loop(0, wide.shape[1] // (2 * SPAN), regroup, 0)
    inside = lax.broadcasted_iota(jnp.int32, slots.shape[1:], 0) < slot_rows
    for slot, place in enumerate(order):
        slots[place] = jnp.where(inside, flat[pl.ds(slot * slot_rows, slots.shape[1]), :], 0.0).astype(BF)


def pack_gradients(grads, order, slot_rows, padded_rows, width):
    bases, count = row_bases(width, 4 * width)
    flat_rows = max(len(order) * slot_rows, wide_rows(count) * width // 128) + padded_rows
    return pl.pallas_call(
        partial(pack_kernel, order, slot_rows, bases),
        out_shape=jax.ShapeDtypeStruct((len(order), padded_rows, 128), BF),
        in_specs=[pl.BlockSpec(memory_space=pltpu.VMEM)] * len(grads),
        out_specs=pl.BlockSpec(memory_space=pltpu.VMEM),
        scratch_shapes=[pltpu.VMEM((flat_rows, 128), F32), pltpu.VMEM((3, wide_rows(count), 128), F32)],
        compiler_params=pltpu.CompilerParams(vmem_limit_bytes=VMEM_BYTES),
        name="pack_gradients",
    )(*grads)


def device_step(images, cotangent, kv_sides, w):
    positions = jnp.arange(TOKENS, dtype=jnp.int32)
    limit = 2 * kv_sides[:, None]
    mask = ((positions[None] // GRID < limit) & (positions[None] % GRID < limit)).astype(F32)
    mask = jnp.broadcast_to(mask[:, None, :], (mask.shape[0], 8, TOKENS))
    perm = jnp.asarray(patch_order(), BF)
    pre, patches, reduced, memory, mixed, lse, middle, post = attention_forward(
        kv_sides, images, mask, perm, w["vec"], w["rows"], w["wqt"], w["wr"], w["wk"], w["wvt"], w["wot"]
    )
    output, grad_post, gwe, gwst, gtaps, gbias = feed_forward(
        post, cotangent, mask, middle, w["we"], w["wst"], w["taps"], w["vec"]
    )
    grad_images, gwo, gwq, gpair, gwr, gcols, grows = attention_backward(
        kv_sides, images, cotangent, mask, pre, patches, reduced, memory, mixed, lse, middle, grad_post,
        perm, w["vec"], w["rows"], w["wq"], w["wqt"], w["wr"], w["wk"], w["wv"], w["wvt"], w["wo"],
    )
    return output, grad_images, (gwe, gwst, gtaps, gbias, gwo, gwq, gpair, gwr, gcols, grows)


def step(on_grid, images, cotangent, kv_sides, params, first_moment, second_moment):
    width = images.shape[2]
    axes = ("dp", "fsdp")
    outer, inner = lax.axis_size("dp"), lax.axis_size("fsdp")
    slot_rows = params.shape[0] // 128
    padded_rows = -(-slot_rows // 32) * 32
    own = jnp.pad(params.reshape(slot_rows, 128).astype(BF), ((0, padded_rows - slot_rows), (0, 0)))
    order = list(range(outer * inner))
    if on_grid:
        weights = gather_weights(own, slot_rows, width)
    else:
        weights = unpack_weights(lax.all_gather(own, axes), order, slot_rows, width)
    output, grad_images, grads = device_step(
        images.transpose(0, 2, 1), cotangent.transpose(0, 2, 1), kv_sides, weights
    )
    if on_grid:
        shard, squares = reduce_gradients(grads, slot_rows, padded_rows, width)
        squares = jnp.sum(squares)
    else:
        slots = pack_gradients(grads, order, slot_rows, padded_rows, width)
        shard = lax.psum_scatter(slots.astype(F32), axes)
        squares = lax.psum(jnp.sum(shard * shard), axes)
    shard = shard[:slot_rows].reshape(-1)
    grad_norm = jnp.sqrt(squares)
    clipped = shard * jnp.minimum(1.0, CLIP_NORM / (grad_norm + 1e-06))
    new_first = BETA_FIRST * first_moment + (1.0 - BETA_FIRST) * clipped
    new_second = BETA_SECOND * second_moment + (1.0 - BETA_SECOND) * clipped * clipped
    first_hat = new_first / (1.0 - BETA_FIRST**STEP)
    second_hat = new_second / (1.0 - BETA_SECOND**STEP)
    new_params = params - RATE * (first_hat / (jnp.sqrt(second_hat) + EPSILON) + DECAY * params)
    return (
        output.transpose(0, 2, 1),
        grad_images.transpose(0, 2, 1),
        grad_norm,
        new_first,
        new_second,
        new_params,
    )


def solution(mesh):
    data = P(("dp", "fsdp"), None, None)
    flat = P(("dp", "fsdp"))
    on_grid = dict(mesh.shape) == {"dp": 4, "fsdp": 8}
    return jax.shard_map(
        partial(step, on_grid),
        mesh=mesh,
        in_specs=(data, data, flat, flat, flat, flat),
        out_specs=(data, data, P(), flat, flat, flat),
        check_vma=False,
    )
```

```python
from functools import partial
import math

import jax
import jax.numpy as jnp
import numpy as np
from jax import lax
from jax.experimental import pallas as pl
from jax.experimental.pallas import tpu as pltpu
from jax.sharding import PartitionSpec as P

HEADS = 5
HEAD_DIM = 64
GRID = 48
KV = 24
STEP = 10

CLIP_NORM = 1.0
BETA_FIRST = 0.9
BETA_SECOND = 0.999
RATE = 0.04
DECAY = 0.05
EPSILON = 1e-08

F32 = jnp.float32
BF = jnp.bfloat16
NN = (((1,), (0,)), ((), ()))
NT = (((1,), (1,)), ((), ()))
TOKENS = GRID * GRID
KEYS = KV * KV
PITCH = GRID + 8
EXT = 16
DEPTH = 512
LOG2E = math.log2(math.e)
QUERY_SCALE = HEAD_DIM**-0.5 * LOG2E
GELU_A = math.sqrt(2.0 / math.pi)
GELU_B = GELU_A * 0.044715
VMEM_BYTES = 63 * 1024 * 1024


def mm(left, right, dims=NN):
    return lax.dot_general(left, right, dims, preferred_element_type=F32)


def patch_order():
    matrix = np.zeros((8 * GRID, 8 * GRID), np.float32)
    for p in range(4):
        for a in range(4):
            for b in range(KV):
                matrix[p * 96 + a * KV + b, (2 * a + p // 2) * GRID + 2 * b + p % 2] = 1.0
    return matrix


def fold_rows(x):
    return jnp.sum(x.reshape(x.shape[0] // 8, 8, x.shape[1]), axis=0)


def norm_columns(x):
    scale = 1.0 / x.shape[0]
    centred = x - jnp.sum(x, axis=0, keepdims=True) * scale
    rstd = lax.rsqrt(jnp.sum(centred * centred, axis=0, keepdims=True) * scale + 1e-06)
    return centred * rstd, rstd


def norm_columns_back(normed, rstd, scaled):
    scale = 1.0 / scaled.shape[0]
    plain = jnp.sum(scaled, axis=0, keepdims=True) * scale
    mixed = jnp.sum(scaled * normed, axis=0, keepdims=True) * scale
    return rstd * (scaled - plain - normed * mixed)


def norm_rows(x):
    centred = x - jnp.mean(x, axis=-1, keepdims=True)
    rstd = lax.rsqrt(jnp.mean(centred * centred, axis=-1, keepdims=True) + 1e-06)
    return centred * rstd, rstd


def norm_rows_back(normed, rstd, scaled):
    plain = jnp.mean(scaled, axis=-1, keepdims=True)
    mixed = jnp.mean(scaled * normed, axis=-1, keepdims=True)
    return rstd * (scaled - plain - normed * mixed)


def first_row(row, rows=EXT):
    index = lax.broadcasted_iota(jnp.int32, (rows, row.shape[-1]), 0)
    return jnp.where(index == 0, row, 0.0)


def three_parts(x):
    high = x.astype(BF).astype(F32)
    middle = (x - high).astype(BF).astype(F32)
    return high, middle, (x - high - middle).astype(BF).astype(F32)


def whole(x):
    zeros = (0,) * len(x.shape)
    return pl.BlockSpec(x.shape, lambda *_: zeros)


FAR = pl.BlockSpec(memory_space=pl.ANY)


def near(x):
    return pltpu.VMEM((1,) + tuple(x.shape[1:]), x.dtype)


def per_image(x, **kwargs):
    zeros = (0,) * (len(x.shape) - 1)
    return pl.BlockSpec((1,) + tuple(x.shape[1:]), lambda i, *_: (i,) + zeros, **kwargs)


def key_columns(ref, side, h_range, ones_from, ones_to, with_mask):
    lane = lax.broadcasted_iota(jnp.int32, (KV, 64), 1)
    cell = lax.broadcasted_iota(jnp.int32, (KV, 64), 0)
    ones = jnp.where((lane >= ones_from) & (lane <= ones_to), 1.0, 0.0)
    for a in range(KV):
        block = ones
        if with_mask:
            bias = jnp.where((cell < side) & (a < side), 0.0, -1e30)
            block = jnp.where(lane == 0, bias, ones)
        block = block.astype(BF)
        for h in h_range:
            ref[h, a * KV : (a + 1) * KV, 64:128] = block


def attention_forward_kernel(
    sides, images, mask, perm, vec, rows, wqt, wr, wk, wvt, wot,
    pre_far, patches_far, reduced_far, memory_far, mixed_far, lse, middle, post,
    pre, patches, reduced, memory, mixed, key_ref, value_ref, sems,
):
    i = pl.program_id(0)
    width = images.shape[1]
    far = (pre_far, patches_far, reduced_far, memory_far, mixed_far)
    kept = (pre, patches, reduced, memory, mixed)
    away = [pltpu.make_async_copy(y, x.at[pl.ds(i, 1)], sems.at[k]) for k, (x, y) in enumerate(zip(far, kept))]

    def first_norm(t, _):
        for u in range(3):
            at = pl.ds(pl.multiple_of(t * 384 + u * 128, 128), 128)
            x = images[0, :, at].astype(F32) * mask[0, 0:1, at]
            normed, _unused = norm_columns(x)
            pre[0, 0:width, at] = (normed * vec[0] + vec[1]).astype(BF)
            pre[0, width : width + EXT, at] = first_row(jnp.ones((1, 128), F32)).astype(BF)
        return 0

    lax.fori_loop(0, TOKENS // 384, first_norm, 0)
    for t in range(TOKENS // 384):
        picked = mm(perm[...], pre[0, 0:width, t * 384 : (t + 1) * 384], NT).astype(BF)
        for p in range(4):
            patches[0, p, t * 96 : (t + 1) * 96, :] = picked[p * 96 : (p + 1) * 96]
    away[0].start()
    away[1].start()

    total = rows[0:1, :]
    for p in range(4):
        total = total + mm(patches[0, p], wr[p])
    reduced[0] = total
    normed, _unused = norm_rows(total)
    memory[0, :, 0:width] = (normed * rows[1:2, :] + rows[2:3, :]).astype(BF)
    lane = lax.broadcasted_iota(jnp.int32, (KEYS, 64), 1)
    memory[0, :, width : width + 64] = jnp.where(lane == 0, 1.0, 0.0).astype(BF)
    away[2].start()
    away[3].start()
    keys = mm(memory[0, :, 0:width], wk[...]).astype(BF)
    key_columns(key_ref, sides[i], range(HEADS), 1, 0, True)
    values = mm(wvt[...], memory[0], NT).astype(BF)
    ones = first_row(jnp.ones((1, KEYS), F32)).astype(BF)
    for h in range(HEADS):
        at = slice(h * HEAD_DIM, (h + 1) * HEAD_DIM)
        key_ref[h, :, 0:HEAD_DIM] = keys[:, at]
        value_ref[h, 0:HEAD_DIM, :] = values[at]
        value_ref[h, HEAD_DIM : HEAD_DIM + EXT, :] = ones
    mixed[0, width : width + EXT, :] = first_row(jnp.ones((1, TOKENS), F32)).astype(BF)
    queries = (mm(wqt[...], pre[0]) * QUERY_SCALE).astype(BF)
    tail = first_row(jnp.ones((1, TOKENS), F32), 64).astype(BF)
    for h in range(HEADS):
        at = slice(h * HEAD_DIM, (h + 1) * HEAD_DIM)
        scores = mm(key_ref[h], jnp.concatenate([queries[at], tail], axis=0))
        top = jnp.max(scores, axis=0, keepdims=True)
        weights = jnp.exp2(scores - top).astype(BF)
        out = mm(value_ref[h], weights)
        total = out[HEAD_DIM : HEAD_DIM + 1]
        mixed[0, at, :] = (out[0:HEAD_DIM] * (1.0 / total)).astype(BF)
        lse[0, h : h + 1, :] = top + jnp.log2(total)

    away[4].start()
    middle[0] = mm(wot[...], mixed[0])

    def second_norm(t, _):
        for u in range(3):
            at = pl.ds(pl.multiple_of(t * 384 + u * 128, 128), 128)
            here = mask[0, 0:1, at]
            x = images[0, :, at].astype(F32) * here + middle[0, :, at]
            middle[0, :, at] = x
            normed, _unused = norm_columns(x)
            post[0, 0:width, at] = ((normed * vec[2] + vec[3]) * here).astype(BF)
            post[0, width : width + EXT, at] = first_row(here).astype(BF)
        return 0

    lax.fori_loop(0, TOKENS // 384, second_norm, 0)
    for copy in away:
        copy.wait()


def attention_forward(sides, images, mask, perm, vec, rows, wqt, wr, wk, wvt, wot):
    n, width, tokens = images.shape
    shape = jax.ShapeDtypeStruct
    outs = [
        shape((n, width + EXT, tokens), BF),
        shape((n, 4, KEYS, width), BF),
        shape((n, KEYS, width), F32),
        shape((n, KEYS, width + 64), BF),
        shape((n, width + EXT, tokens), BF),
        shape((n, 8, tokens), F32),
        shape((n, width, tokens), F32),
        shape((n, width + EXT, tokens), BF),
    ]
    weights = (perm, vec, rows, wqt, wr, wk, wvt, wot)
    return pl.pallas_call(
        attention_forward_kernel,
        grid_spec=pltpu.PrefetchScalarGridSpec(
            num_scalar_prefetch=1,
            grid=(n,),
            in_specs=[per_image(images), per_image(mask)] + [whole(x) for x in weights],
            out_specs=[FAR] * 5 + [per_image(x) for x in outs[5:]],
            scratch_shapes=[near(x) for x in outs[:5]]
            + [
                pltpu.VMEM((HEADS, KEYS, 128), BF),
                pltpu.VMEM((HEADS, HEAD_DIM + EXT, KEYS), BF),
                pltpu.SemaphoreType.DMA((5,)),
            ],
        ),
        out_shape=outs,
        compiler_params=pltpu.CompilerParams(vmem_limit_bytes=VMEM_BYTES),
        name="attention_forward",
    )(sides, images, mask, *weights)


def feed_forward_kernel(
    post_next, cot_next, mask_next, we_next, wst_next, taps,
    post, cot, mask, middle_far, we, wst, vec,
    output, grad_post, gwe, gwst, gtaps, gbias,
    padded_0, padded_1, grad_padded, grad_act, act_0, act_1, grad_exp_0, grad_exp_1,
    post_rows, out_grad_rows, out_grad, total, middle, middle_sem,
):
    s = pl.program_id(0)
    last = pl.num_programs(0) - 1
    width, block = cot.shape[1], wst.shape[1]
    blocks = gwst.shape[1] // block
    halves = block // 128
    rows = 16
    chunks = GRID // rows
    span = rows * GRID
    js = pl.ds(pl.multiple_of(lax.rem(s, blocks) * block, block), block)
    js_done = pl.ds(pl.multiple_of(lax.rem(jnp.maximum(s - 1, 0), blocks) * block, block), block)

    def tokens(t):
        return pl.ds(pl.multiple_of(t * span, span), span)

    def expand(t, padded, we, wst):
        at = tokens(t)
        filled = mm(post_rows[at, :], we[...])
        for h in range(halves):
            for r in range(rows):
                start = pl.multiple_of((t * rows + r + 1) * PITCH + 8, 8)
                padded[h, pl.ds(start, GRID), :] = filled[r * GRID : (r + 1) * GRID, h * 128 : (h + 1) * 128]
        grad_act[at, :] = mm(out_grad_rows[at, :], wst[...])

    def finish(t, act, grad_exp):
        at = tokens(t)
        total[:, at] += mm(wst[0:width, :], act[at, :], NT)
        grad_post[0, :, at] += mm(we[0:width, :], grad_exp[at, :], NT)
        gwst[:, js_done] += mm(out_grad[:, at], act[at, :])
        gwe[:, js_done] += mm(post[0, :, at], grad_exp[at, :])

    def convolve(t, padded, act):
        for h in range(halves):
            hs = slice(h * 128, (h + 1) * 128)
            w = [jnp.broadcast_to(0.5 * taps[k : k + 1, hs], (GRID, 128)).astype(BF) for k in range(10)]
            sums = jnp.zeros((8, 128), F32)
            open_rows = {}
            for q in range(-1, rows + 1):
                base = (t * rows + q + 1) * PITCH + 8
                x = [padded[h, pl.ds(base + d, GRID), :].astype(BF) for d in (-1, 0, 1)]
                for a in (2, 1, 0):
                    r = q + 1 - a
                    if 0 <= r < rows:
                        part = w[3 * a] * x[0] + w[3 * a + 1] * x[1] + w[3 * a + 2] * x[2]
                        open_rows[r] = part + open_rows.get(r, w[9])
                r = q - 1
                if r < 0:
                    continue
                at = pl.ds(pl.multiple_of((t * rows + r) * GRID, GRID), GRID)
                gelu, slope = gelu_pair(open_rows.pop(r))
                act[at, hs] = gelu
                grad = (grad_act[at, hs].astype(BF) * slope).astype(F32)
                start = pl.multiple_of((t * rows + r + 1) * PITCH + 8, 8)
                grad_padded[h, pl.ds(start, GRID), :] = grad
                sums = sums + fold_rows(grad)
            cols = pl.ds(pl.multiple_of(lax.rem(s, blocks) * block + h * 128, 128), 128)
            gtaps[72:80, cols] += sums

    def convolve_back(t, padded, grad_exp):
        for h in range(halves):
            hs = slice(h * 128, (h + 1) * 128)
            w = [jnp.broadcast_to(taps[k : k + 1, hs], (GRID, 128)).astype(BF) for k in range(9)]
            sums = [jnp.zeros((8, 128), F32) for _ in range(9)]
            waiting = {}
            open_rows = {}
            x = {}
            for q in range(-1, rows + 1):
                base = (t * rows + q + 1) * PITCH + 8
                grads = [grad_padded[h, pl.ds(base + 1 - b, GRID), :].astype(BF) for b in range(3)]
                if q + 1 < rows:
                    start = pl.multiple_of((t * rows + q + 2) * PITCH + 8, 8)
                    x[q + 1] = padded[h, pl.ds(start, GRID), :].astype(BF)
                for a in range(3):
                    r = q + a - 1
                    if not 0 <= r < rows:
                        continue
                    part = w[3 * a] * grads[0] + w[3 * a + 1] * grads[1] + w[3 * a + 2] * grads[2]
                    open_rows[r] = part + open_rows[r] if r in open_rows else part
                    for b in range(3):
                        k = 3 * a + b
                        product = x[r] * grads[b]
                        product = product[0:16] + product[16:32] + product[32:48]
                        waiting[k] = waiting[k] + product if k in waiting else product
                        if r % 4 == 3:
                            product = waiting.pop(k).astype(F32)
                            sums[k] = sums[k] + product[0:8] + product[8:16]
                r = q - 1
                if r >= 0:
                    at = pl.ds(pl.multiple_of((t * rows + r) * GRID, GRID), GRID)
                    grad_exp[at, hs] = open_rows.pop(r)
                    x.pop(r)
            cols = pl.ds(pl.multiple_of(lax.rem(s, blocks) * block + h * 128, 128), 128)
            for k in range(9):
                gtaps[8 * k : 8 * k + 8, cols] += sums[k]

    @pl.when(s == 0)
    def _():
        for ref in (act_1, grad_exp_1, out_grad, gwe, gwst, gtaps, gbias):
            ref[...] = jnp.zeros_like(ref)
        for ref in (post_rows, out_grad_rows):
            ref[:, 256:DEPTH] = jnp.zeros((TOKENS, DEPTH - 256), BF)
        for ref in (padded_0, padded_1, grad_padded):
            for h in range(halves):
                ref[h, 0 : PITCH + 8, :] = jnp.zeros((PITCH + 8, 128), F32)
                ref[h, (GRID + 1) * PITCH :, :] = jnp.zeros((PITCH + 8, 128), F32)
                for r in range(1, GRID):
                    ref[h, (r + 1) * PITCH : (r + 1) * PITCH + 8, :] = jnp.zeros((8, 128), F32)

    @pl.when((s == 0) | ((lax.rem(s + 1, blocks) == 0) & (s + 1 < last)))
    def _():
        for t in range(TOKENS // 384):
            at = slice(t * 384, (t + 1) * 384)
            grad = cot_next[0, :, at].astype(F32) * mask_next[0, 0:1, at]
            gbias[...] += grad[:, 0:128] + grad[:, 128:256] + grad[:, 256:384]
            out_grad_rows[at, 0:width] = (0.5 * grad).astype(BF).T
            post_rows[at, 0 : width + EXT] = post_next[0, :, at].T

    fetch = pltpu.make_async_copy(middle_far.at[pl.ds(jnp.maximum(s - 1, 0) // blocks, 1)], middle, middle_sem)

    @pl.when(lax.rem(s, blocks) == 1)
    def _():
        fetch.start()
        for t in range(TOKENS // 384):
            at = slice(t * 384, (t + 1) * 384)
            out_grad[:, at] = (cot[0, :, at].astype(F32) * mask[0, 0:1, at]).astype(BF)

    @pl.when((s == 0) | (lax.rem(s, blocks) == 1))
    def _():
        total[...] = jnp.zeros_like(total)
        grad_post[...] = jnp.zeros_like(grad_post)

    @pl.when(s == 0)
    def _():
        def first(t, _):
            expand(t, padded_0, we, wst)
            return 0

        lax.fori_loop(0, chunks, first, 0)

    def work(padded, padded_next, act, act_done, grad_exp, grad_exp_done):
        def forward(t, _):
            finish(t, act_done, grad_exp_done)
            convolve(t, padded, act)
            return 0

        def backward(t, _):
            expand(t, padded_next, we_next, wst_next)
            convolve_back(t, padded, grad_exp)
            return 0

        lax.fori_loop(0, chunks, forward, 0)
        lax.fori_loop(0, chunks, backward, 0)

    @pl.when((s < last) & (lax.rem(s, 2) == 0))
    def _():
        work(padded_0, padded_1, act_0, act_1, grad_exp_0, grad_exp_1)

    @pl.when((s < last) & (lax.rem(s, 2) == 1))
    def _():
        work(padded_1, padded_0, act_1, act_0, grad_exp_1, grad_exp_0)

    @pl.when(s == last)
    def _():
        def rest(t, _):
            @pl.when(lax.rem(s, 2) == 0)
            def _():
                finish(t, act_1, grad_exp_1)

            @pl.when(lax.rem(s, 2) == 1)
            def _():
                finish(t, act_0, grad_exp_0)

            return 0

        lax.fori_loop(0, chunks, rest, 0)

    @pl.when((s > 0) & (lax.rem(s, blocks) == 0))
    def _():
        fetch.wait()
        for t in range(TOKENS // 128):
            at = slice(t * 128, (t + 1) * 128)
            output[0, :, at] = ((middle[0, :, at] + total[:, at] + vec[4]) * mask[0, 0:1, at]).astype(BF)


def gelu_pair(half):
    kind = half.dtype.type
    square = half * half
    upper = jnp.tanh(half * (kind(8.0 * GELU_B) * square + kind(2.0 * GELU_A))) + kind(1.0)
    gelu = half * upper
    return gelu, upper + gelu * (kind(2.0) - upper) * (kind(24.0 * GELU_B) * square + kind(2.0 * GELU_A))


def feed_forward(post, cot, mask, middle, we, wst, taps, vec, block=256):
    n, width, tokens = cot.shape
    hidden = wst.shape[1]
    blocks = hidden // block
    count = n * blocks
    shape = jax.ShapeDtypeStruct
    outs = [
        shape((n, width, tokens), BF),
        shape((n, width, tokens), F32),
        shape((width + EXT, hidden), F32),
        shape((width, hidden), F32),
        shape((80, hidden), F32),
        shape((width, 128), F32),
    ]

    def ahead(s):
        return jnp.minimum(s + 1, count - 1)

    def behind(s):
        return jnp.maximum(s - 1, 0)

    def image(x, step):
        zeros = (0,) * (len(x.shape) - 1)
        return pl.BlockSpec((1,) + tuple(x.shape[1:]), lambda s: (step(s) // blocks,) + zeros)

    def columns(x, step):
        return pl.BlockSpec((x.shape[0], block), lambda s: (0, lax.rem(step(s), blocks)))

    return pl.pallas_call(
        feed_forward_kernel,
        grid=(count + 1,),
        in_specs=[image(x, ahead) for x in (post, cot, mask)]
        + [columns(we, ahead), columns(wst, ahead), columns(taps, lambda s: jnp.minimum(s, count - 1))]
        + [image(x, behind) for x in (post, cot, mask)]
        + [FAR, columns(we, behind), columns(wst, behind), whole(vec)],
        out_specs=[image(x, behind) for x in outs[:2]] + [whole(x) for x in outs[2:]],
        out_shape=outs,
        scratch_shapes=[pltpu.VMEM((block // 128, (GRID + 2) * PITCH + 8, 128), F32)] * 3
        + [pltpu.VMEM((tokens, block), F32)]
        + [pltpu.VMEM((tokens, block), BF)] * 4
        + [
            pltpu.VMEM((tokens, DEPTH), BF),
            pltpu.VMEM((tokens, DEPTH), BF),
            pltpu.VMEM((width, tokens), BF),
            pltpu.VMEM((width, tokens), F32),
            near(middle),
            pltpu.SemaphoreType.DMA(()),
        ],
        compiler_params=pltpu.CompilerParams(vmem_limit_bytes=VMEM_BYTES),
        name="feed_forward",
    )(post, cot, mask, we, wst, taps, post, cot, mask, middle, we, wst, vec)


def attention_backward_kernel(
    sides, mixed_far, pre_far, memory_far, reduced_far, patches_far, images_far, cot, mask, lse, middle, grad_post,
    perm, vec, rows, wq, wqt, wr, wk, wv, wvt, wo,
    grad_images, gwo, gwq, gpair, gwr, gcols, grows,
    branch, grad_mixed, queries, grad_queries, key_ref, value_ref, keys_t, grad_keys, grad_values, grad_patches,
    mixed, pre, memory, reduced, patches, images, sems,
):
    i = pl.program_id(0)
    width = cot.shape[1]
    far = (mixed_far, pre_far, memory_far, reduced_far, patches_far, images_far)
    kept = (mixed, pre, memory, reduced, patches, images)
    fetch = [pltpu.make_async_copy(x.at[pl.ds(i, 1)], y, sems.at[k]) for k, (x, y) in enumerate(zip(far, kept))]
    for copy in fetch:
        copy.start()

    @pl.when(i == 0)
    def _():
        for ref in (gwo, gwq, gpair, gwr, gcols, grows):
            ref[...] = jnp.zeros_like(ref)

    def mlp_norm_back(t, _):
        gain = shift = jnp.zeros((width, 128), F32)
        for u in range(3):
            at = pl.ds(pl.multiple_of(t * 384 + u * 128, 128), 128)
            here = mask[0, 0:1, at]
            normed, rstd = norm_columns(middle[0, :, at])
            grad = grad_post[0, :, at] * here
            gain = gain + grad * normed
            shift = shift + grad
            grad = cot[0, :, at].astype(F32) * here + norm_columns_back(normed, rstd, grad * vec[2])
            grad_images[0, :, at] = grad
            branch[:, at] = grad.astype(BF)
        gcols[2] += gain
        gcols[3] += shift
        return 0

    lax.fori_loop(0, TOKENS // 384, mlp_norm_back, 0)
    fetch[0].wait()
    gwo[...] += mm(mixed[0], branch[...], NT)
    grad_mixed[...] = mm(wo[...], branch[...]).astype(BF)
    fetch[1].wait()
    queries[...] = (mm(wqt[...], pre[0]) * QUERY_SCALE).astype(BF)
    fetch[2].wait()
    keys = mm(memory[0, :, 0:width], wk[...]).astype(BF)
    keys_t[...] = keys.T
    values = mm(wvt[...], memory[0], NT).astype(BF).T
    key_columns(key_ref, sides[i], range(HEADS), 1, 3, True)
    key_columns(value_ref, sides[i], range(HEADS), 1, 3, False)
    for h in range(HEADS):
        at = slice(h * HEAD_DIM, (h + 1) * HEAD_DIM)
        key_ref[h, :, 0:HEAD_DIM] = keys[:, at]
        value_ref[h, :, 0:HEAD_DIM] = values[:, at]

    span = TOKENS // 3
    index = lax.broadcasted_iota(jnp.int32, (64, span), 0)
    grad_values[...] = jnp.zeros_like(grad_values)
    grad_keys[...] = jnp.zeros_like(grad_keys)

    def part(t, _):
        at = pl.ds(pl.multiple_of(t * span, 128), span)
        for h in range(HEADS):
            hs = slice(h * HEAD_DIM, (h + 1) * HEAD_DIM)
            one, two, three = three_parts(-lse[0, h : h + 1, at])
            tail = jnp.where(index == 2, two, jnp.where(index == 3, three, 0.0))
            tail = jnp.where(index == 0, 1.0, jnp.where(index == 1, one, tail)).astype(BF)
            query = queries[hs, at]
            attend = jnp.exp2(mm(key_ref[h], jnp.concatenate([query, tail], axis=0)))
            low = attend.astype(BF)
            grad = grad_mixed[hs, at]
            inner = grad.astype(F32) * mixed[0, hs, at].astype(F32)
            one, two, three = three_parts(-jnp.sum(inner, axis=0, keepdims=True))
            tail = jnp.where(index == 2, two, jnp.where(index == 3, three, 0.0))
            tail = jnp.where(index == 1, one, tail).astype(BF)
            grad_attend = mm(value_ref[h], jnp.concatenate([grad, tail], axis=0))
            grad_scores = (attend * grad_attend).astype(BF)
            grad_values[hs, :] += mm(grad, low, NT)
            grad_keys[hs, :] += mm(query, grad_scores, NT) * (1.0 / LOG2E)
            grad_queries[hs, at] = (mm(keys_t[hs, :], grad_scores) * HEAD_DIM**-0.5).astype(BF)
        return 0

    lax.fori_loop(0, TOKENS // span, part, 0)

    low_keys = grad_keys[...].astype(BF)
    low_values = grad_values[...].astype(BF)
    gpair[0:width, :] += mm(low_keys, memory[0])
    gpair[width : 2 * width, :] += mm(low_values, memory[0])
    grad_memory = mm(low_keys.T, wk[...], NT) + mm(low_values.T, wv[...], NT)
    fetch[3].wait()
    normed, rstd = norm_rows(reduced[0])
    grows[8:16, :] += fold_rows(grad_memory * normed)
    grows[16:24, :] += fold_rows(grad_memory)
    grad_reduced = norm_rows_back(normed, rstd, grad_memory * rows[1:2, :]).astype(BF)
    grows[0:8, :] += fold_rows(grad_reduced.astype(F32))
    grad_reduced_t = grad_reduced.T
    fetch[4].wait()
    for p in range(4):
        gwr[p] += mm(grad_reduced_t, patches[0, p])
        grad_patches[p] = mm(grad_reduced, wr[p], NT).astype(BF)
    gwq[...] += mm(pre[0], grad_queries[...], NT)

    def pre_norm_back(t, _):
        at = pl.ds(pl.multiple_of(t * 384, 128), 384)
        grad_pre = mm(wq[...], grad_queries[:, at])
        start = pl.ds(pl.multiple_of(t * 96, 32), 96)
        picked = jnp.concatenate([grad_patches[p, start, :] for p in range(4)], axis=0)
        grad_pre = grad_pre + mm(picked.T, perm[...])
        gain = shift = jnp.zeros((width, 128), F32)
        for u in range(3):
            at = pl.ds(pl.multiple_of(t * 384 + u * 128, 128), 128)
            here = mask[0, 0:1, at]
            normed, rstd = norm_columns(images[0, :, at].astype(F32) * here)
            grad = grad_pre[:, u * 128 : (u + 1) * 128]
            gain = gain + grad * normed
            shift = shift + grad
            back = norm_columns_back(normed, rstd, grad * vec[0])
            grad_images[0, :, at] = (grad_images[0, :, at] + back) * here
        gcols[0] += gain
        gcols[1] += shift
        return 0

    fetch[5].wait()
    lax.fori_loop(0, TOKENS // 384, pre_norm_back, 0)


def attention_backward(
    sides, images, cot, mask, pre, patches, reduced, memory, mixed, lse, middle, grad_post,
    perm, vec, rows, wq, wqt, wr, wk, wv, wvt, wo,
):
    n, width, tokens = images.shape
    shape = jax.ShapeDtypeStruct
    outs = [
        shape((n, width, tokens), F32),
        shape((width + EXT, width), F32),
        shape((width + EXT, width), F32),
        shape((2 * width, width + 64), F32),
        shape((4, width, width), F32),
        shape((4, width, 128), F32),
        shape((24, width), F32),
    ]
    one = {"pipeline_mode": pl.Buffered(1)}
    far = (mixed, pre, memory, reduced, patches, images)
    inputs = (cot, mask, lse, middle, grad_post)
    weights = (perm, vec, rows, wq, wqt, wr, wk, wv, wvt, wo)
    return pl.pallas_call(
        attention_backward_kernel,
        grid_spec=pltpu.PrefetchScalarGridSpec(
            num_scalar_prefetch=1,
            grid=(n,),
            in_specs=[FAR] * 6 + [per_image(x) for x in inputs] + [whole(x) for x in weights],
            out_specs=[per_image(outs[0], **one)] + [whole(x) for x in outs[1:]],
            scratch_shapes=[
                pltpu.VMEM((width, tokens), BF),
                pltpu.VMEM((width, tokens), BF),
                pltpu.VMEM((width, tokens), BF),
                pltpu.VMEM((width, tokens), BF),
                pltpu.VMEM((HEADS, KEYS, 128), BF),
                pltpu.VMEM((HEADS, KEYS, 128), BF),
                pltpu.VMEM((width, KEYS), BF),
                pltpu.VMEM((width, KEYS), F32),
                pltpu.VMEM((width, KEYS), F32),
                pltpu.VMEM((4, KEYS, width), BF),
            ]
            + [near(x) for x in far]
            + [pltpu.SemaphoreType.DMA((6,))],
        ),
        out_shape=outs,
        compiler_params=pltpu.CompilerParams(vmem_limit_bytes=VMEM_BYTES),
        name="attention_backward",
    )(sides, *far, *inputs, *weights)

MESH = pl.DeviceIdType.MESH


class Place:
    def __init__(self):
        self.dp = lax.axis_index("dp")
        self.fsdp = lax.axis_index("fsdp")
        self.y, self.x = self.dp // 2, self.dp % 2
        self.z, self.core = self.fsdp // 2, self.fsdp % 2
        self.other_core = 1 - self.core
        self.beside_x = (self.dp + 1 - 2 * self.x, self.fsdp)
        self.beside_y = (self.dp + 2 - 4 * self.y, self.fsdp)
        self.across = (3 - self.dp, self.fsdp)
        self.beside_core = (self.dp, self.fsdp + 1 - 2 * self.core)
        self.others = (self.z + 1 - 2 * (self.z % 2), 2 - self.z // 2, 3 * (1 - self.z // 2))

    def at_z(self, z):
        return (self.dp, z * 2 + self.core)

    def along_z(self, k):
        return self.at_z((self.z + k) % 4)

    def call(self, partners):
        barrier = pltpu.get_barrier_semaphore()
        for device in partners:
            pl.semaphore_signal(barrier, inc=1, device_id=device, device_id_type=MESH)

    def answer(self, count):
        pl.semaphore_wait(pltpu.get_barrier_semaphore(), count)


class Sender:
    def __init__(self, send, recv):
        self.send, self.recv, self.started = send, recv, []

    def __call__(self, source, target, device, recv=None):
        k = len(self.started)
        copy = pltpu.make_async_remote_copy(
            src_ref=source,
            dst_ref=target,
            send_sem=self.send.at[k],
            recv_sem=self.recv.at[k] if recv is None else recv,
            device_id=device,
            device_id_type=MESH,
        )
        copy.start()
        self.started.append(copy)
        return copy

    def finish(self):
        for copy in self.started:
            copy.wait_send()


def gather_kernel(slot_rows, bases, own, *refs):
    outs, (slots, wide, line, own_sem, send_sem, recv_sem, z_sem) = refs[:13], refs[13:]
    me = Place()
    half = own.shape[0] // 2
    first, second = pl.ds(0, half), pl.ds(half, half)
    send = Sender(send_sem, recv_sem)
    copy = pltpu.make_async_copy(own, slots.at[me.core, me.dp, me.z], own_sem)
    copy.start()
    me.call([me.beside_core, me.beside_x, me.beside_y] + [me.at_z(z) for z in me.others])
    me.answer(6)
    own_slot = slots.at[me.core, me.dp, me.z]

    def send_z(j):
        return send(own, own_slot, me.at_z(me.others[j]), z_sem.at[me.z])

    send_z(0)
    x_copies = [send(own, own_slot, me.beside_x)]
    y_copies = [send(own, own_slot, me.beside_y)]
    core_copies = [(send(own, own_slot, me.beside_core), me.dp, me.z)]
    send_z(1)
    half_copies = []
    order = (me.z,) + me.others

    def open_slot(core, dp, z):
        spread_slot(slots[core, dp, z], (dp * 8 + z * 2 + core), slot_rows, line, wide)

    def forward(k):
        z = order[k]
        x_copies[k].wait_recv()
        slot = slots.at[me.core, me.beside_x[0], z]
        half_copies.append(send(slot.at[first], slot.at[first], me.beside_y))
        core_copies.append((send(slot, slot, me.beside_core), me.beside_x[0], z))
        y_copies[k].wait_recv()
        slot = slots.at[me.core, me.beside_y[0], z]
        half_copies.append(send(slot.at[second], slot.at[second], me.beside_x))
        core_copies.append((send(slot, slot, me.beside_core), me.beside_y[0], z))
        open_slot(me.core, me.beside_x[0], z)
        open_slot(me.core, me.beside_y[0], z)

    copy.wait()
    open_slot(me.core, me.dp, me.z)
    forward(0)
    for k in (1, 2, 3):
        z = order[k]
        slot = slots.at[me.core, me.dp, z]
        pltpu.make_async_remote_copy(
            src_ref=own,
            dst_ref=slot,
            send_sem=send_sem.at[0],
            recv_sem=z_sem.at[z],
            device_id=me.at_z(z),
            device_id_type=MESH,
        ).wait_recv()
        x_copies.append(send(slot, slot, me.beside_x))
        y_copies.append(send(slot, slot, me.beside_y))
        core_copies.append((send(slot, slot, me.beside_core), me.dp, z))
        if k == 1:
            send_z(2)
        open_slot(me.core, me.dp, z)
        forward(k)
    for k in range(4):
        half_copies[2 * k].wait_recv()
        half_copies[2 * k + 1].wait_recv()
        slot = slots.at[me.core, me.across[0], order[k]]
        core_copies.append((send(slot, slot, me.beside_core), me.across[0], order[k]))
        open_slot(me.core, me.across[0], order[k])
    for copied, dp, z in core_copies:
        copied.wait_recv()
        open_slot(me.other_core, dp, z)
    send.finish()
    write_weights(bases, wide, *outs)


def gather_weights(own, slot_rows, width):
    bases, count = row_bases(width, 4 * width)
    outs = weight_shapes(width)
    copies = 35
    values = pl.pallas_call(
        partial(gather_kernel, slot_rows, bases),
        out_shape=list(outs.values()),
        in_specs=[pl.BlockSpec(memory_space=pltpu.VMEM)],
        out_specs=[pl.BlockSpec(memory_space=pltpu.VMEM)] * len(outs),
        scratch_shapes=[
            pltpu.VMEM((2, 4, 4) + own.shape, BF),
            pltpu.VMEM((3, -(-32 * slot_rows * 128 // width // 8) * 8 + 8, 128), F32),
            pltpu.VMEM(own.shape, F32),
            pltpu.SemaphoreType.DMA(()),
            pltpu.SemaphoreType.DMA((copies,)),
            pltpu.SemaphoreType.DMA((copies,)),
            pltpu.SemaphoreType.DMA((4,)),
        ],
        compiler_params=pltpu.CompilerParams(
            collective_id=0, has_side_effects=True, vmem_limit_bytes=VMEM_BYTES
        ),
        name="gather_weights",
    )(own)
    return dict(zip(outs, values, strict=True))


def reduce_kernel(slot_rows, bases, *refs):
    grads, (shard, squares) = refs[:10], refs[10:12]
    wide, line, own, core_out, core_in, y_in, x_in, x_last, y_last, z_in, small, send_sem, recv_sem = refs[12:]
    me = Place()
    rows = shard.shape[0]
    half = rows // 2
    first, second = pl.ds(0, half), pl.ds(half, half)
    send = Sender(send_sem, recv_sem)
    peers = [(me.dp, (me.z + k) % 4 * 2 + core) for k in range(4) for core in (me.core, me.other_core)][1:]
    planes = [me.beside_x, me.beside_y, me.across]
    me.call(peers + planes)
    collect_gradients(bases, wide, *grads)
    line[...] = jnp.zeros_like(line)
    me.answer(len(peers + planes))
    units = [(me.z + k) % 4 for k in (2, 1, 3, 0)]
    core_copies, y_copies, x_copies, last = [], [], [], []
    other_x, other_y = 1 - me.x, 1 - me.y

    def give(k):
        z = units[k]
        for dp in range(4):
            join_slot(wide, dp * 8 + z * 2 + me.other_core, slot_rows, line)
            core_out[z, dp] = line[...].astype(BF)
        core_copies.append(send(core_out.at[z], core_in.at[z], me.beside_core))
        for dp in range(4):
            join_slot(wide, dp * 8 + z * 2 + me.core, slot_rows, line)
            own[z, dp] = line[...]

    def cores(k):
        z = units[k]
        core_copies[k].wait_recv()
        for dp in range(4):
            core_in[z, dp] = (core_in[z, dp].astype(F32) + own[z, dp]).astype(BF)
        y_copies.append(
            [send(core_in.at[z, 2 * other_y + x, first], y_in.at[z, x], me.beside_y) for x in range(2)]
        )
        x_copies.append(
            [send(core_in.at[z, 2 * y + other_x, second], x_in.at[z, y], me.beside_x) for y in range(2)]
        )

    def plane(k):
        z = units[k]
        for copied in y_copies[k]:
            copied.wait_recv()
        y_in[z, other_x] = (
            y_in[z, other_x].astype(F32) + core_in[z, 2 * me.y + other_x, first].astype(F32)
        ).astype(BF)
        to_x = send(y_in.at[z, other_x], x_last.at[z], me.beside_x)
        for copied in x_copies[k]:
            copied.wait_recv()
        x_in[z, other_y] = (
            x_in[z, other_y].astype(F32) + core_in[z, 2 * other_y + me.x, second].astype(F32)
        ).astype(BF)
        last.append((to_x, send(x_in.at[z, other_y], y_last.at[z], me.beside_y)))

    z_copies = []

    def column(k):
        z = units[k]
        for copied in last[k]:
            copied.wait_recv()
        low = y_in[z, me.x].astype(F32) + core_in[z, me.dp, first].astype(F32) + x_last[z].astype(F32)
        high = x_in[z, me.y].astype(F32) + core_in[z, me.dp, second].astype(F32) + y_last[z].astype(F32)
        if k == 3:
            shard[first, :] = low
            shard[second, :] = high
        else:
            z_in[k, first] = low.astype(BF)
            z_in[k, second] = high.astype(BF)
            z_copies.append(send(z_in.at[k], z_in.at[k + 3], me.at_z(z)))

    give(0)
    give(1)
    cores(0)
    give(2)
    cores(1)
    plane(0)
    give(3)
    cores(2)
    plane(1)
    column(0)
    cores(3)
    plane(2)
    column(1)
    plane(3)
    column(2)
    column(3)
    for k in (0, 1, 2):
        z_copies[k].wait_recv()
        shard[...] += z_in[k + 3].astype(F32)
    total = shard[0:8, :] * shard[0:8, :]
    for k in range(1, rows // 8):
        part = shard[8 * k : 8 * k + 8, :]
        total = total + part * part
    small[0] = total
    small[2 + me.fsdp] = total
    copies = [send(small.at[0], small.at[2 + me.fsdp], device) for device in peers]
    for copied in copies:
        copied.wait_recv()
    total = small[2]
    for k in range(1, 8):
        total = total + small[2 + k]
    small[1] = total
    small[10 + me.dp] = total
    copies = [send(small.at[1], small.at[10 + me.dp], device) for device in planes]
    for copied in copies:
        copied.wait_recv()
    squares[...] = ((small[10] + small[11]) + small[12]) + small[13]
    send.finish()


def reduce_gradients(grads, slot_rows, rows, width):
    bases, _ = row_bases(width, 4 * width)
    half = rows // 2
    count = 4 + 16 + 8 + 3 + 7 + 3
    return pl.pallas_call(
        partial(reduce_kernel, slot_rows, bases),
        out_shape=[jax.ShapeDtypeStruct((rows, 128), F32), jax.ShapeDtypeStruct((8, 128), F32)],
        in_specs=[pl.BlockSpec(memory_space=pltpu.VMEM)] * len(grads),
        out_specs=[pl.BlockSpec(memory_space=pltpu.VMEM)] * 2,
        scratch_shapes=[
            pltpu.VMEM((3, -(-32 * slot_rows * 128 // width // 8) * 8 + 8, 128), F32),
            pltpu.VMEM((rows, 128), F32),
            pltpu.VMEM((4, 4, rows, 128), F32),
            pltpu.VMEM((4, 4, rows, 128), BF),
            pltpu.VMEM((4, 4, rows, 128), BF),
            pltpu.VMEM((4, 2, half, 128), BF),
            pltpu.VMEM((4, 2, half, 128), BF),
            pltpu.VMEM((4, half, 128), BF),
            pltpu.VMEM((4, half, 128), BF),
            pltpu.VMEM((6, rows, 128), BF),
            pltpu.VMEM((14, 8, 128), F32),
            pltpu.SemaphoreType.DMA((count,)),
            pltpu.SemaphoreType.DMA((count,)),
        ],
        compiler_params=pltpu.CompilerParams(
            collective_id=1, has_side_effects=True, vmem_limit_bytes=VMEM_BYTES
        ),
        name="reduce_gradients",
    )(*grads)


def layout_shapes(model_width, hidden_width):
    return [
        ("pre_gain", (model_width,)),
        ("pre_shift", (model_width,)),
        ("query_weight", (model_width, model_width)),
        ("query_bias", (model_width,)),
        ("reduce_weight", (4 * model_width, model_width)),
        ("reduce_bias", (model_width,)),
        ("reduce_gain", (model_width,)),
        ("reduce_shift", (model_width,)),
        ("pair_weight", (model_width, 2 * model_width)),
        ("value_bias", (model_width,)),
        ("output_weight", (model_width, model_width)),
        ("output_bias", (model_width,)),
        ("mlp_gain", (model_width,)),
        ("mlp_shift", (model_width,)),
        ("expand_weight", (model_width, hidden_width)),
        ("expand_bias", (hidden_width,)),
        ("spatial_weight", (9, hidden_width)),
        ("spatial_bias", (hidden_width,)),
        ("shrink_weight", (hidden_width, model_width)),
        ("shrink_bias", (model_width,)),
    ]


def row_bases(width, hidden):
    bases = {}
    row = 0
    for name, shape in layout_shapes(width, hidden):
        bases[name] = row
        row += math.prod(shape) // width
    return bases, row


SPAN = 96


def regroup_lines(read, write, low):
    part = [read(k) for k in range(5)]
    turned = [pltpu.roll(part[k], 64, 1) for k in (2, 3, 4)]
    for k in range(3):
        write(0, k, part[k])
    write(1, 0, jnp.where(low, turned[0], turned[1]))
    write(1, 1, jnp.where(low, turned[1], turned[2]))
    write(1, 2, turned[2])


def spread_slot(values, slot, slot_rows, line, wide):
    pairs = slot_rows // 5
    line[...] = values.astype(F32)

    def part(start, count):
        low = lax.broadcasted_iota(jnp.int32, (count, 128), 1) < 64

        def write(parity, k, value):
            wide[k, pl.ds(slot * (2 * pairs) + 2 * start + parity, count, stride=2), :] = value

        regroup_lines(lambda k: line[pl.ds(5 * start + k, count, stride=5), :], write, low)

    part(0, pairs // 8 * 8)
    if pairs % 8:
        part(pairs // 8 * 8, pairs % 8)


def unpack_kernel(order, slot_rows, bases, slots, *refs):
    outs, (flat, wide) = refs[:13], refs[13:]
    for slot, place in enumerate(order):
        flat[pl.ds(slot * slot_rows, slots.shape[1]), :] = slots[place].astype(F32)
    low = lax.broadcasted_iota(jnp.int32, (SPAN, 128), 1) < 64

    def regroup(t, _):
        def write(parity, k, value):
            wide[k, pl.ds(t * (2 * SPAN) + parity, SPAN, stride=2), :] = value

        regroup_lines(lambda k: flat[pl.ds(t * (5 * SPAN) + k, SPAN, stride=5), :], write, low)
        return 0

    lax.fori_loop(0, wide.shape[1] // (2 * SPAN), regroup, 0)
    write_weights(bases, wide, *outs)


def write_weights(bases, wide, vec, rows, wq, wqt, wr, wk, wv, wvt, wo, wot, we, wst, taps):
    width = wq.shape[0]
    hidden = wst.shape[1]

    def take(base, count, stride=1):
        at = pl.ds(base, count, stride=stride) if stride > 1 else pl.ds(base, count)
        return jnp.concatenate([wide[0, at, :], wide[1, at, :], wide[2, at, :][:, 0 : width - 256]], axis=1)

    def take_hidden(base, count):
        return jnp.concatenate([take(base + q, count, hidden // width) for q in range(hidden // width)], axis=1)

    def bordered(weight, bias, extra):
        index = lax.broadcasted_iota(jnp.int32, (extra, weight.shape[1]), 0)
        return jnp.concatenate([weight, jnp.where(index == 0, bias, 0.0)], axis=0)

    names = ("pre_gain", "pre_shift", "mlp_gain", "mlp_shift", "shrink_bias")
    for k, name in enumerate(names):
        vec[k] = jnp.broadcast_to(take(bases[name], 1), (128, width)).T
    for k, name in enumerate(("reduce_bias", "reduce_gain", "reduce_shift")):
        rows[k : k + 1, :] = take(bases[name], 1)
    query = take(bases["query_weight"], width)
    wq[...] = query.astype(BF)
    wqt[...] = bordered(query, take(bases["query_bias"], 1), EXT).T.astype(BF)
    for p in range(4):
        wr[p] = take(bases["reduce_weight"] + p * width, width).astype(BF)
    wk[...] = take(bases["pair_weight"], width, 2).astype(BF)
    value = take(bases["pair_weight"] + 1, width, 2)
    wv[...] = value.astype(BF)
    wvt[...] = bordered(value, take(bases["value_bias"], 1), 64).T.astype(BF)
    out = take(bases["output_weight"], width)
    wo[...] = out.astype(BF)
    wot[...] = bordered(out, take(bases["output_bias"], 1), EXT).T.astype(BF)
    we[0:width, :] = take_hidden(bases["expand_weight"], width).astype(BF)
    we[width:DEPTH, :] = first_row(take_hidden(bases["expand_bias"], 1), DEPTH - width).astype(BF)
    taps[0:9, :] = take_hidden(bases["spatial_weight"], 9)
    taps[9:10, :] = take_hidden(bases["spatial_bias"], 1)
    wst[width:DEPTH, :] = jnp.zeros((DEPTH - width, hidden), BF)
    for k in range(hidden // 128):
        wst[0:width, 128 * k : 128 * k + 128] = take(bases["shrink_weight"] + 128 * k, 128).T.astype(BF)


def wide_rows(count):
    return -(-count // (2 * SPAN)) * 2 * SPAN


def weight_shapes(width):
    hidden = 4 * width
    shape = jax.ShapeDtypeStruct
    return dict(
        vec=shape((5, width, 128), F32),
        rows=shape((3, width), F32),
        wq=shape((width, width), BF),
        wqt=shape((width, width + EXT), BF),
        wr=shape((4, width, width), BF),
        wk=shape((width, width), BF),
        wv=shape((width, width), BF),
        wvt=shape((width, width + 64), BF),
        wo=shape((width, width), BF),
        wot=shape((width, width + EXT), BF),
        we=shape((DEPTH, hidden), BF),
        wst=shape((DEPTH, hidden), BF),
        taps=shape((10, hidden), F32),
    )


def unpack_weights(slots, order, slot_rows, width):
    bases, count = row_bases(width, 4 * width)
    outs = weight_shapes(width)
    flat_rows = max(len(order) * slot_rows, wide_rows(count) * width // 128) + slots.shape[1]
    values = pl.pallas_call(
        partial(unpack_kernel, order, slot_rows, bases),
        out_shape=list(outs.values()),
        in_specs=[pl.BlockSpec(memory_space=pltpu.VMEM)],
        out_specs=[pl.BlockSpec(memory_space=pltpu.VMEM)] * len(outs),
        scratch_shapes=[pltpu.VMEM((flat_rows, 128), F32), pltpu.VMEM((3, wide_rows(count), 128), F32)],
        compiler_params=pltpu.CompilerParams(vmem_limit_bytes=VMEM_BYTES),
        name="unpack_weights",
    )(slots)
    return dict(zip(outs, values, strict=True))


def collect_gradients(bases, wide, gwe, gwst, gtaps, gbias, gwo, gwq, gpair, gwr, gcols, grows):
    width = gwst.shape[0]
    hidden = gwst.shape[1]
    used = bases["shrink_bias"] + 1
    for k in range(3):
        wide[k, pl.ds(used, wide.shape[1] - used), :] = jnp.zeros((wide.shape[1] - used, 128), F32)

    def put(base, value, stride=1):
        count = value.shape[0]
        at = pl.ds(base, count, stride=stride) if stride > 1 else pl.ds(base, count)
        wide[0, at, :] = value[:, 0:128]
        wide[1, at, :] = value[:, 128:256]
        wide[2, at, 0 : width - 256] = value[:, 256:width]

    for k, name in enumerate(("pre_gain", "pre_shift", "mlp_gain", "mlp_shift")):
        put(bases[name], jnp.sum(gcols[k].T, axis=0, keepdims=True))
    put(bases["shrink_bias"], jnp.sum(gbias[...].T, axis=0, keepdims=True))
    for k, name in enumerate(("reduce_bias", "reduce_gain", "reduce_shift")):
        put(bases[name], jnp.sum(grows[8 * k : 8 * k + 8, :], axis=0, keepdims=True))
    put(bases["query_weight"], gwq[0 : width + 1, :])
    for p in range(4):
        put(bases["reduce_weight"] + p * width, gwr[p].T)
    put(bases["pair_weight"], gpair[0:width, :].T[0:width], 2)
    value = gpair[width : 2 * width, :].T
    put(bases["pair_weight"] + 1, value[0:width], 2)
    put(bases["value_bias"], value[width : width + 1])
    put(bases["output_weight"], gwo[0 : width + 1, :])
    sums = jnp.concatenate(
        [jnp.sum(gtaps[8 * k : 8 * k + 8, :], axis=0, keepdims=True) for k in range(10)], axis=0
    )
    for q in range(hidden // width):
        put(bases["expand_weight"] + q, gwe[0 : width + 1, q * width : (q + 1) * width], hidden // width)
        put(bases["spatial_weight"] + q, sums[:, q * width : (q + 1) * width], hidden // width)
    for k in range(hidden // 128):
        put(bases["shrink_weight"] + 128 * k, gwst[:, 128 * k : 128 * k + 128].T)

def join_lines(read, write, low):
    turned = [pltpu.roll(read(1, k), 64, 1) for k in range(3)]
    write(0, read(0, 0))
    write(1, read(0, 1))
    write(2, jnp.where(low, read(0, 2), turned[0]))
    write(3, jnp.where(low, turned[0], turned[1]))
    write(4, jnp.where(low, turned[1], turned[2]))


def join_slot(wide, slot, slot_rows, line):
    pairs = slot_rows // 5

    def part(start, count):
        low = lax.broadcasted_iota(jnp.int32, (count, 128), 1) < 64

        def read(parity, k):
            return wide[k, pl.ds(slot * (2 * pairs) + 2 * start + parity, count, stride=2), :]

        def write(k, value):
            line[pl.ds(5 * start + k, count, stride=5), :] = value

        join_lines(read, write, low)

    part(0, pairs // 8 * 8)
    if pairs % 8:
        part(pairs // 8 * 8, pairs % 8)


def pack_kernel(order, slot_rows, bases, *refs):
    grads, (slots, flat, wide) = refs[:10], refs[10:]
    collect_gradients(bases, wide, *grads)
    done = wide.shape[1] * 5 // 2
    flat[done:, :] = jnp.zeros((flat.shape[0] - done, 128), F32)
    low = lax.broadcasted_iota(jnp.int32, (SPAN, 128), 1) < 64

    def regroup(t, _):
        def read(parity, k):
            return wide[k, pl.ds(t * (2 * SPAN) + parity, SPAN, stride=2), :]

        def write(k, value):
            flat[pl.ds(t * (5 * SPAN) + k, SPAN, stride=5), :] = value

        join_lines(read, write, low)
        return 0

    lax.fori_loop(0, wide.shape[1] // (2 * SPAN), regroup, 0)
    inside = lax.broadcasted_iota(jnp.int32, slots.shape[1:], 0) < slot_rows
    for slot, place in enumerate(order):
        slots[place] = jnp.where(inside, flat[pl.ds(slot * slot_rows, slots.shape[1]), :], 0.0).astype(BF)


def pack_gradients(grads, order, slot_rows, padded_rows, width):
    bases, count = row_bases(width, 4 * width)
    flat_rows = max(len(order) * slot_rows, wide_rows(count) * width // 128) + padded_rows
    return pl.pallas_call(
        partial(pack_kernel, order, slot_rows, bases),
        out_shape=jax.ShapeDtypeStruct((len(order), padded_rows, 128), BF),
        in_specs=[pl.BlockSpec(memory_space=pltpu.VMEM)] * len(grads),
        out_specs=pl.BlockSpec(memory_space=pltpu.VMEM),
        scratch_shapes=[pltpu.VMEM((flat_rows, 128), F32), pltpu.VMEM((3, wide_rows(count), 128), F32)],
        compiler_params=pltpu.CompilerParams(vmem_limit_bytes=VMEM_BYTES),
        name="pack_gradients",
    )(*grads)


def device_step(images, cotangent, kv_sides, w):
    positions = jnp.arange(TOKENS, dtype=jnp.int32)
    limit = 2 * kv_sides[:, None]
    mask = ((positions[None] // GRID < limit) & (positions[None] % GRID < limit)).astype(F32)
    mask = jnp.broadcast_to(mask[:, None, :], (mask.shape[0], 8, TOKENS))
    perm = jnp.asarray(patch_order(), BF)
    pre, patches, reduced, memory, mixed, lse, middle, post = attention_forward(
        kv_sides, images, mask, perm, w["vec"], w["rows"], w["wqt"], w["wr"], w["wk"], w["wvt"], w["wot"]
    )
    output, grad_post, gwe, gwst, gtaps, gbias = feed_forward(
        post, cotangent, mask, middle, w["we"], w["wst"], w["taps"], w["vec"]
    )
    grad_images, gwo, gwq, gpair, gwr, gcols, grows = attention_backward(
        kv_sides, images, cotangent, mask, pre, patches, reduced, memory, mixed, lse, middle, grad_post,
        perm, w["vec"], w["rows"], w["wq"], w["wqt"], w["wr"], w["wk"], w["wv"], w["wvt"], w["wo"],
    )
    return output, grad_images, (gwe, gwst, gtaps, gbias, gwo, gwq, gpair, gwr, gcols, grows)


def step(on_grid, images, cotangent, kv_sides, params, first_moment, second_moment):
    width = images.shape[2]
    axes = ("dp", "fsdp")
    outer, inner = lax.axis_size("dp"), lax.axis_size("fsdp")
    slot_rows = params.shape[0] // 128
    padded_rows = -(-slot_rows // 32) * 32
    own = jnp.pad(params.reshape(slot_rows, 128).astype(BF), ((0, padded_rows - slot_rows), (0, 0)))
    order = list(range(outer * inner))
    if on_grid:
        weights = gather_weights(own, slot_rows, width)
    else:
        weights = unpack_weights(lax.all_gather(own, axes), order, slot_rows, width)
    output, grad_images, grads = device_step(
        images.transpose(0, 2, 1), cotangent.transpose(0, 2, 1), kv_sides, weights
    )
    if on_grid:
        shard, squares = reduce_gradients(grads, slot_rows, padded_rows, width)
        squares = jnp.sum(squares)
    else:
        slots = pack_gradients(grads, order, slot_rows, padded_rows, width)
        shard = lax.psum_scatter(slots.astype(F32), axes)
        squares = lax.psum(jnp.sum(shard * shard), axes)
    shard = shard[:slot_rows].reshape(-1)
    grad_norm = jnp.sqrt(squares)
    clipped = shard * jnp.minimum(1.0, CLIP_NORM / (grad_norm + 1e-06))
    new_first = BETA_FIRST * first_moment + (1.0 - BETA_FIRST) * clipped
    new_second = BETA_SECOND * second_moment + (1.0 - BETA_SECOND) * clipped * clipped
    first_hat = new_first / (1.0 - BETA_FIRST**STEP)
    second_hat = new_second / (1.0 - BETA_SECOND**STEP)
    new_params = params - RATE * (first_hat / (jnp.sqrt(second_hat) + EPSILON) + DECAY * params)
    return (
        output.transpose(0, 2, 1),
        grad_images.transpose(0, 2, 1),
        grad_norm,
        new_first,
        new_second,
        new_params,
    )


def solution(mesh):
    data = P(("dp", "fsdp"), None, None)
    flat = P(("dp", "fsdp"))
    on_grid = dict(mesh.shape) == {"dp": 4, "fsdp": 8}
    return jax.shard_map(
        partial(step, on_grid),
        mesh=mesh,
        in_specs=(data, data, flat, flat, flat, flat),
        out_specs=(data, data, P(), flat, flat, flat),
        check_vma=False,
    )
```

```python
from functools import partial
import math

import jax
import jax.numpy as jnp
import numpy as np
from jax import lax
from jax.experimental import pallas as pl
from jax.experimental.pallas import tpu as pltpu
from jax.sharding import PartitionSpec as P

HEADS = 5
HEAD_DIM = 64
GRID = 48
KV = 24
STEP = 10

CLIP_NORM = 1.0
BETA_FIRST = 0.9
BETA_SECOND = 0.999
RATE = 0.04
DECAY = 0.05
EPSILON = 1e-08

F32 = jnp.float32
BF = jnp.bfloat16
NN = (((1,), (0,)), ((), ()))
NT = (((1,), (1,)), ((), ()))
TOKENS = GRID * GRID
KEYS = KV * KV
PITCH = GRID + 8
EXT = 16
DEPTH = 512
LOG2E = math.log2(math.e)
QUERY_SCALE = HEAD_DIM**-0.5 * LOG2E
GELU_A = math.sqrt(2.0 / math.pi)
GELU_B = GELU_A * 0.044715
VMEM_BYTES = 63 * 1024 * 1024


def mm(left, right, dims=NN):
    return lax.dot_general(left, right, dims, preferred_element_type=F32)


def patch_order():
    matrix = np.zeros((8 * GRID, 8 * GRID), np.float32)
    for p in range(4):
        for a in range(4):
            for b in range(KV):
                matrix[p * 96 + a * KV + b, (2 * a + p // 2) * GRID + 2 * b + p % 2] = 1.0
    return matrix


def fold_rows(x):
    return jnp.sum(x.reshape(x.shape[0] // 8, 8, x.shape[1]), axis=0)


def norm_columns(x):
    scale = 1.0 / x.shape[0]
    centred = x - jnp.sum(x, axis=0, keepdims=True) * scale
    rstd = lax.rsqrt(jnp.sum(centred * centred, axis=0, keepdims=True) * scale + 1e-06)
    return centred * rstd, rstd


def norm_columns_back(normed, rstd, scaled):
    scale = 1.0 / scaled.shape[0]
    plain = jnp.sum(scaled, axis=0, keepdims=True) * scale
    mixed = jnp.sum(scaled * normed, axis=0, keepdims=True) * scale
    return rstd * (scaled - plain - normed * mixed)


def norm_rows(x):
    centred = x - jnp.mean(x, axis=-1, keepdims=True)
    rstd = lax.rsqrt(jnp.mean(centred * centred, axis=-1, keepdims=True) + 1e-06)
    return centred * rstd, rstd


def norm_rows_back(normed, rstd, scaled):
    plain = jnp.mean(scaled, axis=-1, keepdims=True)
    mixed = jnp.mean(scaled * normed, axis=-1, keepdims=True)
    return rstd * (scaled - plain - normed * mixed)


def first_row(row, rows=EXT):
    index = lax.broadcasted_iota(jnp.int32, (rows, row.shape[-1]), 0)
    return jnp.where(index == 0, row, 0.0)


def three_parts(x):
    high = x.astype(BF).astype(F32)
    middle = (x - high).astype(BF).astype(F32)
    return high, middle, (x - high - middle).astype(BF).astype(F32)


def whole(x):
    zeros = (0,) * len(x.shape)
    return pl.BlockSpec(x.shape, lambda *_: zeros)


FAR = pl.BlockSpec(memory_space=pl.ANY)


def near(x):
    return pltpu.VMEM((1,) + tuple(x.shape[1:]), x.dtype)


def per_image(x, **kwargs):
    zeros = (0,) * (len(x.shape) - 1)
    return pl.BlockSpec((1,) + tuple(x.shape[1:]), lambda i, *_: (i,) + zeros, **kwargs)


def key_columns(ref, side, h_range, ones_from, ones_to, with_mask):
    lane = lax.broadcasted_iota(jnp.int32, (KV, 64), 1)
    cell = lax.broadcasted_iota(jnp.int32, (KV, 64), 0)
    ones = jnp.where((lane >= ones_from) & (lane <= ones_to), 1.0, 0.0)
    for a in range(KV):
        block = ones
        if with_mask:
            bias = jnp.where((cell < side) & (a < side), 0.0, -1e30)
            block = jnp.where(lane == 0, bias, ones)
        block = block.astype(BF)
        for h in h_range:
            ref[h, a * KV : (a + 1) * KV, 64:128] = block


def attention_forward_kernel(
    sides, images, mask, perm, vec, rows, wqt, wr, wk, wvt, wot,
    pre_far, patches_far, reduced_far, memory_far, mixed_far, lse, middle, post,
    pre, patches, reduced, memory, mixed, key_ref, value_ref, sems,
):
    i = pl.program_id(0)
    width = images.shape[1]
    far = (pre_far, patches_far, reduced_far, memory_far, mixed_far)
    kept = (pre, patches, reduced, memory, mixed)
    away = [pltpu.make_async_copy(y, x.at[pl.ds(i, 1)], sems.at[k]) for k, (x, y) in enumerate(zip(far, kept))]

    def first_norm(t, _):
        for u in range(3):
            at = pl.ds(pl.multiple_of(t * 384 + u * 128, 128), 128)
            x = images[0, :, at].astype(F32) * mask[0, 0:1, at]
            normed, _unused = norm_columns(x)
            pre[0, 0:width, at] = (normed * vec[0] + vec[1]).astype(BF)
            pre[0, width : width + EXT, at] = first_row(jnp.ones((1, 128), F32)).astype(BF)
        return 0

    lax.fori_loop(0, TOKENS // 384, first_norm, 0)
    for t in range(TOKENS // 384):
        picked = mm(perm[...], pre[0, 0:width, t * 384 : (t + 1) * 384], NT).astype(BF)
        for p in range(4):
            patches[0, p, t * 96 : (t + 1) * 96, :] = picked[p * 96 : (p + 1) * 96]
    away[0].start()
    away[1].start()

    total = rows[0:1, :]
    for p in range(4):
        total = total + mm(patches[0, p], wr[p])
    reduced[0] = total
    normed, _unused = norm_rows(total)
    memory[0, :, 0:width] = (normed * rows[1:2, :] + rows[2:3, :]).astype(BF)
    lane = lax.broadcasted_iota(jnp.int32, (KEYS, 64), 1)
    memory[0, :, width : width + 64] = jnp.where(lane == 0, 1.0, 0.0).astype(BF)
    away[2].start()
    away[3].start()
    keys = mm(memory[0, :, 0:width], wk[...]).astype(BF)
    key_columns(key_ref, sides[i], range(HEADS), 1, 0, True)
    values = mm(wvt[...], memory[0], NT).astype(BF)
    ones = first_row(jnp.ones((1, KEYS), F32)).astype(BF)
    for h in range(HEADS):
        at = slice(h * HEAD_DIM, (h + 1) * HEAD_DIM)
        key_ref[h, :, 0:HEAD_DIM] = keys[:, at]
        value_ref[h, 0:HEAD_DIM, :] = values[at]
        value_ref[h, HEAD_DIM : HEAD_DIM + EXT, :] = ones
    mixed[0, width : width + EXT, :] = first_row(jnp.ones((1, TOKENS), F32)).astype(BF)
    queries = (mm(wqt[...], pre[0]) * QUERY_SCALE).astype(BF)
    tail = first_row(jnp.ones((1, TOKENS), F32), 64).astype(BF)
    for h in range(HEADS):
        at = slice(h * HEAD_DIM, (h + 1) * HEAD_DIM)
        scores = mm(key_ref[h], jnp.concatenate([queries[at], tail], axis=0))
        top = jnp.max(scores, axis=0, keepdims=True)
        weights = jnp.exp2(scores - top).astype(BF)
        out = mm(value_ref[h], weights)
        total = out[HEAD_DIM : HEAD_DIM + 1]
        mixed[0, at, :] = (out[0:HEAD_DIM] * (1.0 / total)).astype(BF)
        lse[0, h : h + 1, :] = top + jnp.log2(total)

    away[4].start()
    middle[0] = mm(wot[...], mixed[0])

    def second_norm(t, _):
        for u in range(3):
            at = pl.ds(pl.multiple_of(t * 384 + u * 128, 128), 128)
            here = mask[0, 0:1, at]
            x = images[0, :, at].astype(F32) * here + middle[0, :, at]
            middle[0, :, at] = x
            normed, _unused = norm_columns(x)
            post[0, 0:width, at] = ((normed * vec[2] + vec[3]) * here).astype(BF)
            post[0, width : width + EXT, at] = first_row(here).astype(BF)
        return 0

    lax.fori_loop(0, TOKENS // 384, second_norm, 0)
    for copy in away:
        copy.wait()


def attention_forward(sides, images, mask, perm, vec, rows, wqt, wr, wk, wvt, wot):
    n, width, tokens = images.shape
    shape = jax.ShapeDtypeStruct
    outs = [
        shape((n, width + EXT, tokens), BF),
        shape((n, 4, KEYS, width), BF),
        shape((n, KEYS, width), F32),
        shape((n, KEYS, width + 64), BF),
        shape((n, width + EXT, tokens), BF),
        shape((n, 8, tokens), F32),
        shape((n, width, tokens), F32),
        shape((n, width + EXT, tokens), BF),
    ]
    weights = (perm, vec, rows, wqt, wr, wk, wvt, wot)
    return pl.pallas_call(
        attention_forward_kernel,
        grid_spec=pltpu.PrefetchScalarGridSpec(
            num_scalar_prefetch=1,
            grid=(n,),
            in_specs=[per_image(images), per_image(mask)] + [whole(x) for x in weights],
            out_specs=[FAR] * 5 + [per_image(x) for x in outs[5:]],
            scratch_shapes=[near(x) for x in outs[:5]]
            + [
                pltpu.VMEM((HEADS, KEYS, 128), BF),
                pltpu.VMEM((HEADS, HEAD_DIM + EXT, KEYS), BF),
                pltpu.SemaphoreType.DMA((5,)),
            ],
        ),
        out_shape=outs,
        compiler_params=pltpu.CompilerParams(vmem_limit_bytes=VMEM_BYTES),
        name="attention_forward",
    )(sides, images, mask, *weights)


def feed_forward_kernel(
    post_next, cot_next, mask_next, we_next, wst_next, taps,
    post, cot, mask, middle_far, we, wst, vec,
    output, grad_post, gwe, gwst, gtaps, gbias,
    padded_0, padded_1, grad_padded, grad_act, act_0, act_1, grad_exp_0, grad_exp_1,
    post_rows, out_grad_rows, out_grad, total, middle, middle_sem,
):
    s = pl.program_id(0)
    last = pl.num_programs(0) - 1
    width, block = cot.shape[1], wst.shape[1]
    blocks = gwst.shape[1] // block
    halves = block // 128
    rows = 16
    chunks = GRID // rows
    span = rows * GRID
    js = pl.ds(pl.multiple_of(lax.rem(s, blocks) * block, block), block)
    js_done = pl.ds(pl.multiple_of(lax.rem(jnp.maximum(s - 1, 0), blocks) * block, block), block)

    def tokens(t):
        return pl.ds(pl.multiple_of(t * span, span), span)

    def expand(t, padded, we, wst):
        at = tokens(t)
        filled = mm(post_rows[at, :], we[...])
        for h in range(halves):
            for r in range(rows):
                start = pl.multiple_of((t * rows + r + 1) * PITCH + 8, 8)
                padded[h, pl.ds(start, GRID), :] = filled[r * GRID : (r + 1) * GRID, h * 128 : (h + 1) * 128]
        grad_act[at, :] = mm(out_grad_rows[at, :], wst[...])

    def finish(t, act, grad_exp):
        at = tokens(t)
        total[:, at] += mm(wst[0:width, :], act[at, :], NT)
        grad_post[0, :, at] += mm(we[0:width, :], grad_exp[at, :], NT)
        gwst[:, js_done] += mm(out_grad[:, at], act[at, :])
        gwe[:, js_done] += mm(post[0, :, at], grad_exp[at, :])

    def convolve(t, padded, act):
        for h in range(halves):
            hs = slice(h * 128, (h + 1) * 128)
            w = [jnp.broadcast_to(0.5 * taps[k : k + 1, hs], (GRID, 128)).astype(BF) for k in range(10)]
            sums = jnp.zeros((8, 128), F32)
            open_rows = {}
            for q in range(-1, rows + 1):
                base = (t * rows + q + 1) * PITCH + 8
                x = [padded[h, pl.ds(base + d, GRID), :].astype(BF) for d in (-1, 0, 1)]
                for a in (2, 1, 0):
                    r = q + 1 - a
                    if 0 <= r < rows:
                        part = w[3 * a] * x[0] + w[3 * a + 1] * x[1] + w[3 * a + 2] * x[2]
                        open_rows[r] = part + open_rows.get(r, w[9])
                r = q - 1
                if r < 0:
                    continue
                at = pl.ds(pl.multiple_of((t * rows + r) * GRID, GRID), GRID)
                gelu, slope = gelu_pair(open_rows.pop(r))
                act[at, hs] = gelu
                grad = (grad_act[at, hs].astype(BF) * slope).astype(F32)
                start = pl.multiple_of((t * rows + r + 1) * PITCH + 8, 8)
                grad_padded[h, pl.ds(start, GRID), :] = grad
                sums = sums + fold_rows(grad)
            cols = pl.ds(pl.multiple_of(lax.rem(s, blocks) * block + h * 128, 128), 128)
            gtaps[72:80, cols] += sums

    def convolve_back(t, padded, grad_exp):
        for h in range(halves):
            hs = slice(h * 128, (h + 1) * 128)
            w = [jnp.broadcast_to(taps[k : k + 1, hs], (GRID, 128)).astype(BF) for k in range(9)]
            sums = [jnp.zeros((8, 128), F32) for _ in range(9)]
            waiting = {}
            open_rows = {}
            x = {}
            for q in range(-1, rows + 1):
                base = (t * rows + q + 1) * PITCH + 8
                grads = [grad_padded[h, pl.ds(base + 1 - b, GRID), :].astype(BF) for b in range(3)]
                if q + 1 < rows:
                    start = pl.multiple_of((t * rows + q + 2) * PITCH + 8, 8)
                    x[q + 1] = padded[h, pl.ds(start, GRID), :].astype(BF)
                for a in range(3):
                    r = q + a - 1
                    if not 0 <= r < rows:
                        continue
                    part = w[3 * a] * grads[0] + w[3 * a + 1] * grads[1] + w[3 * a + 2] * grads[2]
                    open_rows[r] = part + open_rows[r] if r in open_rows else part
                    for b in range(3):
                        k = 3 * a + b
                        product = x[r] * grads[b]
                        product = product[0:16] + product[16:32] + product[32:48]
                        waiting[k] = waiting[k] + product if k in waiting else product
                        if r % 4 == 3:
                            product = waiting.pop(k).astype(F32)
                            sums[k] = sums[k] + product[0:8] + product[8:16]
                r = q - 1
                if r >= 0:
                    at = pl.ds(pl.multiple_of((t * rows + r) * GRID, GRID), GRID)
                    grad_exp[at, hs] = open_rows.pop(r)
                    x.pop(r)
            cols = pl.ds(pl.multiple_of(lax.rem(s, blocks) * block + h * 128, 128), 128)
            for k in range(9):
                gtaps[8 * k : 8 * k + 8, cols] += sums[k]

    @pl.when(s == 0)
    def _():
        for ref in (act_1, grad_exp_1, out_grad, gwe, gwst, gtaps, gbias):
            ref[...] = jnp.zeros_like(ref)
        for ref in (post_rows, out_grad_rows):
            ref[:, 256:DEPTH] = jnp.zeros((TOKENS, DEPTH - 256), BF)
        for ref in (padded_0, padded_1, grad_padded):
            for h in range(halves):
                ref[h, 0 : PITCH + 8, :] = jnp.zeros((PITCH + 8, 128), F32)
                ref[h, (GRID + 1) * PITCH :, :] = jnp.zeros((PITCH + 8, 128), F32)
                for r in range(1, GRID):
                    ref[h, (r + 1) * PITCH : (r + 1) * PITCH + 8, :] = jnp.zeros((8, 128), F32)

    @pl.when((s == 0) | ((lax.rem(s + 1, blocks) == 0) & (s + 1 < last)))
    def _():
        for t in range(TOKENS // 384):
            at = slice(t * 384, (t + 1) * 384)
            grad = cot_next[0, :, at].astype(F32) * mask_next[0, 0:1, at]
            gbias[...] += grad[:, 0:128] + grad[:, 128:256] + grad[:, 256:384]
            out_grad_rows[at, 0:width] = (0.5 * grad).astype(BF).T
            post_rows[at, 0 : width + EXT] = post_next[0, :, at].T

    fetch = pltpu.make_async_copy(middle_far.at[pl.ds(jnp.maximum(s - 1, 0) // blocks, 1)], middle, middle_sem)

    @pl.when(lax.rem(s, blocks) == 1)
    def _():
        fetch.start()
        for t in range(TOKENS // 384):
            at = slice(t * 384, (t + 1) * 384)
            out_grad[:, at] = (cot[0, :, at].astype(F32) * mask[0, 0:1, at]).astype(BF)

    @pl.when((s == 0) | (lax.rem(s, blocks) == 1))
    def _():
        total[...] = jnp.zeros_like(total)
        grad_post[...] = jnp.zeros_like(grad_post)

    @pl.when(s == 0)
    def _():
        def first(t, _):
            expand(t, padded_0, we, wst)
            return 0

        lax.fori_loop(0, chunks, first, 0)

    def work(padded, padded_next, act, act_done, grad_exp, grad_exp_done):
        def forward(t, _):
            finish(t, act_done, grad_exp_done)
            convolve(t, padded, act)
            return 0

        def backward(t, _):
            expand(t, padded_next, we_next, wst_next)
            convolve_back(t, padded, grad_exp)
            return 0

        lax.fori_loop(0, chunks, forward, 0)
        lax.fori_loop(0, chunks, backward, 0)

    @pl.when((s < last) & (lax.rem(s, 2) == 0))
    def _():
        work(padded_0, padded_1, act_0, act_1, grad_exp_0, grad_exp_1)

    @pl.when((s < last) & (lax.rem(s, 2) == 1))
    def _():
        work(padded_1, padded_0, act_1, act_0, grad_exp_1, grad_exp_0)

    @pl.when(s == last)
    def _():
        def rest(t, _):
            @pl.when(lax.rem(s, 2) == 0)
            def _():
                finish(t, act_1, grad_exp_1)

            @pl.when(lax.rem(s, 2) == 1)
            def _():
                finish(t, act_0, grad_exp_0)

            return 0

        lax.fori_loop(0, chunks, rest, 0)

    @pl.when((s > 0) & (lax.rem(s, blocks) == 0))
    def _():
        fetch.wait()
        for t in range(TOKENS // 128):
            at = slice(t * 128, (t + 1) * 128)
            output[0, :, at] = ((middle[0, :, at] + total[:, at] + vec[4]) * mask[0, 0:1, at]).astype(BF)


def gelu_pair(half):
    kind = half.dtype.type
    square = half * half
    upper = jnp.tanh(half * (kind(8.0 * GELU_B) * square + kind(2.0 * GELU_A))) + kind(1.0)
    gelu = half * upper
    return gelu, upper + gelu * (kind(2.0) - upper) * (kind(24.0 * GELU_B) * square + kind(2.0 * GELU_A))


def feed_forward(post, cot, mask, middle, we, wst, taps, vec, block=256):
    n, width, tokens = cot.shape
    hidden = wst.shape[1]
    blocks = hidden // block
    count = n * blocks
    shape = jax.ShapeDtypeStruct
    outs = [
        shape((n, width, tokens), BF),
        shape((n, width, tokens), F32),
        shape((width + EXT, hidden), F32),
        shape((width, hidden), F32),
        shape((80, hidden), F32),
        shape((width, 128), F32),
    ]

    def ahead(s):
        return jnp.minimum(s + 1, count - 1)

    def behind(s):
        return jnp.maximum(s - 1, 0)

    def image(x, step):
        zeros = (0,) * (len(x.shape) - 1)
        return pl.BlockSpec((1,) + tuple(x.shape[1:]), lambda s: (step(s) // blocks,) + zeros)

    def columns(x, step):
        return pl.BlockSpec((x.shape[0], block), lambda s: (0, lax.rem(step(s), blocks)))

    return pl.pallas_call(
        feed_forward_kernel,
        grid=(count + 1,),
        in_specs=[image(x, ahead) for x in (post, cot, mask)]
        + [columns(we, ahead), columns(wst, ahead), columns(taps, lambda s: jnp.minimum(s, count - 1))]
        + [image(x, behind) for x in (post, cot, mask)]
        + [FAR, columns(we, behind), columns(wst, behind), whole(vec)],
        out_specs=[image(x, behind) for x in outs[:2]] + [whole(x) for x in outs[2:]],
        out_shape=outs,
        scratch_shapes=[pltpu.VMEM((block // 128, (GRID + 2) * PITCH + 8, 128), F32)] * 3
        + [pltpu.VMEM((tokens, block), F32)]
        + [pltpu.VMEM((tokens, block), BF)] * 4
        + [
            pltpu.VMEM((tokens, DEPTH), BF),
            pltpu.VMEM((tokens, DEPTH), BF),
            pltpu.VMEM((width, tokens), BF),
            pltpu.VMEM((width, tokens), F32),
            near(middle),
            pltpu.SemaphoreType.DMA(()),
        ],
        compiler_params=pltpu.CompilerParams(vmem_limit_bytes=VMEM_BYTES),
        name="feed_forward",
    )(post, cot, mask, we, wst, taps, post, cot, mask, middle, we, wst, vec)


def attention_backward_kernel(
    sides, mixed_far, pre_far, memory_far, reduced_far, patches_far, images_far, cot, mask, lse, middle, grad_post,
    perm, vec, rows, wq, wqt, wr, wk, wv, wvt, wo,
    grad_images, gwo, gwq, gpair, gwr, gcols, grows,
    branch, grad_mixed, queries, grad_queries, key_ref, value_ref, keys_t, grad_keys, grad_values, grad_patches,
    mixed, pre, memory, reduced, patches, images, sems,
):
    i = pl.program_id(0)
    width = cot.shape[1]
    far = (mixed_far, pre_far, memory_far, reduced_far, patches_far, images_far)
    kept = (mixed, pre, memory, reduced, patches, images)
    fetch = [pltpu.make_async_copy(x.at[pl.ds(i, 1)], y, sems.at[k]) for k, (x, y) in enumerate(zip(far, kept))]
    for copy in fetch:
        copy.start()

    @pl.when(i == 0)
    def _():
        for ref in (gwo, gwq, gpair, gwr, gcols, grows):
            ref[...] = jnp.zeros_like(ref)

    def mlp_norm_back(t, _):
        gain = shift = jnp.zeros((width, 128), F32)
        for u in range(3):
            at = pl.ds(pl.multiple_of(t * 384 + u * 128, 128), 128)
            here = mask[0, 0:1, at]
            normed, rstd = norm_columns(middle[0, :, at])
            grad = grad_post[0, :, at] * here
            gain = gain + grad * normed
            shift = shift + grad
            grad = cot[0, :, at].astype(F32) * here + norm_columns_back(normed, rstd, grad * vec[2])
            grad_images[0, :, at] = grad
            branch[:, at] = grad.astype(BF)
        gcols[2] += gain
        gcols[3] += shift
        return 0

    lax.fori_loop(0, TOKENS // 384, mlp_norm_back, 0)
    fetch[0].wait()
    gwo[...] += mm(mixed[0], branch[...], NT)
    grad_mixed[...] = mm(wo[...], branch[...]).astype(BF)
    fetch[1].wait()
    queries[...] = (mm(wqt[...], pre[0]) * QUERY_SCALE).astype(BF)
    fetch[2].wait()
    keys = mm(memory[0, :, 0:width], wk[...]).astype(BF)
    keys_t[...] = keys.T
    values = mm(wvt[...], memory[0], NT).astype(BF).T
    key_columns(key_ref, sides[i], range(HEADS), 1, 3, True)
    key_columns(value_ref, sides[i], range(HEADS), 1, 3, False)
    for h in range(HEADS):
        at = slice(h * HEAD_DIM, (h + 1) * HEAD_DIM)
        key_ref[h, :, 0:HEAD_DIM] = keys[:, at]
        value_ref[h, :, 0:HEAD_DIM] = values[:, at]

    span = TOKENS // 3
    index = lax.broadcasted_iota(jnp.int32, (64, span), 0)
    grad_values[...] = jnp.zeros_like(grad_values)
    grad_keys[...] = jnp.zeros_like(grad_keys)

    def part(t, _):
        at = pl.ds(pl.multiple_of(t * span, 128), span)
        for h in range(HEADS):
            hs = slice(h * HEAD_DIM, (h + 1) * HEAD_DIM)
            one, two, three = three_parts(-lse[0, h : h + 1, at])
            tail = jnp.where(index == 2, two, jnp.where(index == 3, three, 0.0))
            tail = jnp.where(index == 0, 1.0, jnp.where(index == 1, one, tail)).astype(BF)
            query = queries[hs, at]
            attend = jnp.exp2(mm(key_ref[h], jnp.concatenate([query, tail], axis=0)))
            low = attend.astype(BF)
            grad = grad_mixed[hs, at]
            inner = grad.astype(F32) * mixed[0, hs, at].astype(F32)
            one, two, three = three_parts(-jnp.sum(inner, axis=0, keepdims=True))
            tail = jnp.where(index == 2, two, jnp.where(index == 3, three, 0.0))
            tail = jnp.where(index == 1, one, tail).astype(BF)
            grad_attend = mm(value_ref[h], jnp.concatenate([grad, tail], axis=0))
            grad_scores = (attend * grad_attend).astype(BF)
            grad_values[hs, :] += mm(grad, low, NT)
            grad_keys[hs, :] += mm(query, grad_scores, NT) * (1.0 / LOG2E)
            grad_queries[hs, at] = (mm(keys_t[hs, :], grad_scores) * HEAD_DIM**-0.5).astype(BF)
        return 0

    lax.fori_loop(0, TOKENS // span, part, 0)

    low_keys = grad_keys[...].astype(BF)
    low_values = grad_values[...].astype(BF)
    gpair[0:width, :] += mm(low_keys, memory[0])
    gpair[width : 2 * width, :] += mm(low_values, memory[0])
    grad_memory = mm(low_keys.T, wk[...], NT) + mm(low_values.T, wv[...], NT)
    fetch[3].wait()
    normed, rstd = norm_rows(reduced[0])
    grows[8:16, :] += fold_rows(grad_memory * normed)
    grows[16:24, :] += fold_rows(grad_memory)
    grad_reduced = norm_rows_back(normed, rstd, grad_memory * rows[1:2, :]).astype(BF)
    grows[0:8, :] += fold_rows(grad_reduced.astype(F32))
    grad_reduced_t = grad_reduced.T
    fetch[4].wait()
    for p in range(4):
        gwr[p] += mm(grad_reduced_t, patches[0, p])
        grad_patches[p] = mm(grad_reduced, wr[p], NT).astype(BF)
    gwq[...] += mm(pre[0], grad_queries[...], NT)

    def pre_norm_back(t, _):
        at = pl.ds(pl.multiple_of(t * 384, 128), 384)
        grad_pre = mm(wq[...], grad_queries[:, at])
        start = pl.ds(pl.multiple_of(t * 96, 32), 96)
        picked = jnp.concatenate([grad_patches[p, start, :] for p in range(4)], axis=0)
        grad_pre = grad_pre + mm(picked.T, perm[...])
        gain = shift = jnp.zeros((width, 128), F32)
        for u in range(3):
            at = pl.ds(pl.multiple_of(t * 384 + u * 128, 128), 128)
            here = mask[0, 0:1, at]
            normed, rstd = norm_columns(images[0, :, at].astype(F32) * here)
            grad = grad_pre[:, u * 128 : (u + 1) * 128]
            gain = gain + grad * normed
            shift = shift + grad
            back = norm_columns_back(normed, rstd, grad * vec[0])
            grad_images[0, :, at] = (grad_images[0, :, at] + back) * here
        gcols[0] += gain
        gcols[1] += shift
        return 0

    fetch[5].wait()
    lax.fori_loop(0, TOKENS // 384, pre_norm_back, 0)


def attention_backward(
    sides, images, cot, mask, pre, patches, reduced, memory, mixed, lse, middle, grad_post,
    perm, vec, rows, wq, wqt, wr, wk, wv, wvt, wo,
):
    n, width, tokens = images.shape
    shape = jax.ShapeDtypeStruct
    outs = [
        shape((n, width, tokens), F32),
        shape((width + EXT, width), F32),
        shape((width + EXT, width), F32),
        shape((2 * width, width + 64), F32),
        shape((4, width, width), F32),
        shape((4, width, 128), F32),
        shape((24, width), F32),
    ]
    far = (mixed, pre, memory, reduced, patches, images)
    inputs = (cot, mask, lse, middle, grad_post)
    weights = (perm, vec, rows, wq, wqt, wr, wk, wv, wvt, wo)
    return pl.pallas_call(
        attention_backward_kernel,
        grid_spec=pltpu.PrefetchScalarGridSpec(
            num_scalar_prefetch=1,
            grid=(n,),
            in_specs=[FAR] * 6 + [per_image(x) for x in inputs] + [whole(x) for x in weights],
            out_specs=[per_image(outs[0])] + [whole(x) for x in outs[1:]],
            scratch_shapes=[
                pltpu.VMEM((width, tokens), BF),
                pltpu.VMEM((width, tokens), BF),
                pltpu.VMEM((width, tokens), BF),
                pltpu.VMEM((width, tokens), BF),
                pltpu.VMEM((HEADS, KEYS, 128), BF),
                pltpu.VMEM((HEADS, KEYS, 128), BF),
                pltpu.VMEM((width, KEYS), BF),
                pltpu.VMEM((width, KEYS), F32),
                pltpu.VMEM((width, KEYS), F32),
                pltpu.VMEM((4, KEYS, width), BF),
            ]
            + [near(x) for x in far]
            + [pltpu.SemaphoreType.DMA((6,))],
        ),
        out_shape=outs,
        compiler_params=pltpu.CompilerParams(vmem_limit_bytes=VMEM_BYTES),
        name="attention_backward",
    )(sides, *far, *inputs, *weights)

MESH = pl.DeviceIdType.MESH


class Place:
    def __init__(self):
        self.dp = lax.axis_index("dp")
        self.fsdp = lax.axis_index("fsdp")
        self.y, self.x = self.dp // 2, self.dp % 2
        self.z, self.core = self.fsdp // 2, self.fsdp % 2
        self.other_core = 1 - self.core
        self.beside_x = (self.dp + 1 - 2 * self.x, self.fsdp)
        self.beside_y = (self.dp + 2 - 4 * self.y, self.fsdp)
        self.across = (3 - self.dp, self.fsdp)
        self.beside_core = (self.dp, self.fsdp + 1 - 2 * self.core)
        self.others = (self.z + 1 - 2 * (self.z % 2), 2 - self.z // 2, 3 * (1 - self.z // 2))

    def at_z(self, z):
        return (self.dp, z * 2 + self.core)

    def along_z(self, k):
        return self.at_z((self.z + k) % 4)

    def call(self, partners):
        barrier = pltpu.get_barrier_semaphore()
        for device in partners:
            pl.semaphore_signal(barrier, inc=1, device_id=device, device_id_type=MESH)

    def answer(self, count):
        pl.semaphore_wait(pltpu.get_barrier_semaphore(), count)


class Sender:
    def __init__(self, send, recv):
        self.send, self.recv, self.started = send, recv, []

    def __call__(self, source, target, device, recv=None):
        k = len(self.started)
        copy = pltpu.make_async_remote_copy(
            src_ref=source,
            dst_ref=target,
            send_sem=self.send.at[k],
            recv_sem=self.recv.at[k] if recv is None else recv,
            device_id=device,
            device_id_type=MESH,
        )
        copy.start()
        self.started.append(copy)
        return copy

    def finish(self):
        for copy in self.started:
            copy.wait_send()


def gather_kernel(slot_rows, bases, params, *refs):
    outs, (own, slots, wide, line, own_sem, send_sem, recv_sem, z_sem) = refs[:13], refs[13:]
    me = Place()
    me.call([me.beside_core, me.beside_x, me.beside_y] + [me.at_z(z) for z in me.others])
    half = own.shape[0] // 2
    full = slot_rows // 16 * 16
    own[...] = jnp.zeros_like(own)
    own[0:full, :] = params[0:full, :].astype(BF)
    own[full:slot_rows, :] = params[full:slot_rows, :].astype(BF)
    first, second = pl.ds(0, half), pl.ds(half, half)
    send = Sender(send_sem, recv_sem)
    copy = pltpu.make_async_copy(own, slots.at[me.core, me.dp, me.z], own_sem)
    copy.start()
    me.answer(6)
    own_slot = slots.at[me.core, me.dp, me.z]

    def send_z(j):
        return send(own, own_slot, me.at_z(me.others[j]), z_sem.at[me.z])

    send_z(0)
    x_copies = [send(own, own_slot, me.beside_x)]
    y_copies = [send(own, own_slot, me.beside_y)]
    core_copies = [(send(own, own_slot, me.beside_core), me.dp, me.z)]
    send_z(1)
    half_copies = []
    order = (me.z,) + me.others

    def open_slot(core, dp, z):
        spread_slot(slots[core, dp, z], (dp * 8 + z * 2 + core), slot_rows, line, wide)

    def forward(k):
        z = order[k]
        x_copies[k].wait_recv()
        slot = slots.at[me.core, me.beside_x[0], z]
        half_copies.append(send(slot.at[first], slot.at[first], me.beside_y))
        core_copies.append((send(slot, slot, me.beside_core), me.beside_x[0], z))
        y_copies[k].wait_recv()
        slot = slots.at[me.core, me.beside_y[0], z]
        half_copies.append(send(slot.at[second], slot.at[second], me.beside_x))
        core_copies.append((send(slot, slot, me.beside_core), me.beside_y[0], z))
        open_slot(me.core, me.beside_x[0], z)
        open_slot(me.core, me.beside_y[0], z)

    copy.wait()
    open_slot(me.core, me.dp, me.z)
    forward(0)
    for k in (1, 2, 3):
        z = order[k]
        slot = slots.at[me.core, me.dp, z]
        pltpu.make_async_remote_copy(
            src_ref=own,
            dst_ref=slot,
            send_sem=send_sem.at[0],
            recv_sem=z_sem.at[z],
            device_id=me.at_z(z),
            device_id_type=MESH,
        ).wait_recv()
        x_copies.append(send(slot, slot, me.beside_x))
        y_copies.append(send(slot, slot, me.beside_y))
        core_copies.append((send(slot, slot, me.beside_core), me.dp, z))
        if k == 1:
            send_z(2)
        open_slot(me.core, me.dp, z)
        forward(k)
    for k in range(4):
        half_copies[2 * k].wait_recv()
        half_copies[2 * k + 1].wait_recv()
        slot = slots.at[me.core, me.across[0], order[k]]
        core_copies.append((send(slot, slot, me.beside_core), me.across[0], order[k]))
        open_slot(me.core, me.across[0], order[k])
    for copied, dp, z in core_copies:
        copied.wait_recv()
        open_slot(me.other_core, dp, z)
    send.finish()
    write_weights(bases, wide, *outs)


def gather_weights(params, rows, width):
    slot_rows = params.shape[0]
    bases, count = row_bases(width, 4 * width)
    outs = weight_shapes(width)
    copies = 35
    values = pl.pallas_call(
        partial(gather_kernel, slot_rows, bases),
        out_shape=list(outs.values()),
        in_specs=[pl.BlockSpec(memory_space=pltpu.VMEM)],
        out_specs=[pl.BlockSpec(memory_space=pltpu.VMEM)] * len(outs),
        scratch_shapes=[
            pltpu.VMEM((rows, 128), BF),
            pltpu.VMEM((2, 4, 4, rows, 128), BF),
            pltpu.VMEM((3, -(-32 * slot_rows * 128 // width // 8) * 8 + 8, 128), F32),
            pltpu.VMEM((rows, 128), F32),
            pltpu.SemaphoreType.DMA(()),
            pltpu.SemaphoreType.DMA((copies,)),
            pltpu.SemaphoreType.DMA((copies,)),
            pltpu.SemaphoreType.DMA((4,)),
        ],
        compiler_params=pltpu.CompilerParams(
            collective_id=0, has_side_effects=True, vmem_limit_bytes=VMEM_BYTES
        ),
        name="gather_weights",
    )(params)
    return dict(zip(outs, values, strict=True))


def reduce_kernel(slot_rows, bases, *refs):
    grads_far, (shard, squares), grads, fetch_sem = refs[:10], refs[10:12], refs[12:22], refs[22]
    wide, line, own, core_out, core_in, y_in, x_in, x_last, y_last, z_in, small, send_sem, recv_sem = refs[23:]
    me = Place()
    rows = shard.shape[0]
    half = rows // 2
    first, second = pl.ds(0, half), pl.ds(half, half)
    send = Sender(send_sem, recv_sem)
    peers = [(me.dp, (me.z + k) % 4 * 2 + core) for k in range(4) for core in (me.core, me.other_core)][1:]
    planes = [me.beside_x, me.beside_y, me.across]
    me.call(peers + planes)
    fetch = [pltpu.make_async_copy(x, y, fetch_sem.at[k]) for k, (x, y) in enumerate(zip(grads_far, grads))]
    for k in COLLECTED:
        fetch[k].start()
    collect_gradients(bases, wide, *grads, ready=lambda k: fetch[k].wait())
    line[...] = jnp.zeros_like(line)
    me.answer(len(peers + planes))
    units = [(me.z + k) % 4 for k in (2, 1, 3, 0)]
    core_copies, y_copies, x_copies, last = [], [], [], []
    other_x, other_y = 1 - me.x, 1 - me.y

    def give(k):
        z = units[k]
        for dp in range(4):
            join_slot(wide, dp * 8 + z * 2 + me.other_core, slot_rows, line)
            core_out[z, dp] = line[...].astype(BF)
        core_copies.append(send(core_out.at[z], core_in.at[z], me.beside_core))
        for dp in range(4):
            join_slot(wide, dp * 8 + z * 2 + me.core, slot_rows, line)
            own[z, dp] = line[...]

    def cores(k):
        z = units[k]
        core_copies[k].wait_recv()
        for dp in range(4):
            core_in[z, dp] = (core_in[z, dp].astype(F32) + own[z, dp]).astype(BF)
        y_copies.append(
            [send(core_in.at[z, 2 * other_y + x, first], y_in.at[z, x], me.beside_y) for x in range(2)]
        )
        x_copies.append(
            [send(core_in.at[z, 2 * y + other_x, second], x_in.at[z, y], me.beside_x) for y in range(2)]
        )

    def plane(k):
        z = units[k]
        for copied in y_copies[k]:
            copied.wait_recv()
        y_in[z, other_x] = (
            y_in[z, other_x].astype(F32) + core_in[z, 2 * me.y + other_x, first].astype(F32)
        ).astype(BF)
        to_x = send(y_in.at[z, other_x], x_last.at[z], me.beside_x)
        for copied in x_copies[k]:
            copied.wait_recv()
        x_in[z, other_y] = (
            x_in[z, other_y].astype(F32) + core_in[z, 2 * other_y + me.x, second].astype(F32)
        ).astype(BF)
        last.append((to_x, send(x_in.at[z, other_y], y_last.at[z], me.beside_y)))

    z_copies = []

    def column(k):
        z = units[k]
        for copied in last[k]:
            copied.wait_recv()
        low = y_in[z, me.x].astype(F32) + core_in[z, me.dp, first].astype(F32) + x_last[z].astype(F32)
        high = x_in[z, me.y].astype(F32) + core_in[z, me.dp, second].astype(F32) + y_last[z].astype(F32)
        if k == 3:
            shard[first, :] = low
            shard[second, :] = high
        else:
            z_in[k, first] = low.astype(BF)
            z_in[k, second] = high.astype(BF)
            z_copies.append(send(z_in.at[k], z_in.at[k + 3], me.at_z(z)))

    give(0)
    give(1)
    cores(0)
    give(2)
    cores(1)
    plane(0)
    give(3)
    cores(2)
    plane(1)
    column(0)
    cores(3)
    plane(2)
    column(1)
    plane(3)
    column(2)
    column(3)
    for k in (0, 1, 2):
        z_copies[k].wait_recv()
        shard[...] += z_in[k + 3].astype(F32)
    total = shard[0:8, :] * shard[0:8, :]
    for k in range(1, rows // 8):
        part = shard[8 * k : 8 * k + 8, :]
        total = total + part * part
    small[0] = total
    small[2 + me.fsdp] = total
    copies = [send(small.at[0], small.at[2 + me.fsdp], device) for device in peers]
    for copied in copies:
        copied.wait_recv()
    total = small[2]
    for k in range(1, 8):
        total = total + small[2 + k]
    small[1] = total
    small[10 + me.dp] = total
    copies = [send(small.at[1], small.at[10 + me.dp], device) for device in planes]
    for copied in copies:
        copied.wait_recv()
    squares[0, 0] = jnp.sum(((small[10] + small[11]) + small[12]) + small[13])
    send.finish()


def reduce_gradients(grads, slot_rows, rows, width):
    bases, _ = row_bases(width, 4 * width)
    half = rows // 2
    count = 4 + 16 + 8 + 3 + 7 + 3
    return pl.pallas_call(
        partial(reduce_kernel, slot_rows, bases),
        out_shape=[jax.ShapeDtypeStruct((rows, 128), F32), jax.ShapeDtypeStruct((1, 1), F32)],
        in_specs=[FAR] * len(grads),
        out_specs=[pl.BlockSpec(memory_space=pltpu.VMEM), pl.BlockSpec(memory_space=pltpu.SMEM)],
        scratch_shapes=[
            *[pltpu.VMEM(x.shape, x.dtype) for x in grads],
            pltpu.SemaphoreType.DMA((len(grads),)),
            pltpu.VMEM((3, -(-32 * slot_rows * 128 // width // 8) * 8 + 8, 128), F32),
            pltpu.VMEM((rows, 128), F32),
            pltpu.VMEM((4, 4, rows, 128), F32),
            pltpu.VMEM((4, 4, rows, 128), BF),
            pltpu.VMEM((4, 4, rows, 128), BF),
            pltpu.VMEM((4, 2, half, 128), BF),
            pltpu.VMEM((4, 2, half, 128), BF),
            pltpu.VMEM((4, half, 128), BF),
            pltpu.VMEM((4, half, 128), BF),
            pltpu.VMEM((6, rows, 128), BF),
            pltpu.VMEM((14, 8, 128), F32),
            pltpu.SemaphoreType.DMA((count,)),
            pltpu.SemaphoreType.DMA((count,)),
        ],
        compiler_params=pltpu.CompilerParams(
            collective_id=1, has_side_effects=True, vmem_limit_bytes=VMEM_BYTES
        ),
        name="reduce_gradients",
    )(*grads)


def layout_shapes(model_width, hidden_width):
    return [
        ("pre_gain", (model_width,)),
        ("pre_shift", (model_width,)),
        ("query_weight", (model_width, model_width)),
        ("query_bias", (model_width,)),
        ("reduce_weight", (4 * model_width, model_width)),
        ("reduce_bias", (model_width,)),
        ("reduce_gain", (model_width,)),
        ("reduce_shift", (model_width,)),
        ("pair_weight", (model_width, 2 * model_width)),
        ("value_bias", (model_width,)),
        ("output_weight", (model_width, model_width)),
        ("output_bias", (model_width,)),
        ("mlp_gain", (model_width,)),
        ("mlp_shift", (model_width,)),
        ("expand_weight", (model_width, hidden_width)),
        ("expand_bias", (hidden_width,)),
        ("spatial_weight", (9, hidden_width)),
        ("spatial_bias", (hidden_width,)),
        ("shrink_weight", (hidden_width, model_width)),
        ("shrink_bias", (model_width,)),
    ]


def row_bases(width, hidden):
    bases = {}
    row = 0
    for name, shape in layout_shapes(width, hidden):
        bases[name] = row
        row += math.prod(shape) // width
    return bases, row


SPAN = 96


def regroup_lines(read, write, low):
    part = [read(k) for k in range(5)]
    turned = [pltpu.roll(part[k], 64, 1) for k in (2, 3, 4)]
    for k in range(3):
        write(0, k, part[k])
    write(1, 0, jnp.where(low, turned[0], turned[1]))
    write(1, 1, jnp.where(low, turned[1], turned[2]))
    write(1, 2, turned[2])


def spread_slot(values, slot, slot_rows, line, wide):
    pairs = slot_rows // 5
    line[...] = values.astype(F32)

    def part(start, count):
        low = lax.broadcasted_iota(jnp.int32, (count, 128), 1) < 64

        def write(parity, k, value):
            wide[k, pl.ds(slot * (2 * pairs) + 2 * start + parity, count, stride=2), :] = value

        regroup_lines(lambda k: line[pl.ds(5 * start + k, count, stride=5), :], write, low)

    part(0, pairs // 8 * 8)
    if pairs % 8:
        part(pairs // 8 * 8, pairs % 8)


def unpack_kernel(order, slot_rows, bases, slots, *refs):
    outs, (flat, wide) = refs[:13], refs[13:]
    for slot, place in enumerate(order):
        flat[pl.ds(slot * slot_rows, slots.shape[1]), :] = slots[place].astype(F32)
    low = lax.broadcasted_iota(jnp.int32, (SPAN, 128), 1) < 64

    def regroup(t, _):
        def write(parity, k, value):
            wide[k, pl.ds(t * (2 * SPAN) + parity, SPAN, stride=2), :] = value

        regroup_lines(lambda k: flat[pl.ds(t * (5 * SPAN) + k, SPAN, stride=5), :], write, low)
        return 0

    lax.fori_loop(0, wide.shape[1] // (2 * SPAN), regroup, 0)
    write_weights(bases, wide, *outs)


def write_weights(bases, wide, vec, rows, wq, wqt, wr, wk, wv, wvt, wo, wot, we, wst, taps):
    width = wq.shape[0]
    hidden = wst.shape[1]

    def take(base, count, stride=1):
        at = pl.ds(base, count, stride=stride) if stride > 1 else pl.ds(base, count)
        return jnp.concatenate([wide[0, at, :], wide[1, at, :], wide[2, at, :][:, 0 : width - 256]], axis=1)

    def take_hidden(base, count):
        return jnp.concatenate([take(base + q, count, hidden // width) for q in range(hidden // width)], axis=1)

    def bordered(weight, bias, extra):
        index = lax.broadcasted_iota(jnp.int32, (extra, weight.shape[1]), 0)
        return jnp.concatenate([weight, jnp.where(index == 0, bias, 0.0)], axis=0)

    names = ("pre_gain", "pre_shift", "mlp_gain", "mlp_shift", "shrink_bias")
    for k, name in enumerate(names):
        vec[k] = jnp.broadcast_to(take(bases[name], 1), (128, width)).T
    for k, name in enumerate(("reduce_bias", "reduce_gain", "reduce_shift")):
        rows[k : k + 1, :] = take(bases[name], 1)
    query = take(bases["query_weight"], width)
    wq[...] = query.astype(BF)
    wqt[...] = bordered(query, take(bases["query_bias"], 1), EXT).T.astype(BF)
    for p in range(4):
        wr[p] = take(bases["reduce_weight"] + p * width, width).astype(BF)
    wk[...] = take(bases["pair_weight"], width, 2).astype(BF)
    value = take(bases["pair_weight"] + 1, width, 2)
    wv[...] = value.astype(BF)
    wvt[...] = bordered(value, take(bases["value_bias"], 1), 64).T.astype(BF)
    out = take(bases["output_weight"], width)
    wo[...] = out.astype(BF)
    wot[...] = bordered(out, take(bases["output_bias"], 1), EXT).T.astype(BF)
    we[0:width, :] = take_hidden(bases["expand_weight"], width).astype(BF)
    we[width:DEPTH, :] = first_row(take_hidden(bases["expand_bias"], 1), DEPTH - width).astype(BF)
    taps[0:9, :] = take_hidden(bases["spatial_weight"], 9)
    taps[9:10, :] = take_hidden(bases["spatial_bias"], 1)
    wst[width:DEPTH, :] = jnp.zeros((DEPTH - width, hidden), BF)
    for k in range(hidden // 128):
        wst[0:width, 128 * k : 128 * k + 128] = take(bases["shrink_weight"] + 128 * k, 128).T.astype(BF)


def wide_rows(count):
    return -(-count // (2 * SPAN)) * 2 * SPAN


def weight_shapes(width):
    hidden = 4 * width
    shape = jax.ShapeDtypeStruct
    return dict(
        vec=shape((5, width, 128), F32),
        rows=shape((3, width), F32),
        wq=shape((width, width), BF),
        wqt=shape((width, width + EXT), BF),
        wr=shape((4, width, width), BF),
        wk=shape((width, width), BF),
        wv=shape((width, width), BF),
        wvt=shape((width, width + 64), BF),
        wo=shape((width, width), BF),
        wot=shape((width, width + EXT), BF),
        we=shape((DEPTH, hidden), BF),
        wst=shape((DEPTH, hidden), BF),
        taps=shape((10, hidden), F32),
    )


def unpack_weights(slots, order, slot_rows, width):
    bases, count = row_bases(width, 4 * width)
    outs = weight_shapes(width)
    flat_rows = max(len(order) * slot_rows, wide_rows(count) * width // 128) + slots.shape[1]
    values = pl.pallas_call(
        partial(unpack_kernel, order, slot_rows, bases),
        out_shape=list(outs.values()),
        in_specs=[pl.BlockSpec(memory_space=pltpu.VMEM)],
        out_specs=[pl.BlockSpec(memory_space=pltpu.VMEM)] * len(outs),
        scratch_shapes=[pltpu.VMEM((flat_rows, 128), F32), pltpu.VMEM((3, wide_rows(count), 128), F32)],
        compiler_params=pltpu.CompilerParams(vmem_limit_bytes=VMEM_BYTES),
        name="unpack_weights",
    )(slots)
    return dict(zip(outs, values, strict=True))


COLLECTED = (8, 3, 9, 5, 7, 6, 4, 2, 0, 1)


def collect_gradients(bases, wide, gwe, gwst, gtaps, gbias, gwo, gwq, gpair, gwr, gcols, grows, ready=lambda k: None):
    width = gwst.shape[0]
    hidden = gwst.shape[1]
    used = bases["shrink_bias"] + 1
    for k in range(3):
        wide[k, pl.ds(used, wide.shape[1] - used), :] = jnp.zeros((wide.shape[1] - used, 128), F32)

    def put(base, value, stride=1):
        count = value.shape[0]
        at = pl.ds(base, count, stride=stride) if stride > 1 else pl.ds(base, count)
        wide[0, at, :] = value[:, 0:128]
        wide[1, at, :] = value[:, 128:256]
        wide[2, at, 0 : width - 256] = value[:, 256:width]

    ready(8)
    for k, name in enumerate(("pre_gain", "pre_shift", "mlp_gain", "mlp_shift")):
        put(bases[name], jnp.sum(gcols[k].T, axis=0, keepdims=True))
    ready(3)
    put(bases["shrink_bias"], jnp.sum(gbias[...].T, axis=0, keepdims=True))
    ready(9)
    for k, name in enumerate(("reduce_bias", "reduce_gain", "reduce_shift")):
        put(bases[name], jnp.sum(grows[8 * k : 8 * k + 8, :], axis=0, keepdims=True))
    ready(5)
    put(bases["query_weight"], gwq[0 : width + 1, :])
    ready(7)
    for p in range(4):
        put(bases["reduce_weight"] + p * width, gwr[p].T)
    ready(6)
    put(bases["pair_weight"], gpair[0:width, :].T[0:width], 2)
    value = gpair[width : 2 * width, :].T
    put(bases["pair_weight"] + 1, value[0:width], 2)
    put(bases["value_bias"], value[width : width + 1])
    ready(4)
    put(bases["output_weight"], gwo[0 : width + 1, :])
    ready(2)
    sums = jnp.concatenate(
        [jnp.sum(gtaps[8 * k : 8 * k + 8, :], axis=0, keepdims=True) for k in range(10)], axis=0
    )
    ready(0)
    for q in range(hidden // width):
        put(bases["expand_weight"] + q, gwe[0 : width + 1, q * width : (q + 1) * width], hidden // width)
        put(bases["spatial_weight"] + q, sums[:, q * width : (q + 1) * width], hidden // width)
    ready(1)
    for k in range(hidden // 128):
        put(bases["shrink_weight"] + 128 * k, gwst[:, 128 * k : 128 * k + 128].T)

def join_lines(read, write, low):
    turned = [pltpu.roll(read(1, k), 64, 1) for k in range(3)]
    write(0, read(0, 0))
    write(1, read(0, 1))
    write(2, jnp.where(low, read(0, 2), turned[0]))
    write(3, jnp.where(low, turned[0], turned[1]))
    write(4, jnp.where(low, turned[1], turned[2]))


def join_slot(wide, slot, slot_rows, line):
    pairs = slot_rows // 5

    def part(start, count):
        low = lax.broadcasted_iota(jnp.int32, (count, 128), 1) < 64

        def read(parity, k):
            return wide[k, pl.ds(slot * (2 * pairs) + 2 * start + parity, count, stride=2), :]

        def write(k, value):
            line[pl.ds(5 * start + k, count, stride=5), :] = value

        join_lines(read, write, low)

    part(0, pairs // 8 * 8)
    if pairs % 8:
        part(pairs // 8 * 8, pairs % 8)


def pack_kernel(order, slot_rows, bases, *refs):
    grads, (slots, flat, wide) = refs[:10], refs[10:]
    collect_gradients(bases, wide, *grads)
    done = wide.shape[1] * 5 // 2
    flat[done:, :] = jnp.zeros((flat.shape[0] - done, 128), F32)
    low = lax.broadcasted_iota(jnp.int32, (SPAN, 128), 1) < 64

    def regroup(t, _):
        def read(parity, k):
            return wide[k, pl.ds(t * (2 * SPAN) + parity, SPAN, stride=2), :]

        def write(k, value):
            flat[pl.ds(t * (5 * SPAN) + k, SPAN, stride=5), :] = value

        join_lines(read, write, low)
        return 0

    lax.fori_loop(0, wide.shape[1] // (2 * SPAN), regroup, 0)
    inside = lax.broadcasted_iota(jnp.int32, slots.shape[1:], 0) < slot_rows
    for slot, place in enumerate(order):
        slots[place] = jnp.where(inside, flat[pl.ds(slot * slot_rows, slots.shape[1]), :], 0.0).astype(BF)


def pack_gradients(grads, order, slot_rows, padded_rows, width):
    bases, count = row_bases(width, 4 * width)
    flat_rows = max(len(order) * slot_rows, wide_rows(count) * width // 128) + padded_rows
    return pl.pallas_call(
        partial(pack_kernel, order, slot_rows, bases),
        out_shape=jax.ShapeDtypeStruct((len(order), padded_rows, 128), BF),
        in_specs=[pl.BlockSpec(memory_space=pltpu.VMEM)] * len(grads),
        out_specs=pl.BlockSpec(memory_space=pltpu.VMEM),
        scratch_shapes=[pltpu.VMEM((flat_rows, 128), F32), pltpu.VMEM((3, wide_rows(count), 128), F32)],
        compiler_params=pltpu.CompilerParams(vmem_limit_bytes=VMEM_BYTES),
        name="pack_gradients",
    )(*grads)


def device_step(images, cotangent, kv_sides, w):
    positions = jnp.arange(TOKENS, dtype=jnp.int32)
    limit = 2 * kv_sides[:, None]
    mask = ((positions[None] // GRID < limit) & (positions[None] % GRID < limit)).astype(F32)
    mask = mask[:, None, :]
    perm = jnp.asarray(patch_order(), BF)
    pre, patches, reduced, memory, mixed, lse, middle, post = attention_forward(
        kv_sides, images, mask, perm, w["vec"], w["rows"], w["wqt"], w["wr"], w["wk"], w["wvt"], w["wot"]
    )
    output, grad_post, gwe, gwst, gtaps, gbias = feed_forward(
        post, cotangent, mask, middle, w["we"], w["wst"], w["taps"], w["vec"]
    )
    grad_images, gwo, gwq, gpair, gwr, gcols, grows = attention_backward(
        kv_sides, images, cotangent, mask, pre, patches, reduced, memory, mixed, lse, middle, grad_post,
        perm, w["vec"], w["rows"], w["wq"], w["wqt"], w["wr"], w["wk"], w["wv"], w["wvt"], w["wo"],
    )
    return output, grad_images, (gwe, gwst, gtaps, gbias, gwo, gwq, gpair, gwr, gcols, grows)


def step(on_grid, images, cotangent, kv_sides, params, first_moment, second_moment):
    width = images.shape[2]
    axes = ("dp", "fsdp")
    outer, inner = lax.axis_size("dp"), lax.axis_size("fsdp")
    slot_rows = params.shape[0] // 128
    padded_rows = -(-slot_rows // 32) * 32
    order = list(range(outer * inner))
    if on_grid:
        weights = gather_weights(params.reshape(slot_rows, 128), padded_rows, width)
    else:
        own = jnp.pad(params.reshape(slot_rows, 128).astype(BF), ((0, padded_rows - slot_rows), (0, 0)))
        weights = unpack_weights(lax.all_gather(own, axes), order, slot_rows, width)
    output, grad_images, grads = device_step(
        images.transpose(0, 2, 1), cotangent.transpose(0, 2, 1), kv_sides, weights
    )
    if on_grid:
        shard, squares = reduce_gradients(grads, slot_rows, padded_rows, width)
        squares = squares[0, 0]
    else:
        slots = pack_gradients(grads, order, slot_rows, padded_rows, width)
        shard = lax.psum_scatter(slots.astype(F32), axes)
        squares = lax.psum(jnp.sum(shard * shard), axes)
    shard = shard[:slot_rows].reshape(-1)
    grad_norm = jnp.sqrt(squares)
    clipped = shard * jnp.minimum(1.0, CLIP_NORM / (grad_norm + 1e-06))
    new_first = BETA_FIRST * first_moment + (1.0 - BETA_FIRST) * clipped
    new_second = BETA_SECOND * second_moment + (1.0 - BETA_SECOND) * clipped * clipped
    first_hat = new_first / (1.0 - BETA_FIRST**STEP)
    second_hat = new_second / (1.0 - BETA_SECOND**STEP)
    new_params = params - RATE * (first_hat / (jnp.sqrt(second_hat) + EPSILON) + DECAY * params)
    return (
        output.transpose(0, 2, 1),
        grad_images.transpose(0, 2, 1),
        grad_norm,
        new_first,
        new_second,
        new_params,
    )


def solution(mesh):
    data = P(("dp", "fsdp"), None, None)
    flat = P(("dp", "fsdp"))
    on_grid = dict(mesh.shape) == {"dp": 4, "fsdp": 8}
    return jax.shard_map(
        partial(step, on_grid),
        mesh=mesh,
        in_specs=(data, data, flat, flat, flat, flat),
        out_specs=(data, data, P(), flat, flat, flat),
        check_vma=False,
    )
```

```python
from functools import partial
import math

import jax
import jax.numpy as jnp
import numpy as np
from jax import lax
from jax.experimental import pallas as pl
from jax.experimental.pallas import tpu as pltpu
from jax.sharding import PartitionSpec as P

HEADS = 5
HEAD_DIM = 64
GRID = 48
KV = 24
STEP = 10

CLIP_NORM = 1.0
BETA_FIRST = 0.9
BETA_SECOND = 0.999
RATE = 0.04
DECAY = 0.05
EPSILON = 1e-08

F32 = jnp.float32
BF = jnp.bfloat16
NN = (((1,), (0,)), ((), ()))
NT = (((1,), (1,)), ((), ()))
TOKENS = GRID * GRID
KEYS = KV * KV
PITCH = GRID + 8
EXT = 16
DEPTH = 512
LOG2E = math.log2(math.e)
QUERY_SCALE = HEAD_DIM**-0.5 * LOG2E
GELU_A = math.sqrt(2.0 / math.pi)
GELU_B = GELU_A * 0.044715
VMEM_BYTES = 63 * 1024 * 1024


def mm(left, right, dims=NN):
    return lax.dot_general(left, right, dims, preferred_element_type=F32)


def patch_order():
    matrix = np.zeros((8 * GRID, 8 * GRID), np.float32)
    for p in range(4):
        for a in range(4):
            for b in range(KV):
                matrix[p * 96 + a * KV + b, (2 * a + p // 2) * GRID + 2 * b + p % 2] = 1.0
    return matrix


def fold_rows(x):
    return jnp.sum(x.reshape(x.shape[0] // 8, 8, x.shape[1]), axis=0)


def norm_columns(x):
    scale = 1.0 / x.shape[0]
    centred = x - jnp.sum(x, axis=0, keepdims=True) * scale
    rstd = lax.rsqrt(jnp.sum(centred * centred, axis=0, keepdims=True) * scale + 1e-06)
    return centred * rstd, rstd


def norm_columns_back(normed, rstd, scaled):
    scale = 1.0 / scaled.shape[0]
    plain = jnp.sum(scaled, axis=0, keepdims=True) * scale
    mixed = jnp.sum(scaled * normed, axis=0, keepdims=True) * scale
    return rstd * (scaled - plain - normed * mixed)


def norm_rows(x):
    centred = x - jnp.mean(x, axis=-1, keepdims=True)
    rstd = lax.rsqrt(jnp.mean(centred * centred, axis=-1, keepdims=True) + 1e-06)
    return centred * rstd, rstd


def norm_rows_back(normed, rstd, scaled):
    plain = jnp.mean(scaled, axis=-1, keepdims=True)
    mixed = jnp.mean(scaled * normed, axis=-1, keepdims=True)
    return rstd * (scaled - plain - normed * mixed)


def first_row(row, rows=EXT):
    index = lax.broadcasted_iota(jnp.int32, (rows, row.shape[-1]), 0)
    return jnp.where(index == 0, row, 0.0)


def three_parts(x):
    high = x.astype(BF).astype(F32)
    middle = (x - high).astype(BF).astype(F32)
    return high, middle, (x - high - middle).astype(BF).astype(F32)


def whole(x):
    zeros = (0,) * len(x.shape)
    return pl.BlockSpec(x.shape, lambda *_: zeros)


FAR = pl.BlockSpec(memory_space=pl.ANY)


def near(x):
    return pltpu.VMEM((1,) + tuple(x.shape[1:]), x.dtype)


def per_image(x, **kwargs):
    zeros = (0,) * (len(x.shape) - 1)
    return pl.BlockSpec((1,) + tuple(x.shape[1:]), lambda i, *_: (i,) + zeros, **kwargs)


def key_columns(ref, side, h_range, ones_from, ones_to, with_mask):
    lane = lax.broadcasted_iota(jnp.int32, (KV, 64), 1)
    cell = lax.broadcasted_iota(jnp.int32, (KV, 64), 0)
    ones = jnp.where((lane >= ones_from) & (lane <= ones_to), 1.0, 0.0)
    for a in range(KV):
        block = ones
        if with_mask:
            bias = jnp.where((cell < side) & (a < side), 0.0, -1e30)
            block = jnp.where(lane == 0, bias, ones)
        block = block.astype(BF)
        for h in h_range:
            ref[h, a * KV : (a + 1) * KV, 64:128] = block


def attention_forward_kernel(
    sides, images, mask, perm, vec, rows, wqt, wr, wk, wvt, wot,
    pre_far, patches_far, reduced_far, memory_far, mixed_far, lse, middle, post,
    pre, patches, reduced, memory, mixed, key_ref, value_ref, sems,
):
    i = pl.program_id(0)
    width = images.shape[1]
    far = (pre_far, patches_far, reduced_far, memory_far, mixed_far)
    kept = (pre, patches, reduced, memory, mixed)
    away = [pltpu.make_async_copy(y, x.at[pl.ds(i, 1)], sems.at[k]) for k, (x, y) in enumerate(zip(far, kept))]

    def first_norm(t, _):
        for u in range(3):
            at = pl.ds(pl.multiple_of(t * 384 + u * 128, 128), 128)
            x = images[0, :, at].astype(F32) * mask[0, 0:1, at]
            normed, _unused = norm_columns(x)
            pre[0, 0:width, at] = (normed * vec[0] + vec[1]).astype(BF)
            pre[0, width : width + EXT, at] = first_row(jnp.ones((1, 128), F32)).astype(BF)
        return 0

    lax.fori_loop(0, TOKENS // 384, first_norm, 0)
    for t in range(TOKENS // 384):
        picked = mm(perm[...], pre[0, 0:width, t * 384 : (t + 1) * 384], NT).astype(BF)
        for p in range(4):
            patches[0, p, t * 96 : (t + 1) * 96, :] = picked[p * 96 : (p + 1) * 96]
    away[0].start()
    away[1].start()

    total = rows[0:1, :]
    for p in range(4):
        total = total + mm(patches[0, p], wr[p])
    reduced[0] = total
    normed, _unused = norm_rows(total)
    memory[0, :, 0:width] = (normed * rows[1:2, :] + rows[2:3, :]).astype(BF)
    lane = lax.broadcasted_iota(jnp.int32, (KEYS, 64), 1)
    memory[0, :, width : width + 64] = jnp.where(lane == 0, 1.0, 0.0).astype(BF)
    away[2].start()
    away[3].start()
    keys = mm(memory[0, :, 0:width], wk[...]).astype(BF)
    key_columns(key_ref, sides[i], range(HEADS), 1, 0, True)
    values = mm(wvt[...], memory[0], NT).astype(BF)
    ones = first_row(jnp.ones((1, KEYS), F32)).astype(BF)
    for h in range(HEADS):
        at = slice(h * HEAD_DIM, (h + 1) * HEAD_DIM)
        key_ref[h, :, 0:HEAD_DIM] = keys[:, at]
        value_ref[h, 0:HEAD_DIM, :] = values[at]
        value_ref[h, HEAD_DIM : HEAD_DIM + EXT, :] = ones
    mixed[0, width : width + EXT, :] = first_row(jnp.ones((1, TOKENS), F32)).astype(BF)
    queries = (mm(wqt[...], pre[0]) * QUERY_SCALE).astype(BF)
    tail = first_row(jnp.ones((1, TOKENS), F32), 64).astype(BF)
    for h in range(HEADS):
        at = slice(h * HEAD_DIM, (h + 1) * HEAD_DIM)
        scores = mm(key_ref[h], jnp.concatenate([queries[at], tail], axis=0))
        top = jnp.max(scores, axis=0, keepdims=True)
        weights = jnp.exp2(scores - top).astype(BF)
        out = mm(value_ref[h], weights)
        total = out[HEAD_DIM : HEAD_DIM + 1]
        mixed[0, at, :] = (out[0:HEAD_DIM] * (1.0 / total)).astype(BF)
        lse[0, h : h + 1, :] = top + jnp.log2(total)

    away[4].start()
    middle[0] = mm(wot[...], mixed[0])

    def second_norm(t, _):
        for u in range(3):
            at = pl.ds(pl.multiple_of(t * 384 + u * 128, 128), 128)
            here = mask[0, 0:1, at]
            x = images[0, :, at].astype(F32) * here + middle[0, :, at]
            middle[0, :, at] = x
            normed, _unused = norm_columns(x)
            post[0, 0:width, at] = ((normed * vec[2] + vec[3]) * here).astype(BF)
            post[0, width : width + EXT, at] = first_row(here).astype(BF)
        return 0

    lax.fori_loop(0, TOKENS // 384, second_norm, 0)
    for copy in away:
        copy.wait()


def attention_forward(sides, images, mask, perm, vec, rows, wqt, wr, wk, wvt, wot):
    n, width, tokens = images.shape
    shape = jax.ShapeDtypeStruct
    outs = [
        shape((n, width + EXT, tokens), BF),
        shape((n, 4, KEYS, width), BF),
        shape((n, KEYS, width), F32),
        shape((n, KEYS, width + 64), BF),
        shape((n, width + EXT, tokens), BF),
        shape((n, 8, tokens), F32),
        shape((n, width, tokens), F32),
        shape((n, width + EXT, tokens), BF),
    ]
    weights = (perm, vec, rows, wqt, wr, wk, wvt, wot)
    return pl.pallas_call(
        attention_forward_kernel,
        grid_spec=pltpu.PrefetchScalarGridSpec(
            num_scalar_prefetch=1,
            grid=(n,),
            in_specs=[per_image(images), per_image(mask)] + [whole(x) for x in weights],
            out_specs=[FAR] * 5 + [per_image(x) for x in outs[5:]],
            scratch_shapes=[near(x) for x in outs[:5]]
            + [
                pltpu.VMEM((HEADS, KEYS, 128), BF),
                pltpu.VMEM((HEADS, HEAD_DIM + EXT, KEYS), BF),
                pltpu.SemaphoreType.DMA((5,)),
            ],
        ),
        out_shape=outs,
        compiler_params=pltpu.CompilerParams(vmem_limit_bytes=VMEM_BYTES),
        name="attention_forward",
    )(sides, images, mask, *weights)


def feed_forward_kernel(
    post_next, cot_next, mask_next, we_next, wst_next, taps,
    post, cot, mask, middle_far, we, wst, vec,
    output, grad_post, gwe, gwst, gtaps, gbias,
    padded_0, padded_1, grad_padded, grad_act, act_0, act_1, grad_exp_0, grad_exp_1,
    post_rows, out_grad_rows, out_grad, total, middle, middle_sem,
):
    s = pl.program_id(0)
    last = pl.num_programs(0) - 1
    width, block = cot.shape[1], wst.shape[1]
    blocks = gwst.shape[1] // block
    halves = block // 128
    rows = 16
    chunks = GRID // rows
    span = rows * GRID
    js = pl.ds(pl.multiple_of(lax.rem(s, blocks) * block, block), block)
    js_done = pl.ds(pl.multiple_of(lax.rem(jnp.maximum(s - 1, 0), blocks) * block, block), block)

    def tokens(t):
        return pl.ds(pl.multiple_of(t * span, span), span)

    def expand(t, padded, we, wst):
        at = tokens(t)
        filled = mm(post_rows[at, :], we[...])
        for h in range(halves):
            for r in range(rows):
                start = pl.multiple_of((t * rows + r + 1) * PITCH + 8, 8)
                padded[h, pl.ds(start, GRID), :] = filled[r * GRID : (r + 1) * GRID, h * 128 : (h + 1) * 128]
        grad_act[at, :] = mm(out_grad_rows[at, :], wst[...])

    def finish(t, act, grad_exp):
        at = tokens(t)
        gwst[:, js_done] += mm(out_grad[:, at], act[at, :])
        gwe[:, js_done] += mm(post[0, :, at], grad_exp[at, :])

    def finish_rest(t, act, grad_exp):
        at = tokens(t)
        total[:, at] += mm(wst[0:width, :], act[at, :], NT)
        grad_post[0, :, at] += mm(we[0:width, :], grad_exp[at, :], NT)

    def convolve(t, padded, act):
        for h in range(halves):
            hs = slice(h * 128, (h + 1) * 128)
            w = [jnp.broadcast_to(0.5 * taps[k : k + 1, hs], (GRID, 128)).astype(BF) for k in range(10)]
            sums = jnp.zeros((8, 128), F32)
            open_rows = {}
            for q in range(-1, rows + 1):
                base = (t * rows + q + 1) * PITCH + 8
                x = [padded[h, pl.ds(base + d, GRID), :].astype(BF) for d in (-1, 0, 1)]
                for a in (2, 1, 0):
                    r = q + 1 - a
                    if 0 <= r < rows:
                        part = w[3 * a] * x[0] + w[3 * a + 1] * x[1] + w[3 * a + 2] * x[2]
                        open_rows[r] = part + open_rows.get(r, w[9])
                r = q - 1
                if r < 0:
                    continue
                at = pl.ds(pl.multiple_of((t * rows + r) * GRID, GRID), GRID)
                gelu, slope = gelu_pair(open_rows.pop(r))
                act[at, hs] = gelu
                grad = (grad_act[at, hs].astype(BF) * slope).astype(F32)
                start = pl.multiple_of((t * rows + r + 1) * PITCH + 8, 8)
                grad_padded[h, pl.ds(start, GRID), :] = grad
                sums = sums + fold_rows(grad)
            cols = pl.ds(pl.multiple_of(lax.rem(s, blocks) * block + h * 128, 128), 128)
            gtaps[72:80, cols] += sums

    def convolve_back(t, padded, grad_exp):
        for h in range(halves):
            hs = slice(h * 128, (h + 1) * 128)
            w = [jnp.broadcast_to(taps[k : k + 1, hs], (GRID, 128)).astype(BF) for k in range(9)]
            sums = [jnp.zeros((8, 128), F32) for _ in range(9)]
            waiting = {}
            open_rows = {}
            x = {}
            for q in range(-1, rows + 1):
                base = (t * rows + q + 1) * PITCH + 8
                grads = [grad_padded[h, pl.ds(base + 1 - b, GRID), :].astype(BF) for b in range(3)]
                if q + 1 < rows:
                    start = pl.multiple_of((t * rows + q + 2) * PITCH + 8, 8)
                    x[q + 1] = padded[h, pl.ds(start, GRID), :].astype(BF)
                for a in range(3):
                    r = q + a - 1
                    if not 0 <= r < rows:
                        continue
                    part = w[3 * a] * grads[0] + w[3 * a + 1] * grads[1] + w[3 * a + 2] * grads[2]
                    open_rows[r] = part + open_rows[r] if r in open_rows else part
                    for b in range(3):
                        k = 3 * a + b
                        product = x[r] * grads[b]
                        product = product[0:16] + product[16:32] + product[32:48]
                        waiting[k] = waiting[k] + product if k in waiting else product
                        if r % 4 == 3:
                            product = waiting.pop(k).astype(F32)
                            sums[k] = sums[k] + product[0:8] + product[8:16]
                r = q - 1
                if r >= 0:
                    at = pl.ds(pl.multiple_of((t * rows + r) * GRID, GRID), GRID)
                    grad_exp[at, hs] = open_rows.pop(r)
                    x.pop(r)
            cols = pl.ds(pl.multiple_of(lax.rem(s, blocks) * block + h * 128, 128), 128)
            for k in range(9):
                gtaps[8 * k : 8 * k + 8, cols] += sums[k]

    @pl.when(s == 0)
    def _():
        for ref in (act_1, grad_exp_1, out_grad, gwe, gwst, gtaps, gbias):
            ref[...] = jnp.zeros_like(ref)
        for ref in (post_rows, out_grad_rows):
            ref[:, 256:DEPTH] = jnp.zeros((TOKENS, DEPTH - 256), BF)
        for ref in (padded_0, padded_1, grad_padded):
            for h in range(halves):
                ref[h, 0 : PITCH + 8, :] = jnp.zeros((PITCH + 8, 128), F32)
                ref[h, (GRID + 1) * PITCH :, :] = jnp.zeros((PITCH + 8, 128), F32)
                for r in range(1, GRID):
                    ref[h, (r + 1) * PITCH : (r + 1) * PITCH + 8, :] = jnp.zeros((8, 128), F32)

    @pl.when((s == 0) | ((lax.rem(s + 1, blocks) == 0) & (s + 1 < last)))
    def _():
        for t in range(TOKENS // 384):
            at = slice(t * 384, (t + 1) * 384)
            grad = cot_next[0, :, at].astype(F32) * mask_next[0, 0:1, at]
            gbias[...] += grad[:, 0:128] + grad[:, 128:256] + grad[:, 256:384]
            out_grad_rows[at, 0:width] = (0.5 * grad).astype(BF).T
            post_rows[at, 0 : width + EXT] = post_next[0, :, at].T

    fetch = pltpu.make_async_copy(middle_far.at[pl.ds(jnp.maximum(s - 1, 0) // blocks, 1)], middle, middle_sem)

    @pl.when(lax.rem(s, blocks) == 1)
    def _():
        fetch.start()
        for t in range(TOKENS // 384):
            at = slice(t * 384, (t + 1) * 384)
            out_grad[:, at] = (cot[0, :, at].astype(F32) * mask[0, 0:1, at]).astype(BF)

    @pl.when((s == 0) | (lax.rem(s, blocks) == 1))
    def _():
        total[...] = jnp.zeros_like(total)
        grad_post[...] = jnp.zeros_like(grad_post)

    @pl.when(s == 0)
    def _():
        def first(t, _):
            expand(t, padded_0, we, wst)
            return 0

        lax.fori_loop(0, chunks, first, 0)

    def work(padded, padded_next, act, act_done, grad_exp, grad_exp_done):
        def forward(t, _):
            finish(t, act_done, grad_exp_done)
            convolve(t, padded, act)
            return 0

        def backward(t, _):
            expand(t, padded_next, we_next, wst_next)
            finish_rest(t, act_done, grad_exp_done)
            convolve_back(t, padded, grad_exp)
            return 0

        lax.fori_loop(0, chunks, forward, 0)
        lax.fori_loop(0, chunks, backward, 0)

    @pl.when((s < last) & (lax.rem(s, 2) == 0))
    def _():
        work(padded_0, padded_1, act_0, act_1, grad_exp_0, grad_exp_1)

    @pl.when((s < last) & (lax.rem(s, 2) == 1))
    def _():
        work(padded_1, padded_0, act_1, act_0, grad_exp_1, grad_exp_0)

    @pl.when(s == last)
    def _():
        def rest(t, _):
            @pl.when(lax.rem(s, 2) == 0)
            def _():
                finish(t, act_1, grad_exp_1)
                finish_rest(t, act_1, grad_exp_1)

            @pl.when(lax.rem(s, 2) == 1)
            def _():
                finish(t, act_0, grad_exp_0)
                finish_rest(t, act_0, grad_exp_0)

            return 0

        lax.fori_loop(0, chunks, rest, 0)

    @pl.when((s > 0) & (lax.rem(s, blocks) == 0))
    def _():
        fetch.wait()
        for t in range(TOKENS // 128):
            at = slice(t * 128, (t + 1) * 128)
            output[0, :, at] = ((middle[0, :, at] + total[:, at] + vec[4]) * mask[0, 0:1, at]).astype(BF)


def gelu_pair(half):
    kind = half.dtype.type
    square = half * half
    upper = jnp.tanh(half * (kind(8.0 * GELU_B) * square + kind(2.0 * GELU_A))) + kind(1.0)
    gelu = half * upper
    return gelu, upper + gelu * (kind(2.0) - upper) * (kind(24.0 * GELU_B) * square + kind(2.0 * GELU_A))


def feed_forward(post, cot, mask, middle, we, wst, taps, vec, block=256):
    n, width, tokens = cot.shape
    hidden = wst.shape[1]
    blocks = hidden // block
    count = n * blocks
    shape = jax.ShapeDtypeStruct
    outs = [
        shape((n, width, tokens), BF),
        shape((n, width, tokens), F32),
        shape((width + EXT, hidden), F32),
        shape((width, hidden), F32),
        shape((80, hidden), F32),
        shape((width, 128), F32),
    ]

    def ahead(s):
        return jnp.minimum(s + 1, count - 1)

    def behind(s):
        return jnp.maximum(s - 1, 0)

    def image(x, step):
        zeros = (0,) * (len(x.shape) - 1)
        return pl.BlockSpec((1,) + tuple(x.shape[1:]), lambda s: (step(s) // blocks,) + zeros)

    def columns(x, step):
        return pl.BlockSpec((x.shape[0], block), lambda s: (0, lax.rem(step(s), blocks)))

    return pl.pallas_call(
        feed_forward_kernel,
        grid=(count + 1,),
        in_specs=[image(x, ahead) for x in (post, cot, mask)]
        + [columns(we, ahead), columns(wst, ahead), columns(taps, lambda s: jnp.minimum(s, count - 1))]
        + [image(x, behind) for x in (post, cot, mask)]
        + [FAR, columns(we, behind), columns(wst, behind), whole(vec)],
        out_specs=[image(x, behind) for x in outs[:2]] + [whole(x) for x in outs[2:]],
        out_shape=outs,
        scratch_shapes=[pltpu.VMEM((block // 128, (GRID + 2) * PITCH + 8, 128), F32)] * 3
        + [pltpu.VMEM((tokens, block), F32)]
        + [pltpu.VMEM((tokens, block), BF)] * 4
        + [
            pltpu.VMEM((tokens, DEPTH), BF),
            pltpu.VMEM((tokens, DEPTH), BF),
            pltpu.VMEM((width, tokens), BF),
            pltpu.VMEM((width, tokens), F32),
            near(middle),
            pltpu.SemaphoreType.DMA(()),
        ],
        compiler_params=pltpu.CompilerParams(vmem_limit_bytes=VMEM_BYTES),
        name="feed_forward",
    )(post, cot, mask, we, wst, taps, post, cot, mask, middle, we, wst, vec)


def attention_backward_kernel(
    sides, mixed_far, pre_far, memory_far, reduced_far, patches_far, images_far, cot, mask, lse, middle, grad_post,
    perm, vec, rows, wq, wqt, wr, wk, wv, wvt, wo,
    grad_images, gwo, gwq, gpair, gwr, gcols, grows,
    branch, grad_mixed, queries, grad_queries, key_ref, value_ref, keys_t, grad_keys, grad_values, grad_patches,
    mixed, pre, memory, reduced, patches, images, sems,
):
    i = pl.program_id(0)
    width = cot.shape[1]
    far = (mixed_far, pre_far, memory_far, reduced_far, patches_far, images_far)
    kept = (mixed, pre, memory, reduced, patches, images)
    fetch = [pltpu.make_async_copy(x.at[pl.ds(i, 1)], y, sems.at[k]) for k, (x, y) in enumerate(zip(far, kept))]
    for copy in fetch:
        copy.start()

    @pl.when(i == 0)
    def _():
        for ref in (gwo, gwq, gpair, gwr, gcols, grows):
            ref[...] = jnp.zeros_like(ref)

    def mlp_norm_back(t, _):
        gain = shift = jnp.zeros((width, 128), F32)
        for u in range(3):
            at = pl.ds(pl.multiple_of(t * 384 + u * 128, 128), 128)
            here = mask[0, 0:1, at]
            normed, rstd = norm_columns(middle[0, :, at])
            grad = grad_post[0, :, at] * here
            gain = gain + grad * normed
            shift = shift + grad
            grad = cot[0, :, at].astype(F32) * here + norm_columns_back(normed, rstd, grad * vec[2])
            grad_images[0, :, at] = grad
            branch[:, at] = grad.astype(BF)
        gcols[2] += gain
        gcols[3] += shift
        return 0

    lax.fori_loop(0, TOKENS // 384, mlp_norm_back, 0)
    fetch[0].wait()
    gwo[...] += mm(mixed[0], branch[...], NT)
    grad_mixed[...] = mm(wo[...], branch[...]).astype(BF)
    fetch[1].wait()
    queries[...] = (mm(wqt[...], pre[0]) * QUERY_SCALE).astype(BF)
    fetch[2].wait()
    keys = mm(memory[0, :, 0:width], wk[...]).astype(BF)
    keys_t[...] = keys.T
    values = mm(wvt[...], memory[0], NT).astype(BF).T
    key_columns(key_ref, sides[i], range(HEADS), 1, 3, True)
    key_columns(value_ref, sides[i], range(HEADS), 1, 3, False)
    for h in range(HEADS):
        at = slice(h * HEAD_DIM, (h + 1) * HEAD_DIM)
        key_ref[h, :, 0:HEAD_DIM] = keys[:, at]
        value_ref[h, :, 0:HEAD_DIM] = values[:, at]

    span = TOKENS // 3
    index = lax.broadcasted_iota(jnp.int32, (64, span), 0)
    grad_values[...] = jnp.zeros_like(grad_values)
    grad_keys[...] = jnp.zeros_like(grad_keys)

    def part(t, _):
        at = pl.ds(pl.multiple_of(t * span, 128), span)
        for h in range(HEADS):
            hs = slice(h * HEAD_DIM, (h + 1) * HEAD_DIM)
            one, two, three = three_parts(-lse[0, h : h + 1, at])
            tail = jnp.where(index == 2, two, jnp.where(index == 3, three, 0.0))
            tail = jnp.where(index == 0, 1.0, jnp.where(index == 1, one, tail)).astype(BF)
            query = queries[hs, at]
            attend = jnp.exp2(mm(key_ref[h], jnp.concatenate([query, tail], axis=0)))
            low = attend.astype(BF)
            grad = grad_mixed[hs, at]
            inner = grad.astype(F32) * mixed[0, hs, at].astype(F32)
            one, two, three = three_parts(-jnp.sum(inner, axis=0, keepdims=True))
            tail = jnp.where(index == 2, two, jnp.where(index == 3, three, 0.0))
            tail = jnp.where(index == 1, one, tail).astype(BF)
            grad_attend = mm(value_ref[h], jnp.concatenate([grad, tail], axis=0))
            grad_scores = (attend * grad_attend).astype(BF)
            grad_values[hs, :] += mm(grad, low, NT)
            grad_keys[hs, :] += mm(query, grad_scores, NT) * (1.0 / LOG2E)
            grad_queries[hs, at] = (mm(keys_t[hs, :], grad_scores) * HEAD_DIM**-0.5).astype(BF)
        return 0

    lax.fori_loop(0, TOKENS // span, part, 0)

    low_keys = grad_keys[...].astype(BF)
    low_values = grad_values[...].astype(BF)
    gpair[0:width, :] += mm(low_keys, memory[0])
    gpair[width : 2 * width, :] += mm(low_values, memory[0])
    grad_memory = mm(low_keys.T, wk[...], NT) + mm(low_values.T, wv[...], NT)
    fetch[3].wait()
    normed, rstd = norm_rows(reduced[0])
    grows[8:16, :] += fold_rows(grad_memory * normed)
    grows[16:24, :] += fold_rows(grad_memory)
    grad_reduced = norm_rows_back(normed, rstd, grad_memory * rows[1:2, :]).astype(BF)
    grows[0:8, :] += fold_rows(grad_reduced.astype(F32))
    grad_reduced_t = grad_reduced.T
    fetch[4].wait()
    for p in range(4):
        gwr[p] += mm(grad_reduced_t, patches[0, p])
        grad_patches[p] = mm(grad_reduced, wr[p], NT).astype(BF)
    gwq[...] += mm(pre[0], grad_queries[...], NT)

    def pre_norm_back(t, _):
        at = pl.ds(pl.multiple_of(t * 384, 128), 384)
        grad_pre = mm(wq[...], grad_queries[:, at])
        start = pl.ds(pl.multiple_of(t * 96, 32), 96)
        picked = jnp.concatenate([grad_patches[p, start, :] for p in range(4)], axis=0)
        grad_pre = grad_pre + mm(picked.T, perm[...])
        gain = shift = jnp.zeros((width, 128), F32)
        for u in range(3):
            at = pl.ds(pl.multiple_of(t * 384 + u * 128, 128), 128)
            here = mask[0, 0:1, at]
            normed, rstd = norm_columns(images[0, :, at].astype(F32) * here)
            grad = grad_pre[:, u * 128 : (u + 1) * 128]
            gain = gain + grad * normed
            shift = shift + grad
            back = norm_columns_back(normed, rstd, grad * vec[0])
            grad_images[0, :, at] = (grad_images[0, :, at] + back) * here
        gcols[0] += gain
        gcols[1] += shift
        return 0

    fetch[5].wait()
    lax.fori_loop(0, TOKENS // 384, pre_norm_back, 0)


def attention_backward(
    sides, images, cot, mask, pre, patches, reduced, memory, mixed, lse, middle, grad_post,
    perm, vec, rows, wq, wqt, wr, wk, wv, wvt, wo,
):
    n, width, tokens = images.shape
    shape = jax.ShapeDtypeStruct
    outs = [
        shape((n, width, tokens), F32),
        shape((width + EXT, width), F32),
        shape((width + EXT, width), F32),
        shape((2 * width, width + 64), F32),
        shape((4, width, width), F32),
        shape((4, width, 128), F32),
        shape((24, width), F32),
    ]
    far = (mixed, pre, memory, reduced, patches, images)
    inputs = (cot, mask, lse, middle, grad_post)
    weights = (perm, vec, rows, wq, wqt, wr, wk, wv, wvt, wo)
    return pl.pallas_call(
        attention_backward_kernel,
        grid_spec=pltpu.PrefetchScalarGridSpec(
            num_scalar_prefetch=1,
            grid=(n,),
            in_specs=[FAR] * 6 + [per_image(x) for x in inputs] + [whole(x) for x in weights],
            out_specs=[per_image(outs[0])] + [whole(x) for x in outs[1:]],
            scratch_shapes=[
                pltpu.VMEM((width, tokens), BF),
                pltpu.VMEM((width, tokens), BF),
                pltpu.VMEM((width, tokens), BF),
                pltpu.VMEM((width, tokens), BF),
                pltpu.VMEM((HEADS, KEYS, 128), BF),
                pltpu.VMEM((HEADS, KEYS, 128), BF),
                pltpu.VMEM((width, KEYS), BF),
                pltpu.VMEM((width, KEYS), F32),
                pltpu.VMEM((width, KEYS), F32),
                pltpu.VMEM((4, KEYS, width), BF),
            ]
            + [near(x) for x in far]
            + [pltpu.SemaphoreType.DMA((6,))],
        ),
        out_shape=outs,
        compiler_params=pltpu.CompilerParams(vmem_limit_bytes=VMEM_BYTES),
        name="attention_backward",
    )(sides, *far, *inputs, *weights)

MESH = pl.DeviceIdType.MESH


class Place:
    def __init__(self):
        self.dp = lax.axis_index("dp")
        self.fsdp = lax.axis_index("fsdp")
        self.y, self.x = self.dp // 2, self.dp % 2
        self.z, self.core = self.fsdp // 2, self.fsdp % 2
        self.other_core = 1 - self.core
        self.beside_x = (self.dp + 1 - 2 * self.x, self.fsdp)
        self.beside_y = (self.dp + 2 - 4 * self.y, self.fsdp)
        self.across = (3 - self.dp, self.fsdp)
        self.beside_core = (self.dp, self.fsdp + 1 - 2 * self.core)
        self.others = (self.z + 1 - 2 * (self.z % 2), 2 - self.z // 2, 3 * (1 - self.z // 2))

    def at_z(self, z):
        return (self.dp, z * 2 + self.core)

    def along_z(self, k):
        return self.at_z((self.z + k) % 4)

    def call(self, partners):
        barrier = pltpu.get_barrier_semaphore()
        for device in partners:
            pl.semaphore_signal(barrier, inc=1, device_id=device, device_id_type=MESH)

    def answer(self, count):
        pl.semaphore_wait(pltpu.get_barrier_semaphore(), count)


class Sender:
    def __init__(self, send, recv):
        self.send, self.recv, self.started = send, recv, []

    def __call__(self, source, target, device, recv=None):
        k = len(self.started)
        copy = pltpu.make_async_remote_copy(
            src_ref=source,
            dst_ref=target,
            send_sem=self.send.at[k],
            recv_sem=self.recv.at[k] if recv is None else recv,
            device_id=device,
            device_id_type=MESH,
        )
        copy.start()
        self.started.append(copy)
        return copy

    def finish(self):
        for copy in self.started:
            copy.wait_send()


def gather_kernel(slot_rows, bases, params, *refs):
    outs, (own, slots, wide, line, own_sem, send_sem, recv_sem, z_sem) = refs[:13], refs[13:]
    me = Place()
    me.call([me.beside_core, me.beside_x, me.beside_y] + [me.at_z(z) for z in me.others])
    half = own.shape[0] // 2
    full = slot_rows // 16 * 16
    own[...] = jnp.zeros_like(own)
    own[0:full, :] = params[0:full, :].astype(BF)
    own[full:slot_rows, :] = params[full:slot_rows, :].astype(BF)
    first, second = pl.ds(0, half), pl.ds(half, half)
    send = Sender(send_sem, recv_sem)
    copy = pltpu.make_async_copy(own, slots.at[me.core, me.dp, me.z], own_sem)
    copy.start()
    me.answer(6)
    own_slot = slots.at[me.core, me.dp, me.z]

    def send_z(j):
        return send(own, own_slot, me.at_z(me.others[j]), z_sem.at[me.z])

    send_z(0)
    x_copies = [send(own, own_slot, me.beside_x)]
    y_copies = [send(own, own_slot, me.beside_y)]
    core_copies = [(send(own, own_slot, me.beside_core), me.dp, me.z)]
    send_z(1)
    half_copies = []
    order = (me.z,) + me.others

    def open_slot(core, dp, z):
        spread_slot(slots[core, dp, z], (dp * 8 + z * 2 + core), slot_rows, line, wide)

    def forward(k):
        z = order[k]
        x_copies[k].wait_recv()
        slot = slots.at[me.core, me.beside_x[0], z]
        half_copies.append(send(slot.at[first], slot.at[first], me.beside_y))
        core_copies.append((send(slot, slot, me.beside_core), me.beside_x[0], z))
        y_copies[k].wait_recv()
        slot = slots.at[me.core, me.beside_y[0], z]
        half_copies.append(send(slot.at[second], slot.at[second], me.beside_x))
        core_copies.append((send(slot, slot, me.beside_core), me.beside_y[0], z))
        open_slot(me.core, me.beside_x[0], z)
        open_slot(me.core, me.beside_y[0], z)

    copy.wait()
    open_slot(me.core, me.dp, me.z)
    forward(0)
    for k in (1, 2, 3):
        z = order[k]
        slot = slots.at[me.core, me.dp, z]
        pltpu.make_async_remote_copy(
            src_ref=own,
            dst_ref=slot,
            send_sem=send_sem.at[0],
            recv_sem=z_sem.at[z],
            device_id=me.at_z(z),
            device_id_type=MESH,
        ).wait_recv()
        x_copies.append(send(slot, slot, me.beside_x))
        y_copies.append(send(slot, slot, me.beside_y))
        core_copies.append((send(slot, slot, me.beside_core), me.dp, z))
        if k == 1:
            send_z(2)
        open_slot(me.core, me.dp, z)
        forward(k)
    for k in range(4):
        half_copies[2 * k].wait_recv()
        half_copies[2 * k + 1].wait_recv()
        slot = slots.at[me.core, me.across[0], order[k]]
        core_copies.append((send(slot, slot, me.beside_core), me.across[0], order[k]))
        open_slot(me.core, me.across[0], order[k])
    for copied, dp, z in core_copies:
        copied.wait_recv()
        open_slot(me.other_core, dp, z)
    send.finish()
    write_weights(bases, wide, *outs)


def gather_weights(params, rows, width):
    slot_rows = params.shape[0]
    bases, count = row_bases(width, 4 * width)
    outs = weight_shapes(width)
    copies = 35
    values = pl.pallas_call(
        partial(gather_kernel, slot_rows, bases),
        out_shape=list(outs.values()),
        in_specs=[pl.BlockSpec(memory_space=pltpu.VMEM)],
        out_specs=[pl.BlockSpec(memory_space=pltpu.VMEM)] * len(outs),
        scratch_shapes=[
            pltpu.VMEM((rows, 128), BF),
            pltpu.VMEM((2, 4, 4, rows, 128), BF),
            pltpu.VMEM((3, -(-32 * slot_rows * 128 // width // 8) * 8 + 8, 128), F32),
            pltpu.VMEM((rows, 128), F32),
            pltpu.SemaphoreType.DMA(()),
            pltpu.SemaphoreType.DMA((copies,)),
            pltpu.SemaphoreType.DMA((copies,)),
            pltpu.SemaphoreType.DMA((4,)),
        ],
        compiler_params=pltpu.CompilerParams(
            collective_id=0, has_side_effects=True, vmem_limit_bytes=VMEM_BYTES
        ),
        name="gather_weights",
    )(params)
    return dict(zip(outs, values, strict=True))


def reduce_kernel(slot_rows, bases, *refs):
    grads_far, (shard, squares), grads, fetch_sem = refs[:10], refs[10:12], refs[12:22], refs[22]
    wide, line, own, core_out, core_in, y_in, x_in, x_last, y_last, z_in, small, send_sem, recv_sem = refs[23:]
    me = Place()
    rows = shard.shape[0]
    half = rows // 2
    first, second = pl.ds(0, half), pl.ds(half, half)
    send = Sender(send_sem, recv_sem)
    peers = [(me.dp, (me.z + k) % 4 * 2 + core) for k in range(4) for core in (me.core, me.other_core)][1:]
    planes = [me.beside_x, me.beside_y, me.across]
    me.call(peers + planes)
    fetch = [pltpu.make_async_copy(x, y, fetch_sem.at[k]) for k, (x, y) in enumerate(zip(grads_far, grads))]
    for k in COLLECTED:
        fetch[k].start()
    collect_gradients(bases, wide, *grads, ready=lambda k: fetch[k].wait())
    line[...] = jnp.zeros_like(line)
    me.answer(len(peers + planes))
    units = [(me.z + k) % 4 for k in (2, 1, 3, 0)]
    core_copies, y_copies, x_copies, last = [], [], [], []
    other_x, other_y = 1 - me.x, 1 - me.y

    def give(k):
        z = units[k]
        for dp in range(4):
            join_slot(wide, dp * 8 + z * 2 + me.other_core, slot_rows, line)
            core_out[z, dp] = line[...].astype(BF)
        core_copies.append(send(core_out.at[z], core_in.at[z], me.beside_core))
        for dp in range(4):
            join_slot(wide, dp * 8 + z * 2 + me.core, slot_rows, line)
            own[z, dp] = line[...]

    def cores(k):
        z = units[k]
        core_copies[k].wait_recv()
        for dp in range(4):
            core_in[z, dp] = (core_in[z, dp].astype(F32) + own[z, dp]).astype(BF)
        y_copies.append(
            [send(core_in.at[z, 2 * other_y + x, first], y_in.at[z, x], me.beside_y) for x in range(2)]
        )
        x_copies.append(
            [send(core_in.at[z, 2 * y + other_x, second], x_in.at[z, y], me.beside_x) for y in range(2)]
        )

    def plane(k):
        z = units[k]
        for copied in y_copies[k]:
            copied.wait_recv()
        y_in[z, other_x] = (
            y_in[z, other_x].astype(F32) + core_in[z, 2 * me.y + other_x, first].astype(F32)
        ).astype(BF)
        to_x = send(y_in.at[z, other_x], x_last.at[z], me.beside_x)
        for copied in x_copies[k]:
            copied.wait_recv()
        x_in[z, other_y] = (
            x_in[z, other_y].astype(F32) + core_in[z, 2 * other_y + me.x, second].astype(F32)
        ).astype(BF)
        last.append((to_x, send(x_in.at[z, other_y], y_last.at[z], me.beside_y)))

    z_copies = []

    def column(k):
        z = units[k]
        for copied in last[k]:
            copied.wait_recv()
        low = y_in[z, me.x].astype(F32) + core_in[z, me.dp, first].astype(F32) + x_last[z].astype(F32)
        high = x_in[z, me.y].astype(F32) + core_in[z, me.dp, second].astype(F32) + y_last[z].astype(F32)
        if k == 3:
            shard[first, :] = low
            shard[second, :] = high
        else:
            z_in[k, first] = low.astype(BF)
            z_in[k, second] = high.astype(BF)
            z_copies.append(send(z_in.at[k], z_in.at[k + 3], me.at_z(z)))

    give(0)
    give(1)
    cores(0)
    give(2)
    cores(1)
    plane(0)
    give(3)
    cores(2)
    plane(1)
    column(0)
    cores(3)
    plane(2)
    column(1)
    plane(3)
    column(2)
    column(3)
    for k in (0, 1, 2):
        z_copies[k].wait_recv()
        shard[...] += z_in[k + 3].astype(F32)
    total = shard[0:8, :] * shard[0:8, :]
    for k in range(1, rows // 8):
        part = shard[8 * k : 8 * k + 8, :]
        total = total + part * part
    small[0] = total
    small[2 + me.fsdp] = total
    copies = [send(small.at[0], small.at[2 + me.fsdp], device) for device in peers]
    for copied in copies:
        copied.wait_recv()
    total = small[2]
    for k in range(1, 8):
        total = total + small[2 + k]
    small[1] = total
    small[10 + me.dp] = total
    copies = [send(small.at[1], small.at[10 + me.dp], device) for device in planes]
    for copied in copies:
        copied.wait_recv()
    squares[0, 0] = jnp.sum(((small[10] + small[11]) + small[12]) + small[13])
    send.finish()


def reduce_gradients(grads, slot_rows, rows, width):
    bases, _ = row_bases(width, 4 * width)
    half = rows // 2
    count = 4 + 16 + 8 + 3 + 7 + 3
    return pl.pallas_call(
        partial(reduce_kernel, slot_rows, bases),
        out_shape=[jax.ShapeDtypeStruct((rows, 128), F32), jax.ShapeDtypeStruct((1, 1), F32)],
        in_specs=[FAR] * len(grads),
        out_specs=[pl.BlockSpec(memory_space=pltpu.VMEM), pl.BlockSpec(memory_space=pltpu.SMEM)],
        scratch_shapes=[
            *[pltpu.VMEM(x.shape, x.dtype) for x in grads],
            pltpu.SemaphoreType.DMA((len(grads),)),
            pltpu.VMEM((3, -(-32 * slot_rows * 128 // width // 8) * 8 + 8, 128), F32),
            pltpu.VMEM((rows, 128), F32),
            pltpu.VMEM((4, 4, rows, 128), F32),
            pltpu.VMEM((4, 4, rows, 128), BF),
            pltpu.VMEM((4, 4, rows, 128), BF),
            pltpu.VMEM((4, 2, half, 128), BF),
            pltpu.VMEM((4, 2, half, 128), BF),
            pltpu.VMEM((4, half, 128), BF),
            pltpu.VMEM((4, half, 128), BF),
            pltpu.VMEM((6, rows, 128), BF),
            pltpu.VMEM((14, 8, 128), F32),
            pltpu.SemaphoreType.DMA((count,)),
            pltpu.SemaphoreType.DMA((count,)),
        ],
        compiler_params=pltpu.CompilerParams(
            collective_id=1, has_side_effects=True, vmem_limit_bytes=VMEM_BYTES
        ),
        name="reduce_gradients",
    )(*grads)


def layout_shapes(model_width, hidden_width):
    return [
        ("pre_gain", (model_width,)),
        ("pre_shift", (model_width,)),
        ("query_weight", (model_width, model_width)),
        ("query_bias", (model_width,)),
        ("reduce_weight", (4 * model_width, model_width)),
        ("reduce_bias", (model_width,)),
        ("reduce_gain", (model_width,)),
        ("reduce_shift", (model_width,)),
        ("pair_weight", (model_width, 2 * model_width)),
        ("value_bias", (model_width,)),
        ("output_weight", (model_width, model_width)),
        ("output_bias", (model_width,)),
        ("mlp_gain", (model_width,)),
        ("mlp_shift", (model_width,)),
        ("expand_weight", (model_width, hidden_width)),
        ("expand_bias", (hidden_width,)),
        ("spatial_weight", (9, hidden_width)),
        ("spatial_bias", (hidden_width,)),
        ("shrink_weight", (hidden_width, model_width)),
        ("shrink_bias", (model_width,)),
    ]


def row_bases(width, hidden):
    bases = {}
    row = 0
    for name, shape in layout_shapes(width, hidden):
        bases[name] = row
        row += math.prod(shape) // width
    return bases, row


SPAN = 96


def regroup_lines(read, write, low):
    part = [read(k) for k in range(5)]
    turned = [pltpu.roll(part[k], 64, 1) for k in (2, 3, 4)]
    for k in range(3):
        write(0, k, part[k])
    write(1, 0, jnp.where(low, turned[0], turned[1]))
    write(1, 1, jnp.where(low, turned[1], turned[2]))
    write(1, 2, turned[2])


def spread_slot(values, slot, slot_rows, line, wide):
    pairs = slot_rows // 5
    line[...] = values.astype(F32)

    def part(start, count):
        low = lax.broadcasted_iota(jnp.int32, (count, 128), 1) < 64

        def write(parity, k, value):
            wide[k, pl.ds(slot * (2 * pairs) + 2 * start + parity, count, stride=2), :] = value

        regroup_lines(lambda k: line[pl.ds(5 * start + k, count, stride=5), :], write, low)

    part(0, pairs // 8 * 8)
    if pairs % 8:
        part(pairs // 8 * 8, pairs % 8)


def unpack_kernel(order, slot_rows, bases, slots, *refs):
    outs, (flat, wide) = refs[:13], refs[13:]
    for slot, place in enumerate(order):
        flat[pl.ds(slot * slot_rows, slots.shape[1]), :] = slots[place].astype(F32)
    low = lax.broadcasted_iota(jnp.int32, (SPAN, 128), 1) < 64

    def regroup(t, _):
        def write(parity, k, value):
            wide[k, pl.ds(t * (2 * SPAN) + parity, SPAN, stride=2), :] = value

        regroup_lines(lambda k: flat[pl.ds(t * (5 * SPAN) + k, SPAN, stride=5), :], write, low)
        return 0

    lax.fori_loop(0, wide.shape[1] // (2 * SPAN), regroup, 0)
    write_weights(bases, wide, *outs)


def write_weights(bases, wide, vec, rows, wq, wqt, wr, wk, wv, wvt, wo, wot, we, wst, taps):
    width = wq.shape[0]
    hidden = wst.shape[1]

    def take(base, count, stride=1):
        at = pl.ds(base, count, stride=stride) if stride > 1 else pl.ds(base, count)
        return jnp.concatenate([wide[0, at, :], wide[1, at, :], wide[2, at, :][:, 0 : width - 256]], axis=1)

    def take_hidden(base, count):
        return jnp.concatenate([take(base + q, count, hidden // width) for q in range(hidden // width)], axis=1)

    def bordered(weight, bias, extra):
        index = lax.broadcasted_iota(jnp.int32, (extra, weight.shape[1]), 0)
        return jnp.concatenate([weight, jnp.where(index == 0, bias, 0.0)], axis=0)

    names = ("pre_gain", "pre_shift", "mlp_gain", "mlp_shift", "shrink_bias")
    for k, name in enumerate(names):
        vec[k] = jnp.broadcast_to(take(bases[name], 1), (128, width)).T
    for k, name in enumerate(("reduce_bias", "reduce_gain", "reduce_shift")):
        rows[k : k + 1, :] = take(bases[name], 1)
    query = take(bases["query_weight"], width)
    wq[...] = query.astype(BF)
    wqt[...] = bordered(query, take(bases["query_bias"], 1), EXT).T.astype(BF)
    for p in range(4):
        wr[p] = take(bases["reduce_weight"] + p * width, width).astype(BF)
    wk[...] = take(bases["pair_weight"], width, 2).astype(BF)
    value = take(bases["pair_weight"] + 1, width, 2)
    wv[...] = value.astype(BF)
    wvt[...] = bordered(value, take(bases["value_bias"], 1), 64).T.astype(BF)
    out = take(bases["output_weight"], width)
    wo[...] = out.astype(BF)
    wot[...] = bordered(out, take(bases["output_bias"], 1), EXT).T.astype(BF)
    we[0:width, :] = take_hidden(bases["expand_weight"], width).astype(BF)
    we[width:DEPTH, :] = first_row(take_hidden(bases["expand_bias"], 1), DEPTH - width).astype(BF)
    taps[0:9, :] = take_hidden(bases["spatial_weight"], 9)
    taps[9:10, :] = take_hidden(bases["spatial_bias"], 1)
    wst[width:DEPTH, :] = jnp.zeros((DEPTH - width, hidden), BF)
    for k in range(hidden // 128):
        wst[0:width, 128 * k : 128 * k + 128] = take(bases["shrink_weight"] + 128 * k, 128).T.astype(BF)


def wide_rows(count):
    return -(-count // (2 * SPAN)) * 2 * SPAN


def weight_shapes(width):
    hidden = 4 * width
    shape = jax.ShapeDtypeStruct
    return dict(
        vec=shape((5, width, 128), F32),
        rows=shape((3, width), F32),
        wq=shape((width, width), BF),
        wqt=shape((width, width + EXT), BF),
        wr=shape((4, width, width), BF),
        wk=shape((width, width), BF),
        wv=shape((width, width), BF),
        wvt=shape((width, width + 64), BF),
        wo=shape((width, width), BF),
        wot=shape((width, width + EXT), BF),
        we=shape((DEPTH, hidden), BF),
        wst=shape((DEPTH, hidden), BF),
        taps=shape((10, hidden), F32),
    )


def unpack_weights(slots, order, slot_rows, width):
    bases, count = row_bases(width, 4 * width)
    outs = weight_shapes(width)
    flat_rows = max(len(order) * slot_rows, wide_rows(count) * width // 128) + slots.shape[1]
    values = pl.pallas_call(
        partial(unpack_kernel, order, slot_rows, bases),
        out_shape=list(outs.values()),
        in_specs=[pl.BlockSpec(memory_space=pltpu.VMEM)],
        out_specs=[pl.BlockSpec(memory_space=pltpu.VMEM)] * len(outs),
        scratch_shapes=[pltpu.VMEM((flat_rows, 128), F32), pltpu.VMEM((3, wide_rows(count), 128), F32)],
        compiler_params=pltpu.CompilerParams(vmem_limit_bytes=VMEM_BYTES),
        name="unpack_weights",
    )(slots)
    return dict(zip(outs, values, strict=True))


COLLECTED = (8, 3, 9, 5, 7, 6, 4, 2, 0, 1)


def collect_gradients(bases, wide, gwe, gwst, gtaps, gbias, gwo, gwq, gpair, gwr, gcols, grows, ready=lambda k: None):
    width = gwst.shape[0]
    hidden = gwst.shape[1]
    used = bases["shrink_bias"] + 1
    for k in range(3):
        wide[k, pl.ds(used, wide.shape[1] - used), :] = jnp.zeros((wide.shape[1] - used, 128), F32)

    def put(base, value, stride=1):
        count = value.shape[0]
        at = pl.ds(base, count, stride=stride) if stride > 1 else pl.ds(base, count)
        wide[0, at, :] = value[:, 0:128]
        wide[1, at, :] = value[:, 128:256]
        wide[2, at, 0 : width - 256] = value[:, 256:width]

    ready(8)
    for k, name in enumerate(("pre_gain", "pre_shift", "mlp_gain", "mlp_shift")):
        put(bases[name], jnp.sum(gcols[k].T, axis=0, keepdims=True))
    ready(3)
    put(bases["shrink_bias"], jnp.sum(gbias[...].T, axis=0, keepdims=True))
    ready(9)
    for k, name in enumerate(("reduce_bias", "reduce_gain", "reduce_shift")):
        put(bases[name], jnp.sum(grows[8 * k : 8 * k + 8, :], axis=0, keepdims=True))
    ready(5)
    put(bases["query_weight"], gwq[0 : width + 1, :])
    ready(7)
    for p in range(4):
        put(bases["reduce_weight"] + p * width, gwr[p].T)
    ready(6)
    put(bases["pair_weight"], gpair[0:width, :].T[0:width], 2)
    value = gpair[width : 2 * width, :].T
    put(bases["pair_weight"] + 1, value[0:width], 2)
    put(bases["value_bias"], value[width : width + 1])
    ready(4)
    put(bases["output_weight"], gwo[0 : width + 1, :])
    ready(2)
    sums = jnp.concatenate(
        [jnp.sum(gtaps[8 * k : 8 * k + 8, :], axis=0, keepdims=True) for k in range(10)], axis=0
    )
    ready(0)
    for q in range(hidden // width):
        put(bases["expand_weight"] + q, gwe[0 : width + 1, q * width : (q + 1) * width], hidden // width)
        put(bases["spatial_weight"] + q, sums[:, q * width : (q + 1) * width], hidden // width)
    ready(1)
    for k in range(hidden // 128):
        put(bases["shrink_weight"] + 128 * k, gwst[:, 128 * k : 128 * k + 128].T)

def join_lines(read, write, low):
    turned = [pltpu.roll(read(1, k), 64, 1) for k in range(3)]
    write(0, read(0, 0))
    write(1, read(0, 1))
    write(2, jnp.where(low, read(0, 2), turned[0]))
    write(3, jnp.where(low, turned[0], turned[1]))
    write(4, jnp.where(low, turned[1], turned[2]))


def join_slot(wide, slot, slot_rows, line):
    pairs = slot_rows // 5

    def part(start, count):
        low = lax.broadcasted_iota(jnp.int32, (count, 128), 1) < 64

        def read(parity, k):
            return wide[k, pl.ds(slot * (2 * pairs) + 2 * start + parity, count, stride=2), :]

        def write(k, value):
            line[pl.ds(5 * start + k, count, stride=5), :] = value

        join_lines(read, write, low)

    part(0, pairs // 8 * 8)
    if pairs % 8:
        part(pairs // 8 * 8, pairs % 8)


def pack_kernel(order, slot_rows, bases, *refs):
    grads, (slots, flat, wide) = refs[:10], refs[10:]
    collect_gradients(bases, wide, *grads)
    done = wide.shape[1] * 5 // 2
    flat[done:, :] = jnp.zeros((flat.shape[0] - done, 128), F32)
    low = lax.broadcasted_iota(jnp.int32, (SPAN, 128), 1) < 64

    def regroup(t, _):
        def read(parity, k):
            return wide[k, pl.ds(t * (2 * SPAN) + parity, SPAN, stride=2), :]

        def write(k, value):
            flat[pl.ds(t * (5 * SPAN) + k, SPAN, stride=5), :] = value

        join_lines(read, write, low)
        return 0

    lax.fori_loop(0, wide.shape[1] // (2 * SPAN), regroup, 0)
    inside = lax.broadcasted_iota(jnp.int32, slots.shape[1:], 0) < slot_rows
    for slot, place in enumerate(order):
        slots[place] = jnp.where(inside, flat[pl.ds(slot * slot_rows, slots.shape[1]), :], 0.0).astype(BF)


def pack_gradients(grads, order, slot_rows, padded_rows, width):
    bases, count = row_bases(width, 4 * width)
    flat_rows = max(len(order) * slot_rows, wide_rows(count) * width // 128) + padded_rows
    return pl.pallas_call(
        partial(pack_kernel, order, slot_rows, bases),
        out_shape=jax.ShapeDtypeStruct((len(order), padded_rows, 128), BF),
        in_specs=[pl.BlockSpec(memory_space=pltpu.VMEM)] * len(grads),
        out_specs=pl.BlockSpec(memory_space=pltpu.VMEM),
        scratch_shapes=[pltpu.VMEM((flat_rows, 128), F32), pltpu.VMEM((3, wide_rows(count), 128), F32)],
        compiler_params=pltpu.CompilerParams(vmem_limit_bytes=VMEM_BYTES),
        name="pack_gradients",
    )(*grads)


def device_step(images, cotangent, kv_sides, w):
    positions = jnp.arange(TOKENS, dtype=jnp.int32)
    limit = 2 * kv_sides[:, None]
    mask = ((positions[None] // GRID < limit) & (positions[None] % GRID < limit)).astype(F32)
    mask = mask[:, None, :]
    perm = jnp.asarray(patch_order(), BF)
    pre, patches, reduced, memory, mixed, lse, middle, post = attention_forward(
        kv_sides, images, mask, perm, w["vec"], w["rows"], w["wqt"], w["wr"], w["wk"], w["wvt"], w["wot"]
    )
    output, grad_post, gwe, gwst, gtaps, gbias = feed_forward(
        post, cotangent, mask, middle, w["we"], w["wst"], w["taps"], w["vec"]
    )
    grad_images, gwo, gwq, gpair, gwr, gcols, grows = attention_backward(
        kv_sides, images, cotangent, mask, pre, patches, reduced, memory, mixed, lse, middle, grad_post,
        perm, w["vec"], w["rows"], w["wq"], w["wqt"], w["wr"], w["wk"], w["wv"], w["wvt"], w["wo"],
    )
    return output, grad_images, (gwe, gwst, gtaps, gbias, gwo, gwq, gpair, gwr, gcols, grows)


def step(on_grid, images, cotangent, kv_sides, params, first_moment, second_moment):
    width = images.shape[2]
    axes = ("dp", "fsdp")
    outer, inner = lax.axis_size("dp"), lax.axis_size("fsdp")
    slot_rows = params.shape[0] // 128
    padded_rows = -(-slot_rows // 32) * 32
    order = list(range(outer * inner))
    if on_grid:
        weights = gather_weights(params.reshape(slot_rows, 128), padded_rows, width)
    else:
        own = jnp.pad(params.reshape(slot_rows, 128).astype(BF), ((0, padded_rows - slot_rows), (0, 0)))
        weights = unpack_weights(lax.all_gather(own, axes), order, slot_rows, width)
    output, grad_images, grads = device_step(
        images.transpose(0, 2, 1), cotangent.transpose(0, 2, 1), kv_sides, weights
    )
    if on_grid:
        shard, squares = reduce_gradients(grads, slot_rows, padded_rows, width)
        squares = squares[0, 0]
    else:
        slots = pack_gradients(grads, order, slot_rows, padded_rows, width)
        shard = lax.psum_scatter(slots.astype(F32), axes)
        squares = lax.psum(jnp.sum(shard * shard), axes)
    shard = shard[:slot_rows].reshape(-1)
    grad_norm = jnp.sqrt(squares)
    clipped = shard * jnp.minimum(1.0, CLIP_NORM / (grad_norm + 1e-06))
    new_first = BETA_FIRST * first_moment + (1.0 - BETA_FIRST) * clipped
    new_second = BETA_SECOND * second_moment + (1.0 - BETA_SECOND) * clipped * clipped
    first_hat = new_first / (1.0 - BETA_FIRST**STEP)
    second_hat = new_second / (1.0 - BETA_SECOND**STEP)
    new_params = params - RATE * (first_hat / (jnp.sqrt(second_hat) + EPSILON) + DECAY * params)
    return (
        output.transpose(0, 2, 1),
        grad_images.transpose(0, 2, 1),
        grad_norm,
        new_first,
        new_second,
        new_params,
    )


def solution(mesh):
    data = P(("dp", "fsdp"), None, None)
    flat = P(("dp", "fsdp"))
    on_grid = dict(mesh.shape) == {"dp": 4, "fsdp": 8}
    return jax.shard_map(
        partial(step, on_grid),
        mesh=mesh,
        in_specs=(data, data, flat, flat, flat, flat),
        out_specs=(data, data, P(), flat, flat, flat),
        check_vma=False,
    )
```

```python
from functools import partial
import math

import jax
import jax.numpy as jnp
import numpy as np
from jax import lax
from jax.experimental import pallas as pl
from jax.experimental.pallas import tpu as pltpu
from jax.sharding import PartitionSpec as P

HEADS = 5
HEAD_DIM = 64
GRID = 48
KV = 24
STEP = 10

CLIP_NORM = 1.0
BETA_FIRST = 0.9
BETA_SECOND = 0.999
RATE = 0.04
DECAY = 0.05
EPSILON = 1e-08

F32 = jnp.float32
BF = jnp.bfloat16
NN = (((1,), (0,)), ((), ()))
NT = (((1,), (1,)), ((), ()))
TOKENS = GRID * GRID
KEYS = KV * KV
PITCH = GRID + 8
EXT = 16
DEPTH = 512
LOG2E = math.log2(math.e)
QUERY_SCALE = HEAD_DIM**-0.5 * LOG2E
GELU_A = math.sqrt(2.0 / math.pi)
GELU_B = GELU_A * 0.044715
VMEM_BYTES = 63 * 1024 * 1024


def mm(left, right, dims=NN):
    return lax.dot_general(left, right, dims, preferred_element_type=F32)


def patch_order():
    matrix = np.zeros((8 * GRID, 8 * GRID), np.float32)
    for p in range(4):
        for a in range(4):
            for b in range(KV):
                matrix[p * 96 + a * KV + b, (2 * a + p // 2) * GRID + 2 * b + p % 2] = 1.0
    return matrix


def fold_rows(x):
    return jnp.sum(x.reshape(x.shape[0] // 8, 8, x.shape[1]), axis=0)


def norm_columns(x):
    scale = 1.0 / x.shape[0]
    centred = x - jnp.sum(x, axis=0, keepdims=True) * scale
    rstd = lax.rsqrt(jnp.sum(centred * centred, axis=0, keepdims=True) * scale + 1e-06)
    return centred * rstd, rstd


def norm_columns_back(normed, rstd, scaled):
    scale = 1.0 / scaled.shape[0]
    plain = jnp.sum(scaled, axis=0, keepdims=True) * scale
    mixed = jnp.sum(scaled * normed, axis=0, keepdims=True) * scale
    return rstd * (scaled - plain - normed * mixed)


def norm_rows(x):
    centred = x - jnp.mean(x, axis=-1, keepdims=True)
    rstd = lax.rsqrt(jnp.mean(centred * centred, axis=-1, keepdims=True) + 1e-06)
    return centred * rstd, rstd


def norm_rows_back(normed, rstd, scaled):
    plain = jnp.mean(scaled, axis=-1, keepdims=True)
    mixed = jnp.mean(scaled * normed, axis=-1, keepdims=True)
    return rstd * (scaled - plain - normed * mixed)


def first_row(row, rows=EXT):
    index = lax.broadcasted_iota(jnp.int32, (rows, row.shape[-1]), 0)
    return jnp.where(index == 0, row, 0.0)


def three_parts(x):
    high = x.astype(BF).astype(F32)
    middle = (x - high).astype(BF).astype(F32)
    return high, middle, (x - high - middle).astype(BF).astype(F32)


def whole(x):
    zeros = (0,) * len(x.shape)
    return pl.BlockSpec(x.shape, lambda *_: zeros)


FAR = pl.BlockSpec(memory_space=pl.ANY)


def near(x):
    return pltpu.VMEM((1,) + tuple(x.shape[1:]), x.dtype)


def per_image(x, **kwargs):
    zeros = (0,) * (len(x.shape) - 1)
    return pl.BlockSpec((1,) + tuple(x.shape[1:]), lambda i, *_: (i,) + zeros, **kwargs)


def key_columns(ref, side, h_range, ones_from, ones_to, with_mask):
    lane = lax.broadcasted_iota(jnp.int32, (KV, 64), 1)
    cell = lax.broadcasted_iota(jnp.int32, (KV, 64), 0)
    ones = jnp.where((lane >= ones_from) & (lane <= ones_to), 1.0, 0.0)
    for a in range(KV):
        block = ones
        if with_mask:
            bias = jnp.where((cell < side) & (a < side), 0.0, -1e30)
            block = jnp.where(lane == 0, bias, ones)
        block = block.astype(BF)
        for h in h_range:
            ref[h, a * KV : (a + 1) * KV, 64:128] = block


def attention_forward_kernel(
    sides, images, mask, perm, vec, rows, wqt, wr, wk, wvt, wot,
    pre_far, patches_far, reduced_far, memory_far, mixed_far, lse, middle, post,
    pre, patches, reduced, memory, mixed, key_ref, value_ref, sems,
):
    i = pl.program_id(0)
    width = images.shape[1]
    far = (pre_far, patches_far, reduced_far, memory_far, mixed_far)
    kept = (pre, patches, reduced, memory, mixed)
    away = [pltpu.make_async_copy(y, x.at[pl.ds(i, 1)], sems.at[k]) for k, (x, y) in enumerate(zip(far, kept))]

    def first_norm(t, _):
        for u in range(3):
            at = pl.ds(pl.multiple_of(t * 384 + u * 128, 128), 128)
            x = images[0, :, at].astype(F32) * mask[0, 0:1, at]
            normed, _unused = norm_columns(x)
            pre[0, 0:width, at] = (normed * vec[0] + vec[1]).astype(BF)
            pre[0, width : width + EXT, at] = first_row(jnp.ones((1, 128), F32)).astype(BF)
        return 0

    lax.fori_loop(0, TOKENS // 384, first_norm, 0)
    for t in range(TOKENS // 384):
        picked = mm(perm[...], pre[0, 0:width, t * 384 : (t + 1) * 384], NT).astype(BF)
        for p in range(4):
            patches[0, p, t * 96 : (t + 1) * 96, :] = picked[p * 96 : (p + 1) * 96]
    away[0].start()
    away[1].start()

    total = rows[0:1, :]
    for p in range(4):
        total = total + mm(patches[0, p], wr[p])
    reduced[0] = total
    normed, _unused = norm_rows(total)
    memory[0, :, 0:width] = (normed * rows[1:2, :] + rows[2:3, :]).astype(BF)
    lane = lax.broadcasted_iota(jnp.int32, (KEYS, 64), 1)
    memory[0, :, width : width + 64] = jnp.where(lane == 0, 1.0, 0.0).astype(BF)
    away[2].start()
    away[3].start()
    keys = mm(memory[0, :, 0:width], wk[...]).astype(BF)
    key_columns(key_ref, sides[i], range(HEADS), 1, 0, True)
    values = mm(wvt[...], memory[0], NT).astype(BF)
    ones = first_row(jnp.ones((1, KEYS), F32)).astype(BF)
    for h in range(HEADS):
        at = slice(h * HEAD_DIM, (h + 1) * HEAD_DIM)
        key_ref[h, :, 0:HEAD_DIM] = keys[:, at]
        value_ref[h, 0:HEAD_DIM, :] = values[at]
        value_ref[h, HEAD_DIM : HEAD_DIM + EXT, :] = ones
    mixed[0, width : width + EXT, :] = first_row(jnp.ones((1, TOKENS), F32)).astype(BF)
    queries = (mm(wqt[...], pre[0]) * QUERY_SCALE).astype(BF)
    tail = first_row(jnp.ones((1, TOKENS), F32), 64).astype(BF)
    for h in range(HEADS):
        at = slice(h * HEAD_DIM, (h + 1) * HEAD_DIM)
        scores = mm(key_ref[h], jnp.concatenate([queries[at], tail], axis=0))
        top = jnp.max(scores, axis=0, keepdims=True)
        weights = jnp.exp2(scores - top).astype(BF)
        out = mm(value_ref[h], weights)
        total = out[HEAD_DIM : HEAD_DIM + 1]
        mixed[0, at, :] = (out[0:HEAD_DIM] * (1.0 / total)).astype(BF)
        lse[0, h : h + 1, :] = top + jnp.log2(total)

    away[4].start()
    middle[0] = mm(wot[...], mixed[0])

    def second_norm(t, _):
        for u in range(3):
            at = pl.ds(pl.multiple_of(t * 384 + u * 128, 128), 128)
            here = mask[0, 0:1, at]
            x = images[0, :, at].astype(F32) * here + middle[0, :, at]
            middle[0, :, at] = x
            normed, _unused = norm_columns(x)
            post[0, 0:width, at] = ((normed * vec[2] + vec[3]) * here).astype(BF)
            post[0, width : width + EXT, at] = first_row(here).astype(BF)
        return 0

    lax.fori_loop(0, TOKENS // 384, second_norm, 0)
    for copy in away:
        copy.wait()


def attention_forward(sides, images, mask, perm, vec, rows, wqt, wr, wk, wvt, wot):
    n, width, tokens = images.shape
    shape = jax.ShapeDtypeStruct
    outs = [
        shape((n, width + EXT, tokens), BF),
        shape((n, 4, KEYS, width), BF),
        shape((n, KEYS, width), F32),
        shape((n, KEYS, width + 64), BF),
        shape((n, width + EXT, tokens), BF),
        shape((n, 8, tokens), F32),
        shape((n, width, tokens), F32),
        shape((n, width + EXT, tokens), BF),
    ]
    weights = (perm, vec, rows, wqt, wr, wk, wvt, wot)
    return pl.pallas_call(
        attention_forward_kernel,
        grid_spec=pltpu.PrefetchScalarGridSpec(
            num_scalar_prefetch=1,
            grid=(n,),
            in_specs=[per_image(images), per_image(mask)] + [whole(x) for x in weights],
            out_specs=[FAR] * 5 + [per_image(x) for x in outs[5:]],
            scratch_shapes=[near(x) for x in outs[:5]]
            + [
                pltpu.VMEM((HEADS, KEYS, 128), BF),
                pltpu.VMEM((HEADS, HEAD_DIM + EXT, KEYS), BF),
                pltpu.SemaphoreType.DMA((5,)),
            ],
        ),
        out_shape=outs,
        compiler_params=pltpu.CompilerParams(vmem_limit_bytes=VMEM_BYTES),
        name="attention_forward",
    )(sides, images, mask, *weights)


def feed_forward_kernel(
    post_next, cot_next, mask_next, we_next, wst_next, taps,
    post, cot, mask, middle_far, we, wst, vec,
    output, grad_post, gwe, gwst, gtaps, gbias,
    padded_0, padded_1, grad_padded, grad_act, act_0, act_1, grad_exp_0, grad_exp_1,
    post_rows, out_grad_rows, out_grad, total, middle, middle_sem,
):
    s = pl.program_id(0)
    last = pl.num_programs(0) - 1
    width, block = cot.shape[1], wst.shape[1]
    blocks = gwst.shape[1] // block
    halves = block // 128
    rows = 16
    chunks = GRID // rows
    span = rows * GRID
    js = pl.ds(pl.multiple_of(lax.rem(s, blocks) * block, block), block)
    js_done = pl.ds(pl.multiple_of(lax.rem(jnp.maximum(s - 1, 0), blocks) * block, block), block)

    def tokens(t):
        return pl.ds(pl.multiple_of(t * span, span), span)

    def expand(t, padded, we, wst):
        at = tokens(t)
        filled = mm(post_rows[at, :], we[...])
        for h in range(halves):
            for r in range(rows):
                start = pl.multiple_of((t * rows + r + 1) * PITCH + 8, 8)
                padded[h, pl.ds(start, GRID), :] = filled[r * GRID : (r + 1) * GRID, h * 128 : (h + 1) * 128]
        grad_act[at, :] = mm(out_grad_rows[at, :], wst[...])

    def finish(t, act, grad_exp):
        at = tokens(t)
        gwst[:, js_done] += mm(out_grad[:, at], act[at, :])
        gwe[:, js_done] += mm(post[0, :, at], grad_exp[at, :])

    def finish_rest(t, act, grad_exp):
        at = tokens(t)
        total[:, at] += mm(wst[0:width, :], act[at, :], NT)
        grad_post[0, :, at] += mm(we[0:width, :], grad_exp[at, :], NT)

    def convolve(t, padded, act):
        for h in range(halves):
            hs = slice(h * 128, (h + 1) * 128)
            w = [jnp.broadcast_to(0.5 * taps[k : k + 1, hs], (GRID, 128)).astype(BF) for k in range(10)]
            sums = jnp.zeros((8, 128), F32)
            open_rows = {}
            for q in range(-1, rows + 1):
                base = (t * rows + q + 1) * PITCH + 8
                x = [padded[h, pl.ds(base + d, GRID), :].astype(BF) for d in (-1, 0, 1)]
                for a in (2, 1, 0):
                    r = q + 1 - a
                    if 0 <= r < rows:
                        part = w[3 * a] * x[0] + w[3 * a + 1] * x[1] + w[3 * a + 2] * x[2]
                        open_rows[r] = part + open_rows.get(r, w[9])
                r = q - 1
                if r < 0:
                    continue
                at = pl.ds(pl.multiple_of((t * rows + r) * GRID, GRID), GRID)
                gelu, slope = gelu_pair(open_rows.pop(r))
                act[at, hs] = gelu
                grad = (grad_act[at, hs].astype(BF) * slope).astype(F32)
                start = pl.multiple_of((t * rows + r + 1) * PITCH + 8, 8)
                grad_padded[h, pl.ds(start, GRID), :] = grad
                sums = sums + fold_rows(grad)
            cols = pl.ds(pl.multiple_of(lax.rem(s, blocks) * block + h * 128, 128), 128)
            gtaps[72:80, cols] += sums

    def convolve_back(t, padded, grad_exp):
        for h in range(halves):
            hs = slice(h * 128, (h + 1) * 128)
            w = [jnp.broadcast_to(taps[k : k + 1, hs], (GRID, 128)).astype(BF) for k in range(9)]
            sums = [jnp.zeros((8, 128), F32) for _ in range(9)]
            waiting = {}
            open_rows = {}
            x = {}
            for q in range(-1, rows + 1):
                base = (t * rows + q + 1) * PITCH + 8
                grads = [grad_padded[h, pl.ds(base + 1 - b, GRID), :].astype(BF) for b in range(3)]
                if q + 1 < rows:
                    start = pl.multiple_of((t * rows + q + 2) * PITCH + 8, 8)
                    x[q + 1] = padded[h, pl.ds(start, GRID), :].astype(BF)
                for a in range(3):
                    r = q + a - 1
                    if not 0 <= r < rows:
                        continue
                    part = w[3 * a] * grads[0] + w[3 * a + 1] * grads[1] + w[3 * a + 2] * grads[2]
                    open_rows[r] = part + open_rows[r] if r in open_rows else part
                    for b in range(3):
                        k = 3 * a + b
                        product = x[r] * grads[b]
                        product = product[0:16] + product[16:32] + product[32:48]
                        waiting[k] = waiting[k] + product if k in waiting else product
                        if r % 4 == 3:
                            product = waiting.pop(k).astype(F32)
                            sums[k] = sums[k] + product[0:8] + product[8:16]
                r = q - 1
                if r >= 0:
                    at = pl.ds(pl.multiple_of((t * rows + r) * GRID, GRID), GRID)
                    grad_exp[at, hs] = open_rows.pop(r)
                    x.pop(r)
            cols = pl.ds(pl.multiple_of(lax.rem(s, blocks) * block + h * 128, 128), 128)
            for k in range(9):
                gtaps[8 * k : 8 * k + 8, cols] += sums[k]

    @pl.when(s == 0)
    def _():
        for ref in (act_1, grad_exp_1, out_grad, gwe, gwst, gtaps, gbias):
            ref[...] = jnp.zeros_like(ref)
        for ref in (post_rows, out_grad_rows):
            ref[:, 256:DEPTH] = jnp.zeros((TOKENS, DEPTH - 256), BF)
        for ref in (padded_0, padded_1, grad_padded):
            for h in range(halves):
                ref[h, 0 : PITCH + 8, :] = jnp.zeros((PITCH + 8, 128), F32)
                ref[h, (GRID + 1) * PITCH :, :] = jnp.zeros((PITCH + 8, 128), F32)
                for r in range(1, GRID):
                    ref[h, (r + 1) * PITCH : (r + 1) * PITCH + 8, :] = jnp.zeros((8, 128), F32)

    @pl.when((s == 0) | ((lax.rem(s + 1, blocks) == 0) & (s + 1 < last)))
    def _():
        for t in range(TOKENS // 384):
            at = slice(t * 384, (t + 1) * 384)
            grad = cot_next[0, :, at].astype(F32) * mask_next[0, 0:1, at]
            gbias[...] += grad[:, 0:128] + grad[:, 128:256] + grad[:, 256:384]
            out_grad_rows[at, 0:width] = (0.5 * grad).astype(BF).T
            post_rows[at, 0 : width + EXT] = post_next[0, :, at].T

    fetch = pltpu.make_async_copy(middle_far.at[pl.ds(jnp.maximum(s - 1, 0) // blocks, 1)], middle, middle_sem)

    @pl.when(lax.rem(s, blocks) == 1)
    def _():
        fetch.start()
        for t in range(TOKENS // 384):
            at = slice(t * 384, (t + 1) * 384)
            out_grad[:, at] = (cot[0, :, at].astype(F32) * mask[0, 0:1, at]).astype(BF)

    @pl.when((s == 0) | (lax.rem(s, blocks) == 1))
    def _():
        total[...] = jnp.zeros_like(total)
        grad_post[...] = jnp.zeros_like(grad_post)

    @pl.when(s == 0)
    def _():
        def first(t, _):
            expand(t, padded_0, we, wst)
            return 0

        lax.fori_loop(0, chunks, first, 0)

    def work(padded, padded_next, act, act_done, grad_exp, grad_exp_done):
        def forward(t, _):
            finish(t, act_done, grad_exp_done)
            convolve(t, padded, act)
            return 0

        def backward(t, _):
            expand(t, padded_next, we_next, wst_next)
            finish_rest(t, act_done, grad_exp_done)
            convolve_back(t, padded, grad_exp)
            return 0

        lax.fori_loop(0, chunks, forward, 0)
        lax.fori_loop(0, chunks, backward, 0)

    @pl.when((s < last) & (lax.rem(s, 2) == 0))
    def _():
        work(padded_0, padded_1, act_0, act_1, grad_exp_0, grad_exp_1)

    @pl.when((s < last) & (lax.rem(s, 2) == 1))
    def _():
        work(padded_1, padded_0, act_1, act_0, grad_exp_1, grad_exp_0)

    @pl.when(s == last)
    def _():
        def rest(t, _):
            @pl.when(lax.rem(s, 2) == 0)
            def _():
                finish(t, act_1, grad_exp_1)
                finish_rest(t, act_1, grad_exp_1)

            @pl.when(lax.rem(s, 2) == 1)
            def _():
                finish(t, act_0, grad_exp_0)
                finish_rest(t, act_0, grad_exp_0)

            return 0

        lax.fori_loop(0, chunks, rest, 0)

    @pl.when((s > 0) & (lax.rem(s, blocks) == 0))
    def _():
        fetch.wait()
        for t in range(TOKENS // 128):
            at = slice(t * 128, (t + 1) * 128)
            output[0, :, at] = ((middle[0, :, at] + total[:, at] + vec[4]) * mask[0, 0:1, at]).astype(BF)


def gelu_pair(half):
    kind = half.dtype.type
    square = half * half
    upper = jnp.tanh(half * (kind(8.0 * GELU_B) * square + kind(2.0 * GELU_A))) + kind(1.0)
    gelu = half * upper
    return gelu, upper + gelu * (kind(2.0) - upper) * (kind(24.0 * GELU_B) * square + kind(2.0 * GELU_A))


def feed_forward(post, cot, mask, middle, we, wst, taps, vec, block=256):
    n, width, tokens = cot.shape
    hidden = wst.shape[1]
    blocks = hidden // block
    count = n * blocks
    shape = jax.ShapeDtypeStruct
    outs = [
        shape((n, width, tokens), BF),
        shape((n, width, tokens), F32),
        shape((width + EXT, hidden), F32),
        shape((width, hidden), F32),
        shape((80, hidden), F32),
        shape((width, 128), F32),
    ]

    def ahead(s):
        return jnp.minimum(s + 1, count - 1)

    def behind(s):
        return jnp.maximum(s - 1, 0)

    def image(x, step):
        zeros = (0,) * (len(x.shape) - 1)
        return pl.BlockSpec((1,) + tuple(x.shape[1:]), lambda s: (step(s) // blocks,) + zeros)

    def columns(x, step):
        return pl.BlockSpec((x.shape[0], block), lambda s: (0, lax.rem(step(s), blocks)))

    return pl.pallas_call(
        feed_forward_kernel,
        grid=(count + 1,),
        in_specs=[image(x, ahead) for x in (post, cot, mask)]
        + [columns(we, ahead), columns(wst, ahead), columns(taps, lambda s: jnp.minimum(s, count - 1))]
        + [image(x, behind) for x in (post, cot, mask)]
        + [FAR, columns(we, behind), columns(wst, behind), whole(vec)],
        out_specs=[image(x, behind) for x in outs[:2]] + [whole(x) for x in outs[2:]],
        out_shape=outs,
        scratch_shapes=[pltpu.VMEM((block // 128, (GRID + 2) * PITCH + 8, 128), F32)] * 3
        + [pltpu.VMEM((tokens, block), F32)]
        + [pltpu.VMEM((tokens, block), BF)] * 4
        + [
            pltpu.VMEM((tokens, DEPTH), BF),
            pltpu.VMEM((tokens, DEPTH), BF),
            pltpu.VMEM((width, tokens), BF),
            pltpu.VMEM((width, tokens), F32),
            near(middle),
            pltpu.SemaphoreType.DMA(()),
        ],
        compiler_params=pltpu.CompilerParams(vmem_limit_bytes=VMEM_BYTES),
        name="feed_forward",
    )(post, cot, mask, we, wst, taps, post, cot, mask, middle, we, wst, vec)


def attention_backward_kernel(
    sides, mixed_far, pre_far, memory_far, reduced_far, patches_far, images_far, cot, mask, lse, middle, grad_post,
    perm, vec, rows, wq, wqt, wr, wk, wv, wvt, wo,
    grad_images, gwo, gwq, gpair, gwr, gcols, grows,
    branch, grad_mixed, queries, grad_queries, key_ref, value_ref, keys_t, grad_keys, grad_values, grad_patches,
    mixed, pre, memory, reduced, patches, images, sems,
):
    i = pl.program_id(0)
    width = cot.shape[1]
    far = (mixed_far, pre_far, memory_far, reduced_far, patches_far, images_far)
    kept = (mixed, pre, memory, reduced, patches, images)
    fetch = [pltpu.make_async_copy(x.at[pl.ds(i, 1)], y, sems.at[k]) for k, (x, y) in enumerate(zip(far, kept))]
    for copy in fetch:
        copy.start()

    @pl.when(i == 0)
    def _():
        for ref in (gwo, gwq, gpair, gwr, gcols, grows):
            ref[...] = jnp.zeros_like(ref)

    def mlp_norm_back(t, _):
        gain = shift = jnp.zeros((width, 128), F32)
        for u in range(3):
            at = pl.ds(pl.multiple_of(t * 384 + u * 128, 128), 128)
            here = mask[0, 0:1, at]
            normed, rstd = norm_columns(middle[0, :, at])
            grad = grad_post[0, :, at] * here
            gain = gain + grad * normed
            shift = shift + grad
            grad = cot[0, :, at].astype(F32) * here + norm_columns_back(normed, rstd, grad * vec[2])
            grad_images[0, :, at] = grad
            branch[:, at] = grad.astype(BF)
        gcols[2] += gain
        gcols[3] += shift
        return 0

    lax.fori_loop(0, TOKENS // 384, mlp_norm_back, 0)
    fetch[0].wait()
    gwo[...] += mm(mixed[0], branch[...], NT)
    grad_mixed[...] = mm(wo[...], branch[...]).astype(BF)
    fetch[1].wait()
    queries[...] = (mm(wqt[...], pre[0]) * QUERY_SCALE).astype(BF)
    fetch[2].wait()
    keys = mm(memory[0, :, 0:width], wk[...]).astype(BF)
    keys_t[...] = keys.T
    values = mm(wvt[...], memory[0], NT).astype(BF).T
    key_columns(key_ref, sides[i], range(HEADS), 1, 3, True)
    key_columns(value_ref, sides[i], range(HEADS), 1, 3, False)
    for h in range(HEADS):
        at = slice(h * HEAD_DIM, (h + 1) * HEAD_DIM)
        key_ref[h, :, 0:HEAD_DIM] = keys[:, at]
        value_ref[h, :, 0:HEAD_DIM] = values[:, at]

    span = TOKENS // 3
    index = lax.broadcasted_iota(jnp.int32, (64, span), 0)
    grad_values[...] = jnp.zeros_like(grad_values)
    grad_keys[...] = jnp.zeros_like(grad_keys)

    def part(t, _):
        at = pl.ds(pl.multiple_of(t * span, 128), span)
        for h in range(HEADS):
            hs = slice(h * HEAD_DIM, (h + 1) * HEAD_DIM)
            one, two, three = three_parts(-lse[0, h : h + 1, at])
            tail = jnp.where(index == 2, two, jnp.where(index == 3, three, 0.0))
            tail = jnp.where(index == 0, 1.0, jnp.where(index == 1, one, tail)).astype(BF)
            query = queries[hs, at]
            attend = jnp.exp2(mm(key_ref[h], jnp.concatenate([query, tail], axis=0)))
            low = attend.astype(BF)
            grad = grad_mixed[hs, at]
            inner = grad.astype(F32) * mixed[0, hs, at].astype(F32)
            one, two, three = three_parts(-jnp.sum(inner, axis=0, keepdims=True))
            tail = jnp.where(index == 2, two, jnp.where(index == 3, three, 0.0))
            tail = jnp.where(index == 1, one, tail).astype(BF)
            grad_attend = mm(value_ref[h], jnp.concatenate([grad, tail], axis=0))
            grad_scores = (attend * grad_attend).astype(BF)
            grad_values[hs, :] += mm(grad, low, NT)
            grad_keys[hs, :] += mm(query, grad_scores, NT) * (1.0 / LOG2E)
            grad_queries[hs, at] = (mm(keys_t[hs, :], grad_scores) * HEAD_DIM**-0.5).astype(BF)
        return 0

    lax.fori_loop(0, TOKENS // span, part, 0)

    low_keys = grad_keys[...].astype(BF)
    low_values = grad_values[...].astype(BF)
    gpair[0:width, :] += mm(low_keys, memory[0])
    gpair[width : 2 * width, :] += mm(low_values, memory[0])
    grad_memory = mm(low_keys.T, wk[...], NT) + mm(low_values.T, wv[...], NT)
    fetch[3].wait()
    normed, rstd = norm_rows(reduced[0])
    grows[8:16, :] += fold_rows(grad_memory * normed)
    grows[16:24, :] += fold_rows(grad_memory)
    grad_reduced = norm_rows_back(normed, rstd, grad_memory * rows[1:2, :]).astype(BF)
    grows[0:8, :] += fold_rows(grad_reduced.astype(F32))
    grad_reduced_t = grad_reduced.T
    fetch[4].wait()
    for p in range(4):
        gwr[p] += mm(grad_reduced_t, patches[0, p])
        grad_patches[p] = mm(grad_reduced, wr[p], NT).astype(BF)
    gwq[...] += mm(pre[0], grad_queries[...], NT)

    def pre_norm_back(t, _):
        at = pl.ds(pl.multiple_of(t * 384, 128), 384)
        grad_pre = mm(wq[...], grad_queries[:, at])
        start = pl.ds(pl.multiple_of(t * 96, 32), 96)
        picked = jnp.concatenate([grad_patches[p, start, :] for p in range(4)], axis=0)
        grad_pre = grad_pre + mm(picked.T, perm[...])
        gain = shift = jnp.zeros((width, 128), F32)
        for u in range(3):
            at = pl.ds(pl.multiple_of(t * 384 + u * 128, 128), 128)
            here = mask[0, 0:1, at]
            normed, rstd = norm_columns(images[0, :, at].astype(F32) * here)
            grad = grad_pre[:, u * 128 : (u + 1) * 128]
            gain = gain + grad * normed
            shift = shift + grad
            back = norm_columns_back(normed, rstd, grad * vec[0])
            grad_images[0, :, at] = (grad_images[0, :, at] + back) * here
        gcols[0] += gain
        gcols[1] += shift
        return 0

    fetch[5].wait()
    lax.fori_loop(0, TOKENS // 384, pre_norm_back, 0)


def attention_backward(
    sides, images, cot, mask, pre, patches, reduced, memory, mixed, lse, middle, grad_post,
    perm, vec, rows, wq, wqt, wr, wk, wv, wvt, wo,
):
    n, width, tokens = images.shape
    shape = jax.ShapeDtypeStruct
    outs = [
        shape((n, width, tokens), F32),
        shape((width + EXT, width), F32),
        shape((width + EXT, width), F32),
        shape((2 * width, width + 64), F32),
        shape((4, width, width), F32),
        shape((4, width, 128), F32),
        shape((24, width), F32),
    ]
    far = (mixed, pre, memory, reduced, patches, images)
    inputs = (cot, mask, lse, middle, grad_post)
    weights = (perm, vec, rows, wq, wqt, wr, wk, wv, wvt, wo)
    return pl.pallas_call(
        attention_backward_kernel,
        grid_spec=pltpu.PrefetchScalarGridSpec(
            num_scalar_prefetch=1,
            grid=(n,),
            in_specs=[FAR] * 6 + [per_image(x) for x in inputs] + [whole(x) for x in weights],
            out_specs=[per_image(outs[0])] + [whole(x) for x in outs[1:]],
            scratch_shapes=[
                pltpu.VMEM((width, tokens), BF),
                pltpu.VMEM((width, tokens), BF),
                pltpu.VMEM((width, tokens), BF),
                pltpu.VMEM((width, tokens), BF),
                pltpu.VMEM((HEADS, KEYS, 128), BF),
                pltpu.VMEM((HEADS, KEYS, 128), BF),
                pltpu.VMEM((width, KEYS), BF),
                pltpu.VMEM((width, KEYS), F32),
                pltpu.VMEM((width, KEYS), F32),
                pltpu.VMEM((4, KEYS, width), BF),
            ]
            + [near(x) for x in far]
            + [pltpu.SemaphoreType.DMA((6,))],
        ),
        out_shape=outs,
        compiler_params=pltpu.CompilerParams(vmem_limit_bytes=VMEM_BYTES),
        name="attention_backward",
    )(sides, *far, *inputs, *weights)

MESH = pl.DeviceIdType.MESH


class Place:
    def __init__(self):
        self.dp = lax.axis_index("dp")
        self.fsdp = lax.axis_index("fsdp")
        self.y, self.x = self.dp // 2, self.dp % 2
        self.z, self.core = self.fsdp // 2, self.fsdp % 2
        self.other_core = 1 - self.core
        self.beside_x = (self.dp + 1 - 2 * self.x, self.fsdp)
        self.beside_y = (self.dp + 2 - 4 * self.y, self.fsdp)
        self.across = (3 - self.dp, self.fsdp)
        self.beside_core = (self.dp, self.fsdp + 1 - 2 * self.core)
        self.others = (self.z + 1 - 2 * (self.z % 2), 2 - self.z // 2, 3 * (1 - self.z // 2))

    def at_z(self, z):
        return (self.dp, z * 2 + self.core)

    def along_z(self, k):
        return self.at_z((self.z + k) % 4)

    def call(self, partners):
        barrier = pltpu.get_barrier_semaphore()
        for device in partners:
            pl.semaphore_signal(barrier, inc=1, device_id=device, device_id_type=MESH)

    def answer(self, count):
        pl.semaphore_wait(pltpu.get_barrier_semaphore(), count)


class Sender:
    def __init__(self, send, recv):
        self.send, self.recv, self.started = send, recv, []

    def __call__(self, source, target, device, recv=None):
        k = len(self.started)
        copy = pltpu.make_async_remote_copy(
            src_ref=source,
            dst_ref=target,
            send_sem=self.send.at[k],
            recv_sem=self.recv.at[k] if recv is None else recv,
            device_id=device,
            device_id_type=MESH,
        )
        copy.start()
        self.started.append(copy)
        return copy

    def finish(self):
        for copy in self.started:
            copy.wait_send()


def gather_kernel(slot_rows, bases, params, *refs):
    outs, (own, slots, wide, line, own_sem, send_sem, recv_sem, z_sem) = refs[:13], refs[13:]
    me = Place()
    me.call([me.beside_core, me.beside_x, me.beside_y] + [me.at_z(z) for z in me.others])
    half = own.shape[0] // 2
    full = slot_rows // 16 * 16
    own[...] = jnp.zeros_like(own)
    own[0:full, :] = params[0:full, :].astype(BF)
    own[full:slot_rows, :] = params[full:slot_rows, :].astype(BF)
    first, second = pl.ds(0, half), pl.ds(half, half)
    send = Sender(send_sem, recv_sem)
    copy = pltpu.make_async_copy(own, slots.at[me.core, me.dp, me.z], own_sem)
    copy.start()
    me.answer(6)
    own_slot = slots.at[me.core, me.dp, me.z]

    def send_z(j):
        return send(own, own_slot, me.at_z(me.others[j]), z_sem.at[me.z])

    send_z(0)
    x_copies = [send(own, own_slot, me.beside_x)]
    y_copies = [send(own, own_slot, me.beside_y)]
    core_copies = [(send(own, own_slot, me.beside_core), me.dp, me.z)]
    send_z(1)
    half_copies = []
    order = (me.z,) + me.others

    def open_slot(core, dp, z):
        spread_slot(slots[core, dp, z], (dp * 8 + z * 2 + core), slot_rows, line, wide)

    def forward(k):
        z = order[k]
        x_copies[k].wait_recv()
        slot = slots.at[me.core, me.beside_x[0], z]
        half_copies.append(send(slot.at[first], slot.at[first], me.beside_y))
        core_copies.append((send(slot, slot, me.beside_core), me.beside_x[0], z))
        y_copies[k].wait_recv()
        slot = slots.at[me.core, me.beside_y[0], z]
        half_copies.append(send(slot.at[second], slot.at[second], me.beside_x))
        core_copies.append((send(slot, slot, me.beside_core), me.beside_y[0], z))
        open_slot(me.core, me.beside_x[0], z)
        open_slot(me.core, me.beside_y[0], z)

    copy.wait()
    open_slot(me.core, me.dp, me.z)
    forward(0)
    for k in (1, 2, 3):
        z = order[k]
        slot = slots.at[me.core, me.dp, z]
        pltpu.make_async_remote_copy(
            src_ref=own,
            dst_ref=slot,
            send_sem=send_sem.at[0],
            recv_sem=z_sem.at[z],
            device_id=me.at_z(z),
            device_id_type=MESH,
        ).wait_recv()
        x_copies.append(send(slot, slot, me.beside_x))
        y_copies.append(send(slot, slot, me.beside_y))
        core_copies.append((send(slot, slot, me.beside_core), me.dp, z))
        if k == 1:
            send_z(2)
        open_slot(me.core, me.dp, z)
        forward(k)
    for k in range(4):
        half_copies[2 * k].wait_recv()
        half_copies[2 * k + 1].wait_recv()
        slot = slots.at[me.core, me.across[0], order[k]]
        core_copies.append((send(slot, slot, me.beside_core), me.across[0], order[k]))
        open_slot(me.core, me.across[0], order[k])
    for copied, dp, z in core_copies:
        copied.wait_recv()
        open_slot(me.other_core, dp, z)
    send.finish()
    write_weights(bases, wide, *outs)


def gather_weights(params, rows, width):
    slot_rows = params.shape[0]
    bases, count = row_bases(width, 4 * width)
    outs = weight_shapes(width)
    copies = 35
    values = pl.pallas_call(
        partial(gather_kernel, slot_rows, bases),
        out_shape=list(outs.values()),
        in_specs=[pl.BlockSpec(memory_space=pltpu.VMEM)],
        out_specs=[pl.BlockSpec(memory_space=pltpu.VMEM)] * len(outs),
        scratch_shapes=[
            pltpu.VMEM((rows, 128), BF),
            pltpu.VMEM((2, 4, 4, rows, 128), BF),
            pltpu.VMEM((3, -(-32 * slot_rows * 128 // width // 8) * 8 + 24, 128), F32),
            pltpu.VMEM((rows + 48, 128), F32),
            pltpu.SemaphoreType.DMA(()),
            pltpu.SemaphoreType.DMA((copies,)),
            pltpu.SemaphoreType.DMA((copies,)),
            pltpu.SemaphoreType.DMA((4,)),
        ],
        compiler_params=pltpu.CompilerParams(
            collective_id=0, has_side_effects=True, vmem_limit_bytes=VMEM_BYTES
        ),
        name="gather_weights",
    )(params)
    return dict(zip(outs, values, strict=True))


def reduce_kernel(slot_rows, bases, *refs):
    grads_far, (shard, squares), grads, fetch_sem = refs[:10], refs[10:12], refs[12:22], refs[22]
    wide, line, own, core_out, core_in, y_in, x_in, x_last, y_last, z_in, small, send_sem, recv_sem = refs[23:]
    me = Place()
    rows = shard.shape[0]
    half = rows // 2
    first, second = pl.ds(0, half), pl.ds(half, half)
    send = Sender(send_sem, recv_sem)
    peers = [(me.dp, (me.z + k) % 4 * 2 + core) for k in range(4) for core in (me.core, me.other_core)][1:]
    planes = [me.beside_x, me.beside_y, me.across]
    me.call(peers + planes)
    fetch = [pltpu.make_async_copy(x, y, fetch_sem.at[k]) for k, (x, y) in enumerate(zip(grads_far, grads))]
    for k in COLLECTED:
        fetch[k].start()
    collect_gradients(bases, wide, *grads, ready=lambda k: fetch[k].wait())
    line[...] = jnp.zeros_like(line)
    me.answer(len(peers + planes))
    units = [(me.z + k) % 4 for k in (2, 1, 3, 0)]
    core_copies, y_copies, x_copies, last = [], [], [], []
    other_x, other_y = 1 - me.x, 1 - me.y

    def give(k):
        z = units[k]
        for dp in range(4):
            join_slot(wide, dp * 8 + z * 2 + me.other_core, slot_rows, line)
            core_out[z, dp] = line[0:rows, :].astype(BF)
        core_copies.append(send(core_out.at[z], core_in.at[z], me.beside_core))
        for dp in range(4):
            join_slot(wide, dp * 8 + z * 2 + me.core, slot_rows, line)
            own[z, dp] = line[0:rows, :]

    def cores(k):
        z = units[k]
        core_copies[k].wait_recv()
        for dp in range(4):
            core_in[z, dp] = (core_in[z, dp].astype(F32) + own[z, dp]).astype(BF)
        y_copies.append(
            [send(core_in.at[z, 2 * other_y + x, first], y_in.at[z, x], me.beside_y) for x in range(2)]
        )
        x_copies.append(
            [send(core_in.at[z, 2 * y + other_x, second], x_in.at[z, y], me.beside_x) for y in range(2)]
        )

    def plane(k):
        z = units[k]
        for copied in y_copies[k]:
            copied.wait_recv()
        y_in[z, other_x] = (
            y_in[z, other_x].astype(F32) + core_in[z, 2 * me.y + other_x, first].astype(F32)
        ).astype(BF)
        to_x = send(y_in.at[z, other_x], x_last.at[z], me.beside_x)
        for copied in x_copies[k]:
            copied.wait_recv()
        x_in[z, other_y] = (
            x_in[z, other_y].astype(F32) + core_in[z, 2 * other_y + me.x, second].astype(F32)
        ).astype(BF)
        last.append((to_x, send(x_in.at[z, other_y], y_last.at[z], me.beside_y)))

    z_copies = []

    def column(k):
        z = units[k]
        for copied in last[k]:
            copied.wait_recv()
        low = y_in[z, me.x].astype(F32) + core_in[z, me.dp, first].astype(F32) + x_last[z].astype(F32)
        high = x_in[z, me.y].astype(F32) + core_in[z, me.dp, second].astype(F32) + y_last[z].astype(F32)
        if k == 3:
            shard[first, :] = low
            shard[second, :] = high
        else:
            z_in[k, first] = low.astype(BF)
            z_in[k, second] = high.astype(BF)
            z_copies.append(send(z_in.at[k], z_in.at[k + 3], me.at_z(z)))

    give(0)
    give(1)
    cores(0)
    give(2)
    cores(1)
    plane(0)
    give(3)
    cores(2)
    plane(1)
    column(0)
    cores(3)
    plane(2)
    column(1)
    plane(3)
    column(2)
    column(3)
    for k in (0, 1, 2):
        z_copies[k].wait_recv()
        shard[...] += z_in[k + 3].astype(F32)
    total = shard[0:8, :] * shard[0:8, :]
    for k in range(1, rows // 8):
        part = shard[8 * k : 8 * k + 8, :]
        total = total + part * part
    small[0] = total
    small[2 + me.fsdp] = total
    copies = [send(small.at[0], small.at[2 + me.fsdp], device) for device in peers]
    for copied in copies:
        copied.wait_recv()
    total = small[2]
    for k in range(1, 8):
        total = total + small[2 + k]
    small[1] = total
    small[10 + me.dp] = total
    copies = [send(small.at[1], small.at[10 + me.dp], device) for device in planes]
    for copied in copies:
        copied.wait_recv()
    squares[0, 0] = jnp.sum(((small[10] + small[11]) + small[12]) + small[13])
    send.finish()


def reduce_gradients(grads, slot_rows, rows, width):
    bases, _ = row_bases(width, 4 * width)
    half = rows // 2
    count = 4 + 16 + 8 + 3 + 7 + 3
    return pl.pallas_call(
        partial(reduce_kernel, slot_rows, bases),
        out_shape=[jax.ShapeDtypeStruct((rows, 128), F32), jax.ShapeDtypeStruct((1, 1), F32)],
        in_specs=[FAR] * len(grads),
        out_specs=[pl.BlockSpec(memory_space=pltpu.VMEM), pl.BlockSpec(memory_space=pltpu.SMEM)],
        scratch_shapes=[
            *[pltpu.VMEM(x.shape, x.dtype) for x in grads],
            pltpu.SemaphoreType.DMA((len(grads),)),
            pltpu.VMEM((3, -(-32 * slot_rows * 128 // width // 8) * 8 + 24, 128), F32),
            pltpu.VMEM((rows + 48, 128), F32),
            pltpu.VMEM((4, 4, rows, 128), F32),
            pltpu.VMEM((4, 4, rows, 128), BF),
            pltpu.VMEM((4, 4, rows, 128), BF),
            pltpu.VMEM((4, 2, half, 128), BF),
            pltpu.VMEM((4, 2, half, 128), BF),
            pltpu.VMEM((4, half, 128), BF),
            pltpu.VMEM((4, half, 128), BF),
            pltpu.VMEM((6, rows, 128), BF),
            pltpu.VMEM((14, 8, 128), F32),
            pltpu.SemaphoreType.DMA((count,)),
            pltpu.SemaphoreType.DMA((count,)),
        ],
        compiler_params=pltpu.CompilerParams(
            collective_id=1, has_side_effects=True, vmem_limit_bytes=VMEM_BYTES
        ),
        name="reduce_gradients",
    )(*grads)


def layout_shapes(model_width, hidden_width):
    return [
        ("pre_gain", (model_width,)),
        ("pre_shift", (model_width,)),
        ("query_weight", (model_width, model_width)),
        ("query_bias", (model_width,)),
        ("reduce_weight", (4 * model_width, model_width)),
        ("reduce_bias", (model_width,)),
        ("reduce_gain", (model_width,)),
        ("reduce_shift", (model_width,)),
        ("pair_weight", (model_width, 2 * model_width)),
        ("value_bias", (model_width,)),
        ("output_weight", (model_width, model_width)),
        ("output_bias", (model_width,)),
        ("mlp_gain", (model_width,)),
        ("mlp_shift", (model_width,)),
        ("expand_weight", (model_width, hidden_width)),
        ("expand_bias", (hidden_width,)),
        ("spatial_weight", (9, hidden_width)),
        ("spatial_bias", (hidden_width,)),
        ("shrink_weight", (hidden_width, model_width)),
        ("shrink_bias", (model_width,)),
    ]


def row_bases(width, hidden):
    bases = {}
    row = 0
    for name, shape in layout_shapes(width, hidden):
        bases[name] = row
        row += math.prod(shape) // width
    return bases, row


SPAN = 96


def regroup_lines(read, write, low):
    part = [read(k) for k in range(5)]
    turned = [pltpu.roll(part[k], 64, 1) for k in (2, 3, 4)]
    for k in range(3):
        write(0, k, part[k])
    write(1, 0, jnp.where(low, turned[0], turned[1]))
    write(1, 1, jnp.where(low, turned[1], turned[2]))
    write(1, 2, turned[2])


def spread_slot(values, slot, slot_rows, line, wide):
    pairs = slot_rows // 5
    line[0 : values.shape[0], :] = values.astype(F32)

    def part(start, count):
        low = lax.broadcasted_iota(jnp.int32, (count, 128), 1) < 64

        def write(parity, k, value):
            wide[k, pl.ds(slot * (2 * pairs) + 2 * start + parity, count, stride=2), :] = value

        regroup_lines(lambda k: line[pl.ds(5 * start + k, count, stride=5), :], write, low)

    part(0, pairs // 8 * 8)
    if pairs % 8:
        part(pairs // 8 * 8, pairs % 8)


def unpack_kernel(order, slot_rows, bases, slots, *refs):
    outs, (flat, wide) = refs[:13], refs[13:]
    for slot, place in enumerate(order):
        flat[pl.ds(slot * slot_rows, slots.shape[1]), :] = slots[place].astype(F32)
    low = lax.broadcasted_iota(jnp.int32, (SPAN, 128), 1) < 64

    def regroup(t, _):
        def write(parity, k, value):
            wide[k, pl.ds(t * (2 * SPAN) + parity, SPAN, stride=2), :] = value

        regroup_lines(lambda k: flat[pl.ds(t * (5 * SPAN) + k, SPAN, stride=5), :], write, low)
        return 0

    lax.fori_loop(0, wide.shape[1] // (2 * SPAN), regroup, 0)
    write_weights(bases, wide, *outs)


def write_weights(bases, wide, vec, rows, wq, wqt, wr, wk, wv, wvt, wo, wot, we, wst, taps):
    width = wq.shape[0]
    hidden = wst.shape[1]

    def take(base, count, stride=1):
        at = pl.ds(base, count, stride=stride) if stride > 1 else pl.ds(base, count)
        return jnp.concatenate([wide[0, at, :], wide[1, at, :], wide[2, at, :][:, 0 : width - 256]], axis=1)

    def take_hidden(base, count):
        return jnp.concatenate([take(base + q, count, hidden // width) for q in range(hidden // width)], axis=1)

    def bordered(weight, bias, extra):
        index = lax.broadcasted_iota(jnp.int32, (extra, weight.shape[1]), 0)
        return jnp.concatenate([weight, jnp.where(index == 0, bias, 0.0)], axis=0)

    names = ("pre_gain", "pre_shift", "mlp_gain", "mlp_shift", "shrink_bias")
    for k, name in enumerate(names):
        vec[k] = jnp.broadcast_to(take(bases[name], 1), (128, width)).T
    for k, name in enumerate(("reduce_bias", "reduce_gain", "reduce_shift")):
        rows[k : k + 1, :] = take(bases[name], 1)
    query = take(bases["query_weight"], width)
    wq[...] = query.astype(BF)
    wqt[...] = bordered(query, take(bases["query_bias"], 1), EXT).T.astype(BF)
    for p in range(4):
        wr[p] = take(bases["reduce_weight"] + p * width, width).astype(BF)
    wk[...] = take(bases["pair_weight"], width, 2).astype(BF)
    value = take(bases["pair_weight"] + 1, width, 2)
    wv[...] = value.astype(BF)
    wvt[...] = bordered(value, take(bases["value_bias"], 1), 64).T.astype(BF)
    out = take(bases["output_weight"], width)
    wo[...] = out.astype(BF)
    wot[...] = bordered(out, take(bases["output_bias"], 1), EXT).T.astype(BF)
    we[0:width, :] = take_hidden(bases["expand_weight"], width).astype(BF)
    we[width:DEPTH, :] = first_row(take_hidden(bases["expand_bias"], 1), DEPTH - width).astype(BF)
    taps[0:9, :] = take_hidden(bases["spatial_weight"], 9)
    taps[9:10, :] = take_hidden(bases["spatial_bias"], 1)
    wst[width:DEPTH, :] = jnp.zeros((DEPTH - width, hidden), BF)
    for k in range(hidden // 128):
        wst[0:width, 128 * k : 128 * k + 128] = take(bases["shrink_weight"] + 128 * k, 128).T.astype(BF)


def wide_rows(count):
    return -(-count // (2 * SPAN)) * 2 * SPAN


def weight_shapes(width):
    hidden = 4 * width
    shape = jax.ShapeDtypeStruct
    return dict(
        vec=shape((5, width, 128), F32),
        rows=shape((3, width), F32),
        wq=shape((width, width), BF),
        wqt=shape((width, width + EXT), BF),
        wr=shape((4, width, width), BF),
        wk=shape((width, width), BF),
        wv=shape((width, width), BF),
        wvt=shape((width, width + 64), BF),
        wo=shape((width, width), BF),
        wot=shape((width, width + EXT), BF),
        we=shape((DEPTH, hidden), BF),
        wst=shape((DEPTH, hidden), BF),
        taps=shape((10, hidden), F32),
    )


def unpack_weights(slots, order, slot_rows, width):
    bases, count = row_bases(width, 4 * width)
    outs = weight_shapes(width)
    flat_rows = max(len(order) * slot_rows, wide_rows(count) * width // 128) + slots.shape[1]
    values = pl.pallas_call(
        partial(unpack_kernel, order, slot_rows, bases),
        out_shape=list(outs.values()),
        in_specs=[pl.BlockSpec(memory_space=pltpu.VMEM)],
        out_specs=[pl.BlockSpec(memory_space=pltpu.VMEM)] * len(outs),
        scratch_shapes=[pltpu.VMEM((flat_rows, 128), F32), pltpu.VMEM((3, wide_rows(count), 128), F32)],
        compiler_params=pltpu.CompilerParams(vmem_limit_bytes=VMEM_BYTES),
        name="unpack_weights",
    )(slots)
    return dict(zip(outs, values, strict=True))


COLLECTED = (8, 3, 9, 5, 7, 6, 4, 2, 0, 1)


def collect_gradients(bases, wide, gwe, gwst, gtaps, gbias, gwo, gwq, gpair, gwr, gcols, grows, ready=lambda k: None):
    width = gwst.shape[0]
    hidden = gwst.shape[1]
    used = bases["shrink_bias"] + 1
    for k in range(3):
        wide[k, pl.ds(used, wide.shape[1] - used), :] = jnp.zeros((wide.shape[1] - used, 128), F32)

    def put(base, value, stride=1):
        count = value.shape[0]
        at = pl.ds(base, count, stride=stride) if stride > 1 else pl.ds(base, count)
        wide[0, at, :] = value[:, 0:128]
        wide[1, at, :] = value[:, 128:256]
        wide[2, at, 0 : width - 256] = value[:, 256:width]

    ready(8)
    for k, name in enumerate(("pre_gain", "pre_shift", "mlp_gain", "mlp_shift")):
        put(bases[name], jnp.sum(gcols[k].T, axis=0, keepdims=True))
    ready(3)
    put(bases["shrink_bias"], jnp.sum(gbias[...].T, axis=0, keepdims=True))
    ready(9)
    for k, name in enumerate(("reduce_bias", "reduce_gain", "reduce_shift")):
        put(bases[name], jnp.sum(grows[8 * k : 8 * k + 8, :], axis=0, keepdims=True))
    ready(5)
    put(bases["query_weight"], gwq[0 : width + 1, :])
    ready(7)
    for p in range(4):
        put(bases["reduce_weight"] + p * width, gwr[p].T)
    ready(6)
    put(bases["pair_weight"], gpair[0:width, :].T[0:width], 2)
    value = gpair[width : 2 * width, :].T
    put(bases["pair_weight"] + 1, value[0:width], 2)
    put(bases["value_bias"], value[width : width + 1])
    ready(4)
    put(bases["output_weight"], gwo[0 : width + 1, :])
    ready(2)
    sums = jnp.concatenate(
        [jnp.sum(gtaps[8 * k : 8 * k + 8, :], axis=0, keepdims=True) for k in range(10)], axis=0
    )
    ready(0)
    for q in range(hidden // width):
        put(bases["expand_weight"] + q, gwe[0 : width + 1, q * width : (q + 1) * width], hidden // width)
        put(bases["spatial_weight"] + q, sums[:, q * width : (q + 1) * width], hidden // width)
    ready(1)
    for k in range(hidden // 128):
        put(bases["shrink_weight"] + 128 * k, gwst[:, 128 * k : 128 * k + 128].T)

def join_lines(read, write, low):
    turned = [pltpu.roll(read(1, k), 64, 1) for k in range(3)]
    write(0, read(0, 0))
    write(1, read(0, 1))
    write(2, jnp.where(low, read(0, 2), turned[0]))
    write(3, jnp.where(low, turned[0], turned[1]))
    write(4, jnp.where(low, turned[1], turned[2]))


def join_slot(wide, slot, slot_rows, line):
    pairs = slot_rows // 5

    def part(start, count):
        low = lax.broadcasted_iota(jnp.int32, (count, 128), 1) < 64

        def read(parity, k):
            return wide[k, pl.ds(slot * (2 * pairs) + 2 * start + parity, count, stride=2), :]

        def write(k, value):
            line[pl.ds(5 * start + k, count, stride=5), :] = value

        join_lines(read, write, low)

    part(0, pairs // 8 * 8)
    if pairs % 8:
        part(pairs // 8 * 8, pairs % 8)


def pack_kernel(order, slot_rows, bases, *refs):
    grads, (slots, flat, wide) = refs[:10], refs[10:]
    collect_gradients(bases, wide, *grads)
    done = wide.shape[1] * 5 // 2
    flat[done:, :] = jnp.zeros((flat.shape[0] - done, 128), F32)
    low = lax.broadcasted_iota(jnp.int32, (SPAN, 128), 1) < 64

    def regroup(t, _):
        def read(parity, k):
            return wide[k, pl.ds(t * (2 * SPAN) + parity, SPAN, stride=2), :]

        def write(k, value):
            flat[pl.ds(t * (5 * SPAN) + k, SPAN, stride=5), :] = value

        join_lines(read, write, low)
        return 0

    lax.fori_loop(0, wide.shape[1] // (2 * SPAN), regroup, 0)
    inside = lax.broadcasted_iota(jnp.int32, slots.shape[1:], 0) < slot_rows
    for slot, place in enumerate(order):
        slots[place] = jnp.where(inside, flat[pl.ds(slot * slot_rows, slots.shape[1]), :], 0.0).astype(BF)


def pack_gradients(grads, order, slot_rows, padded_rows, width):
    bases, count = row_bases(width, 4 * width)
    flat_rows = max(len(order) * slot_rows, wide_rows(count) * width // 128) + padded_rows
    return pl.pallas_call(
        partial(pack_kernel, order, slot_rows, bases),
        out_shape=jax.ShapeDtypeStruct((len(order), padded_rows, 128), BF),
        in_specs=[pl.BlockSpec(memory_space=pltpu.VMEM)] * len(grads),
        out_specs=pl.BlockSpec(memory_space=pltpu.VMEM),
        scratch_shapes=[pltpu.VMEM((flat_rows, 128), F32), pltpu.VMEM((3, wide_rows(count), 128), F32)],
        compiler_params=pltpu.CompilerParams(vmem_limit_bytes=VMEM_BYTES),
        name="pack_gradients",
    )(*grads)


def device_step(images, cotangent, kv_sides, w):
    positions = jnp.arange(TOKENS, dtype=jnp.int32)
    limit = 2 * kv_sides[:, None]
    mask = ((positions[None] // GRID < limit) & (positions[None] % GRID < limit)).astype(F32)
    mask = mask[:, None, :]
    perm = jnp.asarray(patch_order(), BF)
    pre, patches, reduced, memory, mixed, lse, middle, post = attention_forward(
        kv_sides, images, mask, perm, w["vec"], w["rows"], w["wqt"], w["wr"], w["wk"], w["wvt"], w["wot"]
    )
    output, grad_post, gwe, gwst, gtaps, gbias = feed_forward(
        post, cotangent, mask, middle, w["we"], w["wst"], w["taps"], w["vec"]
    )
    grad_images, gwo, gwq, gpair, gwr, gcols, grows = attention_backward(
        kv_sides, images, cotangent, mask, pre, patches, reduced, memory, mixed, lse, middle, grad_post,
        perm, w["vec"], w["rows"], w["wq"], w["wqt"], w["wr"], w["wk"], w["wv"], w["wvt"], w["wo"],
    )
    return output, grad_images, (gwe, gwst, gtaps, gbias, gwo, gwq, gpair, gwr, gcols, grows)


def step(on_grid, images, cotangent, kv_sides, params, first_moment, second_moment):
    width = images.shape[2]
    axes = ("dp", "fsdp")
    outer, inner = lax.axis_size("dp"), lax.axis_size("fsdp")
    slot_rows = params.shape[0] // 128
    padded_rows = -(-slot_rows // 32) * 32
    order = list(range(outer * inner))
    if on_grid:
        weights = gather_weights(params.reshape(slot_rows, 128), padded_rows, width)
    else:
        own = jnp.pad(params.reshape(slot_rows, 128).astype(BF), ((0, padded_rows - slot_rows), (0, 0)))
        weights = unpack_weights(lax.all_gather(own, axes), order, slot_rows, width)
    output, grad_images, grads = device_step(
        images.transpose(0, 2, 1), cotangent.transpose(0, 2, 1), kv_sides, weights
    )
    if on_grid:
        shard, squares = reduce_gradients(grads, slot_rows, padded_rows, width)
        squares = squares[0, 0]
    else:
        slots = pack_gradients(grads, order, slot_rows, padded_rows, width)
        shard = lax.psum_scatter(slots.astype(F32), axes)
        squares = lax.psum(jnp.sum(shard * shard), axes)
    shard = shard[:slot_rows].reshape(-1)
    grad_norm = jnp.sqrt(squares)
    clipped = shard * jnp.minimum(1.0, CLIP_NORM / (grad_norm + 1e-06))
    new_first = BETA_FIRST * first_moment + (1.0 - BETA_FIRST) * clipped
    new_second = BETA_SECOND * second_moment + (1.0 - BETA_SECOND) * clipped * clipped
    first_hat = new_first / (1.0 - BETA_FIRST**STEP)
    second_hat = new_second / (1.0 - BETA_SECOND**STEP)
    new_params = params - RATE * (first_hat / (jnp.sqrt(second_hat) + EPSILON) + DECAY * params)
    return (
        output.transpose(0, 2, 1),
        grad_images.transpose(0, 2, 1),
        grad_norm,
        new_first,
        new_second,
        new_params,
    )


def solution(mesh):
    data = P(("dp", "fsdp"), None, None)
    flat = P(("dp", "fsdp"))
    on_grid = dict(mesh.shape) == {"dp": 4, "fsdp": 8}
    return jax.shard_map(
        partial(step, on_grid),
        mesh=mesh,
        in_specs=(data, data, flat, flat, flat, flat),
        out_specs=(data, data, P(), flat, flat, flat),
        check_vma=False,
    )
```
